256 devices in a mesh: lon: 8 (over y, x_hi), lat: 16 (over z, core), batch: 2 (over x_lo).
Axes of the slice: x: 4 (x_hi: 2, x_lo: 2; x = x_hi * 2 + x_lo), y: 4, z: 8, core: 2. Of those that a mesh axis runs over, the one named last changes fastest.
Arguments:
- fields: bfloat16 [576, 384, 512], P(('batch', 'lat'), 'lon'), parts along dimension 0, may hold values from -6 to 6
- grad_out: bfloat16 [576, 384, 512], P(('batch', 'lat'), 'lon'), parts along dimension 0, may hold values from -6 to 6
- layernorm_gain: float32 [512], replicated, may hold values from 0.1 to 1.9
- qkv_weight: bfloat16 [512, 1536], replicated, may hold values from -0.25 to 0.25
- proj_weight: bfloat16 [512, 512], replicated, may hold values from -0.25 to 0.25
- bias_table: float32 [8, 253], replicated, may hold values from -4 to 350
- sea_mask: int32 [576, 384], P(('batch', 'lat'), 'lon'), parts along dimension 0, may hold values from 0 to 1, as said below
Outputs:
- updated: bfloat16 [576, 384, 512], P(('batch', 'lat'), 'lon'), parts along dimension 0
- grad_in: bfloat16 [576, 384, 512], P(('batch', 'lat'), 'lon'), parts along dimension 0
- grad_gain: float32 [1024], P('batch'), parts along dimension 0
- grad_bias: float32 [16, 253], P('batch'), parts along dimension 0
- grad_qkv: float32 [1024, 1536], P(('batch', 'lon', 'lat')), parts along dimension 0
- grad_proj: float32 [1024, 512], P(('batch', 'lon', 'lat')), parts along dimension 0
The draws below stay inside these ranges and needn't reach their ends.
There are 2 independent parts, one for each index of `batch`. The reference program is written for one: setup_inputs(seed, part) draws one part's arguments, and reference() takes and returns one part's arrays. A program takes and returns all parts, laid end to end along the dimension named above; an argument that names none is the same for every part. Nothing has to cross between parts.
Inputs may be any that keep to these rules, and one draw needn't show every extreme that they name: `sea_mask`: among the shifted windows whose rows r and columns s lie in one device's block (r from the device's first row, s from its first column, as defined in the reference program), at most 9 hold a sea token; in every draw some device has exactly 9.
All inputs are finite; a program needn't handle non-finite values.
Results may differ from the reference program's by a relative error of at most 0.0093.
Values may be sent and summed in bfloat16 or wider, within the bound.
A program may use at most 128 MiB of HBM per device.

```python
import jax
import jax.numpy as jnp
import numpy as np
from jax import lax

C = 512
HEADS = 8
HEAD_DIM = 64
WIN_LAT = 6
WIN_LON = 12
LAT_DEV = 18
LON_DEV = 48
LAT = 288
LON = 384
REL = 253
WIN_DEV = 12
ACT_CAP = 9


def draw_bias_table(key, part):
    key = jax.random.fold_in(key, 23)
    base = jnp.clip(jax.random.normal(key, (HEADS, REL), jnp.float32), -4.0, 4.0)
    return base


def draw_sea_mask(key, part):
    key = jax.random.fold_in(key, 11)
    key_count, key_pick, key_rank, key_cells = jax.random.split(key, 4)
    dev_rows = LAT // LAT_DEV
    dev_cols = LON // LON_DEV
    win_rows = LAT_DEV // WIN_LAT
    win_cols = LON_DEV // WIN_LON
    devices = dev_rows * dev_cols
    counts = jax.random.randint(key_count, (devices,), 1, ACT_CAP + 1)
    chosen = jax.random.randint(key_pick, (), 0, devices)
    counts = jnp.where(jnp.arange(devices) == chosen, ACT_CAP, counts)
    ranking = jax.random.randint(key_rank, (devices, WIN_DEV), 0, 1 << 20) * WIN_DEV + jnp.arange(WIN_DEV)
    places = jnp.argsort(jnp.argsort(ranking, axis=1), axis=1)
    active = (places < counts[:, None]).astype(jnp.int32)
    active = active.reshape(dev_rows, dev_cols, win_rows, win_cols).transpose(0, 2, 1, 3)
    active = active.reshape(dev_rows * win_rows, dev_cols * win_cols)
    cells = jax.random.randint(key_cells, (LAT, LON), 0, 10)
    token_sea = (cells < 6).astype(jnp.int32)
    row_pos = jnp.arange(LAT) % WIN_LAT
    col_pos = jnp.arange(LON) % WIN_LON
    corner = jnp.logical_and(row_pos[:, None] == 0, col_pos[None, :] == 0).astype(jnp.int32)
    grid_active = jnp.repeat(jnp.repeat(active, WIN_LAT, axis=0), WIN_LON, axis=1)
    framed = grid_active * jnp.maximum(token_sea, corner)
    return jnp.roll(framed, (WIN_LAT // 2, WIN_LON // 2), (0, 1))


def shard_levels(key, extent, cuts, low, top_value):
    loudness = 1.0
    for axis_at, shards_of in cuts:
        draws = jax.random.uniform(jax.random.fold_in(jax.random.fold_in(key, 6), axis_at), (shards_of,), jnp.float32, low / len(cuts), top_value / len(cuts))
        loudness = loudness * jnp.repeat(jnp.exp(draws), extent[axis_at] // shards_of).reshape((-1,) + (1,) * (len(extent) - 1 - axis_at))
    return loudness


def normal_values(key, dims, deviation, most, cuts=(), held_as=jnp.bfloat16):
    result = jax.random.normal(key, dims, jnp.float32) * deviation
    if len(cuts) > 0:
        result = shard_levels(key, dims, cuts, -0.22, 0.18) * result
    return jnp.clip(result, min=-most, max=most).astype(held_as)


def setup_inputs(seed: int = 0, part: int = 0) -> dict:
    key_list = jax.random.split(jax.random.key(seed), 8)
    own_keys = jax.random.split(jax.random.fold_in(key_list[7], part), 8)
    return {
        "fields": normal_values(own_keys[0], (LAT, LON, C), 1.0, 6.0, ((0, 16), (1, 8))),
        "grad_out": normal_values(own_keys[1], (LAT, LON, C), 1.0, 6.0, ((0, 16), (1, 8))),
        "layernorm_gain": jnp.clip(1.0 + 0.18 * jax.random.normal(key_list[2], (C,), jnp.float32), 0.1, 1.9),
        "qkv_weight": normal_values(key_list[3], (C, 3 * C), C ** -0.5, 0.25),
        "proj_weight": normal_values(key_list[4], (C, C), C ** -0.5, 0.25),
        "bias_table": draw_bias_table(jax.random.fold_in(key_list[7], 71), part),
        "sea_mask": draw_sea_mask(jax.random.fold_in(jax.random.fold_in(key_list[7], part), 71), part),
    }


def relative_index():
    places = np.arange(WIN_LAT * WIN_LON)
    row_of = places // WIN_LON
    col_of = places % WIN_LON
    return (row_of[:, None] - row_of[None, :] + WIN_LAT - 1) * (2 * WIN_LON - 1) + (col_of[:, None] - col_of[None, :] + WIN_LON - 1)

def contract(form, left, right):
    return jnp.einsum(form, left.astype(jnp.float32), right.astype(jnp.float32))

def window_forward(windows_x, window_sea, window_class, layernorm_gain, qkv_weight, proj_weight, position_bias):
    win_count, tokens, model_width = windows_x.shape
    score_scale = HEAD_DIM ** (-0.5)
    fields32 = windows_x.astype(jnp.float32)
    average = lax.optimization_barrier(jnp.mean(fields32, axis=-1, keepdims=True))
    mean_removed = fields32 - average
    inverse_deviation = lax.rsqrt(lax.optimization_barrier(jnp.mean(mean_removed * mean_removed, axis=-1, keepdims=True)) + 1e-05)
    standardized_input = mean_removed * inverse_deviation
    normalized_input = (standardized_input * layernorm_gain).astype(jnp.bfloat16)
    packed = contract('btc,cf->btf', normalized_input, qkv_weight).astype(jnp.bfloat16)
    head_parts = packed.reshape(win_count, tokens, 3, HEADS, HEAD_DIM)
    query_rows = head_parts[:, :, 0]
    key_portion = head_parts[:, :, 1]
    value_rows = head_parts[:, :, 2]
    scores = contract('bqhd,bkhd->bhqk', query_rows, key_portion) * score_scale + position_bias[None]
    allowed = window_class[:, None, :, None] == window_class[:, None, None, :]
    scores = jnp.where(allowed, scores, -1000000000.0)
    attention_weights = jax.nn.softmax(scores, axis=-1)
    rounded_values = attention_weights.astype(jnp.bfloat16)
    attended_tokens = contract('bhqk,bkhd->bqhd', rounded_values, value_rows).astype(jnp.bfloat16).reshape(win_count, tokens, model_width)
    projected = contract('btc,cd->btd', attended_tokens, proj_weight)
    ocean_weight = window_sea.astype(jnp.float32)[..., None]
    sublayer_output = (fields32 + ocean_weight * projected).astype(jnp.bfloat16)
    return (sublayer_output, (standardized_input, inverse_deviation, normalized_input, query_rows, key_portion, value_rows, attention_weights, rounded_values, attended_tokens, ocean_weight))

def window_backward(saved_residuals, window_dy, layernorm_gain, qkv_weight, proj_weight):
    standardized_input, inverse_deviation, normalized_input, query_rows, key_portion, value_rows, attention_weights, rounded_values, attended_tokens, ocean_weight = saved_residuals
    win_count, tokens, model_width = normalized_input.shape
    score_scale = HEAD_DIM ** (-0.5)
    dy_float = window_dy.astype(jnp.float32)
    grad_z = (ocean_weight * dy_float).astype(jnp.bfloat16)
    grad_mixed = contract('btd,cd->btc', grad_z, proj_weight).astype(jnp.bfloat16)
    grad_heads = grad_mixed.reshape(win_count, tokens, HEADS, HEAD_DIM)
    grad_probs = contract('bqhd,bkhd->bhqk', grad_heads, value_rows)
    grad_values = contract('bhqk,bqhd->bkhd', rounded_values, grad_heads).astype(jnp.bfloat16)
    grad_scores = attention_weights * (grad_probs - lax.optimization_barrier(jnp.sum(attention_weights * grad_probs, axis=-1, keepdims=True)))
    scaled = (grad_scores * score_scale).astype(jnp.bfloat16)
    grad_query = contract('bhqk,bkhd->bqhd', scaled, key_portion).astype(jnp.bfloat16)
    grad_keys = contract('bhqk,bqhd->bkhd', scaled, query_rows).astype(jnp.bfloat16)
    grad_packed = jnp.stack([grad_query, grad_keys, grad_values], axis=2).reshape(win_count, tokens, 3 * model_width)
    gradient_normalized = contract('btf,cf->btc', grad_packed, qkv_weight)
    gain_product = lax.optimization_barrier(jnp.sum(gradient_normalized * standardized_input, axis=(0, 1)))
    gradient_standardized = gradient_normalized * layernorm_gain
    inner_product = gradient_standardized - lax.optimization_barrier(jnp.mean(gradient_standardized, axis=-1, keepdims=True)) - standardized_input * lax.optimization_barrier(jnp.mean(gradient_standardized * standardized_input, axis=-1, keepdims=True))
    grad_fields = (dy_float + inverse_deviation * inner_product).astype(jnp.bfloat16)
    bias_term = lax.optimization_barrier(jnp.sum(grad_scores, axis=0))
    return (grad_fields, grad_packed, grad_z, gain_product, bias_term)

def to_windows(grid):
    lat_wins = grid.shape[0] // WIN_LAT
    lon_wins = grid.shape[1] // WIN_LON
    shaped = grid.reshape(lat_wins, WIN_LAT, lon_wins, WIN_LON, grid.shape[2]).transpose(0, 2, 1, 3, 4)
    return shaped.reshape(lat_wins, lon_wins, WIN_LAT * WIN_LON, grid.shape[2])

def from_windows(windows):
    lat_wins, lon_wins = (windows.shape[0], windows.shape[1])
    shaped = windows.reshape(lat_wins, lon_wins, WIN_LAT, WIN_LON, windows.shape[-1]).transpose(0, 2, 1, 3, 4)
    return shaped.reshape(lat_wins * WIN_LAT, lon_wins * WIN_LON, windows.shape[-1])

def reference(fields, grad_out, layernorm_gain, qkv_weight, proj_weight, bias_table, sea_mask):
    half_lat = WIN_LAT // 2
    half_lon = WIN_LON // 2
    rolled_x = jnp.roll(fields, (-half_lat, -half_lon), (0, 1))
    rolled_dy = jnp.roll(grad_out, (-half_lat, -half_lon), (0, 1))
    rolled_sea = jnp.roll(sea_mask, (-half_lat, -half_lon), (0, 1))
    wrap_side = (jnp.arange(LAT) >= LAT - half_lat).astype(jnp.int32)
    rolled_class = rolled_sea + 2 * wrap_side[:, None]
    windows_x = to_windows(rolled_x)
    windows_dy = to_windows(rolled_dy)
    windows_sea = to_windows(rolled_sea[..., None])[..., 0]
    windows_class = to_windows(rolled_class[..., None])[..., 0]
    rel_index = relative_index()
    position_bias = bias_table[:, rel_index]

    def visit(totals, block_item):
        block_x, block_dy, block_sea, block_class = block_item
        block_out, saved_residuals = window_forward(block_x, block_sea, block_class, layernorm_gain, qkv_weight, proj_weight, position_bias)
        block_dx, grad_packed, grad_z, gain_product, bias_term = window_backward(saved_residuals, block_dy, layernorm_gain, qkv_weight, proj_weight)
        normalized_input = saved_residuals[2]
        attended_tokens = saved_residuals[8]
        qkv_total = totals[0] + jnp.dot(normalized_input.reshape(-1, C).T, grad_packed.reshape(-1, 3 * C), preferred_element_type=jnp.float32)
        proj_total = totals[1] + jnp.dot(attended_tokens.reshape(-1, C).T, grad_z.reshape(-1, C), preferred_element_type=jnp.float32)
        return ((qkv_total, proj_total, totals[2] + gain_product, totals[3] + bias_term), (block_out, block_dx))
    start_totals = (jnp.zeros((C, 3 * C), jnp.float32), jnp.zeros((C, C), jnp.float32), jnp.zeros((C,), jnp.float32), jnp.zeros((HEADS, WIN_LAT * WIN_LON, WIN_LAT * WIN_LON), jnp.float32))
    totals, (out_windows, dx_windows) = lax.scan(visit, start_totals, (windows_x, windows_dy, windows_sea, windows_class))
    updated = jnp.roll(from_windows(out_windows), (half_lat, half_lon), (0, 1))
    grad_in = jnp.roll(from_windows(dx_windows), (half_lat, half_lon), (0, 1))
    grad_bias = jnp.zeros((HEADS, REL), jnp.float32).at[:, rel_index.reshape(-1)].add(totals[3].reshape(HEADS, -1))
    return (updated, grad_in, totals[2], grad_bias, totals[0], totals[1])
```

```python
import functools

import jax
import jax.numpy as jnp
import numpy as np
from jax import lax
from jax.experimental import pallas as pl
from jax.experimental.pallas import tpu as pltpu
from jax.sharding import PartitionSpec as P

MESH = pl.DeviceIdType.MESH
F32 = jnp.float32
BF16 = jnp.bfloat16
C = 512
HEADS = 8
PAIRS = 4
WIN_LAT = 6
WIN_LON = 12
HALF_LAT = 3
HALF_LON = 6
T = 72
TP = 80
SLOTS = 9
ROWS = SLOTS * TP
RP = 768
REL = 253
X0, D0, M0, FW = 0, 512, 1024, 1152
EPS = 1e-5


def nn(a, b, **kw):
    return lax.dot_general(a, b, (((1,), (0,)), ((), ())), preferred_element_type=F32, **kw)


def nt(a, b, **kw):
    return lax.dot_general(a, b, (((1,), (1,)), ((), ())), preferred_element_type=F32, **kw)


def tn(a, b, **kw):
    return lax.dot_general(a, b, (((0,), (0,)), ((), ())), preferred_element_type=F32, **kw)


def pad_rows(v, rows):
    return jnp.concatenate([v, jnp.zeros((rows - v.shape[0], v.shape[1]), v.dtype)], axis=0)


def kernel(dims, cols, *refs):
    ny, nx, nz = dims
    nlon, nlat = ny * nx, 2 * nz
    nxz = nx * nz
    lat_dev, lon_dev = 18, 48
    wrows, wcols = lat_dev // WIN_LAT, lon_dev // WIN_LON
    nwin = wrows * wcols
    half = C // 2
    ysz = half // ny
    share = ysz // nxz
    nchunk = len(cols)

    it = iter(refs)
    take = lambda n=None: next(it) if n is None else [next(it) for _ in range(n)]
    x_ref, dy_ref, mask_ref, gain_ref, wqkv, wproj, table, perm, selr, self_ = take(10)
    upd, gin, gain_out, bias_out, gqkv, gproj = take(6)
    frame, win, colf, colsend, colrecv, rowsend, rowrecv, cornrecv = take(8)
    idx = take()
    tb, bias2, madd, xhat, invd, normed, gz, gm, packed, mixed, ntp, mtp, probs, dp3, gnacc, bacc = take(16)
    res, of, tmp = take(3)
    ocs, ors, ocr, orr, occ = take(5)
    chunks = [take(7) for _ in range(nchunk)]
    sm, smc, smy, smx = take(4)
    hs, hr, os_, or_, as_, ar, ys, yr, xs, xr, ss, sr = take(12)

    lon = lax.axis_index("lon")
    lat = lax.axis_index("lat")
    y, xh = lon // nx, lon % nx
    z, core = lat // 2, lat % 2

    def dev(a, b):
        return {"lon": a, "lat": b}

    partner = dev(lon, z * 2 + (1 - core))
    ypeer = [dev(((y + d) % ny) * nx + xh, lat) for d in range(1, ny)]
    xzd = [(a, b) for a in range(nx) for b in range(nz) if (a, b) != (0, 0)]
    xzpeer = [dev(y * nx + (xh + a) % nx, ((z + b) % nz) * 2 + core) for a, b in xzd]
    west, east = (lon + nlon - 1) % nlon, (lon + 1) % nlon
    north, south = (lat + nlat - 1) % nlat, (lat + 1) % nlat
    back = [dev(west, lat), dev(lon, north), dev(west, north)]
    forth = [dev(east, lat), dev(lon, south), dev(east, south)]

    barrier = pltpu.get_barrier_semaphore()
    everyone = [partner] + ypeer + xzpeer + back + forth
    for d in everyone:
        pl.semaphore_signal(barrier, inc=1, device_id=d, device_id_type=MESH)

    sends = []

    def send(src, dst, ssem, rsem, d):
        copy = pltpu.make_async_remote_copy(
            src_ref=src, dst_ref=dst, send_sem=ssem, recv_sem=rsem, device_id=d, device_id_type=MESH
        )
        copy.start()
        sends.append(copy)
        return copy

    lane_row = lax.broadcasted_iota(jnp.int32, (lat_dev, lat_dev * 128), 1) // 128
    pick = (lane_row == lax.broadcasted_iota(jnp.int32, (lat_dev, lat_dev * 128), 0)).astype(F32)
    sea = tn(mask_ref[...].astype(F32), pick)
    for r in range(lat_dev):
        frame[r, 0:lon_dev, X0 : X0 + C] = x_ref[r].astype(F32)
        frame[r, 0:lon_dev, D0 : D0 + C] = dy_ref[r].astype(F32)
        frame[r, 0:lon_dev, M0:FW] = sea[:, 128 * r : 128 * r + 128]
    colf[96:112, :] = jnp.zeros((16, FW), F32)
    for r in range(lat_dev):
        colf[6 * r : 6 * r + 6, :] = frame[r, 0:HALF_LON, :]
    colsend[...] = colf[...].astype(BF16)
    for r in range(HALF_LAT):
        rowsend[r] = frame[r, 0:lon_dev, :].astype(BF16)
    pl.semaphore_wait(barrier, len(everyone))
    halo = [
        send(colsend, colrecv, hs.at[0], hr.at[0], back[0]),
        send(rowsend, rowrecv, hs.at[1], hr.at[1], back[1]),
        send(colsend.at[0:32], cornrecv, hs.at[2], hr.at[2], back[2]),
    ]

    tb[...] = jnp.zeros_like(tb)
    tb[:, 0:REL] = table[...]
    hi = lax.Precision.HIGHEST
    for h in range(HEADS):
        line = jnp.broadcast_to(tb[h : h + 1, :], (128, 256))
        rolled = pltpu.roll(pltpu.roll(line, 2, 1), 128, 1, stride=1, stride_axis=0)
        both = nt(nn(selr[...], rolled[:, 0:128], precision=hi), selr[...], precision=hi)
        bias2[h // 2, TP * (h % 2) : TP * (h % 2) + TP, :] = both[0:TP]

    halo[0].wait_recv()
    colf[...] = colrecv[...].astype(F32)
    for r in range(lat_dev):
        frame[r, lon_dev : lon_dev + HALF_LON, :] = colf[6 * r : 6 * r + 6, :]
    halo[2].wait_recv()
    colf[0:32, :] = cornrecv[...].astype(F32)
    for r in range(HALF_LAT):
        frame[lat_dev + r, lon_dev : lon_dev + HALF_LON, :] = colf[6 * r : 6 * r + 6, :]
    halo[1].wait_recv()
    for r in range(HALF_LAT):
        frame[lat_dev + r, 0:lon_dev, :] = rowrecv[r].astype(F32)

    for w in range(nwin):
        wr, wc = w // wcols, w % wcols
        win[w, T:TP, :] = jnp.zeros((TP - T, FW), F32)
        for i in range(WIN_LAT):
            c0 = HALF_LON + WIN_LON * wc
            win[w, WIN_LON * i : WIN_LON * i + WIN_LON, :] = frame[
                HALF_LAT + WIN_LAT * wr + i, c0 : c0 + WIN_LON, :
            ]

    active = [(jnp.max(win[w, :, M0:FW]) > 0.5).astype(jnp.int32) for w in range(nwin)]
    total = functools.reduce(lambda a, b: a + b, active)
    place, seen = [], jnp.int32(0)
    for w in range(nwin):
        place.append(jnp.where(active[w] > 0, seen, total + (w - seen)))
        seen = seen + active[w]
    for k in range(SLOTS):
        slot = jnp.int32(0)
        for w in range(nwin):
            slot = slot + jnp.where(place[w] == k, w, 0)
        idx[k] = slot

    at_end = (lat == nlat - 1).astype(F32)
    gain = gain_ref[...]
    zero_tail = jnp.zeros((RP - ROWS, C), BF16)
    normed[ROWS:RP, :] = zero_tail
    gz[ROWS:RP, :] = zero_tail
    mixed[ROWS:RP, :] = zero_tail
    for p in range(PAIRS):
        dp3[p, ROWS:RP, :] = jnp.zeros((RP - ROWS, 384), BF16)

    def rows_of(k):
        return pl.ds(pl.multiple_of(k * TP, TP), TP)

    def ln_step(k, carry):
        w = idx[k]
        x = win[w, :, X0 : X0 + C]
        mean = jnp.mean(x, axis=1, keepdims=True)
        xc = x - mean
        inv = lax.rsqrt(jnp.mean(xc * xc, axis=1, keepdims=True) + EPS)
        hat = xc * inv
        rows = rows_of(k)
        xhat[rows, :] = hat
        invd[rows, :] = jnp.broadcast_to(inv, (TP, 128))
        normed[rows, :] = (hat * gain).astype(BF16)
        m = win[w, :, M0:FW]
        gz[rows, :] = (win[w, :, D0 : D0 + C] * jnp.concatenate([m] * 4, axis=1)).astype(BF16)
        keys = jnp.transpose(pad_rows(m, 128))[0:TP, :]
        side_a = lax.broadcasted_iota(jnp.int32, (TP, 128), 0) >= T // 2
        side_b = lax.broadcasted_iota(jnp.int32, (TP, 128), 1) >= T // 2
        apart = jnp.where(side_a != side_b, 1.0, 0.0)
        wrap = at_end * jnp.where(w >= nwin - wcols, 1.0, 0.0)
        open_ = keys * (1.0 - apart * wrap)
        madd[k] = (open_ - 1.0) * 1e9
        return carry

    lax.fori_loop(0, SLOTS, ln_step, 0)

    packed[...] = nn(normed[0:ROWS, :], wqkv[...]).astype(BF16)
    gm[...] = nt(gz[0:ROWS, :], wproj[...]).astype(BF16)
    ntp[...] = nt(perm[...], normed[...]).astype(BF16)

    lane = lax.broadcasted_iota(jnp.int32, (TP, 128), 1)
    low = lane < 64
    one_lo = jnp.where(low, 1.0, 0.0).astype(BF16)
    one_hi = jnp.where(low, 0.0, 1.0).astype(BF16)
    q_lo = jnp.where(low, 0.125, 0.0).astype(BF16)
    q_hi = jnp.where(low, 0.0, 0.125).astype(BF16)

    def attend(k, carry):
        rows = rows_of(k)
        add = madd[k]
        add2 = jnp.concatenate([add, add], axis=0)
        scores = []
        for p in range(PAIRS):
            q = packed[rows, 128 * p : 128 * p + 128]
            kk = pad_rows(packed[rows, C + 128 * p : C + 128 * p + 128], 128)
            q2 = jnp.concatenate([q * q_lo, q * q_hi], axis=0)
            scores.append(nt(q2, kk) + bias2[p] + add2)
        weights = []
        for p in range(PAIRS):
            s = scores[p]
            e = jnp.exp(s - jnp.max(s, axis=1, keepdims=True))
            weights.append(e * (1.0 / jnp.sum(e, axis=1, keepdims=True)))
        for p in range(PAIRS):
            probs[k * PAIRS + p] = weights[p]
            v = pad_rows(packed[rows, 2 * C + 128 * p : 2 * C + 128 * p + 128], 128)
            mix = nn(weights[p].astype(BF16), v)
            mixed[rows, 128 * p : 128 * p + 128] = jnp.where(low, mix[0:TP], mix[TP : 2 * TP]).astype(BF16)
        return carry

    lax.fori_loop(0, SLOTS, attend, 0)

    def chunk_start(c, lhs, rhs):
        asend, arecv, own = chunks[c][0:3]
        right = rhs[...]
        other = pl.multiple_of((1 - core) * half, half)
        mine = pl.multiple_of(core * half, half)
        asend[...] = nn(lhs[pl.ds(other, half), :], right).astype(BF16)
        copy = send(asend, arecv, as_.at[c], ar.at[c], partner)
        own[...] = nn(lhs[pl.ds(mine, half), :], right)
        return [copy]

    def chunk_y(c, copies):
        asend, arecv, own, ysend, yrecv = chunks[c][0:5]
        copies[0].wait_recv()
        s = own[...] + arecv[...].astype(F32)
        own[...] = s
        ysend[...] = s.astype(BF16)
        out = []
        for d in range(1, ny):
            start = pl.multiple_of(((y + d) % ny) * ysz, ysz)
            out.append(
                send(ysend.at[pl.ds(start, ysz)], yrecv.at[d - 1], ys.at[c, d - 1], yr.at[c, d - 1], ypeer[d - 1])
            )
        return out

    def chunk_x(c, copies):
        own, ysend, yrecv, xsend, xrecv = chunks[c][2:7]
        s = own[pl.ds(pl.multiple_of(y * ysz, ysz), ysz), :]
        for d in range(1, ny):
            copies[d - 1].wait_recv()
            s = s + yrecv[d - 1].astype(F32)
        for j in range(nxz):
            xsend[j] = s[share * j : share * j + share]
        out = []
        for i, (a, b) in enumerate(xzd):
            j = ((xh + a) % nx) * nz + (z + b) % nz
            out.append(send(xsend.at[j], xrecv.at[i], xs.at[c, i], xr.at[c, i], xzpeer[i]))
        return out

    def chunk_end(c, copies):
        xsend, xrecv = chunks[c][5:7]
        s = xsend[xh * nz + z]
        for i, copy in enumerate(copies):
            copy.wait_recv()
            s = s + xrecv[i]
        if c == 0:
            gproj[...] = s
        else:
            p = c - 1
            for part in range(3):
                gqkv[:, C * part + 128 * p : C * part + 128 * p + 128] = s[:, 128 * part : 128 * part + 128]

    def window_back(o, lane0):
        for w in range(nwin):
            wr, wc = w // wcols, w % wcols
            got = res[jnp.minimum(place[w], SLOTS - 1)]
            tmp[...] = jnp.where(place[w] < SLOTS, got, win[w, :, lane0 : lane0 + C])
            for i in range(WIN_LAT):
                c0 = HALF_LON + WIN_LON * wc
                of[o, HALF_LAT + WIN_LAT * wr + i, c0 : c0 + WIN_LON, :] = tmp[
                    WIN_LON * i : WIN_LON * i + WIN_LON, :
                ]
        colf[0:112, 0:C] = jnp.zeros((112, C), F32)
        for r in range(HALF_LAT, lat_dev):
            colf[6 * r : 6 * r + 6, 0:C] = of[o, r, lon_dev : lon_dev + HALF_LON, :]
        ocs[o, 0:112] = colf[0:112, 0:C].astype(BF16)
        for r in range(HALF_LAT):
            colf[6 * r : 6 * r + 6, 0:C] = of[o, lat_dev + r, lon_dev : lon_dev + HALF_LON, :]
            ors[o, r] = of[o, lat_dev + r, 0:lon_dev, :].astype(BF16)
        ocs[o, 112:144] = colf[0:32, 0:C].astype(BF16)
        return [
            send(ocs.at[o, 0:112], ocr.at[o], os_.at[o, 0], or_.at[o, 0], forth[0]),
            send(ors.at[o], orr.at[o], os_.at[o, 1], or_.at[o, 1], forth[1]),
            send(ocs.at[o, 112:144], occ.at[o], os_.at[o, 2], or_.at[o, 2], forth[2]),
        ]

    def finish(o, copies, out):
        copies[1].wait_recv()
        for r in range(HALF_LAT):
            of[o, r, 0:lon_dev, :] = orr[o, r].astype(F32)
        copies[0].wait_recv()
        colf[0:112, 0:C] = ocr[o].astype(F32)
        for r in range(HALF_LAT, lat_dev):
            of[o, r, 0:HALF_LON, :] = colf[6 * r : 6 * r + 6, 0:C]
        copies[2].wait_recv()
        colf[0:32, 0:C] = occ[o].astype(F32)
        for r in range(HALF_LAT):
            of[o, r, 0:HALF_LON, :] = colf[6 * r : 6 * r + 6, 0:C]
        for r in range(lat_dev):
            out[r] = of[o, r, 0:lon_dev, :].astype(BF16)

    mtp[...] = nt(perm[...], mixed[...]).astype(BF16)
    st = {}
    st[0] = chunk_start(0, mtp, gz)

    gnacc[...] = nn(mixed[0:ROWS, :], wproj[...])

    def updated_step(k, carry):
        w = idx[k]
        m = win[w, :, M0:FW]
        res[k] = win[w, :, X0 : X0 + C] + jnp.concatenate([m] * 4, axis=1) * gnacc[rows_of(k), :]
        return carry

    lax.fori_loop(0, SLOTS, updated_step, 0)
    out_copies = [window_back(0, X0), None]

    def backward(p):
        bacc[p] = jnp.zeros((2 * TP, 128), F32)

        def step(i, carry):
            ks = [3 * i + j for j in range(3)]
            d2s, dps, q2s, kps = [], [], [], []
            for k in ks:
                rows = rows_of(k)
                d = gm[rows, 128 * p : 128 * p + 128]
                d2s.append(jnp.concatenate([d * one_lo, d * one_hi], axis=0))
                q = packed[rows, 128 * p : 128 * p + 128]
                q2s.append(jnp.concatenate([q * q_lo, q * q_hi], axis=0))
                kps.append(pad_rows(packed[rows, C + 128 * p : C + 128 * p + 128], 128))
                v = pad_rows(packed[rows, 2 * C + 128 * p : 2 * C + 128 * p + 128], 128)
                dps.append(nt(d2s[-1], v))
            dss, dvs = [], []
            for j, k in enumerate(ks):
                pr = probs[k * PAIRS + p]
                t = pr * dps[j]
                dss.append(t - pr * jnp.sum(t, axis=1, keepdims=True))
                dvs.append(tn(pr.astype(BF16), d2s[j]))
            bacc[p] += dss[0] + dss[1] + dss[2]
            for j, k in enumerate(ks):
                rows = rows_of(k)
                ds = dss[j].astype(BF16)
                dq2 = nn(ds, kps[j])
                dq = jnp.where(low, dq2[0:TP], dq2[TP : 2 * TP]) * 0.125
                dk = tn(ds, q2s[j])
                dp3[p, rows, 0:128] = dq.astype(BF16)
                dp3[p, rows, 128:256] = dk[0:TP].astype(BF16)
                dp3[p, rows, 256:384] = dvs[j][0:TP].astype(BF16)
            return carry

        lax.fori_loop(0, SLOTS // 3, step, 0)

    def weight_pair(p):
        return jnp.concatenate([wqkv[:, C * part + 128 * p : C * part + 128 * p + 128] for part in range(3)], axis=1)

    def grad_normed(p):
        g = nt(dp3[p, 0:ROWS, :], weight_pair(p))
        gnacc[...] = g if p == 0 else gnacc[...] + g

    for p in range(PAIRS):
        backward(p)
        st[p + 1] = chunk_start(p + 1, ntp, dp3.at[p])
        if p >= 0:
            st[p] = chunk_y(p, st[p])
        if p >= 1:
            st[p - 1] = chunk_x(p - 1, st[p - 1])
        grad_normed(p)

    sm[...] = jnp.zeros_like(sm)
    for h in range(HEADS):
        g = pad_rows(bacc[h // 2, TP * (h % 2) : TP * (h % 2) + TP, :], 128)
        spread = nn(tn(self_[...], g, precision=hi), selr[...], precision=hi)
        wide = jnp.concatenate([spread, jnp.zeros((128, 128), F32)], axis=1)
        sm[h : h + 1, :] = jnp.sum(pltpu.roll(wide, 0, 1, stride=1, stride_axis=0), axis=0, keepdims=True)

    st[4] = chunk_y(4, st[4])
    st[3] = chunk_x(3, st[3])

    def norm_back(k, total):
        w = idx[k]
        rows = rows_of(k)
        gn = gnacc[rows, :]
        hat = xhat[rows, :]
        g = gn * gain
        prod = g * hat
        inner = g - jnp.mean(g, axis=1, keepdims=True) - hat * jnp.mean(prod, axis=1, keepdims=True)
        inv = jnp.concatenate([invd[rows, :]] * 4, axis=1)
        res[k] = win[w, :, D0 : D0 + C] + inv * inner
        return total + jnp.sum(gn * hat, axis=0, keepdims=True)

    gsum = lax.fori_loop(0, SLOTS, norm_back, jnp.zeros((1, C), F32))
    sm[8:9, :] = gsum[:, 0:256]
    sm[9:10, :] = gsum[:, 256:512]
    sma = send(sm, smc, ss.at[0], sr.at[0], partner)
    out_copies[1] = window_back(1, D0)

    st[4] = chunk_x(4, st[4])
    sma.wait_recv()
    smy[y] = sm[...] + smc[...]
    smys = [send(smy.at[y], smy.at[y], ss.at[d], sr.at[d], ypeer[d - 1]) for d in range(1, ny)]
    finish(0, out_copies[0], upd)
    for c in range(nchunk - 1):
        chunk_end(c, st[c])
    for copy in smys:
        copy.wait_recv()
    acc = smy[0]
    for j in range(1, ny):
        acc = acc + smy[j]
    here = xh * nz + z
    smx[here] = acc
    smxs = [send(smx.at[here], smx.at[here], ss.at[ny + i], sr.at[ny + i], xzpeer[i]) for i in range(len(xzd))]
    finish(1, out_copies[1], gin)
    chunk_end(nchunk - 1, st[nchunk - 1])
    for copy in smxs:
        copy.wait_recv()
    acc = smx[0]
    for j in range(1, nxz):
        acc = acc + smx[j]
    bias_out[...] = acc[0:HEADS, 0:REL]
    gain_out[:, 0:256] = acc[8:9, :]
    gain_out[:, 256:512] = acc[9:10, :]
    for copy in sends:
        copy.wait_send()


def constants(ny, nx, nz):
    share = C // (ny * nx * nz * 2)
    perm = np.zeros((C, C), np.float32)
    for core in range(2):
        for y in range(ny):
            for xh in range(nx):
                for z in range(nz):
                    to = (((core * ny + y) * nx + xh) * nz + z) * share
                    start = (((y * nx + xh) * nz + z) * 2 + core) * share
                    perm[to + np.arange(share), start + np.arange(share)] = 1
    a = np.arange(T)
    pa = (a // WIN_LON) * (2 * WIN_LON - 1) + a % WIN_LON
    selr = np.zeros((128, 128), np.float32)
    selr[a, 126 - pa] = 1
    self_ = np.zeros((128, 128), np.float32)
    self_[a, pa] = 1
    return perm, selr, self_


def solution(mesh):
    nlon, nlat = mesh.shape["lon"], mesh.shape["lat"]
    nx, nz = 2, nlat // 2
    ny = nlon // nx
    nxz = nx * nz
    half = C // 2
    ysz = half // ny
    share = ysz // nxz
    cols = [C] + [384] * PAIRS
    lat_dev, lon_dev = 18, 48
    nwin = 12
    vm = pltpu.VMEM
    dma = lambda *s: pltpu.SemaphoreType.DMA(s)
    perm, selr, self_ = constants(ny, nx, nz)

    def on_device(fields, grad_out, layernorm_gain, qkv_weight, proj_weight, bias_table, sea_mask):
        scratch = [
            vm((lat_dev + 3, 56, FW), F32),
            vm((nwin, TP, FW), F32),
            vm((112, FW), F32),
            vm((112, FW), BF16),
            vm((112, FW), BF16),
            vm((3, lon_dev, FW), BF16),
            vm((3, lon_dev, FW), BF16),
            vm((32, FW), BF16),
            pltpu.SMEM((16,), jnp.int32),
            vm((HEADS, 256), F32),
            vm((PAIRS, 2 * TP, 128), F32),
            vm((SLOTS, TP, 128), F32),
            vm((ROWS, C), F32),
            vm((ROWS, 128), F32),
            vm((RP, C), BF16),
            vm((RP, C), BF16),
            vm((ROWS, C), BF16),
            vm((ROWS, 3 * C), BF16),
            vm((RP, C), BF16),
            vm((C, RP), BF16),
            vm((C, RP), BF16),
            vm((SLOTS * PAIRS, 2 * TP, 128), F32),
            vm((PAIRS, RP, 384), BF16),
            vm((ROWS, C), F32),
            vm((PAIRS, 2 * TP, 128), F32),
            vm((SLOTS, TP, C), F32),
            vm((2, lat_dev + 3, 56, C), F32),
            vm((TP, C), F32),
            vm((2, 144, C), BF16),
            vm((2, 3, lon_dev, C), BF16),
            vm((2, 112, C), BF16),
            vm((2, 3, lon_dev, C), BF16),
            vm((2, 32, C), BF16),
        ]
        for n in cols:
            scratch += [
                vm((half, n), BF16),
                vm((half, n), BF16),
                vm((half, n), F32),
                vm((half, n), BF16),
                vm((ny - 1, ysz, n), BF16),
                vm((nxz, share, n), F32),
                vm((nxz - 1, share, n), F32),
            ]
        scratch += [vm((16, 256), F32), vm((16, 256), F32), vm((ny, 16, 256), F32), vm((nxz, 16, 256), F32)]
        nc = len(cols)
        small = ny + nxz - 1
        scratch += [
            dma(3), dma(3), dma(2, 3), dma(2, 3), dma(nc), dma(nc), dma(nc, ny - 1), dma(nc, ny - 1),
            dma(nc, nxz - 1), dma(nc, nxz - 1), dma(small), dma(small),
        ]
        whole = pl.BlockSpec(memory_space=vm)
        outs = pl.pallas_call(
            functools.partial(kernel, (ny, nx, nz), cols),
            out_shape=(
                jax.ShapeDtypeStruct((lat_dev, lon_dev, C), BF16),
                jax.ShapeDtypeStruct((lat_dev, lon_dev, C), BF16),
                jax.ShapeDtypeStruct((1, C), F32),
                jax.ShapeDtypeStruct((HEADS, REL), F32),
                jax.ShapeDtypeStruct((share, 3 * C), F32),
                jax.ShapeDtypeStruct((share, C), F32),
            ),
            in_specs=[whole] * 10,
            out_specs=(whole,) * 6,
            scratch_shapes=scratch,
            compiler_params=pltpu.CompilerParams(
                collective_id=0, has_side_effects=True, vmem_limit_bytes=60 * 1024 * 1024
            ),
        )(
            fields, grad_out, sea_mask, layernorm_gain.reshape(1, C), qkv_weight, proj_weight, bias_table,
            jnp.asarray(perm, BF16), jnp.asarray(selr, F32), jnp.asarray(self_, F32),
        )
        updated, grad_in, grad_gain, grad_bias, grad_qkv, grad_proj = outs
        return (updated, grad_in, grad_gain.reshape(C), grad_bias, grad_qkv, grad_proj)

    grid = P(("batch", "lat"), "lon", None)
    return jax.shard_map(
        on_device,
        mesh=mesh,
        in_specs=(grid, grid, P(), P(), P(), P(), P(("batch", "lat"), "lon")),
        out_specs=(
            grid,
            grid,
            P("batch"),
            P("batch", None),
            P(("batch", "lon", "lat"), None),
            P(("batch", "lon", "lat"), None),
        ),
        check_vma=False,
    )
```

```python
import functools

import jax
import jax.numpy as jnp
import numpy as np
from jax import lax
from jax.experimental import pallas as pl
from jax.experimental.pallas import tpu as pltpu
from jax.sharding import PartitionSpec as P

MESH = pl.DeviceIdType.MESH
F32 = jnp.float32
BF16 = jnp.bfloat16
C = 512
HEADS = 8
PAIRS = 4
WIN_LAT = 6
WIN_LON = 12
HALF_LAT = 3
HALF_LON = 6
T = 72
TP = 80
SLOTS = 9
ROWS = SLOTS * TP
RP = 768
REL = 253
X0, M0, D0, FW = 0, 512, 640, 1152
XW, DW = 640, 512
EARLY = 3
EPS = 1e-5


def nn(a, b, **kw):
    return lax.dot_general(a, b, (((1,), (0,)), ((), ())), preferred_element_type=F32, **kw)


def nt(a, b, **kw):
    return lax.dot_general(a, b, (((1,), (1,)), ((), ())), preferred_element_type=F32, **kw)


def tn(a, b, **kw):
    return lax.dot_general(a, b, (((0,), (0,)), ((), ())), preferred_element_type=F32, **kw)


def pad_rows(v, rows):
    return jnp.concatenate([v, jnp.zeros((rows - v.shape[0], v.shape[1]), v.dtype)], axis=0)


def kernel(dims, cols, *refs):
    ny, nx, nz = dims
    nlon, nlat = ny * nx, 2 * nz
    nxz = nx * nz
    lat_dev, lon_dev = 18, 48
    wrows, wcols = lat_dev // WIN_LAT, lon_dev // WIN_LON
    nwin = wrows * wcols
    half = C // 2
    ysz = half // ny
    share = ysz // nxz
    nchunk = len(cols)

    it = iter(refs)
    take = lambda n=None: next(it) if n is None else [next(it) for _ in range(n)]
    x_ref, dy_ref, mask_ref, gain_ref, wqkv, wproj, table, perm, selr, self_ = take(10)
    upd, gin, gain_out, bias_out, gqkv, gproj = take(6)
    frame, win, colf = take(3)
    halos = [take(5) for _ in range(2)]
    idx = take()
    tb, bias2, madd, xhat, invd, normed, gz, gm, packed, mixed, ntp, mtp, probs, dp3, gnacc, bacc = take(16)
    res, of = take(2)
    ocs, ors, ocr, orr, occ = take(5)
    chunks = [take(7) for _ in range(nchunk)]
    sums = [take(4) for _ in range(2)]
    hs, hr, os_, or_, as_, ar, ys, yr, xs, xr, ss, sr = take(12)

    lon = lax.axis_index("lon")
    lat = lax.axis_index("lat")
    y, xh = lon // nx, lon % nx
    z, core = lat // 2, lat % 2

    def dev(a, b):
        return {"lon": a, "lat": b}

    partner = dev(lon, z * 2 + (1 - core))
    ypeer = [dev(((y + d) % ny) * nx + xh, lat) for d in range(1, ny)]
    xzd = [(a, b) for a in range(nx) for b in range(nz) if (a, b) != (0, 0)]
    xzpeer = [dev(y * nx + (xh + a) % nx, ((z + b) % nz) * 2 + core) for a, b in xzd]
    west, east = (lon + nlon - 1) % nlon, (lon + 1) % nlon
    north, south = (lat + nlat - 1) % nlat, (lat + 1) % nlat
    back = [dev(west, lat), dev(lon, north), dev(west, north)]
    forth = [dev(east, lat), dev(lon, south), dev(east, south)]

    barrier = pltpu.get_barrier_semaphore()
    everyone = [partner] + ypeer + xzpeer + back + forth
    for d in everyone:
        pl.semaphore_signal(barrier, inc=1, device_id=d, device_id_type=MESH)

    sends = []

    def send(src, dst, ssem, rsem, d):
        copy = pltpu.make_async_remote_copy(
            src_ref=src, dst_ref=dst, send_sem=ssem, recv_sem=rsem, device_id=d, device_id_type=MESH
        )
        copy.start()
        sends.append(copy)
        return copy

    lane_row = lax.broadcasted_iota(jnp.int32, (lat_dev, lat_dev * 128), 1) // 128
    pick = (lane_row == lax.broadcasted_iota(jnp.int32, (lat_dev, lat_dev * 128), 0)).astype(F32)
    sea = tn(mask_ref[...].astype(F32), pick)
    colf[96:112, :] = jnp.zeros((16, FW), F32)

    def halo_pack(h, lanes):
        colsend, colrecv, rowsend, rowrecv, cornrecv = halos[h]
        for r in range(lat_dev):
            colf[6 * r : 6 * r + 6, lanes] = frame[r, 0:HALF_LON, lanes]
        colsend[...] = colf[:, lanes].astype(BF16)
        for r in range(HALF_LAT):
            rowsend[r] = frame[r, 0:lon_dev, lanes].astype(BF16)

    def halo_send(h):
        colsend, colrecv, rowsend, rowrecv, cornrecv = halos[h]
        return [
            send(colsend, colrecv, hs.at[h, 0], hr.at[h, 0], back[0]),
            send(rowsend, rowrecv, hs.at[h, 1], hr.at[h, 1], back[1]),
            send(colsend.at[0:32], cornrecv, hs.at[h, 2], hr.at[h, 2], back[2]),
        ]

    def halo_land(h, lanes, copies):
        colsend, colrecv, rowsend, rowrecv, cornrecv = halos[h]
        copies[1].wait_recv()
        for r in range(HALF_LAT):
            frame[lat_dev + r, 0:lon_dev, lanes] = rowrecv[r].astype(F32)
        copies[2].wait_recv()
        colf[0:32, lanes] = cornrecv[...].astype(F32)
        for r in range(HALF_LAT):
            frame[lat_dev + r, lon_dev : lon_dev + HALF_LON, lanes] = colf[6 * r : 6 * r + 6, lanes]
        copies[0].wait_recv()
        colf[:, lanes] = colrecv[...].astype(F32)
        for r in range(lat_dev):
            frame[r, lon_dev : lon_dev + HALF_LON, lanes] = colf[6 * r : 6 * r + 6, lanes]

    xlanes, dlanes = slice(X0, X0 + XW), slice(D0, D0 + DW)
    for r in range(lat_dev):
        frame[r, 0:lon_dev, X0 : X0 + C] = x_ref[r].astype(F32)
        frame[r, 0:lon_dev, M0 : M0 + 128] = sea[:, 128 * r : 128 * r + 128]
    halo_pack(0, xlanes)
    pl.semaphore_wait(barrier, len(everyone))
    xcopies = halo_send(0)
    for r in range(lat_dev):
        frame[r, 0:lon_dev, D0 : D0 + C] = dy_ref[r].astype(F32)
    halo_pack(1, dlanes)
    dcopies = halo_send(1)

    tb[...] = jnp.zeros_like(tb)
    tb[:, 0:REL] = table[...]
    hi = lax.Precision.HIGHEST
    for h in range(HEADS):
        line = jnp.broadcast_to(tb[h : h + 1, :], (128, 256))
        rolled = pltpu.roll(pltpu.roll(line, 2, 1), 128, 1, stride=1, stride_axis=0)
        both = nt(nt(selr[...], rolled[:, 0:128], precision=hi), selr[...], precision=hi)
        bias2[h // 2, TP * (h % 2) : TP * (h % 2) + TP, :] = both[0:TP]

    zero_tail = jnp.zeros((RP - ROWS, C), BF16)
    normed[ROWS:RP, :] = zero_tail
    gz[ROWS:RP, :] = zero_tail
    mixed[ROWS:RP, :] = zero_tail
    for p in range(PAIRS):
        dp3[p, ROWS:RP, :] = jnp.zeros((RP - ROWS, 384), BF16)
    for w in range(nwin):
        win[w, T:TP, :] = jnp.zeros((TP - T, FW), F32)

    def cut(w, lanes):
        wr, wc = w // wcols, w % wcols
        c0 = HALF_LON + WIN_LON * wc
        for i in range(WIN_LAT):
            win[w, WIN_LON * i : WIN_LON * i + WIN_LON, lanes] = frame[
                HALF_LAT + WIN_LAT * wr + i, c0 : c0 + WIN_LON, lanes
            ]

    def holds_sea(w):
        return (jnp.max(win[w, :, M0 : M0 + 128]) > 0.5).astype(jnp.int32)

    def ranks(flags, counted):
        total = jnp.int32(0)
        for f, c in zip(flags, counted):
            total = total + f * c
        out, on, off = [], jnp.int32(0), total
        for f, c in zip(flags, counted):
            out.append(jnp.where(f > 0, on, off))
            on = on + f * c
            off = off + (1 - f) * c
        return out

    def slot_window(k, places):
        slot = jnp.int32(0)
        for w, at in places:
            slot = slot + jnp.where(at == k, w, 0)
        idx[k] = slot

    inner = [w for w in range(nwin) if w // wcols < wrows - 1 and w % wcols < wcols - 1]
    outer = [w for w in range(nwin) if w not in inner]
    active = [None] * nwin
    place = [None] * nwin

    at_end = (lat == nlat - 1).astype(F32)
    gain = gain_ref[...]

    def rows_of(k):
        return pl.ds(pl.multiple_of(k * TP, TP), TP)

    def ln_step(k, carry):
        w = idx[k]
        x = win[w, :, X0 : X0 + C]
        mean = jnp.mean(x, axis=1, keepdims=True)
        xc = x - mean
        inv = lax.rsqrt(jnp.mean(xc * xc, axis=1, keepdims=True) + EPS)
        hat = xc * inv
        rows = rows_of(k)
        xhat[rows, :] = hat
        invd[rows, :] = jnp.broadcast_to(inv, (TP, 128))
        normed[rows, :] = (hat * gain).astype(BF16)
        keys = win[w, :, M0 : M0 + 128]
        side_b = lax.broadcasted_iota(jnp.int32, (TP, 128), 0) >= T // 2
        side_a = lax.broadcasted_iota(jnp.int32, (TP, 128), 1) >= T // 2
        apart = jnp.where(side_a != side_b, 1.0, 0.0)
        wrap = at_end * jnp.where(w >= nwin - wcols, 1.0, 0.0)
        madd[k] = (keys * (1.0 - apart * wrap) - 1.0) * 1e9
        return carry

    def dy_step(k, carry):
        w = idx[k]
        m = win[w, :, M0 : M0 + 128]
        gz[rows_of(k), :] = (win[w, :, D0 : D0 + C] * jnp.concatenate([m] * 4, axis=1)).astype(BF16)
        return carry

    lane = lax.broadcasted_iota(jnp.int32, (TP, 128), 1)
    low = lane < 64
    one_lo = jnp.where(low, 1.0, 0.0).astype(BF16)
    one_hi = jnp.where(low, 0.0, 1.0).astype(BF16)
    q_lo = jnp.where(low, 0.125, 0.0).astype(BF16)
    q_hi = jnp.where(low, 0.0, 0.125).astype(BF16)

    def both_heads(v, lo, hi_):
        return jnp.concatenate([v * lo, v * hi_], axis=0)

    def join_heads(v):
        return jnp.where(low, v[0:TP], v[TP : 2 * TP])

    def per_head(v):
        return v.reshape(2, TP, 128)

    def attend(k, carry):
        rows = rows_of(k)
        add = madd[k]
        add2 = jnp.concatenate([add, add], axis=0)
        scores = []
        for p in range(PAIRS):
            q = pad_rows(packed[rows, 128 * p : 128 * p + 128], 128)
            k2 = both_heads(packed[rows, C + 128 * p : C + 128 * p + 128], q_lo, q_hi)
            scores.append(nt(k2, q) + bias2[p] + add2)
        for p in range(PAIRS):
            s = per_head(scores[p])
            e = jnp.exp(s - jnp.max(s, axis=1, keepdims=True))
            pr = (e * (1.0 / jnp.sum(e, axis=1, keepdims=True))).reshape(2 * TP, 128)
            probs[k * PAIRS + p] = pr
            v2 = both_heads(packed[rows, 2 * C + 128 * p : 2 * C + 128 * p + 128], one_lo, one_hi)
            mixed[rows, 128 * p : 128 * p + 128] = tn(pr.astype(BF16), v2)[0:TP].astype(BF16)
        return carry

    def forward(first, last):
        lax.fori_loop(first, last, ln_step, 0)
        rows = slice(first * TP, last * TP)
        packed[rows, :] = nn(normed[rows, :], wqkv[...]).astype(BF16)
        lax.fori_loop(first, last, attend, 0)

    for w in inner:
        cut(w, slice(0, FW))
        active[w] = holds_sea(w)
    inner_rank = ranks([active[w] for w in inner], [1] * len(inner))
    for k in range(EARLY):
        slot_window(k, list(zip(inner, inner_rank)))
    forward(0, EARLY)

    halo_land(0, xlanes, xcopies)
    for w in outer:
        cut(w, xlanes)
        active[w] = holds_sea(w)
    rest = [jnp.int32(1)] * nwin
    for w, at in zip(inner, inner_rank):
        rest[w] = (at >= EARLY).astype(jnp.int32)
    late_rank = ranks(active, rest)
    for w in range(nwin):
        place[w] = late_rank[w] + EARLY
    for w, at in zip(inner, inner_rank):
        place[w] = jnp.where(at < EARLY, at, place[w])
    for k in range(EARLY, SLOTS):
        slot_window(k, list(enumerate(place)))
    forward(EARLY, SLOTS)

    halo_land(1, dlanes, dcopies)
    for w in outer:
        cut(w, dlanes)
    lax.fori_loop(0, SLOTS, dy_step, 0)
    gm[...] = nt(gz[0:ROWS, :], wproj[...]).astype(BF16)
    ntp[...] = nt(perm[...], normed[...]).astype(BF16)

    def chunk_start(c, lhs, rhs):
        asend, arecv, own = chunks[c][0:3]
        right = rhs[...]
        other = pl.multiple_of((1 - core) * half, half)
        mine = pl.multiple_of(core * half, half)
        asend[...] = nn(lhs[pl.ds(other, half), :], right).astype(BF16)
        copy = send(asend, arecv, as_.at[c], ar.at[c], partner)
        own[...] = nn(lhs[pl.ds(mine, half), :], right)
        return [copy]

    def chunk_y(c, copies):
        asend, arecv, own, ysend, yrecv = chunks[c][0:5]
        copies[0].wait_recv()
        s = own[...] + arecv[...].astype(F32)
        own[...] = s
        ysend[...] = s.astype(BF16)
        out = []
        for d in range(1, ny):
            start = pl.multiple_of(((y + d) % ny) * ysz, ysz)
            out.append(
                send(ysend.at[pl.ds(start, ysz)], yrecv.at[d - 1], ys.at[c, d - 1], yr.at[c, d - 1], ypeer[d - 1])
            )
        return out

    def chunk_x(c, copies):
        own, ysend, yrecv, xsend, xrecv = chunks[c][2:7]
        s = own[pl.ds(pl.multiple_of(y * ysz, ysz), ysz), :]
        for d in range(1, ny):
            copies[d - 1].wait_recv()
            s = s + yrecv[d - 1].astype(F32)
        for j in range(nxz):
            xsend[j] = s[share * j : share * j + share]
        out = []
        for i, (a, b) in enumerate(xzd):
            j = ((xh + a) % nx) * nz + (z + b) % nz
            out.append(send(xsend.at[j], xrecv.at[i], xs.at[c, i], xr.at[c, i], xzpeer[i]))
        return out

    def chunk_end(c, copies):
        xsend, xrecv = chunks[c][5:7]
        s = xsend[xh * nz + z]
        for i, copy in enumerate(copies):
            copy.wait_recv()
            s = s + xrecv[i]
        if c == 0:
            gproj[...] = s
        else:
            p = c - 1
            for part in range(3):
                gqkv[:, C * part + 128 * p : C * part + 128 * p + 128] = s[:, 128 * part : 128 * part + 128]

    def window_back(o, lane0):
        for w in range(nwin):
            wr, wc = w // wcols, w % wcols
            slot = jnp.minimum(place[w], SLOTS - 1)
            for i in range(WIN_LAT):
                c0 = HALF_LON + WIN_LON * wc
                at = slice(WIN_LON * i, WIN_LON * i + WIN_LON)
                of[o, HALF_LAT + WIN_LAT * wr + i, c0 : c0 + WIN_LON, :] = jnp.where(
                    place[w] < SLOTS, res[slot, at, :], win[w, at, lane0 : lane0 + C]
                )
        colf[0:112, 0:C] = jnp.zeros((112, C), F32)
        for r in range(HALF_LAT, lat_dev):
            colf[6 * r : 6 * r + 6, 0:C] = of[o, r, lon_dev : lon_dev + HALF_LON, :]
        ocs[o, 0:112] = colf[0:112, 0:C].astype(BF16)
        for r in range(HALF_LAT):
            colf[6 * r : 6 * r + 6, 0:C] = of[o, lat_dev + r, lon_dev : lon_dev + HALF_LON, :]
            ors[o, r] = of[o, lat_dev + r, 0:lon_dev, :].astype(BF16)
        ocs[o, 112:144] = colf[0:32, 0:C].astype(BF16)
        return [
            send(ocs.at[o, 0:112], ocr.at[o], os_.at[o, 0], or_.at[o, 0], forth[0]),
            send(ors.at[o], orr.at[o], os_.at[o, 1], or_.at[o, 1], forth[1]),
            send(ocs.at[o, 112:144], occ.at[o], os_.at[o, 2], or_.at[o, 2], forth[2]),
        ]

    def finish(o, copies, out):
        copies[1].wait_recv()
        for r in range(HALF_LAT):
            of[o, r, 0:lon_dev, :] = orr[o, r].astype(F32)
        copies[0].wait_recv()
        colf[0:112, 0:C] = ocr[o].astype(F32)
        for r in range(HALF_LAT, lat_dev):
            of[o, r, 0:HALF_LON, :] = colf[6 * r : 6 * r + 6, 0:C]
        copies[2].wait_recv()
        colf[0:32, 0:C] = occ[o].astype(F32)
        for r in range(HALF_LAT):
            of[o, r, 0:HALF_LON, :] = colf[6 * r : 6 * r + 6, 0:C]
        for r in range(lat_dev):
            out[r] = of[o, r, 0:lon_dev, :].astype(BF16)

    mtp[...] = nt(perm[...], mixed[...]).astype(BF16)
    st = {}
    st[0] = chunk_start(0, mtp, gz)

    gnacc[...] = nn(mixed[0:ROWS, :], wproj[...])

    def updated_step(k, carry):
        w = idx[k]
        m = win[w, :, M0 : M0 + 128]
        res[k] = win[w, :, X0 : X0 + C] + jnp.concatenate([m] * 4, axis=1) * gnacc[rows_of(k), :]
        return carry

    lax.fori_loop(0, SLOTS, updated_step, 0)
    out_copies = [window_back(0, X0), None]

    def backward(p):
        bacc[p] = jnp.zeros((2 * TP, 128), F32)

        def step(i, carry):
            ks = [3 * i + j for j in range(3)]
            ds_, dps = [], []
            for k in ks:
                rows = rows_of(k)
                ds_.append(pad_rows(gm[rows, 128 * p : 128 * p + 128], 128))
                v2 = both_heads(packed[rows, 2 * C + 128 * p : 2 * C + 128 * p + 128], one_lo, one_hi)
                dps.append(nt(v2, ds_[-1]))
            dss, dvs = [], []
            for j, k in enumerate(ks):
                pr = probs[k * PAIRS + p]
                t = pr * dps[j]
                dot = jnp.sum(per_head(t), axis=1, keepdims=True)
                dss.append((per_head(t) - per_head(pr) * dot).reshape(2 * TP, 128))
                dvs.append(nn(pr.astype(BF16), ds_[j]))
            bacc[p] += dss[0] + dss[1] + dss[2]
            for j, k in enumerate(ks):
                rows = rows_of(k)
                ds = dss[j].astype(BF16)
                q = pad_rows(packed[rows, 128 * p : 128 * p + 128], 128)
                k2 = both_heads(packed[rows, C + 128 * p : C + 128 * p + 128], q_lo, q_hi)
                dk2 = nn(ds, q)
                dq = tn(ds, k2)
                dp3[p, rows, 0:128] = dq[0:TP].astype(BF16)
                dp3[p, rows, 128:256] = (join_heads(dk2) * 0.125).astype(BF16)
                dp3[p, rows, 256:384] = join_heads(dvs[j]).astype(BF16)
            return carry

        lax.fori_loop(0, SLOTS // 3, step, 0)

    def weight_pair(p):
        return jnp.concatenate([wqkv[:, C * part + 128 * p : C * part + 128 * p + 128] for part in range(3)], axis=1)

    def grad_normed(p):
        g = nt(dp3[p, 0:ROWS, :], weight_pair(p))
        gnacc[...] = g if p == 0 else gnacc[...] + g

    for p in range(PAIRS):
        backward(p)
        st[p + 1] = chunk_start(p + 1, ntp, dp3.at[p])
        if p >= 0:
            st[p] = chunk_y(p, st[p])
        if p >= 1:
            st[p - 1] = chunk_x(p - 1, st[p - 1])
        grad_normed(p)

    def sum_core(g):
        sm, smc = sums[g][0:2]
        return send(sm, smc, ss.at[g, 0], sr.at[g, 0], partner)

    def sum_y(g, copy):
        sm, smc, smy, smx = sums[g]
        copy.wait_recv()
        smy[y] = sm[...] + smc[...]
        return [
            send(smy.at[y], smy.at[y], ss.at[g, d], sr.at[g, d], ypeer[d - 1]) for d in range(1, ny)
        ]

    def sum_xz(g, copies):
        sm, smc, smy, smx = sums[g]
        for copy in copies:
            copy.wait_recv()
        acc = smy[0]
        for j in range(1, ny):
            acc = acc + smy[j]
        here = xh * nz + z
        smx[here] = acc
        return [
            send(smx.at[here], smx.at[here], ss.at[g, ny + i], sr.at[g, ny + i], xzpeer[i])
            for i in range(len(xzd))
        ]

    def sum_end(g, copies):
        smx = sums[g][3]
        for copy in copies:
            copy.wait_recv()
        acc = smx[0]
        for j in range(1, nxz):
            acc = acc + smx[j]
        return acc

    for h in range(HEADS):
        g = pad_rows(bacc[h // 2, TP * (h % 2) : TP * (h % 2) + TP, :], 128)
        spread = tn(self_[...], tn(g, selr[...], precision=hi), precision=hi)
        wide = jnp.concatenate([spread, jnp.zeros((128, 128), F32)], axis=1)
        sums[0][0][h : h + 1, :] = jnp.sum(pltpu.roll(wide, 0, 1, stride=1, stride_axis=0), axis=0, keepdims=True)
    bias_copies = sum_core(0)

    def norm_back(k, total):
        w = idx[k]
        rows = rows_of(k)
        gn = gnacc[rows, :]
        hat = xhat[rows, :]
        g = gn * gain
        prod = g * hat
        mid = g - jnp.mean(g, axis=1, keepdims=True) - hat * jnp.mean(prod, axis=1, keepdims=True)
        inv = jnp.concatenate([invd[rows, :]] * 4, axis=1)
        res[k] = win[w, :, D0 : D0 + C] + inv * mid
        return total + jnp.sum(gn * hat, axis=0, keepdims=True)

    gsum = lax.fori_loop(0, SLOTS, norm_back, jnp.zeros((1, C), F32))
    sums[1][0][...] = jnp.zeros((8, 128), F32)
    for j in range(4):
        sums[1][0][j : j + 1, :] = gsum[:, 128 * j : 128 * j + 128]
    gain_copies = sum_core(1)
    st[4] = chunk_y(4, st[4])
    out_copies[1] = window_back(1, D0)

    st[3] = chunk_x(3, st[3])
    bias_copies = sum_y(0, bias_copies)
    gain_copies = sum_y(1, gain_copies)
    st[4] = chunk_x(4, st[4])
    bias_copies = sum_xz(0, bias_copies)
    gain_copies = sum_xz(1, gain_copies)
    finish(0, out_copies[0], upd)
    for c in range(nchunk - 1):
        chunk_end(c, st[c])
    finish(1, out_copies[1], gin)
    bias_out[...] = sum_end(0, bias_copies)[:, 0:REL]
    chunk_end(nchunk - 1, st[nchunk - 1])
    acc = sum_end(1, gain_copies)
    for j in range(4):
        gain_out[:, 128 * j : 128 * j + 128] = acc[j : j + 1, :]
    for copy in sends:
        copy.wait_send()


def hand_over(*refs):
    sem = refs[12]
    copies = [pltpu.make_async_copy(refs[i], refs[6 + i], sem.at[i]) for i in range(6)]
    for copy in copies:
        copy.start()
    for copy in copies:
        copy.wait()


def constants(ny, nx, nz):
    share = C // (ny * nx * nz * 2)
    perm = np.zeros((C, C), np.float32)
    for core in range(2):
        for y in range(ny):
            for xh in range(nx):
                for z in range(nz):
                    to = (((core * ny + y) * nx + xh) * nz + z) * share
                    start = (((y * nx + xh) * nz + z) * 2 + core) * share
                    perm[to + np.arange(share), start + np.arange(share)] = 1
    a = np.arange(T)
    pa = (a // WIN_LON) * (2 * WIN_LON - 1) + a % WIN_LON
    selr = np.zeros((128, 128), np.float32)
    selr[a, 126 - pa] = 1
    self_ = np.zeros((128, 128), np.float32)
    self_[a, pa] = 1
    return perm, selr, self_


def solution(mesh):
    nlon, nlat = mesh.shape["lon"], mesh.shape["lat"]
    nx, nz = 2, nlat // 2
    ny = nlon // nx
    nxz = nx * nz
    half = C // 2
    ysz = half // ny
    share = ysz // nxz
    cols = [C] + [384] * PAIRS
    lat_dev, lon_dev = 18, 48
    nwin = 12
    vm = pltpu.VMEM
    dma = lambda *s: pltpu.SemaphoreType.DMA(s)
    perm, selr, self_ = constants(ny, nx, nz)

    def on_device(fields, grad_out, layernorm_gain, qkv_weight, proj_weight, bias_table, sea_mask):
        scratch = [
            vm((lat_dev + 3, 56, FW), F32),
            vm((nwin, TP, FW), F32),
            vm((112, FW), F32),
        ]
        for wide in (XW, DW):
            scratch += [
                vm((112, wide), BF16),
                vm((112, wide), BF16),
                vm((3, lon_dev, wide), BF16),
                vm((3, lon_dev, wide), BF16),
                vm((32, wide), BF16),
            ]
        scratch += [
            pltpu.SMEM((16,), jnp.int32),
            vm((HEADS, 256), F32),
            vm((PAIRS, 2 * TP, 128), F32),
            vm((SLOTS, TP, 128), F32),
            vm((ROWS, C), F32),
            vm((ROWS, 128), F32),
            vm((RP, C), BF16),
            vm((RP, C), BF16),
            vm((ROWS, C), BF16),
            vm((ROWS, 3 * C), BF16),
            vm((RP, C), BF16),
            vm((C, RP), BF16),
            vm((C, RP), BF16),
            vm((SLOTS * PAIRS, 2 * TP, 128), F32),
            vm((PAIRS, RP, 384), BF16),
            vm((ROWS, C), F32),
            vm((PAIRS, 2 * TP, 128), F32),
            vm((SLOTS, TP, C), F32),
            vm((2, lat_dev + 3, 56, C), F32),
            vm((2, 144, C), BF16),
            vm((2, 3, lon_dev, C), BF16),
            vm((2, 112, C), BF16),
            vm((2, 3, lon_dev, C), BF16),
            vm((2, 32, C), BF16),
        ]
        for n in cols:
            scratch += [
                vm((half, n), BF16),
                vm((half, n), BF16),
                vm((half, n), F32),
                vm((half, n), BF16),
                vm((ny - 1, ysz, n), BF16),
                vm((nxz, share, n), F32),
                vm((nxz - 1, share, n), F32),
            ]
        for sm in ((8, 256), (8, 128)):
            scratch += [vm(sm, F32), vm(sm, F32), vm((ny,) + sm, F32), vm((nxz,) + sm, F32)]
        nc = len(cols)
        small = ny + nxz - 1
        scratch += [
            dma(2, 3), dma(2, 3), dma(2, 3), dma(2, 3), dma(nc), dma(nc), dma(nc, ny - 1), dma(nc, ny - 1),
            dma(nc, nxz - 1), dma(nc, nxz - 1), dma(2, small), dma(2, small),
        ]
        whole = pl.BlockSpec(memory_space=vm)
        shapes = (
            jax.ShapeDtypeStruct((lat_dev, lon_dev, C), BF16),
            jax.ShapeDtypeStruct((lat_dev, lon_dev, C), BF16),
            jax.ShapeDtypeStruct((1, C), F32),
            jax.ShapeDtypeStruct((HEADS, REL), F32),
            jax.ShapeDtypeStruct((share, 3 * C), F32),
            jax.ShapeDtypeStruct((share, C), F32),
        )
        outs = pl.pallas_call(
            functools.partial(kernel, (ny, nx, nz), cols),
            out_shape=shapes,
            in_specs=[whole] * 10,
            out_specs=(whole,) * 6,
            scratch_shapes=scratch,
            compiler_params=pltpu.CompilerParams(
                collective_id=0, has_side_effects=True, vmem_limit_bytes=60 * 1024 * 1024
            ),
        )(
            fields, grad_out, sea_mask, layernorm_gain.reshape(1, C), qkv_weight, proj_weight, bias_table,
            jnp.asarray(perm, BF16), jnp.asarray(selr, F32), jnp.asarray(self_, F32),
        )
        anywhere = pl.BlockSpec(memory_space=pl.ANY)
        outs = pl.pallas_call(
            hand_over,
            out_shape=shapes,
            in_specs=[anywhere] * 6,
            out_specs=(anywhere,) * 6,
            scratch_shapes=[dma(6)],
            compiler_params=pltpu.CompilerParams(vmem_limit_bytes=60 * 1024 * 1024),
        )(*outs)
        updated, grad_in, grad_gain, grad_bias, grad_qkv, grad_proj = outs
        return (updated, grad_in, grad_gain.reshape(C), grad_bias, grad_qkv, grad_proj)

    grid = P(("batch", "lat"), "lon", None)
    return jax.shard_map(
        on_device,
        mesh=mesh,
        in_specs=(grid, grid, P(), P(), P(), P(), P(("batch", "lat"), "lon")),
        out_specs=(
            grid,
            grid,
            P("batch"),
            P("batch", None),
            P(("batch", "lon", "lat"), None),
            P(("batch", "lon", "lat"), None),
        ),
        check_vma=False,
    )
```

```python
import functools

import jax
import jax.numpy as jnp
import numpy as np
from jax import lax
from jax.experimental import pallas as pl
from jax.experimental.pallas import tpu as pltpu
from jax.sharding import PartitionSpec as P

MESH = pl.DeviceIdType.MESH
F32 = jnp.float32
BF16 = jnp.bfloat16
C = 512
HEADS = 8
PAIRS = 4
WIN_LAT = 6
WIN_LON = 12
HALF_LAT = 3
HALF_LON = 6
T = 72
TP = 80
SLOTS = 9
ROWS = SLOTS * TP
RP = 768
REL = 253
X0, M0, D0, FW = 0, 512, 640, 1152
XW, DW = 640, 512
EARLY = 3
EPS = 1e-5


def nn(a, b, **kw):
    return lax.dot_general(a, b, (((1,), (0,)), ((), ())), preferred_element_type=F32, **kw)


def nt(a, b, **kw):
    return lax.dot_general(a, b, (((1,), (1,)), ((), ())), preferred_element_type=F32, **kw)


def tn(a, b, **kw):
    return lax.dot_general(a, b, (((0,), (0,)), ((), ())), preferred_element_type=F32, **kw)


def pad_rows(v, rows):
    return jnp.concatenate([v, jnp.zeros((rows - v.shape[0], v.shape[1]), v.dtype)], axis=0)


def kernel(dims, cols, *refs):
    ny, nx, nz = dims
    nlon, nlat = ny * nx, 2 * nz
    nxz = nx * nz
    lat_dev, lon_dev = 18, 48
    wrows, wcols = lat_dev // WIN_LAT, lon_dev // WIN_LON
    nwin = wrows * wcols
    half = C // 2
    ysz = half // ny
    share = ysz // nxz
    nchunk = len(cols)

    it = iter(refs)
    take = lambda n=None: next(it) if n is None else [next(it) for _ in range(n)]
    given = take(11)
    results = take(6)
    held = take(11)
    x_ref, mask_ref, dy_ref, table, self_, selft, selrt, gain_ref, wqkv, wproj, perm = held
    staged = take(6)
    upd, gin, gain_out, bias_out, gqkv, gproj = staged
    frame, win, colf = take(3)
    halos = [take(5) for _ in range(2)]
    idx = take()
    tb, bias2, madd, xhat, invd, normed, gz, gm, packed, mixed, ntp, mtp, probs, dp3, gnacc, bacc = take(16)
    res, of = take(2)
    ocs, ors, ocr, orr, occ = take(5)
    chunks = [take(7) for _ in range(nchunk)]
    sums = [take(4) for _ in range(2)]
    hs, hr, os_, or_, as_, ar, ys, yr, xs, xr, ss, sr = take(12)
    ins, outs = take(2)

    lon = lax.axis_index("lon")
    lat = lax.axis_index("lat")
    y, xh = lon // nx, lon % nx
    z, core = lat // 2, lat % 2

    def dev(a, b):
        return {"lon": a, "lat": b}

    partner = dev(lon, z * 2 + (1 - core))
    ypeer = [dev(((y + d) % ny) * nx + xh, lat) for d in range(1, ny)]
    xzd = [(a, b) for a in range(nx) for b in range(nz) if (a, b) != (0, 0)]
    xzpeer = [dev(y * nx + (xh + a) % nx, ((z + b) % nz) * 2 + core) for a, b in xzd]
    west, east = (lon + nlon - 1) % nlon, (lon + 1) % nlon
    north, south = (lat + nlat - 1) % nlat, (lat + 1) % nlat
    back = [dev(west, lat), dev(lon, north), dev(west, north)]
    forth = [dev(east, lat), dev(lon, south), dev(east, south)]

    barrier = pltpu.get_barrier_semaphore()
    everyone = [partner] + ypeer + xzpeer + back + forth
    for d in everyone:
        pl.semaphore_signal(barrier, inc=1, device_id=d, device_id_type=MESH)

    loads = [pltpu.make_async_copy(a, b, ins.at[i]) for i, (a, b) in enumerate(zip(given, held))]
    for load in loads:
        load.start()

    stores = [pltpu.make_async_copy(a, b, outs.at[i]) for i, (a, b) in enumerate(zip(staged, results))]
    sends = []

    def send(src, dst, ssem, rsem, d):
        copy = pltpu.make_async_remote_copy(
            src_ref=src, dst_ref=dst, send_sem=ssem, recv_sem=rsem, device_id=d, device_id_type=MESH
        )
        copy.start()
        sends.append(copy)
        return copy

    lane_row = lax.broadcasted_iota(jnp.int32, (lat_dev, lat_dev * 128), 1) // 128
    pick = (lane_row == lax.broadcasted_iota(jnp.int32, (lat_dev, lat_dev * 128), 0)).astype(F32)
    loads[1].wait()
    sea = tn(mask_ref[...].astype(F32), pick)
    colf[96:112, :] = jnp.zeros((16, FW), F32)

    def halo_pack(h, lanes):
        colsend, colrecv, rowsend, rowrecv, cornrecv = halos[h]
        for r in range(lat_dev):
            colf[6 * r : 6 * r + 6, lanes] = frame[r, 0:HALF_LON, lanes]
        colsend[...] = colf[:, lanes].astype(BF16)
        for r in range(HALF_LAT):
            rowsend[r] = frame[r, 0:lon_dev, lanes].astype(BF16)

    def halo_send(h):
        colsend, colrecv, rowsend, rowrecv, cornrecv = halos[h]
        return [
            send(colsend, colrecv, hs.at[h, 0], hr.at[h, 0], back[0]),
            send(rowsend, rowrecv, hs.at[h, 1], hr.at[h, 1], back[1]),
            send(colsend.at[0:32], cornrecv, hs.at[h, 2], hr.at[h, 2], back[2]),
        ]

    def halo_land(h, lanes, copies):
        colsend, colrecv, rowsend, rowrecv, cornrecv = halos[h]
        copies[1].wait_recv()
        for r in range(HALF_LAT):
            frame[lat_dev + r, 0:lon_dev, lanes] = rowrecv[r].astype(F32)
        copies[2].wait_recv()
        colf[0:32, lanes] = cornrecv[...].astype(F32)
        for r in range(HALF_LAT):
            frame[lat_dev + r, lon_dev : lon_dev + HALF_LON, lanes] = colf[6 * r : 6 * r + 6, lanes]
        copies[0].wait_recv()
        colf[:, lanes] = colrecv[...].astype(F32)
        for r in range(lat_dev):
            frame[r, lon_dev : lon_dev + HALF_LON, lanes] = colf[6 * r : 6 * r + 6, lanes]

    xlanes, dlanes = slice(X0, X0 + XW), slice(D0, D0 + DW)
    loads[0].wait()
    for r in range(lat_dev):
        frame[r, 0:lon_dev, X0 : X0 + C] = x_ref[r].astype(F32)
        frame[r, 0:lon_dev, M0 : M0 + 128] = sea[:, 128 * r : 128 * r + 128]
    halo_pack(0, xlanes)
    pl.semaphore_wait(barrier, len(everyone))
    xcopies = halo_send(0)
    loads[2].wait()
    for r in range(lat_dev):
        frame[r, 0:lon_dev, D0 : D0 + C] = dy_ref[r].astype(F32)
    halo_pack(1, dlanes)
    dcopies = halo_send(1)

    def pieces(v, n):
        out = []
        for i in range(n):
            part = v.astype(BF16)
            out.append(part)
            if i < n - 1:
                v = v - part.astype(F32)
        return out

    for i in range(3, 11):
        loads[i].wait()
    tb[...] = jnp.zeros_like(tb)
    tb[:, 0:REL] = table[...]
    shifted = []
    for h in range(HEADS):
        line = jnp.broadcast_to(tb[h : h + 1, :], (128, 256))
        shifted.append(pltpu.roll(pltpu.roll(line, 2, 1), 128, 1, stride=1, stride_axis=0)[:, 0:128])
    by_query = sum(nn(v, selft[...]) for v in pieces(jnp.concatenate(shifted, axis=0), 3))
    by_query = jnp.concatenate([by_query[128 * h : 128 * h + 128] for h in range(HEADS)], axis=1)
    whole_bias = sum(nn(self_[0:TP, :], v) for v in pieces(by_query, 3))
    for p in range(PAIRS):
        bias2[p] = whole_bias[:, 256 * p : 256 * p + 256]

    zero_tail = jnp.zeros((RP - ROWS, C), BF16)
    normed[ROWS:RP, :] = zero_tail
    gz[ROWS:RP, :] = zero_tail
    mixed[ROWS:RP, :] = zero_tail
    for p in range(PAIRS):
        dp3[p, ROWS:RP, :] = jnp.zeros((RP - ROWS, 384), BF16)
    for w in range(nwin):
        win[w, T:TP, :] = jnp.zeros((TP - T, FW), F32)

    def cut(w, lanes):
        wr, wc = w // wcols, w % wcols
        c0 = HALF_LON + WIN_LON * wc
        for i in range(WIN_LAT):
            win[w, WIN_LON * i : WIN_LON * i + WIN_LON, lanes] = frame[
                HALF_LAT + WIN_LAT * wr + i, c0 : c0 + WIN_LON, lanes
            ]

    def holds_sea(w):
        return (jnp.max(win[w, :, M0 : M0 + 128]) > 0.5).astype(jnp.int32)

    def ranks(flags, counted):
        total = jnp.int32(0)
        for f, c in zip(flags, counted):
            total = total + f * c
        out, on, off = [], jnp.int32(0), total
        for f, c in zip(flags, counted):
            out.append(jnp.where(f > 0, on, off))
            on = on + f * c
            off = off + (1 - f) * c
        return out

    def slot_window(k, places):
        slot = jnp.int32(0)
        for w, at in places:
            slot = slot + jnp.where(at == k, w, 0)
        idx[k] = slot

    inner = [w for w in range(nwin) if w // wcols < wrows - 1 and w % wcols < wcols - 1]
    outer = [w for w in range(nwin) if w not in inner]
    active = [None] * nwin
    place = [None] * nwin

    at_end = (lat == nlat - 1).astype(F32)
    gain = gain_ref[...]

    def rows_of(k):
        return pl.ds(pl.multiple_of(k * TP, TP), TP)

    def by_three(step):
        def body(i, carry):
            for j in range(3):
                carry = step(3 * i + j, carry)
            return carry

        return body

    def ln_step(k, carry):
        w = idx[k]
        x = win[w, :, X0 : X0 + C]
        mean = jnp.mean(x, axis=1, keepdims=True)
        xc = x - mean
        inv = lax.rsqrt(jnp.mean(xc * xc, axis=1, keepdims=True) + EPS)
        hat = xc * inv
        rows = rows_of(k)
        xhat[rows, :] = hat
        invd[rows, :] = jnp.broadcast_to(inv, (TP, 128))
        normed[rows, :] = (hat * gain).astype(BF16)
        keys = win[w, :, M0 : M0 + 128]
        side_b = lax.broadcasted_iota(jnp.int32, (TP, 128), 0) >= T // 2
        side_a = lax.broadcasted_iota(jnp.int32, (TP, 128), 1) >= T // 2
        apart = jnp.where(side_a != side_b, 1.0, 0.0)
        wrap = at_end * jnp.where(w >= nwin - wcols, 1.0, 0.0)
        madd[k] = (keys * (1.0 - apart * wrap) - 1.0) * 1e9
        return carry

    def dy_step(k, carry):
        w = idx[k]
        m = win[w, :, M0 : M0 + 128]
        gz[rows_of(k), :] = (win[w, :, D0 : D0 + C] * jnp.concatenate([m] * 4, axis=1)).astype(BF16)
        return carry

    lane = lax.broadcasted_iota(jnp.int32, (TP, 128), 1)
    low = lane < 64
    one_lo = jnp.where(low, 1.0, 0.0).astype(BF16)
    one_hi = jnp.where(low, 0.0, 1.0).astype(BF16)
    q_lo = jnp.where(low, 0.125, 0.0).astype(BF16)
    q_hi = jnp.where(low, 0.0, 0.125).astype(BF16)

    def both_heads(v, lo, hi):
        return jnp.concatenate([pad_rows(v * lo, 128), pad_rows(v * hi, 128)], axis=0)

    def own_head(v):
        return jnp.transpose(jnp.concatenate([v[0:64, 0:128], v[64:128, 128:256]], axis=0))[0:TP]

    def attend(k, carry):
        rows = rows_of(k)
        add = madd[k]
        add2 = jnp.concatenate([add, add], axis=1)
        scores = []
        for p in range(PAIRS):
            q2 = both_heads(packed[rows, 128 * p : 128 * p + 128], q_lo, q_hi)
            scores.append(nt(packed[rows, C + 128 * p : C + 128 * p + 128], q2) + bias2[p] + add2)
        mixes = []
        for p in range(PAIRS):
            s = scores[p]
            e = jnp.exp(s - jnp.max(s, axis=0, keepdims=True))
            pr = e * (1.0 / jnp.sum(e, axis=0, keepdims=True))
            probs[k * PAIRS + p] = pr
            mixes.append(tn(packed[rows, 2 * C + 128 * p : 2 * C + 128 * p + 128], pr.astype(BF16)))
        for p in range(PAIRS):
            mixed[rows, 128 * p : 128 * p + 128] = own_head(mixes[p]).astype(BF16)
        return carry

    def forward(first, last):
        lax.fori_loop(first // 3, last // 3, by_three(ln_step), 0)
        rows = slice(first * TP, last * TP)
        packed[rows, :] = nn(normed[rows, :], wqkv[...]).astype(BF16)
        lax.fori_loop(first, last, attend, 0)

    for w in inner:
        cut(w, slice(0, FW))
        active[w] = holds_sea(w)
    inner_rank = ranks([active[w] for w in inner], [1] * len(inner))
    for k in range(EARLY):
        slot_window(k, list(zip(inner, inner_rank)))
    forward(0, EARLY)

    halo_land(0, xlanes, xcopies)
    for w in outer:
        cut(w, xlanes)
        active[w] = holds_sea(w)
    rest = [jnp.int32(1)] * nwin
    for w, at in zip(inner, inner_rank):
        rest[w] = (at >= EARLY).astype(jnp.int32)
    late_rank = ranks(active, rest)
    for w in range(nwin):
        place[w] = late_rank[w] + EARLY
    for w, at in zip(inner, inner_rank):
        place[w] = jnp.where(at < EARLY, at, place[w])
    for k in range(EARLY, SLOTS):
        slot_window(k, list(enumerate(place)))
    forward(EARLY, SLOTS)

    halo_land(1, dlanes, dcopies)
    for w in outer:
        cut(w, dlanes)
    lax.fori_loop(0, SLOTS // 3, by_three(dy_step), 0)
    gm[...] = nt(gz[0:ROWS, :], wproj[...]).astype(BF16)
    ntp[...] = nt(perm[...], normed[...]).astype(BF16)

    def chunk_start(c, lhs, rhs):
        asend, arecv, own = chunks[c][0:3]
        right = rhs[...]
        other = pl.multiple_of((1 - core) * half, half)
        mine = pl.multiple_of(core * half, half)
        asend[...] = nn(lhs[pl.ds(other, half), :], right).astype(BF16)
        copy = send(asend, arecv, as_.at[c], ar.at[c], partner)
        own[...] = nn(lhs[pl.ds(mine, half), :], right)
        return [copy]

    def chunk_y(c, copies):
        asend, arecv, own, ysend, yrecv = chunks[c][0:5]
        copies[0].wait_recv()
        s = own[...] + arecv[...].astype(F32)
        own[...] = s
        ysend[...] = s.astype(BF16)
        out = []
        for d in range(1, ny):
            start = pl.multiple_of(((y + d) % ny) * ysz, ysz)
            out.append(
                send(ysend.at[pl.ds(start, ysz)], yrecv.at[d - 1], ys.at[c, d - 1], yr.at[c, d - 1], ypeer[d - 1])
            )
        return out

    def chunk_x(c, copies):
        own, ysend, yrecv, xsend, xrecv = chunks[c][2:7]
        s = own[pl.ds(pl.multiple_of(y * ysz, ysz), ysz), :]
        for d in range(1, ny):
            copies[d - 1].wait_recv()
            s = s + yrecv[d - 1].astype(F32)
        for j in range(nxz):
            xsend[j] = s[share * j : share * j + share]
        out = []
        for i, (a, b) in enumerate(xzd):
            j = ((xh + a) % nx) * nz + (z + b) % nz
            out.append(send(xsend.at[j], xrecv.at[i], xs.at[c, i], xr.at[c, i], xzpeer[i]))
        return out

    def chunk_end(c, copies):
        xsend, xrecv = chunks[c][5:7]
        s = xsend[xh * nz + z]
        for i, copy in enumerate(copies):
            copy.wait_recv()
            s = s + xrecv[i]
        if c == 0:
            gproj[...] = s
        else:
            p = c - 1
            for part in range(3):
                gqkv[:, C * part + 128 * p : C * part + 128 * p + 128] = s[:, 128 * part : 128 * part + 128]

    def window_back(o, lane0):
        for w in range(nwin):
            wr, wc = w // wcols, w % wcols
            slot = jnp.minimum(place[w], SLOTS - 1)
            for i in range(WIN_LAT):
                c0 = HALF_LON + WIN_LON * wc
                at = slice(WIN_LON * i, WIN_LON * i + WIN_LON)
                of[o, HALF_LAT + WIN_LAT * wr + i, c0 : c0 + WIN_LON, :] = jnp.where(
                    place[w] < SLOTS, res[slot, at, :], win[w, at, lane0 : lane0 + C]
                )
        colf[0:112, 0:C] = jnp.zeros((112, C), F32)
        for r in range(HALF_LAT, lat_dev):
            colf[6 * r : 6 * r + 6, 0:C] = of[o, r, lon_dev : lon_dev + HALF_LON, :]
        ocs[o, 0:112] = colf[0:112, 0:C].astype(BF16)
        for r in range(HALF_LAT):
            colf[6 * r : 6 * r + 6, 0:C] = of[o, lat_dev + r, lon_dev : lon_dev + HALF_LON, :]
            ors[o, r] = of[o, lat_dev + r, 0:lon_dev, :].astype(BF16)
        ocs[o, 112:144] = colf[0:32, 0:C].astype(BF16)
        return [
            send(ocs.at[o, 0:112], ocr.at[o], os_.at[o, 0], or_.at[o, 0], forth[0]),
            send(ors.at[o], orr.at[o], os_.at[o, 1], or_.at[o, 1], forth[1]),
            send(ocs.at[o, 112:144], occ.at[o], os_.at[o, 2], or_.at[o, 2], forth[2]),
        ]

    def finish(o, copies, out):
        copies[1].wait_recv()
        for r in range(HALF_LAT):
            of[o, r, 0:lon_dev, :] = orr[o, r].astype(F32)
        copies[0].wait_recv()
        colf[0:112, 0:C] = ocr[o].astype(F32)
        for r in range(HALF_LAT, lat_dev):
            of[o, r, 0:HALF_LON, :] = colf[6 * r : 6 * r + 6, 0:C]
        copies[2].wait_recv()
        colf[0:32, 0:C] = occ[o].astype(F32)
        for r in range(HALF_LAT):
            of[o, r, 0:HALF_LON, :] = colf[6 * r : 6 * r + 6, 0:C]
        for r in range(lat_dev):
            out[r] = of[o, r, 0:lon_dev, :].astype(BF16)

    mtp[...] = nt(perm[...], mixed[...]).astype(BF16)
    st = {}
    st[0] = chunk_start(0, mtp, gz)

    gnacc[...] = nn(mixed[0:ROWS, :], wproj[...])

    def updated_step(k, carry):
        w = idx[k]
        m = win[w, :, M0 : M0 + 128]
        res[k] = win[w, :, X0 : X0 + C] + jnp.concatenate([m] * 4, axis=1) * gnacc[rows_of(k), :]
        return carry

    lax.fori_loop(0, SLOTS // 3, by_three(updated_step), 0)
    out_copies = [window_back(0, X0), None]

    def backward(p):
        bacc[p] = jnp.zeros((TP, 256), F32)

        def step(i, carry):
            ks = [3 * i + j for j in range(3)]
            d2s, dps = [], []
            for k in ks:
                rows = rows_of(k)
                d2s.append(both_heads(gm[rows, 128 * p : 128 * p + 128], one_lo, one_hi))
                dps.append(nt(packed[rows, 2 * C + 128 * p : 2 * C + 128 * p + 128], d2s[-1]))
            dss, dvs = [], []
            for j, k in enumerate(ks):
                pr = probs[k * PAIRS + p]
                t = pr * dps[j]
                dss.append(t - pr * jnp.sum(t, axis=0, keepdims=True))
                dvs.append(nn(pr.astype(BF16), d2s[j]))
            bacc[p] += dss[0] + dss[1] + dss[2]
            dqs = []
            for j, k in enumerate(ks):
                rows = rows_of(k)
                ds = dss[j].astype(BF16)
                q2 = both_heads(packed[rows, 128 * p : 128 * p + 128], q_lo, q_hi)
                dqs.append(tn(packed[rows, C + 128 * p : C + 128 * p + 128], ds))
                dp3[p, rows, 128:256] = nn(ds, q2).astype(BF16)
                dp3[p, rows, 256:384] = dvs[j].astype(BF16)
            for j, k in enumerate(ks):
                dp3[p, rows_of(k), 0:128] = (own_head(dqs[j]) * 0.125).astype(BF16)
            return carry

        lax.fori_loop(0, SLOTS // 3, step, 0)

    def weight_pair(p):
        return jnp.concatenate([wqkv[:, C * part + 128 * p : C * part + 128 * p + 128] for part in range(3)], axis=1)

    def grad_normed(p):
        g = nt(dp3[p, 0:ROWS, :], weight_pair(p))
        gnacc[...] = g if p == 0 else gnacc[...] + g

    for p in range(PAIRS):
        backward(p)
        st[p + 1] = chunk_start(p + 1, ntp, dp3.at[p])
        if p >= 0:
            st[p] = chunk_y(p, st[p])
        if p >= 1:
            st[p - 1] = chunk_x(p - 1, st[p - 1])
        grad_normed(p)

    def sum_core(g):
        sm, smc = sums[g][0:2]
        return send(sm, smc, ss.at[g, 0], sr.at[g, 0], partner)

    def sum_y(g, copy):
        sm, smc, smy, smx = sums[g]
        copy.wait_recv()
        smy[y] = sm[...] + smc[...]
        return [
            send(smy.at[y], smy.at[y], ss.at[g, d], sr.at[g, d], ypeer[d - 1]) for d in range(1, ny)
        ]

    def sum_xz(g, copies):
        sm, smc, smy, smx = sums[g]
        for copy in copies:
            copy.wait_recv()
        acc = smy[0]
        for j in range(1, ny):
            acc = acc + smy[j]
        here = xh * nz + z
        smx[here] = acc
        return [
            send(smx.at[here], smx.at[here], ss.at[g, ny + i], sr.at[g, ny + i], xzpeer[i])
            for i in range(len(xzd))
        ]

    def sum_end(g, copies):
        smx = sums[g][3]
        for copy in copies:
            copy.wait_recv()
        acc = smx[0]
        for j in range(1, nxz):
            acc = acc + smx[j]
        return acc

    def norm_back(k, total):
        w = idx[k]
        rows = rows_of(k)
        gn = gnacc[rows, :]
        hat = xhat[rows, :]
        g = gn * gain
        prod = g * hat
        mid = g - jnp.mean(g, axis=1, keepdims=True) - hat * jnp.mean(prod, axis=1, keepdims=True)
        inv = jnp.concatenate([invd[rows, :]] * 4, axis=1)
        res[k] = win[w, :, D0 : D0 + C] + inv * mid
        return total + jnp.sum(gn * hat, axis=0, keepdims=True)

    gsum = lax.fori_loop(0, SLOTS // 3, by_three(norm_back), jnp.zeros((1, C), F32))
    sums[1][0][...] = jnp.zeros((8, 128), F32)
    for j in range(4):
        sums[1][0][j : j + 1, :] = gsum[:, 128 * j : 128 * j + 128]
    gain_copies = sum_core(1)
    st[4] = chunk_y(4, st[4])
    out_copies[1] = window_back(1, D0)
    st[3] = chunk_x(3, st[3])

    stacked = jnp.concatenate([bacc[h // 2, :, 128 * (h % 2) : 128 * (h % 2) + 128] for h in range(HEADS)], axis=0)
    by_place = sum(nn(v, self_[...]) for v in pieces(stacked, 2))
    by_place = jnp.concatenate([by_place[TP * h : TP * h + TP] for h in range(HEADS)], axis=1)
    spread = sum(nn(selrt[:, 0:TP], v) for v in pieces(by_place, 2))
    for h in range(HEADS):
        wide = jnp.concatenate([spread[:, 128 * h : 128 * h + 128], jnp.zeros((128, 128), F32)], axis=1)
        sums[0][0][h : h + 1, :] = jnp.sum(pltpu.roll(wide, 0, 1, stride=1, stride_axis=0), axis=0, keepdims=True)
    bias_copies = sum_core(0)

    st[4] = chunk_x(4, st[4])
    bias_copies = sum_y(0, bias_copies)
    gain_copies = sum_y(1, gain_copies)
    finish(0, out_copies[0], upd)
    stores[0].start()
    bias_copies = sum_xz(0, bias_copies)
    gain_copies = sum_xz(1, gain_copies)
    for c in range(nchunk - 1):
        chunk_end(c, st[c])
    finish(1, out_copies[1], gin)
    stores[1].start()
    bias_out[...] = sum_end(0, bias_copies)[:, 0:REL]
    chunk_end(nchunk - 1, st[nchunk - 1])
    acc = sum_end(1, gain_copies)
    for j in range(4):
        gain_out[:, 128 * j : 128 * j + 128] = acc[j : j + 1, :]
    for store in stores[2:]:
        store.start()
    for copy in sends:
        copy.wait_send()
    for store in stores:
        store.wait()


def hand_over(*refs):
    arrived, left = refs[18:20]
    steps = []
    for i in range(6):
        rows = refs[i].shape[0]
        size = 3 if i < 2 else rows
        steps += [(i, pl.ds(start, size)) for start in range(0, rows, size)]
    fetches = [
        pltpu.make_async_copy(refs[i].at[at], refs[12 + i].at[at], arrived.at[n]) for n, (i, at) in enumerate(steps)
    ]
    stores = [
        pltpu.make_async_copy(refs[12 + i].at[at], refs[6 + i].at[at], left.at[n]) for n, (i, at) in enumerate(steps)
    ]
    for fetch in fetches:
        fetch.start()
    for fetch, store in zip(fetches, stores):
        fetch.wait()
        store.start()
    for store in stores:
        store.wait()


def constants(ny, nx, nz):
    share = C // (ny * nx * nz * 2)
    perm = np.zeros((C, C), np.float32)
    for core in range(2):
        for y in range(ny):
            for xh in range(nx):
                for z in range(nz):
                    to = (((core * ny + y) * nx + xh) * nz + z) * share
                    start = (((y * nx + xh) * nz + z) * 2 + core) * share
                    perm[to + np.arange(share), start + np.arange(share)] = 1
    a = np.arange(T)
    pa = (a // WIN_LON) * (2 * WIN_LON - 1) + a % WIN_LON
    selrt = np.zeros((128, 128), np.float32)
    selrt[126 - pa, a] = 1
    self_ = np.zeros((128, 128), np.float32)
    self_[a, pa] = 1
    return perm, self_, self_.T, selrt


def solution(mesh):
    nlon, nlat = mesh.shape["lon"], mesh.shape["lat"]
    nx, nz = 2, nlat // 2
    ny = nlon // nx
    nxz = nx * nz
    half = C // 2
    ysz = half // ny
    share = ysz // nxz
    cols = [C] + [384] * PAIRS
    lat_dev, lon_dev = 18, 48
    nwin = 12
    vm = pltpu.VMEM
    dma = lambda *s: pltpu.SemaphoreType.DMA(s)
    perm, self_, selft, selrt = (jnp.asarray(v, BF16) for v in constants(ny, nx, nz))

    def on_device(fields, grad_out, layernorm_gain, qkv_weight, proj_weight, bias_table, sea_mask):
        shapes = (
            jax.ShapeDtypeStruct((lat_dev, lon_dev, C), BF16),
            jax.ShapeDtypeStruct((lat_dev, lon_dev, C), BF16),
            jax.ShapeDtypeStruct((1, C), F32),
            jax.ShapeDtypeStruct((HEADS, REL), F32),
            jax.ShapeDtypeStruct((share, 3 * C), F32),
            jax.ShapeDtypeStruct((share, C), F32),
        )
        scratch = [
            vm((lat_dev, lon_dev, C), BF16),
            vm((lat_dev, lon_dev), jnp.int32),
            vm((lat_dev, lon_dev, C), BF16),
            vm((HEADS, REL), F32),
            vm((128, 128), BF16),
            vm((128, 128), BF16),
            vm((128, 128), BF16),
            vm((1, C), F32),
            vm((C, 3 * C), BF16),
            vm((C, C), BF16),
            vm((C, C), BF16),
        ]
        scratch += [vm(v.shape, v.dtype) for v in shapes]
        scratch += [
            vm((lat_dev + 3, 56, FW), F32),
            vm((nwin, TP, FW), F32),
            vm((112, FW), F32),
        ]
        for wide in (XW, DW):
            scratch += [
                vm((112, wide), BF16),
                vm((112, wide), BF16),
                vm((3, lon_dev, wide), BF16),
                vm((3, lon_dev, wide), BF16),
                vm((32, wide), BF16),
            ]
        scratch += [
            pltpu.SMEM((16,), jnp.int32),
            vm((HEADS, 256), F32),
            vm((PAIRS, TP, 256), F32),
            vm((SLOTS, TP, 128), F32),
            vm((ROWS, C), F32),
            vm((ROWS, 128), F32),
            vm((RP, C), BF16),
            vm((RP, C), BF16),
            vm((ROWS, C), BF16),
            vm((ROWS, 3 * C), BF16),
            vm((RP, C), BF16),
            vm((C, RP), BF16),
            vm((C, RP), BF16),
            vm((SLOTS * PAIRS, TP, 256), F32),
            vm((PAIRS, RP, 384), BF16),
            vm((ROWS, C), F32),
            vm((PAIRS, TP, 256), F32),
            vm((SLOTS, TP, C), F32),
            vm((2, lat_dev + 3, 56, C), F32),
            vm((2, 144, C), BF16),
            vm((2, 3, lon_dev, C), BF16),
            vm((2, 112, C), BF16),
            vm((2, 3, lon_dev, C), BF16),
            vm((2, 32, C), BF16),
        ]
        for n in cols:
            scratch += [
                vm((half, n), BF16),
                vm((half, n), BF16),
                vm((half, n), F32),
                vm((half, n), BF16),
                vm((ny - 1, ysz, n), BF16),
                vm((nxz, share, n), F32),
                vm((nxz - 1, share, n), F32),
            ]
        for sm in ((8, 256), (8, 128)):
            scratch += [vm(sm, F32), vm(sm, F32), vm((ny,) + sm, F32), vm((nxz,) + sm, F32)]
        nc = len(cols)
        small = ny + nxz - 1
        scratch += [
            dma(2, 3), dma(2, 3), dma(2, 3), dma(2, 3), dma(nc), dma(nc), dma(nc, ny - 1), dma(nc, ny - 1),
            dma(nc, nxz - 1), dma(nc, nxz - 1), dma(2, small), dma(2, small), dma(11), dma(6),
        ]
        anywhere = pl.BlockSpec(memory_space=pl.ANY)
        outs = pl.pallas_call(
            functools.partial(kernel, (ny, nx, nz), cols),
            out_shape=shapes,
            in_specs=[anywhere] * 11,
            out_specs=(anywhere,) * 6,
            scratch_shapes=scratch,
            compiler_params=pltpu.CompilerParams(
                collective_id=0, has_side_effects=True, vmem_limit_bytes=60 * 1024 * 1024
            ),
        )(
            fields, sea_mask, grad_out, bias_table, self_, selft, selrt,
            layernorm_gain.reshape(1, C), qkv_weight, proj_weight, perm,
        )
        outs = pl.pallas_call(
            hand_over,
            out_shape=shapes,
            in_specs=[anywhere] * 6,
            out_specs=(anywhere,) * 6,
            scratch_shapes=[vm(v.shape, v.dtype) for v in shapes] + [dma(16), dma(16)],
            compiler_params=pltpu.CompilerParams(vmem_limit_bytes=60 * 1024 * 1024),
        )(*outs)
        updated, grad_in, grad_gain, grad_bias, grad_qkv, grad_proj = outs
        return (updated, grad_in, grad_gain.reshape(C), grad_bias, grad_qkv, grad_proj)

    grid = P(("batch", "lat"), "lon", None)
    return jax.shard_map(
        on_device,
        mesh=mesh,
        in_specs=(grid, grid, P(), P(), P(), P(), P(("batch", "lat"), "lon")),
        out_specs=(
            grid,
            grid,
            P("batch"),
            P("batch", None),
            P(("batch", "lon", "lat"), None),
            P(("batch", "lon", "lat"), None),
        ),
        check_vma=False,
    )
```

```python
import functools

import jax
import jax.numpy as jnp
import numpy as np
from jax import lax
from jax.experimental import pallas as pl
from jax.experimental.pallas import tpu as pltpu
from jax.sharding import PartitionSpec as P

MESH = pl.DeviceIdType.MESH
F32 = jnp.float32
BF16 = jnp.bfloat16
C = 512
HEADS = 8
PAIRS = 4
WIN_LAT = 6
WIN_LON = 12
HALF_LAT = 3
HALF_LON = 6
T = 72
TP = 80
SLOTS = 9
ROWS = SLOTS * TP
RP = 768
REL = 253
X0, M0, D0, FW = 0, 512, 640, 1152
EARLY = 3
EPS = 1e-5


def nn(a, b, **kw):
    return lax.dot_general(a, b, (((1,), (0,)), ((), ())), preferred_element_type=F32, **kw)


def nt(a, b, **kw):
    return lax.dot_general(a, b, (((1,), (1,)), ((), ())), preferred_element_type=F32, **kw)


def tn(a, b, **kw):
    return lax.dot_general(a, b, (((0,), (0,)), ((), ())), preferred_element_type=F32, **kw)


def pad_rows(v, rows):
    return jnp.concatenate([v, jnp.zeros((rows - v.shape[0], v.shape[1]), v.dtype)], axis=0)


def kernel(dims, cols, *refs):
    ny, nx, nz = dims
    nlon, nlat = ny * nx, 2 * nz
    nxz = nx * nz
    lat_dev, lon_dev = 18, 48
    wrows, wcols = lat_dev // WIN_LAT, lon_dev // WIN_LON
    nwin = wrows * wcols
    half = C // 2
    ysz = half // ny
    share = ysz // nxz
    nchunk = len(cols)

    it = iter(refs)
    take = lambda n=None: next(it) if n is None else [next(it) for _ in range(n)]
    given = take(11)
    results = take(6)
    held = take(11)
    x_ref, mask_ref, dy_ref, table, self_, selft, selrt, gain_ref, wqkv, wproj, perm = held
    staged = take(6)
    upd, gin, gain_out, bias_out, gqkv, gproj = staged
    frame, win, colf = take(3)
    halos = [take(5) for _ in range(2)]
    masks = take(3)
    idx = take()
    tb, bias2, madd, xhat, invd, normed, gz, gm, packed, mixed, ntp, mtp, probs, dp3, gnacc, bacc = take(16)
    res, of = take(2)
    ocs, ors, ocr, orr, occ = take(5)
    chunks = [take(8) for _ in range(nchunk)]
    groups = [take(2) for _ in range(2)]
    sums = take(6)
    hs, hr, ms, mr, os_, or_, as_, ar, ys, yr, xs, xr, zs, zr, ss, sr = take(16)
    ins, outs = take(2)

    lon = lax.axis_index("lon")
    lat = lax.axis_index("lat")
    y, xh = lon // nx, lon % nx
    z, core = lat // 2, lat % 2

    def dev(a, b):
        return {"lon": a, "lat": b}

    partner = dev(lon, z * 2 + (1 - core))
    ypeer = [dev(((y + d) % ny) * nx + xh, lat) for d in range(1, ny)]
    xpeer = dev(y * nx + (1 - xh), lat)
    zpeer = [dev(lon, ((z + d) % nz) * 2 + core) for d in range(1, nz)]
    west, east = (lon + nlon - 1) % nlon, (lon + 1) % nlon
    north, south = (lat + nlat - 1) % nlat, (lat + 1) % nlat
    back = [dev(west, lat), dev(lon, north), dev(west, north)]
    forth = [dev(east, lat), dev(lon, south), dev(east, south)]

    barrier = pltpu.get_barrier_semaphore()
    everyone = [partner, xpeer] + ypeer + zpeer + back + forth
    for d in everyone:
        pl.semaphore_signal(barrier, inc=1, device_id=d, device_id_type=MESH)

    loads = [pltpu.make_async_copy(a, b, ins.at[i]) for i, (a, b) in enumerate(zip(given, held))]
    for load in loads:
        load.start()

    stores = [pltpu.make_async_copy(a, b, outs.at[i]) for i, (a, b) in enumerate(zip(staged, results))]
    sends = []

    def send(src, dst, ssem, rsem, d):
        copy = pltpu.make_async_remote_copy(
            src_ref=src, dst_ref=dst, send_sem=ssem, recv_sem=rsem, device_id=d, device_id_type=MESH
        )
        copy.start()
        sends.append(copy)
        return copy

    lane_row = lax.broadcasted_iota(jnp.int32, (lat_dev, lat_dev * 128), 1) // 128
    pick = (lane_row == lax.broadcasted_iota(jnp.int32, (lat_dev, lat_dev * 128), 0)).astype(F32)

    def spread_mask(ref):
        return tn(ref[...].astype(F32), pick)

    loads[1].wait()
    sea = spread_mask(mask_ref)
    colf[96:112, :] = jnp.zeros((16, FW), F32)

    def halo_pack(h, lanes):
        colsend, colrecv, rowsend, rowrecv, cornrecv = halos[h]
        for r in range(lat_dev):
            colf[6 * r : 6 * r + 6, lanes] = frame[r, 0:HALF_LON, lanes]
        colsend[...] = colf[:, lanes].astype(BF16)
        for r in range(HALF_LAT):
            rowsend[r] = frame[r, 0:lon_dev, lanes].astype(BF16)

    def halo_send(h):
        colsend, colrecv, rowsend, rowrecv, cornrecv = halos[h]
        return [
            send(colsend, colrecv, hs.at[h, 0], hr.at[h, 0], back[0]),
            send(rowsend, rowrecv, hs.at[h, 1], hr.at[h, 1], back[1]),
            send(colsend.at[0:32], cornrecv, hs.at[h, 2], hr.at[h, 2], back[2]),
        ]

    def halo_land(h, lanes, copies):
        colsend, colrecv, rowsend, rowrecv, cornrecv = halos[h]
        copies[1].wait_recv()
        for r in range(HALF_LAT):
            frame[lat_dev + r, 0:lon_dev, lanes] = rowrecv[r].astype(F32)
        copies[2].wait_recv()
        colf[0:32, lanes] = cornrecv[...].astype(F32)
        for r in range(HALF_LAT):
            frame[lat_dev + r, lon_dev : lon_dev + HALF_LON, lanes] = colf[6 * r : 6 * r + 6, lanes]
        copies[0].wait_recv()
        colf[:, lanes] = colrecv[...].astype(F32)
        for r in range(lat_dev):
            frame[r, lon_dev : lon_dev + HALF_LON, lanes] = colf[6 * r : 6 * r + 6, lanes]

    xlanes, dlanes = slice(X0, X0 + C), slice(D0, D0 + C)
    loads[0].wait()
    for r in range(lat_dev):
        frame[r, 0:lon_dev, X0 : X0 + C] = x_ref[r].astype(F32)
        frame[r, 0:lon_dev, M0 : M0 + 128] = sea[:, 128 * r : 128 * r + 128]
    halo_pack(0, xlanes)
    pl.semaphore_wait(barrier, len(everyone))
    mcopies = [send(mask_ref, masks[i], ms.at[i], mr.at[i], back[i]) for i in range(3)]
    xcopies = halo_send(0)
    loads[2].wait()
    for r in range(lat_dev):
        frame[r, 0:lon_dev, D0 : D0 + C] = dy_ref[r].astype(F32)
    halo_pack(1, dlanes)
    dcopies = halo_send(1)

    def pieces(v, n):
        out = []
        for i in range(n):
            part = v.astype(BF16)
            out.append(part)
            if i < n - 1:
                v = v - part.astype(F32)
        return out

    for i in range(3, 11):
        loads[i].wait()
    tb[...] = jnp.zeros_like(tb)
    tb[:, 0:REL] = table[...]
    shifted = []
    for h in range(HEADS):
        line = jnp.broadcast_to(tb[h : h + 1, :], (128, 256))
        shifted.append(pltpu.roll(pltpu.roll(line, 2, 1), 128, 1, stride=1, stride_axis=0)[:, 0:128])
    by_query = sum(nn(v, selft[...]) for v in pieces(jnp.concatenate(shifted, axis=0), 3))
    by_query = jnp.concatenate([by_query[128 * h : 128 * h + 128] for h in range(HEADS)], axis=1)
    whole_bias = sum(nn(self_[0:TP, :], v) for v in pieces(by_query, 3))
    for p in range(PAIRS):
        bias2[p] = whole_bias[:, 256 * p : 256 * p + 256]

    zero_tail = jnp.zeros((RP - ROWS, C), BF16)
    normed[ROWS:RP, :] = zero_tail
    gz[ROWS:RP, :] = zero_tail
    mixed[ROWS:RP, :] = zero_tail
    for p in range(PAIRS):
        dp3[p, ROWS:RP, :] = jnp.zeros((RP - ROWS, 384), BF16)
    for w in range(nwin):
        win[w, T:TP, :] = jnp.zeros((TP - T, FW), F32)

    def cut(w, lanes):
        wr, wc = w // wcols, w % wcols
        c0 = HALF_LON + WIN_LON * wc
        for i in range(WIN_LAT):
            win[w, WIN_LON * i : WIN_LON * i + WIN_LON, lanes] = frame[
                HALF_LAT + WIN_LAT * wr + i, c0 : c0 + WIN_LON, lanes
            ]

    def holds_sea(w):
        return (jnp.max(win[w, :, M0 : M0 + 128]) > 0.5).astype(jnp.int32)

    def ranks(flags, counted):
        total = jnp.int32(0)
        for f, c in zip(flags, counted):
            total = total + f * c
        out, on, off = [], jnp.int32(0), total
        for f, c in zip(flags, counted):
            out.append(jnp.where(f > 0, on, off))
            on = on + f * c
            off = off + (1 - f) * c
        return out

    def slot_window(k, places):
        slot = jnp.int32(0)
        for w, at in places:
            slot = slot + jnp.where(at == k, w, 0)
        idx[k] = slot

    inner = [w for w in range(nwin) if w // wcols < wrows - 1 and w % wcols < wcols - 1]
    outer = [w for w in range(nwin) if w not in inner]
    active = [None] * nwin
    place = [None] * nwin

    at_end = (lat == nlat - 1).astype(F32)
    gain = gain_ref[...]

    def rows_of(k):
        return pl.ds(pl.multiple_of(k * TP, TP), TP)

    def by_three(step):
        def body(i, carry):
            for j in range(3):
                carry = step(3 * i + j, carry)
            return carry

        return body

    def ln_step(k, carry):
        w = idx[k]
        x = win[w, :, X0 : X0 + C]
        mean = jnp.mean(x, axis=1, keepdims=True)
        xc = x - mean
        inv = lax.rsqrt(jnp.mean(xc * xc, axis=1, keepdims=True) + EPS)
        hat = xc * inv
        rows = rows_of(k)
        xhat[rows, :] = hat
        invd[rows, :] = jnp.broadcast_to(inv, (TP, 128))
        normed[rows, :] = (hat * gain).astype(BF16)
        keys = win[w, :, M0 : M0 + 128]
        side_b = lax.broadcasted_iota(jnp.int32, (TP, 128), 0) >= T // 2
        side_a = lax.broadcasted_iota(jnp.int32, (TP, 128), 1) >= T // 2
        apart = jnp.where(side_a != side_b, 1.0, 0.0)
        wrap = at_end * jnp.where(w >= nwin - wcols, 1.0, 0.0)
        madd[k] = (keys * (1.0 - apart * wrap) - 1.0) * 1e9
        return carry

    def dy_step(k, carry):
        w = idx[k]
        m = win[w, :, M0 : M0 + 128]
        gz[rows_of(k), :] = (win[w, :, D0 : D0 + C] * jnp.concatenate([m] * 4, axis=1)).astype(BF16)
        return carry

    lane = lax.broadcasted_iota(jnp.int32, (TP, 128), 1)
    low = lane < 64
    one_lo = jnp.where(low, 1.0, 0.0).astype(BF16)
    one_hi = jnp.where(low, 0.0, 1.0).astype(BF16)
    q_lo = jnp.where(low, 0.125, 0.0).astype(BF16)
    q_hi = jnp.where(low, 0.0, 0.125).astype(BF16)

    def both_heads(v, lo, hi):
        return jnp.concatenate([pad_rows(v * lo, 128), pad_rows(v * hi, 128)], axis=0)

    def own_head(v):
        return jnp.transpose(jnp.concatenate([v[0:64, 0:128], v[64:128, 128:256]], axis=0))[0:TP]

    def attend(k, carry):
        rows = rows_of(k)
        add = madd[k]
        add2 = jnp.concatenate([add, add], axis=1)
        scores = []
        for p in range(PAIRS):
            q2 = both_heads(packed[rows, 128 * p : 128 * p + 128], q_lo, q_hi)
            scores.append(nt(packed[rows, C + 128 * p : C + 128 * p + 128], q2) + bias2[p] + add2)
        mixes = []
        for p in range(PAIRS):
            s = scores[p]
            e = jnp.exp(s - jnp.max(s, axis=0, keepdims=True))
            pr = e * (1.0 / jnp.sum(e, axis=0, keepdims=True))
            probs[k * PAIRS + p] = pr
            mixes.append(tn(packed[rows, 2 * C + 128 * p : 2 * C + 128 * p + 128], pr.astype(BF16)))
        for p in range(PAIRS):
            mixed[rows, 128 * p : 128 * p + 128] = own_head(mixes[p]).astype(BF16)
        return carry

    def forward(first, last):
        lax.fori_loop(first // 3, last // 3, by_three(ln_step), 0)
        rows = slice(first * TP, last * TP)
        packed[rows, :] = nn(normed[rows, :], wqkv[...]).astype(BF16)
        lax.fori_loop(first, last, attend, 0)

    for w in inner:
        cut(w, slice(0, FW))
        active[w] = holds_sea(w)
    inner_rank = ranks([active[w] for w in inner], [1] * len(inner))
    for k in range(EARLY):
        slot_window(k, list(zip(inner, inner_rank)))
    forward(0, EARLY)

    mlanes = slice(M0, M0 + 128)
    for copy in mcopies:
        copy.wait_recv()
    sea = spread_mask(masks[0])
    for r in range(lat_dev):
        frame[r, lon_dev : lon_dev + HALF_LON, mlanes] = sea[0:HALF_LON, 128 * r : 128 * r + 128]
    sea = spread_mask(masks[1])
    for r in range(HALF_LAT):
        frame[lat_dev + r, 0:lon_dev, mlanes] = sea[:, 128 * r : 128 * r + 128]
    sea = spread_mask(masks[2])
    for r in range(HALF_LAT):
        frame[lat_dev + r, lon_dev : lon_dev + HALF_LON, mlanes] = sea[0:HALF_LON, 128 * r : 128 * r + 128]
    halo_land(0, xlanes, xcopies)
    for w in outer:
        cut(w, slice(X0, M0 + 128))
        active[w] = holds_sea(w)
    rest = [jnp.int32(1)] * nwin
    for w, at in zip(inner, inner_rank):
        rest[w] = (at >= EARLY).astype(jnp.int32)
    late_rank = ranks(active, rest)
    for w in range(nwin):
        place[w] = late_rank[w] + EARLY
    for w, at in zip(inner, inner_rank):
        place[w] = jnp.where(at < EARLY, at, place[w])
    for k in range(EARLY, SLOTS):
        slot_window(k, list(enumerate(place)))
    forward(EARLY, SLOTS)

    halo_land(1, dlanes, dcopies)
    for w in outer:
        cut(w, dlanes)
    lax.fori_loop(0, SLOTS // 3, by_three(dy_step), 0)
    gm[...] = nt(gz[0:ROWS, :], wproj[...]).astype(BF16)
    ntp[...] = nt(perm[...], normed[...]).astype(BF16)

    def chunk_start(c, lhs, rhs):
        asend, arecv, own = chunks[c][0:3]
        right = rhs[...]
        other = pl.multiple_of((1 - core) * half, half)
        mine = pl.multiple_of(core * half, half)
        asend[...] = nn(lhs[pl.ds(other, half), :], right).astype(BF16)
        copy = send(asend, arecv, as_.at[c], ar.at[c], partner)
        own[...] = nn(lhs[pl.ds(mine, half), :], right)
        return [copy]

    def chunk_y(c, copies):
        asend, arecv, own, ysend, yrecv = chunks[c][0:5]
        copies[0].wait_recv()
        s = own[...] + arecv[...].astype(F32)
        own[...] = s
        ysend[...] = s.astype(BF16)
        out = []
        for d in range(1, ny):
            start = pl.multiple_of(((y + d) % ny) * ysz, ysz)
            out.append(
                send(ysend.at[pl.ds(start, ysz)], yrecv.at[d - 1], ys.at[c, d - 1], yr.at[c, d - 1], ypeer[d - 1])
            )
        return out

    def chunk_x(c, copies):
        own, ysend, yrecv, xsend, xrecv, xown = chunks[c][2:8]
        s = own[pl.ds(pl.multiple_of(y * ysz, ysz), ysz), :]
        for d in range(1, ny):
            copies[d - 1].wait_recv()
            s = s + yrecv[d - 1].astype(F32)
        top, low_half = s[0 : ysz // 2], s[ysz // 2 : ysz]
        first = xh == 0
        xsend[...] = jnp.where(first, low_half, top).astype(BF16)
        xown[...] = jnp.where(first, top, low_half)
        return [send(xsend, xrecv, xs.at[c], xr.at[c], xpeer)]

    def chunk_z(c, copies):
        xsend, xrecv, xown = chunks[c][5:8]
        zsend = groups[0 if c < 4 else 1][0]
        start = sum(cols[:c]) if c < 4 else 0
        copies[0].wait_recv()
        s = xown[...] + xrecv[...].astype(F32)
        for j in range(nz):
            zsend[j, :, start : start + cols[c]] = s[share * j : share * j + share]

    def group_send(g):
        zsend, zrecv = groups[g]
        return [
            send(zsend.at[(z + d) % nz], zrecv.at[d - 1], zs.at[g, d - 1], zr.at[g, d - 1], zpeer[d - 1])
            for d in range(1, nz)
        ]

    def group_end(g, copies):
        zsend, zrecv = groups[g]
        s = zsend[z]
        for i, copy in enumerate(copies):
            copy.wait_recv()
            s = s + zrecv[i]
        start = 0
        for c in range(nchunk):
            if (c < 4) != (g == 0):
                continue
            if c == 0:
                gproj[...] = s[:, 0:C]
            else:
                p = c - 1
                for part in range(3):
                    at = start + 128 * part
                    gqkv[:, C * part + 128 * p : C * part + 128 * p + 128] = s[:, at : at + 128]
            start += cols[c]

    def window_back(o, lane0):
        def place_window(w):
            wr, wc = w // wcols, w % wcols
            slot = jnp.minimum(place[w], SLOTS - 1)
            for i in range(WIN_LAT):
                c0 = HALF_LON + WIN_LON * wc
                at = slice(WIN_LON * i, WIN_LON * i + WIN_LON)
                of[o, HALF_LAT + WIN_LAT * wr + i, c0 : c0 + WIN_LON, :] = jnp.where(
                    place[w] < SLOTS, res[slot, at, :], win[w, at, lane0 : lane0 + C]
                )

        for w in range(wcols - 1, nwin, wcols):
            place_window(w)
        colf[0 : 6 * HALF_LAT, 0:C] = jnp.zeros((6 * HALF_LAT, C), F32)
        for r in range(HALF_LAT, lat_dev):
            colf[6 * r : 6 * r + 6, 0:C] = of[o, r, lon_dev : lon_dev + HALF_LON, :]
        ocs[o, 0:112] = colf[0:112, 0:C].astype(BF16)
        for r in range(HALF_LAT):
            colf[6 * r : 6 * r + 6, 0:C] = of[o, lat_dev + r, lon_dev : lon_dev + HALF_LON, :]
        ocs[o, 112:144] = colf[0:32, 0:C].astype(BF16)
        copies = [
            send(ocs.at[o, 0:112], ocr.at[o], os_.at[o, 0], or_.at[o, 0], forth[0]),
            send(ocs.at[o, 112:144], occ.at[o], os_.at[o, 2], or_.at[o, 2], forth[2]),
        ]
        for w in range(nwin - wcols, nwin - 1):
            place_window(w)
        for r in range(HALF_LAT):
            ors[o, r] = of[o, lat_dev + r, 0:lon_dev, :].astype(BF16)
        copies.insert(1, send(ors.at[o], orr.at[o], os_.at[o, 1], or_.at[o, 1], forth[1]))
        for w in range(nwin - wcols):
            if w % wcols < wcols - 1:
                place_window(w)
        return copies

    def finish(o, copies, out):
        copies[1].wait_recv()
        for r in range(HALF_LAT):
            of[o, r, 0:lon_dev, :] = orr[o, r].astype(F32)
        copies[0].wait_recv()
        colf[0:112, 0:C] = ocr[o].astype(F32)
        for r in range(HALF_LAT, lat_dev):
            of[o, r, 0:HALF_LON, :] = colf[6 * r : 6 * r + 6, 0:C]
        copies[2].wait_recv()
        colf[0:32, 0:C] = occ[o].astype(F32)
        for r in range(HALF_LAT):
            of[o, r, 0:HALF_LON, :] = colf[6 * r : 6 * r + 6, 0:C]
        for r in range(lat_dev):
            out[r] = of[o, r, 0:lon_dev, :].astype(BF16)

    mtp[...] = nt(perm[...], mixed[...]).astype(BF16)
    st = {}
    st[0] = chunk_start(0, mtp, gz)

    gnacc[...] = nn(mixed[0:ROWS, :], wproj[...])

    def updated_step(k, carry):
        w = idx[k]
        m = win[w, :, M0 : M0 + 128]
        res[k] = win[w, :, X0 : X0 + C] + jnp.concatenate([m] * 4, axis=1) * gnacc[rows_of(k), :]
        return carry

    lax.fori_loop(0, SLOTS // 3, by_three(updated_step), 0)
    out_copies = [window_back(0, X0), None]

    def backward(p):
        bacc[p] = jnp.zeros((TP, 256), F32)

        def step(i, carry):
            ks = [3 * i + j for j in range(3)]
            d2s, dps = [], []
            for k in ks:
                rows = rows_of(k)
                d2s.append(both_heads(gm[rows, 128 * p : 128 * p + 128], one_lo, one_hi))
                dps.append(nt(packed[rows, 2 * C + 128 * p : 2 * C + 128 * p + 128], d2s[-1]))
            dss, dvs = [], []
            for j, k in enumerate(ks):
                pr = probs[k * PAIRS + p]
                t = pr * dps[j]
                dss.append(t - pr * jnp.sum(t, axis=0, keepdims=True))
                dvs.append(nn(pr.astype(BF16), d2s[j]))
            bacc[p] += dss[0] + dss[1] + dss[2]
            dqs = []
            for j, k in enumerate(ks):
                rows = rows_of(k)
                ds = dss[j].astype(BF16)
                q2 = both_heads(packed[rows, 128 * p : 128 * p + 128], q_lo, q_hi)
                dqs.append(tn(packed[rows, C + 128 * p : C + 128 * p + 128], ds))
                dp3[p, rows, 128:256] = nn(ds, q2).astype(BF16)
                dp3[p, rows, 256:384] = dvs[j].astype(BF16)
            for j, k in enumerate(ks):
                dp3[p, rows_of(k), 0:128] = (own_head(dqs[j]) * 0.125).astype(BF16)
            return carry

        lax.fori_loop(0, SLOTS // 3, step, 0)

    def weight_pair(p):
        return jnp.concatenate([wqkv[:, C * part + 128 * p : C * part + 128 * p + 128] for part in range(3)], axis=1)

    def grad_normed(p):
        g = nt(dp3[p, 0:ROWS, :], weight_pair(p))
        gnacc[...] = g if p == 0 else gnacc[...] + g

    for p in range(PAIRS):
        backward(p)
        st[p + 1] = chunk_start(p + 1, ntp, dp3.at[p])
        st[p] = chunk_y(p, st[p])
        if p >= 1:
            st[p - 1] = chunk_x(p - 1, st[p - 1])
        if p >= 2:
            chunk_z(p - 2, st[p - 2])
        grad_normed(p)
    st[4] = chunk_y(4, st[4])

    def norm_back(k, total):
        w = idx[k]
        rows = rows_of(k)
        gn = gnacc[rows, :]
        hat = xhat[rows, :]
        g = gn * gain
        prod = g * hat
        mid = g - jnp.mean(g, axis=1, keepdims=True) - hat * jnp.mean(prod, axis=1, keepdims=True)
        inv = jnp.concatenate([invd[rows, :]] * 4, axis=1)
        res[k] = win[w, :, D0 : D0 + C] + inv * mid
        return total + jnp.sum(gn * hat, axis=0, keepdims=True)

    gsum = lax.fori_loop(0, SLOTS // 3, by_three(norm_back), jnp.zeros((1, C), F32))
    out_copies[1] = window_back(1, D0)
    st[3] = chunk_x(3, st[3])

    stacked = jnp.concatenate([bacc[h // 2, :, 128 * (h % 2) : 128 * (h % 2) + 128] for h in range(HEADS)], axis=0)
    by_place = sum(nn(v, self_[...]) for v in pieces(stacked, 2))
    by_place = jnp.concatenate([by_place[TP * h : TP * h + TP] for h in range(HEADS)], axis=1)
    spread = sum(nn(selrt[:, 0:TP], v) for v in pieces(by_place, 2))
    for h in range(HEADS):
        wide = jnp.concatenate([spread[:, 128 * h : 128 * h + 128], jnp.zeros((128, 128), F32)], axis=1)
        sums[0][h : h + 1, 0:256] = jnp.sum(pltpu.roll(wide, 0, 1, stride=1, stride_axis=0), axis=0, keepdims=True)
    sm, smc, smy, sma, smx, smz = sums
    sm[4:8, 256:384] = jnp.zeros((4, 128), F32)
    for j in range(4):
        sm[j : j + 1, 256:384] = gsum[:, 128 * j : 128 * j + 128]
    copy = send(sm, smc, ss.at[0], sr.at[0], partner)
    chunk_z(2, st[2])
    chunk_z(3, st[3])
    group0 = group_send(0)
    st[4] = chunk_x(4, st[4])
    copy.wait_recv()
    smy[y] = sm[...] + smc[...]
    copies = [send(smy.at[y], smy.at[y], ss.at[d], sr.at[d], ypeer[d - 1]) for d in range(1, ny)]
    finish(0, out_copies[0], upd)
    stores[0].start()
    chunk_z(4, st[4])
    group1 = group_send(1)
    for copy in copies:
        copy.wait_recv()
    acc = smy[0]
    for j in range(1, ny):
        acc = acc + smy[j]
    sma[...] = acc
    copy = send(sma, smx, ss.at[ny], sr.at[ny], xpeer)
    group_end(0, group0)
    copy.wait_recv()
    smz[z] = sma[...] + smx[...]
    copies = [send(smz.at[z], smz.at[z], ss.at[ny + d], sr.at[ny + d], zpeer[d - 1]) for d in range(1, nz)]
    finish(1, out_copies[1], gin)
    stores[1].start()
    group_end(1, group1)
    for copy in copies:
        copy.wait_recv()
    acc = smz[0]
    for j in range(1, nz):
        acc = acc + smz[j]
    bias_out[...] = acc[:, 0:REL]
    for j in range(4):
        gain_out[:, 128 * j : 128 * j + 128] = acc[j : j + 1, 256:384]
    for store in stores[2:]:
        store.start()
    for copy in sends:
        copy.wait_send()
    for store in stores:
        store.wait()


def hand_over(*refs):
    arrived, left = refs[18:20]
    steps = []
    for i in range(6):
        rows = refs[i].shape[0]
        size = 3 if i < 2 else rows
        steps += [(i, pl.ds(start, size)) for start in range(0, rows, size)]
    fetches = [
        pltpu.make_async_copy(refs[i].at[at], refs[12 + i].at[at], arrived.at[n]) for n, (i, at) in enumerate(steps)
    ]
    stores = [
        pltpu.make_async_copy(refs[12 + i].at[at], refs[6 + i].at[at], left.at[n]) for n, (i, at) in enumerate(steps)
    ]
    for fetch in fetches:
        fetch.start()
    for fetch, store in zip(fetches, stores):
        fetch.wait()
        store.start()
    for store in stores:
        store.wait()


def constants(ny, nx, nz):
    share = C // (ny * nx * nz * 2)
    perm = np.zeros((C, C), np.float32)
    for core in range(2):
        for y in range(ny):
            for xh in range(nx):
                for z in range(nz):
                    to = (((core * ny + y) * nx + xh) * nz + z) * share
                    start = (((y * nx + xh) * nz + z) * 2 + core) * share
                    perm[to + np.arange(share), start + np.arange(share)] = 1
    a = np.arange(T)
    pa = (a // WIN_LON) * (2 * WIN_LON - 1) + a % WIN_LON
    selrt = np.zeros((128, 128), np.float32)
    selrt[126 - pa, a] = 1
    self_ = np.zeros((128, 128), np.float32)
    self_[a, pa] = 1
    return perm, self_, self_.T, selrt


def solution(mesh):
    nlon, nlat = mesh.shape["lon"], mesh.shape["lat"]
    nx, nz = 2, nlat // 2
    ny = nlon // nx
    nxz = nx * nz
    half = C // 2
    ysz = half // ny
    share = ysz // nxz
    cols = [C] + [384] * PAIRS
    lat_dev, lon_dev = 18, 48
    nwin = 12
    vm = pltpu.VMEM
    dma = lambda *s: pltpu.SemaphoreType.DMA(s)
    perm, self_, selft, selrt = (jnp.asarray(v, BF16) for v in constants(ny, nx, nz))

    def on_device(fields, grad_out, layernorm_gain, qkv_weight, proj_weight, bias_table, sea_mask):
        shapes = (
            jax.ShapeDtypeStruct((lat_dev, lon_dev, C), BF16),
            jax.ShapeDtypeStruct((lat_dev, lon_dev, C), BF16),
            jax.ShapeDtypeStruct((1, C), F32),
            jax.ShapeDtypeStruct((HEADS, REL), F32),
            jax.ShapeDtypeStruct((share, 3 * C), F32),
            jax.ShapeDtypeStruct((share, C), F32),
        )
        scratch = [
            vm((lat_dev, lon_dev, C), BF16),
            vm((lat_dev, lon_dev), jnp.int32),
            vm((lat_dev, lon_dev, C), BF16),
            vm((HEADS, REL), F32),
            vm((128, 128), BF16),
            vm((128, 128), BF16),
            vm((128, 128), BF16),
            vm((1, C), F32),
            vm((C, 3 * C), BF16),
            vm((C, C), BF16),
            vm((C, C), BF16),
        ]
        scratch += [vm(v.shape, v.dtype) for v in shapes]
        scratch += [
            vm((lat_dev + 3, 56, FW), F32),
            vm((nwin, TP, FW), F32),
            vm((112, FW), F32),
        ]
        for wide in (C, C):
            scratch += [
                vm((112, wide), BF16),
                vm((112, wide), BF16),
                vm((3, lon_dev, wide), BF16),
                vm((3, lon_dev, wide), BF16),
                vm((32, wide), BF16),
            ]
        scratch += [vm((lat_dev, lon_dev), jnp.int32)] * 3
        scratch += [
            pltpu.SMEM((16,), jnp.int32),
            vm((HEADS, 256), F32),
            vm((PAIRS, TP, 256), F32),
            vm((SLOTS, TP, 128), F32),
            vm((ROWS, C), F32),
            vm((ROWS, 128), F32),
            vm((RP, C), BF16),
            vm((RP, C), BF16),
            vm((ROWS, C), BF16),
            vm((ROWS, 3 * C), BF16),
            vm((RP, C), BF16),
            vm((C, RP), BF16),
            vm((C, RP), BF16),
            vm((SLOTS * PAIRS, TP, 256), F32),
            vm((PAIRS, RP, 384), BF16),
            vm((ROWS, C), F32),
            vm((PAIRS, TP, 256), F32),
            vm((SLOTS, TP, C), F32),
            vm((2, lat_dev + 3, 56, C), F32),
            vm((2, 144, C), BF16),
            vm((2, 3, lon_dev, C), BF16),
            vm((2, 112, C), BF16),
            vm((2, 3, lon_dev, C), BF16),
            vm((2, 32, C), BF16),
        ]
        for n in cols:
            scratch += [
                vm((half, n), BF16),
                vm((half, n), BF16),
                vm((half, n), F32),
                vm((half, n), BF16),
                vm((ny - 1, ysz, n), BF16),
                vm((ysz // 2, n), BF16),
                vm((ysz // 2, n), BF16),
                vm((ysz // 2, n), F32),
            ]
        for n in (sum(cols[:4]), cols[4]):
            scratch += [vm((nz, share, n), F32), vm((nz - 1, share, n), F32)]
        sm = (8, 384)
        scratch += [vm(sm, F32), vm(sm, F32), vm((ny,) + sm, F32), vm(sm, F32), vm(sm, F32), vm((nz,) + sm, F32)]
        nc = len(cols)
        small = ny + nz
        scratch += [
            dma(2, 3), dma(2, 3), dma(3), dma(3), dma(2, 3), dma(2, 3), dma(nc), dma(nc), dma(nc, ny - 1),
            dma(nc, ny - 1), dma(nc), dma(nc), dma(2, nz - 1), dma(2, nz - 1), dma(small), dma(small), dma(11), dma(6),
        ]
        anywhere = pl.BlockSpec(memory_space=pl.ANY)
        outs = pl.pallas_call(
            functools.partial(kernel, (ny, nx, nz), cols),
            out_shape=shapes,
            in_specs=[anywhere] * 11,
            out_specs=(anywhere,) * 6,
            scratch_shapes=scratch,
            compiler_params=pltpu.CompilerParams(
                collective_id=0, has_side_effects=True, vmem_limit_bytes=60 * 1024 * 1024
            ),
        )(
            fields, sea_mask, grad_out, bias_table, self_, selft, selrt,
            layernorm_gain.reshape(1, C), qkv_weight, proj_weight, perm,
        )
        outs = pl.pallas_call(
            hand_over,
            out_shape=shapes,
            in_specs=[anywhere] * 6,
            out_specs=(anywhere,) * 6,
            scratch_shapes=[vm(v.shape, v.dtype) for v in shapes] + [dma(16), dma(16)],
            compiler_params=pltpu.CompilerParams(vmem_limit_bytes=60 * 1024 * 1024),
        )(*outs)
        updated, grad_in, grad_gain, grad_bias, grad_qkv, grad_proj = outs
        return (updated, grad_in, grad_gain.reshape(C), grad_bias, grad_qkv, grad_proj)

    grid = P(("batch", "lat"), "lon", None)
    return jax.shard_map(
        on_device,
        mesh=mesh,
        in_specs=(grid, grid, P(), P(), P(), P(), P(("batch", "lat"), "lon")),
        out_specs=(
            grid,
            grid,
            P("batch"),
            P("batch", None),
            P(("batch", "lon", "lat"), None),
            P(("batch", "lon", "lat"), None),
        ),
        check_vma=False,
    )
```

```python
import functools

import jax
import jax.numpy as jnp
import numpy as np
from jax import lax
from jax.experimental import pallas as pl
from jax.experimental.pallas import tpu as pltpu
from jax.sharding import PartitionSpec as P

MESH = pl.DeviceIdType.MESH
F32 = jnp.float32
BF16 = jnp.bfloat16
C = 512
HEADS = 8
PAIRS = 4
WIN_LAT = 6
WIN_LON = 12
HALF_LAT = 3
HALF_LON = 6
T = 72
TP = 80
SLOTS = 9
ROWS = SLOTS * TP
RP = 768
REL = 253
X0, M0, D0, FW = 0, 512, 640, 1152
EARLY = 3
EPS = 1e-5


def nn(a, b, **kw):
    return lax.dot_general(a, b, (((1,), (0,)), ((), ())), preferred_element_type=F32, **kw)


def nt(a, b, **kw):
    return lax.dot_general(a, b, (((1,), (1,)), ((), ())), preferred_element_type=F32, **kw)


def tn(a, b, **kw):
    return lax.dot_general(a, b, (((0,), (0,)), ((), ())), preferred_element_type=F32, **kw)


def pad_rows(v, rows):
    return jnp.concatenate([v, jnp.zeros((rows - v.shape[0], v.shape[1]), v.dtype)], axis=0)


def kernel(dims, cols, *refs):
    ny, nx, nz = dims
    nlon, nlat = ny * nx, 2 * nz
    nxz = nx * nz
    lat_dev, lon_dev = 18, 48
    wrows, wcols = lat_dev // WIN_LAT, lon_dev // WIN_LON
    nwin = wrows * wcols
    half = C // 2
    ysz = half // ny
    share = ysz // nxz
    nchunk = len(cols)

    it = iter(refs)
    take = lambda n=None: next(it) if n is None else [next(it) for _ in range(n)]
    given = take(11)
    results = take(6)
    held = take(11)
    x_ref, mask_ref, dy_ref, table, self_, selft, selrt, gain_ref, wqkv, wproj, perm = held
    staged = take(6)
    upd, gin, gain_out, bias_out, gqkv, gproj = staged
    frame, win, colf = take(3)
    halos = [take(5) for _ in range(2)]
    masks = take(3)
    idx = take()
    tb, bias2, madd, xhat, invd, normed, gz, gm, packed, mixed, ntp, mtp, probs, probs16, dv, dqk, gnacc, bacc = take(18)
    res, of = take(2)
    ocs, ors, ocr, orr, occ = take(5)
    chunks = [take(8) for _ in range(nchunk)]
    groups = [take(2) for _ in range(2)]
    sums = take(6)
    hs, hr, ms, mr, os_, or_, as_, ar, ys, yr, xs, xr, zs, zr, ss, sr = take(16)
    ins, outs = take(2)

    lon = lax.axis_index("lon")
    lat = lax.axis_index("lat")
    y, xh = lon // nx, lon % nx
    z, core = lat // 2, lat % 2

    def dev(a, b):
        return {"lon": a, "lat": b}

    partner = dev(lon, z * 2 + (1 - core))
    ypeer = [dev(((y + d) % ny) * nx + xh, lat) for d in range(1, ny)]
    xpeer = dev(y * nx + (1 - xh), lat)
    zpeer = [dev(lon, ((z + d) % nz) * 2 + core) for d in range(1, nz)]
    west, east = (lon + nlon - 1) % nlon, (lon + 1) % nlon
    north, south = (lat + nlat - 1) % nlat, (lat + 1) % nlat
    back = [dev(west, lat), dev(lon, north), dev(west, north)]
    forth = [dev(east, lat), dev(lon, south), dev(east, south)]

    barrier = pltpu.get_barrier_semaphore()
    everyone = [partner, xpeer] + ypeer + zpeer + back + forth
    for d in everyone:
        pl.semaphore_signal(barrier, inc=1, device_id=d, device_id_type=MESH)

    loads = [pltpu.make_async_copy(a, b, ins.at[i]) for i, (a, b) in enumerate(zip(given, held))]
    for load in loads:
        load.start()

    stores = [pltpu.make_async_copy(a, b, outs.at[i]) for i, (a, b) in enumerate(zip(staged, results))]
    sends = []

    def send(src, dst, ssem, rsem, d):
        copy = pltpu.make_async_remote_copy(
            src_ref=src, dst_ref=dst, send_sem=ssem, recv_sem=rsem, device_id=d, device_id_type=MESH
        )
        copy.start()
        sends.append(copy)
        return copy

    lane_row = lax.broadcasted_iota(jnp.int32, (lat_dev, lat_dev * 128), 1) // 128
    pick = (lane_row == lax.broadcasted_iota(jnp.int32, (lat_dev, lat_dev * 128), 0)).astype(F32)

    def spread_mask(ref):
        return tn(ref[...].astype(F32), pick)

    loads[1].wait()
    sea = spread_mask(mask_ref)
    colf[96:112, :] = jnp.zeros((16, FW), F32)

    def halo_pack(h, lanes):
        colsend, colrecv, rowsend, rowrecv, cornrecv = halos[h]
        for r in range(lat_dev):
            colf[6 * r : 6 * r + 6, lanes] = frame[r, 0:HALF_LON, lanes]
        colsend[...] = colf[:, lanes].astype(BF16)
        for r in range(HALF_LAT):
            rowsend[r] = frame[r, 0:lon_dev, lanes].astype(BF16)

    def halo_send(h):
        colsend, colrecv, rowsend, rowrecv, cornrecv = halos[h]
        return [
            send(colsend, colrecv, hs.at[h, 0], hr.at[h, 0], back[0]),
            send(rowsend, rowrecv, hs.at[h, 1], hr.at[h, 1], back[1]),
            send(colsend.at[0:32], cornrecv, hs.at[h, 2], hr.at[h, 2], back[2]),
        ]

    def halo_land(h, lanes, copies):
        colsend, colrecv, rowsend, rowrecv, cornrecv = halos[h]
        copies[1].wait_recv()
        for r in range(HALF_LAT):
            frame[lat_dev + r, 0:lon_dev, lanes] = rowrecv[r].astype(F32)
        copies[2].wait_recv()
        colf[0:32, lanes] = cornrecv[...].astype(F32)
        for r in range(HALF_LAT):
            frame[lat_dev + r, lon_dev : lon_dev + HALF_LON, lanes] = colf[6 * r : 6 * r + 6, lanes]
        copies[0].wait_recv()
        colf[:, lanes] = colrecv[...].astype(F32)
        for r in range(lat_dev):
            frame[r, lon_dev : lon_dev + HALF_LON, lanes] = colf[6 * r : 6 * r + 6, lanes]

    xlanes, dlanes = slice(X0, X0 + C), slice(D0, D0 + C)
    loads[0].wait()
    for r in range(lat_dev):
        frame[r, 0:lon_dev, X0 : X0 + C] = x_ref[r].astype(F32)
        frame[r, 0:lon_dev, M0 : M0 + 128] = sea[:, 128 * r : 128 * r + 128]
    halo_pack(0, xlanes)
    pl.semaphore_wait(barrier, len(everyone))
    mcopies = [send(mask_ref, masks[i], ms.at[i], mr.at[i], back[i]) for i in range(3)]
    xcopies = halo_send(0)
    loads[2].wait()
    for r in range(lat_dev):
        frame[r, 0:lon_dev, D0 : D0 + C] = dy_ref[r].astype(F32)
    halo_pack(1, dlanes)
    dcopies = halo_send(1)

    def pieces(v, n):
        out = []
        for i in range(n):
            part = v.astype(BF16)
            out.append(part)
            if i < n - 1:
                v = v - part.astype(F32)
        return out

    for i in range(3, 11):
        loads[i].wait()
    tb[...] = jnp.zeros_like(tb)
    tb[:, 0:REL] = table[...]
    shifted = []
    for h in range(HEADS):
        line = jnp.broadcast_to(tb[h : h + 1, :], (128, 256))
        shifted.append(pltpu.roll(pltpu.roll(line, 2, 1), 128, 1, stride=1, stride_axis=0)[:, 0:128])
    by_query = sum(nn(v, selft[...]) for v in pieces(jnp.concatenate(shifted, axis=0), 3))
    by_query = jnp.concatenate([by_query[128 * h : 128 * h + 128] for h in range(HEADS)], axis=1)
    whole_bias = sum(nn(self_[0:TP, :], v) for v in pieces(by_query, 3))
    for p in range(PAIRS):
        bias2[p] = whole_bias[:, 256 * p : 256 * p + 256]

    zero_tail = jnp.zeros((RP - ROWS, C), BF16)
    normed[ROWS:RP, :] = zero_tail
    gz[ROWS:RP, :] = zero_tail
    mixed[ROWS:RP, :] = zero_tail
    dv[ROWS:RP, :] = zero_tail
    for p in range(PAIRS):
        dqk[p, ROWS:RP, :] = jnp.zeros((RP - ROWS, 256), BF16)
    for w in range(nwin):
        win[w, T:TP, :] = jnp.zeros((TP - T, FW), F32)

    def cut(w, lanes):
        wr, wc = w // wcols, w % wcols
        c0 = HALF_LON + WIN_LON * wc
        for i in range(WIN_LAT):
            win[w, WIN_LON * i : WIN_LON * i + WIN_LON, lanes] = frame[
                HALF_LAT + WIN_LAT * wr + i, c0 : c0 + WIN_LON, lanes
            ]

    def holds_sea(w):
        return (jnp.max(win[w, :, M0 : M0 + 128]) > 0.5).astype(jnp.int32)

    def ranks(flags, counted):
        total = jnp.int32(0)
        for f, c in zip(flags, counted):
            total = total + f * c
        out, on, off = [], jnp.int32(0), total
        for f, c in zip(flags, counted):
            out.append(jnp.where(f > 0, on, off))
            on = on + f * c
            off = off + (1 - f) * c
        return out

    def slot_window(k, places):
        slot = jnp.int32(0)
        for w, at in places:
            slot = slot + jnp.where(at == k, w, 0)
        idx[k] = slot

    inner = [w for w in range(nwin) if w // wcols < wrows - 1 and w % wcols < wcols - 1]
    outer = [w for w in range(nwin) if w not in inner]
    active = [None] * nwin
    place = [None] * nwin

    at_end = (lat == nlat - 1).astype(F32)
    gain = gain_ref[...]

    def rows_of(k):
        return pl.ds(pl.multiple_of(k * TP, TP), TP)

    def by_three(step):
        def body(i, carry):
            for j in range(3):
                carry = step(3 * i + j, carry)
            return carry

        return body

    def ln_step(k, carry):
        w = idx[k]
        x = win[w, :, X0 : X0 + C]
        mean = jnp.mean(x, axis=1, keepdims=True)
        xc = x - mean
        inv = lax.rsqrt(jnp.mean(xc * xc, axis=1, keepdims=True) + EPS)
        hat = xc * inv
        rows = rows_of(k)
        xhat[rows, :] = hat
        invd[rows, :] = jnp.broadcast_to(inv, (TP, 128))
        normed[rows, :] = (hat * gain).astype(BF16)
        keys = win[w, :, M0 : M0 + 128]
        side_b = lax.broadcasted_iota(jnp.int32, (TP, 128), 0) >= T // 2
        side_a = lax.broadcasted_iota(jnp.int32, (TP, 128), 1) >= T // 2
        apart = jnp.where(side_a != side_b, 1.0, 0.0)
        wrap = at_end * jnp.where(w >= nwin - wcols, 1.0, 0.0)
        madd[k] = (keys * (1.0 - apart * wrap) - 1.0) * 1e9
        return carry

    def dy_step(k, carry):
        w = idx[k]
        m = win[w, :, M0 : M0 + 128]
        gz[rows_of(k), :] = (win[w, :, D0 : D0 + C] * jnp.concatenate([m] * 4, axis=1)).astype(BF16)
        return carry

    lane = lax.broadcasted_iota(jnp.int32, (TP, 128), 1)
    low = lane < 64
    one_lo = jnp.where(low, 1.0, 0.0).astype(BF16)
    one_hi = jnp.where(low, 0.0, 1.0).astype(BF16)
    q_lo = jnp.where(low, 0.125, 0.0).astype(BF16)
    q_hi = jnp.where(low, 0.0, 0.125).astype(BF16)

    def both_heads(v, lo, hi):
        return jnp.concatenate([pad_rows(v * lo, 128), pad_rows(v * hi, 128)], axis=0)

    def stack_heads(v, lo, hi):
        return jnp.concatenate([v * lo, v * hi], axis=0)

    def lanes_to_rows(v):
        return jnp.concatenate([v[:, 0:128], v[:, 128:256]], axis=0)

    def attend(k, carry):
        rows = rows_of(k)
        add = madd[k]
        add2 = jnp.concatenate([add, add], axis=1)
        scores = []
        for p in range(PAIRS):
            q2 = both_heads(packed[rows, 128 * p : 128 * p + 128], q_lo, q_hi)
            scores.append(nt(packed[rows, C + 128 * p : C + 128 * p + 128], q2) + bias2[p] + add2)
        for p in range(PAIRS):
            s = scores[p]
            e = jnp.exp(s - jnp.max(s, axis=0, keepdims=True))
            pr = e * (1.0 / jnp.sum(e, axis=0, keepdims=True))
            probs[k * PAIRS + p] = pr
            pr16 = pr.astype(BF16)
            probs16[k * PAIRS + p] = pr16
            v2 = stack_heads(packed[rows, 2 * C + 128 * p : 2 * C + 128 * p + 128], one_lo, one_hi)
            mixed[rows, 128 * p : 128 * p + 128] = tn(lanes_to_rows(pr16), v2)[0:TP].astype(BF16)
        return carry

    def forward(first, last):
        lax.fori_loop(first // 3, last // 3, by_three(ln_step), 0)
        rows = slice(first * TP, last * TP)
        packed[rows, :] = nn(normed[rows, :], wqkv[...]).astype(BF16)
        lax.fori_loop(first, last, attend, 0)

    for w in inner:
        cut(w, slice(0, FW))
        active[w] = holds_sea(w)
    inner_rank = ranks([active[w] for w in inner], [1] * len(inner))
    for k in range(EARLY):
        slot_window(k, list(zip(inner, inner_rank)))
    forward(0, EARLY)

    mlanes = slice(M0, M0 + 128)
    for copy in mcopies:
        copy.wait_recv()
    sea = spread_mask(masks[0])
    for r in range(lat_dev):
        frame[r, lon_dev : lon_dev + HALF_LON, mlanes] = sea[0:HALF_LON, 128 * r : 128 * r + 128]
    sea = spread_mask(masks[1])
    for r in range(HALF_LAT):
        frame[lat_dev + r, 0:lon_dev, mlanes] = sea[:, 128 * r : 128 * r + 128]
    sea = spread_mask(masks[2])
    for r in range(HALF_LAT):
        frame[lat_dev + r, lon_dev : lon_dev + HALF_LON, mlanes] = sea[0:HALF_LON, 128 * r : 128 * r + 128]
    halo_land(0, xlanes, xcopies)
    for w in outer:
        cut(w, slice(X0, M0 + 128))
        active[w] = holds_sea(w)
    rest = [jnp.int32(1)] * nwin
    for w, at in zip(inner, inner_rank):
        rest[w] = (at >= EARLY).astype(jnp.int32)
    late_rank = ranks(active, rest)
    for w in range(nwin):
        place[w] = late_rank[w] + EARLY
    for w, at in zip(inner, inner_rank):
        place[w] = jnp.where(at < EARLY, at, place[w])
    for k in range(EARLY, SLOTS):
        slot_window(k, list(enumerate(place)))
    forward(EARLY, SLOTS)

    halo_land(1, dlanes, dcopies)
    for w in outer:
        cut(w, dlanes)
    lax.fori_loop(0, SLOTS // 3, by_three(dy_step), 0)
    gm[...] = nt(gz[0:ROWS, :], wproj[...]).astype(BF16)
    ntp[...] = nt(perm[...], normed[...]).astype(BF16)

    def chunk_start(c, lhs, rhs):
        asend, arecv, own = chunks[c][0:3]
        right = rhs[...]
        other = pl.multiple_of((1 - core) * half, half)
        mine = pl.multiple_of(core * half, half)
        asend[...] = nn(lhs[pl.ds(other, half), :], right).astype(BF16)
        copy = send(asend, arecv, as_.at[c], ar.at[c], partner)
        own[...] = nn(lhs[pl.ds(mine, half), :], right)
        return [copy]

    def chunk_y(c, copies):
        asend, arecv, own, ysend, yrecv = chunks[c][0:5]
        copies[0].wait_recv()
        s = own[...] + arecv[...].astype(F32)
        own[...] = s
        ysend[...] = s.astype(BF16)
        out = []
        for d in range(1, ny):
            start = pl.multiple_of(((y + d) % ny) * ysz, ysz)
            out.append(
                send(ysend.at[pl.ds(start, ysz)], yrecv.at[d - 1], ys.at[c, d - 1], yr.at[c, d - 1], ypeer[d - 1])
            )
        return out

    def chunk_x(c, copies):
        own, ysend, yrecv, xsend, xrecv, xown = chunks[c][2:8]
        s = own[pl.ds(pl.multiple_of(y * ysz, ysz), ysz), :]
        for d in range(1, ny):
            copies[d - 1].wait_recv()
            s = s + yrecv[d - 1].astype(F32)
        top, low_half = s[0 : ysz // 2], s[ysz // 2 : ysz]
        first = xh == 0
        xsend[...] = jnp.where(first, low_half, top).astype(BF16)
        xown[...] = jnp.where(first, top, low_half)
        return [send(xsend, xrecv, xs.at[c], xr.at[c], xpeer)]

    def chunk_z(c, copies):
        xsend, xrecv, xown = chunks[c][5:8]
        zsend = groups[0 if c < 5 else 1][0]
        start = sum(cols[:c]) if c < 5 else 0
        copies[0].wait_recv()
        s = xown[...] + xrecv[...].astype(F32)
        for j in range(nz):
            zsend[j, :, start : start + cols[c]] = s[share * j : share * j + share]

    def group_send(g):
        zsend, zrecv = groups[g]
        return [
            send(zsend.at[(z + d) % nz], zrecv.at[d - 1], zs.at[g, d - 1], zr.at[g, d - 1], zpeer[d - 1])
            for d in range(1, nz)
        ]

    def group_end(g, copies):
        zsend, zrecv = groups[g]
        s = zsend[z]
        for i, copy in enumerate(copies):
            copy.wait_recv()
            s = s + zrecv[i]
        start = 0
        for c in range(nchunk):
            if (c < 5) != (g == 0):
                continue
            part = s[:, start : start + cols[c]]
            if c == 0:
                gproj[...] = part
            elif c == 1:
                gqkv[:, 2 * C : 3 * C] = part
            else:
                p = c - 2
                gqkv[:, 128 * p : 128 * p + 128] = part[:, 0:128]
                gqkv[:, C + 128 * p : C + 128 * p + 128] = part[:, 128:256]
            start += cols[c]

    def window_back(o, lane0):
        def place_window(w):
            wr, wc = w // wcols, w % wcols
            slot = jnp.minimum(place[w], SLOTS - 1)
            for i in range(WIN_LAT):
                c0 = HALF_LON + WIN_LON * wc
                at = slice(WIN_LON * i, WIN_LON * i + WIN_LON)
                of[o, HALF_LAT + WIN_LAT * wr + i, c0 : c0 + WIN_LON, :] = jnp.where(
                    place[w] < SLOTS, res[slot, at, :], win[w, at, lane0 : lane0 + C]
                )

        for w in range(wcols - 1, nwin, wcols):
            place_window(w)
        colf[0 : 6 * HALF_LAT, 0:C] = jnp.zeros((6 * HALF_LAT, C), F32)
        for r in range(HALF_LAT, lat_dev):
            colf[6 * r : 6 * r + 6, 0:C] = of[o, r, lon_dev : lon_dev + HALF_LON, :]
        ocs[o, 0:112] = colf[0:112, 0:C].astype(BF16)
        for r in range(HALF_LAT):
            colf[6 * r : 6 * r + 6, 0:C] = of[o, lat_dev + r, lon_dev : lon_dev + HALF_LON, :]
        ocs[o, 112:144] = colf[0:32, 0:C].astype(BF16)
        copies = [
            send(ocs.at[o, 0:112], ocr.at[o], os_.at[o, 0], or_.at[o, 0], forth[0]),
            send(ocs.at[o, 112:144], occ.at[o], os_.at[o, 2], or_.at[o, 2], forth[2]),
        ]
        for w in range(nwin - wcols, nwin - 1):
            place_window(w)
        for r in range(HALF_LAT):
            ors[o, r] = of[o, lat_dev + r, 0:lon_dev, :].astype(BF16)
        copies.insert(1, send(ors.at[o], orr.at[o], os_.at[o, 1], or_.at[o, 1], forth[1]))
        for w in range(nwin - wcols):
            if w % wcols < wcols - 1:
                place_window(w)
        return copies

    def finish(o, copies, out):
        copies[1].wait_recv()
        for r in range(HALF_LAT):
            of[o, r, 0:lon_dev, :] = orr[o, r].astype(F32)
        copies[0].wait_recv()
        colf[0:112, 0:C] = ocr[o].astype(F32)
        for r in range(HALF_LAT, lat_dev):
            of[o, r, 0:HALF_LON, :] = colf[6 * r : 6 * r + 6, 0:C]
        copies[2].wait_recv()
        colf[0:32, 0:C] = occ[o].astype(F32)
        for r in range(HALF_LAT):
            of[o, r, 0:HALF_LON, :] = colf[6 * r : 6 * r + 6, 0:C]
        for r in range(lat_dev):
            out[r] = of[o, r, 0:lon_dev, :].astype(BF16)

    mtp[...] = nt(perm[...], mixed[...]).astype(BF16)
    st = {}
    st[0] = chunk_start(0, mtp, gz)

    def value_step(k, carry):
        rows = rows_of(k)
        for p in range(PAIRS):
            d2 = both_heads(gm[rows, 128 * p : 128 * p + 128], one_lo, one_hi)
            dv[rows, 128 * p : 128 * p + 128] = nn(probs16[k * PAIRS + p], d2).astype(BF16)
        return carry

    lax.fori_loop(0, SLOTS // 3, by_three(value_step), 0)
    st[1] = chunk_start(1, ntp, dv)

    gnacc[...] = nn(mixed[0:ROWS, :], wproj[...])

    def updated_step(k, carry):
        w = idx[k]
        m = win[w, :, M0 : M0 + 128]
        res[k] = win[w, :, X0 : X0 + C] + jnp.concatenate([m] * 4, axis=1) * gnacc[rows_of(k), :]
        return carry

    lax.fori_loop(0, SLOTS // 3, by_three(updated_step), 0)
    out_copies = [window_back(0, X0), None]
    gnacc[...] = nt(dv[0:ROWS, :], wqkv[:, 2 * C : 3 * C])
    st[0] = chunk_y(0, st[0])

    def backward(p):
        bacc[p] = jnp.zeros((TP, 256), F32)

        def step(i, carry):
            ks = [3 * i + j for j in range(3)]
            dps = []
            for k in ks:
                rows = rows_of(k)
                d2 = both_heads(gm[rows, 128 * p : 128 * p + 128], one_lo, one_hi)
                dps.append(nt(packed[rows, 2 * C + 128 * p : 2 * C + 128 * p + 128], d2))
            dss = []
            for j, k in enumerate(ks):
                pr = probs[k * PAIRS + p]
                t = pr * dps[j]
                dss.append(t - pr * jnp.sum(t, axis=0, keepdims=True))
            bacc[p] += dss[0] + dss[1] + dss[2]
            for j, k in enumerate(ks):
                rows = rows_of(k)
                ds = dss[j].astype(BF16)
                q2 = both_heads(packed[rows, 128 * p : 128 * p + 128], q_lo, q_hi)
                k2 = stack_heads(packed[rows, C + 128 * p : C + 128 * p + 128], q_lo, q_hi)
                dqk[p, rows, 0:128] = tn(lanes_to_rows(ds), k2)[0:TP].astype(BF16)
                dqk[p, rows, 128:256] = nn(ds, q2).astype(BF16)
            return carry

        lax.fori_loop(0, SLOTS // 3, step, 0)

    def grad_normed(p):
        weight = jnp.concatenate([wqkv[:, C * i + 128 * p : C * i + 128 * p + 128] for i in range(2)], axis=1)
        gnacc[...] += nt(dqk[p, 0:ROWS, :], weight)

    for p in range(PAIRS):
        backward(p)
        st[p + 2] = chunk_start(p + 2, ntp, dqk.at[p])
        st[p + 1] = chunk_y(p + 1, st[p + 1])
        st[p] = chunk_x(p, st[p])
        if p >= 1:
            chunk_z(p - 1, st[p - 1])
        grad_normed(p)
    st[5] = chunk_y(5, st[5])

    def norm_back(k, total):
        w = idx[k]
        rows = rows_of(k)
        gn = gnacc[rows, :]
        hat = xhat[rows, :]
        g = gn * gain
        prod = g * hat
        mid = g - jnp.mean(g, axis=1, keepdims=True) - hat * jnp.mean(prod, axis=1, keepdims=True)
        inv = jnp.concatenate([invd[rows, :]] * 4, axis=1)
        res[k] = win[w, :, D0 : D0 + C] + inv * mid
        return total + jnp.sum(gn * hat, axis=0, keepdims=True)

    gsum = lax.fori_loop(0, SLOTS // 3, by_three(norm_back), jnp.zeros((1, C), F32))
    out_copies[1] = window_back(1, D0)
    st[4] = chunk_x(4, st[4])

    stacked = jnp.concatenate([bacc[h // 2, :, 128 * (h % 2) : 128 * (h % 2) + 128] for h in range(HEADS)], axis=0)
    by_place = sum(nn(v, self_[...]) for v in pieces(stacked, 2))
    by_place = jnp.concatenate([by_place[TP * h : TP * h + TP] for h in range(HEADS)], axis=1)
    spread = sum(nn(selrt[:, 0:TP], v) for v in pieces(by_place, 2))
    for h in range(HEADS):
        wide = jnp.concatenate([spread[:, 128 * h : 128 * h + 128], jnp.zeros((128, 128), F32)], axis=1)
        sums[0][h : h + 1, 0:256] = jnp.sum(pltpu.roll(wide, 0, 1, stride=1, stride_axis=0), axis=0, keepdims=True)
    sm, smc, smy, sma, smx, smz = sums
    sm[4:8, 256:384] = jnp.zeros((4, 128), F32)
    for j in range(4):
        sm[j : j + 1, 256:384] = gsum[:, 128 * j : 128 * j + 128]
    copy = send(sm, smc, ss.at[0], sr.at[0], partner)
    chunk_z(3, st[3])
    chunk_z(4, st[4])
    group0 = group_send(0)
    st[5] = chunk_x(5, st[5])
    copy.wait_recv()
    smy[y] = sm[...] + smc[...]
    copies = [send(smy.at[y], smy.at[y], ss.at[d], sr.at[d], ypeer[d - 1]) for d in range(1, ny)]
    finish(0, out_copies[0], upd)
    stores[0].start()
    chunk_z(5, st[5])
    group1 = group_send(1)
    for copy in copies:
        copy.wait_recv()
    acc = smy[0]
    for j in range(1, ny):
        acc = acc + smy[j]
    sma[...] = acc
    copy = send(sma, smx, ss.at[ny], sr.at[ny], xpeer)
    group_end(0, group0)
    copy.wait_recv()
    smz[z] = sma[...] + smx[...]
    copies = [send(smz.at[z], smz.at[z], ss.at[ny + d], sr.at[ny + d], zpeer[d - 1]) for d in range(1, nz)]
    finish(1, out_copies[1], gin)
    stores[1].start()
    group_end(1, group1)
    for copy in copies:
        copy.wait_recv()
    acc = smz[0]
    for j in range(1, nz):
        acc = acc + smz[j]
    bias_out[...] = acc[:, 0:REL]
    for j in range(4):
        gain_out[:, 128 * j : 128 * j + 128] = acc[j : j + 1, 256:384]
    for store in stores[2:]:
        store.start()
    for copy in sends:
        copy.wait_send()
    for store in stores:
        store.wait()


def hand_over(*refs):
    arrived, left = refs[18:20]
    steps = []
    for i in range(6):
        rows = refs[i].shape[0]
        size = 3 if i < 2 else rows
        steps += [(i, pl.ds(start, size)) for start in range(0, rows, size)]
    fetches = [
        pltpu.make_async_copy(refs[i].at[at], refs[12 + i].at[at], arrived.at[n]) for n, (i, at) in enumerate(steps)
    ]
    stores = [
        pltpu.make_async_copy(refs[12 + i].at[at], refs[6 + i].at[at], left.at[n]) for n, (i, at) in enumerate(steps)
    ]
    for fetch in fetches:
        fetch.start()
    for fetch, store in zip(fetches, stores):
        fetch.wait()
        store.start()
    for store in stores:
        store.wait()


def constants(ny, nx, nz):
    share = C // (ny * nx * nz * 2)
    perm = np.zeros((C, C), np.float32)
    for core in range(2):
        for y in range(ny):
            for xh in range(nx):
                for z in range(nz):
                    to = (((core * ny + y) * nx + xh) * nz + z) * share
                    start = (((y * nx + xh) * nz + z) * 2 + core) * share
                    perm[to + np.arange(share), start + np.arange(share)] = 1
    a = np.arange(T)
    pa = (a // WIN_LON) * (2 * WIN_LON - 1) + a % WIN_LON
    selrt = np.zeros((128, 128), np.float32)
    selrt[126 - pa, a] = 1
    self_ = np.zeros((128, 128), np.float32)
    self_[a, pa] = 1
    return perm, self_, self_.T, selrt


def solution(mesh):
    nlon, nlat = mesh.shape["lon"], mesh.shape["lat"]
    nx, nz = 2, nlat // 2
    ny = nlon // nx
    nxz = nx * nz
    half = C // 2
    ysz = half // ny
    share = ysz // nxz
    cols = [C, C] + [256] * PAIRS
    lat_dev, lon_dev = 18, 48
    nwin = 12
    vm = pltpu.VMEM
    dma = lambda *s: pltpu.SemaphoreType.DMA(s)
    perm, self_, selft, selrt = (jnp.asarray(v, BF16) for v in constants(ny, nx, nz))

    def on_device(fields, grad_out, layernorm_gain, qkv_weight, proj_weight, bias_table, sea_mask):
        shapes = (
            jax.ShapeDtypeStruct((lat_dev, lon_dev, C), BF16),
            jax.ShapeDtypeStruct((lat_dev, lon_dev, C), BF16),
            jax.ShapeDtypeStruct((1, C), F32),
            jax.ShapeDtypeStruct((HEADS, REL), F32),
            jax.ShapeDtypeStruct((share, 3 * C), F32),
            jax.ShapeDtypeStruct((share, C), F32),
        )
        scratch = [
            vm((lat_dev, lon_dev, C), BF16),
            vm((lat_dev, lon_dev), jnp.int32),
            vm((lat_dev, lon_dev, C), BF16),
            vm((HEADS, REL), F32),
            vm((128, 128), BF16),
            vm((128, 128), BF16),
            vm((128, 128), BF16),
            vm((1, C), F32),
            vm((C, 3 * C), BF16),
            vm((C, C), BF16),
            vm((C, C), BF16),
        ]
        scratch += [vm(v.shape, v.dtype) for v in shapes]
        scratch += [
            vm((lat_dev + 3, 56, FW), F32),
            vm((nwin, TP, FW), F32),
            vm((112, FW), F32),
        ]
        for wide in (C, C):
            scratch += [
                vm((112, wide), BF16),
                vm((112, wide), BF16),
                vm((3, lon_dev, wide), BF16),
                vm((3, lon_dev, wide), BF16),
                vm((32, wide), BF16),
            ]
        scratch += [vm((lat_dev, lon_dev), jnp.int32)] * 3
        scratch += [
            pltpu.SMEM((16,), jnp.int32),
            vm((HEADS, 256), F32),
            vm((PAIRS, TP, 256), F32),
            vm((SLOTS, TP, 128), F32),
            vm((ROWS, C), F32),
            vm((ROWS, 128), F32),
            vm((RP, C), BF16),
            vm((RP, C), BF16),
            vm((ROWS, C), BF16),
            vm((ROWS, 3 * C), BF16),
            vm((RP, C), BF16),
            vm((C, RP), BF16),
            vm((C, RP), BF16),
            vm((SLOTS * PAIRS, TP, 256), F32),
            vm((SLOTS * PAIRS, TP, 256), BF16),
            vm((RP, C), BF16),
            vm((PAIRS, RP, 256), BF16),
            vm((ROWS, C), F32),
            vm((PAIRS, TP, 256), F32),
            vm((SLOTS, TP, C), F32),
            vm((2, lat_dev + 3, 56, C), F32),
            vm((2, 144, C), BF16),
            vm((2, 3, lon_dev, C), BF16),
            vm((2, 112, C), BF16),
            vm((2, 3, lon_dev, C), BF16),
            vm((2, 32, C), BF16),
        ]
        for n in cols:
            scratch += [
                vm((half, n), BF16),
                vm((half, n), BF16),
                vm((half, n), F32),
                vm((half, n), BF16),
                vm((ny - 1, ysz, n), BF16),
                vm((ysz // 2, n), BF16),
                vm((ysz // 2, n), BF16),
                vm((ysz // 2, n), F32),
            ]
        for n in (sum(cols[:5]), cols[5]):
            scratch += [vm((nz, share, n), F32), vm((nz - 1, share, n), F32)]
        sm = (8, 384)
        scratch += [vm(sm, F32), vm(sm, F32), vm((ny,) + sm, F32), vm(sm, F32), vm(sm, F32), vm((nz,) + sm, F32)]
        nc = len(cols)
        small = ny + nz
        scratch += [
            dma(2, 3), dma(2, 3), dma(3), dma(3), dma(2, 3), dma(2, 3), dma(nc), dma(nc), dma(nc, ny - 1),
            dma(nc, ny - 1), dma(nc), dma(nc), dma(2, nz - 1), dma(2, nz - 1), dma(small), dma(small), dma(11), dma(6),
        ]
        anywhere = pl.BlockSpec(memory_space=pl.ANY)
        outs = pl.pallas_call(
            functools.partial(kernel, (ny, nx, nz), cols),
            out_shape=shapes,
            in_specs=[anywhere] * 11,
            out_specs=(anywhere,) * 6,
            scratch_shapes=scratch,
            compiler_params=pltpu.CompilerParams(
                collective_id=0, has_side_effects=True, vmem_limit_bytes=60 * 1024 * 1024
            ),
        )(
            fields, sea_mask, grad_out, bias_table, self_, selft, selrt,
            layernorm_gain.reshape(1, C), qkv_weight, proj_weight, perm,
        )
        outs = pl.pallas_call(
            hand_over,
            out_shape=shapes,
            in_specs=[anywhere] * 6,
            out_specs=(anywhere,) * 6,
            scratch_shapes=[vm(v.shape, v.dtype) for v in shapes] + [dma(16), dma(16)],
            compiler_params=pltpu.CompilerParams(vmem_limit_bytes=60 * 1024 * 1024),
        )(*outs)
        updated, grad_in, grad_gain, grad_bias, grad_qkv, grad_proj = outs
        return (updated, grad_in, grad_gain.reshape(C), grad_bias, grad_qkv, grad_proj)

    grid = P(("batch", "lat"), "lon", None)
    return jax.shard_map(
        on_device,
        mesh=mesh,
        in_specs=(grid, grid, P(), P(), P(), P(), P(("batch", "lat"), "lon")),
        out_specs=(
            grid,
            grid,
            P("batch"),
            P("batch", None),
            P(("batch", "lon", "lat"), None),
            P(("batch", "lon", "lat"), None),
        ),
        check_vma=False,
    )
```

```python
import functools

import jax
import jax.numpy as jnp
import numpy as np
from jax import lax
from jax.experimental import pallas as pl
from jax.experimental.pallas import tpu as pltpu
from jax.sharding import PartitionSpec as P

MESH = pl.DeviceIdType.MESH
F32 = jnp.float32
BF16 = jnp.bfloat16
C = 512
HEADS = 8
PAIRS = 4
WIN_LAT = 6
WIN_LON = 12
HALF_LAT = 3
HALF_LON = 6
T = 72
TP = 80
SLOTS = 9
ROWS = SLOTS * TP
RP = 768
REL = 253
X0, M0, D0, FW = 0, 512, 640, 1152
EARLY = 3
EPS = 1e-5


def nn(a, b, **kw):
    return lax.dot_general(a, b, (((1,), (0,)), ((), ())), preferred_element_type=F32, **kw)


def nt(a, b, **kw):
    return lax.dot_general(a, b, (((1,), (1,)), ((), ())), preferred_element_type=F32, **kw)


def tn(a, b, **kw):
    return lax.dot_general(a, b, (((0,), (0,)), ((), ())), preferred_element_type=F32, **kw)


def pad_rows(v, rows):
    return jnp.concatenate([v, jnp.zeros((rows - v.shape[0], v.shape[1]), v.dtype)], axis=0)


def kernel(dims, cols, *refs):
    ny, nx, nz = dims
    nlon, nlat = ny * nx, 2 * nz
    nxz = nx * nz
    lat_dev, lon_dev = 18, 48
    wrows, wcols = lat_dev // WIN_LAT, lon_dev // WIN_LON
    nwin = wrows * wcols
    half = C // 2
    ysz = half // ny
    share = ysz // nxz
    nchunk = len(cols)

    it = iter(refs)
    take = lambda n=None: next(it) if n is None else [next(it) for _ in range(n)]
    given = take(11)
    results = take(6)
    held = take(11)
    x_ref, mask_ref, dy_ref, table, self_, selft, selrt, gain_ref, wqkv, wproj, perm = held
    staged = take(6)
    upd, gin, gain_out, bias_out, gqkv, gproj = staged
    frame, win, colf = take(3)
    halos = [take(5) for _ in range(2)]
    masks = take(3)
    idx = take()
    tb, bias2, madd, xhat, invd, normed, gz, gm, packed, mixed, ntp, mtp, probs, dp3, gnacc, bacc = take(16)
    res, of = take(2)
    ocs, ors, ocr, orr, occ = take(5)
    chunks = [take(8) for _ in range(nchunk)]
    groups = [take(2) for _ in range(2)]
    sums = take(6)
    hs, hr, ms, mr, os_, or_, as_, ar, ys, yr, xs, xr, zs, zr, ss, sr = take(16)
    ins, outs = take(2)

    lon = lax.axis_index("lon")
    lat = lax.axis_index("lat")
    y, xh = lon // nx, lon % nx
    z, core = lat // 2, lat % 2

    def dev(a, b):
        return {"lon": a, "lat": b}

    partner = dev(lon, z * 2 + (1 - core))
    ypeer = [dev(((y + d) % ny) * nx + xh, lat) for d in range(1, ny)]
    xpeer = dev(y * nx + (1 - xh), lat)
    zpeer = [dev(lon, ((z + d) % nz) * 2 + core) for d in range(1, nz)]
    west, east = (lon + nlon - 1) % nlon, (lon + 1) % nlon
    north, south = (lat + nlat - 1) % nlat, (lat + 1) % nlat
    back = [dev(west, lat), dev(lon, north), dev(west, north)]
    forth = [dev(east, lat), dev(lon, south), dev(east, south)]

    barrier = pltpu.get_barrier_semaphore()
    everyone = [partner, xpeer] + ypeer + zpeer + back + forth
    for d in everyone:
        pl.semaphore_signal(barrier, inc=1, device_id=d, device_id_type=MESH)

    loads = [pltpu.make_async_copy(a, b, ins.at[i]) for i, (a, b) in enumerate(zip(given, held))]
    for load in loads:
        load.start()

    stores = [pltpu.make_async_copy(a, b, outs.at[i]) for i, (a, b) in enumerate(zip(staged, results))]
    sends = []

    def send(src, dst, ssem, rsem, d):
        copy = pltpu.make_async_remote_copy(
            src_ref=src, dst_ref=dst, send_sem=ssem, recv_sem=rsem, device_id=d, device_id_type=MESH
        )
        copy.start()
        sends.append(copy)
        return copy

    lane_row = lax.broadcasted_iota(jnp.int32, (lat_dev, lat_dev * 128), 1) // 128
    pick = (lane_row == lax.broadcasted_iota(jnp.int32, (lat_dev, lat_dev * 128), 0)).astype(F32)

    def spread_mask(ref):
        return tn(ref[...].astype(F32), pick)

    loads[1].wait()
    sea = spread_mask(mask_ref)
    colf[96:112, :] = jnp.zeros((16, FW), F32)

    def halo_pack(h, lanes):
        colsend, colrecv, rowsend, rowrecv, cornrecv = halos[h]
        for r in range(lat_dev):
            colf[6 * r : 6 * r + 6, lanes] = frame[r, 0:HALF_LON, lanes]
        colsend[...] = colf[:, lanes].astype(BF16)
        for r in range(HALF_LAT):
            rowsend[r] = frame[r, 0:lon_dev, lanes].astype(BF16)

    def halo_send(h):
        colsend, colrecv, rowsend, rowrecv, cornrecv = halos[h]
        return [
            send(colsend, colrecv, hs.at[h, 0], hr.at[h, 0], back[0]),
            send(rowsend, rowrecv, hs.at[h, 1], hr.at[h, 1], back[1]),
            send(colsend.at[0:32], cornrecv, hs.at[h, 2], hr.at[h, 2], back[2]),
        ]

    def halo_land(h, lanes, copies):
        colsend, colrecv, rowsend, rowrecv, cornrecv = halos[h]
        copies[1].wait_recv()
        for r in range(HALF_LAT):
            frame[lat_dev + r, 0:lon_dev, lanes] = rowrecv[r].astype(F32)
        copies[2].wait_recv()
        colf[0:32, lanes] = cornrecv[...].astype(F32)
        for r in range(HALF_LAT):
            frame[lat_dev + r, lon_dev : lon_dev + HALF_LON, lanes] = colf[6 * r : 6 * r + 6, lanes]
        copies[0].wait_recv()
        colf[:, lanes] = colrecv[...].astype(F32)
        for r in range(lat_dev):
            frame[r, lon_dev : lon_dev + HALF_LON, lanes] = colf[6 * r : 6 * r + 6, lanes]

    xlanes, dlanes = slice(X0, X0 + C), slice(D0, D0 + C)
    loads[0].wait()
    for r in range(lat_dev):
        frame[r, 0:lon_dev, X0 : X0 + C] = x_ref[r].astype(F32)
        frame[r, 0:lon_dev, M0 : M0 + 128] = sea[:, 128 * r : 128 * r + 128]
    halo_pack(0, xlanes)
    pl.semaphore_wait(barrier, len(everyone))
    mcopies = [send(mask_ref, masks[i], ms.at[i], mr.at[i], back[i]) for i in range(3)]
    xcopies = halo_send(0)
    loads[2].wait()
    for r in range(lat_dev):
        frame[r, 0:lon_dev, D0 : D0 + C] = dy_ref[r].astype(F32)
    halo_pack(1, dlanes)
    dcopies = halo_send(1)

    def pieces(v, n):
        out = []
        for i in range(n):
            part = v.astype(BF16)
            out.append(part)
            if i < n - 1:
                v = v - part.astype(F32)
        return out

    for i in range(3, 11):
        loads[i].wait()
    tb[...] = jnp.zeros_like(tb)
    tb[:, 0:REL] = table[...]
    shifted = []
    for h in range(HEADS):
        line = jnp.broadcast_to(tb[h : h + 1, :], (128, 256))
        shifted.append(pltpu.roll(pltpu.roll(line, 2, 1), 128, 1, stride=1, stride_axis=0)[:, 0:128])
    by_query = sum(nn(v, selft[...]) for v in pieces(jnp.concatenate(shifted, axis=0), 3))
    by_query = jnp.concatenate([by_query[128 * h : 128 * h + 128] for h in range(HEADS)], axis=1)
    whole_bias = sum(nn(self_[0:TP, :], v) for v in pieces(by_query, 3))
    for p in range(PAIRS):
        bias2[p] = whole_bias[:, 256 * p : 256 * p + 256]

    zero_tail = jnp.zeros((RP - ROWS, C), BF16)
    normed[ROWS:RP, :] = zero_tail
    gz[ROWS:RP, :] = zero_tail
    mixed[ROWS:RP, :] = zero_tail
    for p in range(PAIRS):
        dp3[p, ROWS:RP, :] = jnp.zeros((RP - ROWS, 384), BF16)
    for w in range(nwin):
        win[w, T:TP, :] = jnp.zeros((TP - T, FW), F32)

    def cut(w, lanes):
        wr, wc = w // wcols, w % wcols
        c0 = HALF_LON + WIN_LON * wc
        for i in range(WIN_LAT):
            win[w, WIN_LON * i : WIN_LON * i + WIN_LON, lanes] = frame[
                HALF_LAT + WIN_LAT * wr + i, c0 : c0 + WIN_LON, lanes
            ]

    def holds_sea(w):
        return (jnp.max(win[w, :, M0 : M0 + 128]) > 0.5).astype(jnp.int32)

    def ranks(flags, counted):
        total = jnp.int32(0)
        for f, c in zip(flags, counted):
            total = total + f * c
        out, on, off = [], jnp.int32(0), total
        for f, c in zip(flags, counted):
            out.append(jnp.where(f > 0, on, off))
            on = on + f * c
            off = off + (1 - f) * c
        return out

    def slot_window(k, places):
        slot = jnp.int32(0)
        for w, at in places:
            slot = slot + jnp.where(at == k, w, 0)
        idx[k] = slot

    inner = [w for w in range(nwin) if w // wcols < wrows - 1 and w % wcols < wcols - 1]
    outer = [w for w in range(nwin) if w not in inner]
    active = [None] * nwin
    place = [None] * nwin

    at_end = (lat == nlat - 1).astype(F32)
    gain = gain_ref[...]

    def rows_of(k):
        return pl.ds(pl.multiple_of(k * TP, TP), TP)

    def by_three(step):
        def body(i, carry):
            for j in range(3):
                carry = step(3 * i + j, carry)
            return carry

        return body

    def ln_step(k, carry):
        w = idx[k]
        x = win[w, :, X0 : X0 + C]
        mean = jnp.mean(x, axis=1, keepdims=True)
        xc = x - mean
        inv = lax.rsqrt(jnp.mean(xc * xc, axis=1, keepdims=True) + EPS)
        hat = xc * inv
        rows = rows_of(k)
        xhat[rows, :] = hat
        invd[rows, :] = jnp.broadcast_to(inv, (TP, 128))
        normed[rows, :] = (hat * gain).astype(BF16)
        keys = win[w, :, M0 : M0 + 128]
        side_b = lax.broadcasted_iota(jnp.int32, (TP, 128), 0) >= T // 2
        side_a = lax.broadcasted_iota(jnp.int32, (TP, 128), 1) >= T // 2
        apart = jnp.where(side_a != side_b, 1.0, 0.0)
        wrap = at_end * jnp.where(w >= nwin - wcols, 1.0, 0.0)
        madd[k] = (keys * (1.0 - apart * wrap) - 1.0) * 1e9
        return carry

    def dy_step(k, carry):
        w = idx[k]
        m = win[w, :, M0 : M0 + 128]
        gz[rows_of(k), :] = (win[w, :, D0 : D0 + C] * jnp.concatenate([m] * 4, axis=1)).astype(BF16)
        return carry

    lane = lax.broadcasted_iota(jnp.int32, (TP, 128), 1)
    low = lane < 64
    one_lo = jnp.where(low, 1.0, 0.0).astype(BF16)
    one_hi = jnp.where(low, 0.0, 1.0).astype(BF16)
    q_lo = jnp.where(low, 0.125, 0.0).astype(BF16)
    q_hi = jnp.where(low, 0.0, 0.125).astype(BF16)

    def both_heads(v, lo, hi):
        return jnp.concatenate([pad_rows(v * lo, 128), pad_rows(v * hi, 128)], axis=0)

    def own_head(v):
        return jnp.transpose(jnp.concatenate([v[0:64, 0:128], v[64:128, 128:256]], axis=0))[0:TP]

    def attend(i, carry):
        chains = [(3 * i + j, p) for j in range(3) for p in range(PAIRS)]
        scores = []
        for k, p in chains:
            rows = rows_of(k)
            q2 = both_heads(packed[rows, 128 * p : 128 * p + 128], q_lo, q_hi)
            add = madd[k]
            add2 = jnp.concatenate([add, add], axis=1)
            scores.append(nt(packed[rows, C + 128 * p : C + 128 * p + 128], q2) + bias2[p] + add2)
        mixes = []
        for (k, p), s in zip(chains, scores):
            e = jnp.exp(s - jnp.max(s, axis=0, keepdims=True))
            pr = e * (1.0 / jnp.sum(e, axis=0, keepdims=True))
            probs[k * PAIRS + p] = pr
            mixes.append(tn(packed[rows_of(k), 2 * C + 128 * p : 2 * C + 128 * p + 128], pr.astype(BF16)))
        for (k, p), mix in zip(chains, mixes):
            mixed[rows_of(k), 128 * p : 128 * p + 128] = own_head(mix).astype(BF16)
        return carry

    def forward(first, last):
        lax.fori_loop(first // 3, last // 3, by_three(ln_step), 0)
        rows = slice(first * TP, last * TP)
        packed[rows, :] = nn(normed[rows, :], wqkv[...]).astype(BF16)
        lax.fori_loop(first // 3, last // 3, attend, 0)

    for w in inner:
        cut(w, slice(0, FW))
        active[w] = holds_sea(w)
    inner_rank = ranks([active[w] for w in inner], [1] * len(inner))
    for k in range(EARLY):
        slot_window(k, list(zip(inner, inner_rank)))
    forward(0, EARLY)

    mlanes = slice(M0, M0 + 128)
    for copy in mcopies:
        copy.wait_recv()
    sea = spread_mask(masks[0])
    for r in range(lat_dev):
        frame[r, lon_dev : lon_dev + HALF_LON, mlanes] = sea[0:HALF_LON, 128 * r : 128 * r + 128]
    sea = spread_mask(masks[1])
    for r in range(HALF_LAT):
        frame[lat_dev + r, 0:lon_dev, mlanes] = sea[:, 128 * r : 128 * r + 128]
    sea = spread_mask(masks[2])
    for r in range(HALF_LAT):
        frame[lat_dev + r, lon_dev : lon_dev + HALF_LON, mlanes] = sea[0:HALF_LON, 128 * r : 128 * r + 128]
    halo_land(0, xlanes, xcopies)
    for w in outer:
        cut(w, slice(X0, M0 + 128))
        active[w] = holds_sea(w)
    rest = [jnp.int32(1)] * nwin
    for w, at in zip(inner, inner_rank):
        rest[w] = (at >= EARLY).astype(jnp.int32)
    late_rank = ranks(active, rest)
    for w in range(nwin):
        place[w] = late_rank[w] + EARLY
    for w, at in zip(inner, inner_rank):
        place[w] = jnp.where(at < EARLY, at, place[w])
    for k in range(EARLY, SLOTS):
        slot_window(k, list(enumerate(place)))
    forward(EARLY, SLOTS)

    halo_land(1, dlanes, dcopies)
    for w in outer:
        cut(w, dlanes)
    lax.fori_loop(0, SLOTS // 3, by_three(dy_step), 0)
    gm[...] = nt(gz[0:ROWS, :], wproj[...]).astype(BF16)
    ntp[...] = nt(perm[...], normed[...]).astype(BF16)

    def chunk_start(c, lhs, rhs):
        asend, arecv, own = chunks[c][0:3]
        right = rhs[...]
        other = pl.multiple_of((1 - core) * half, half)
        mine = pl.multiple_of(core * half, half)
        asend[...] = nn(lhs[pl.ds(other, half), :], right).astype(BF16)
        copy = send(asend, arecv, as_.at[c], ar.at[c], partner)
        own[...] = nn(lhs[pl.ds(mine, half), :], right)
        return [copy]

    def chunk_y(c, copies):
        asend, arecv, own, ysend, yrecv = chunks[c][0:5]
        copies[0].wait_recv()
        s = own[...] + arecv[...].astype(F32)
        own[...] = s
        ysend[...] = s.astype(BF16)
        out = []
        for d in range(1, ny):
            start = pl.multiple_of(((y + d) % ny) * ysz, ysz)
            out.append(
                send(ysend.at[pl.ds(start, ysz)], yrecv.at[d - 1], ys.at[c, d - 1], yr.at[c, d - 1], ypeer[d - 1])
            )
        return out

    def chunk_x(c, copies):
        own, ysend, yrecv, xsend, xrecv, xown = chunks[c][2:8]
        s = own[pl.ds(pl.multiple_of(y * ysz, ysz), ysz), :]
        for d in range(1, ny):
            copies[d - 1].wait_recv()
            s = s + yrecv[d - 1].astype(F32)
        top, low_half = s[0 : ysz // 2], s[ysz // 2 : ysz]
        first = xh == 0
        xsend[...] = jnp.where(first, low_half, top).astype(BF16)
        xown[...] = jnp.where(first, top, low_half)
        return [send(xsend, xrecv, xs.at[c], xr.at[c], xpeer)]

    def chunk_z(c, copies):
        xsend, xrecv, xown = chunks[c][5:8]
        zsend = groups[0 if c < 4 else 1][0]
        start = sum(cols[:c]) if c < 4 else 0
        copies[0].wait_recv()
        s = xown[...] + xrecv[...].astype(F32)
        for j in range(nz):
            zsend[j, :, start : start + cols[c]] = s[share * j : share * j + share]

    def group_send(g):
        zsend, zrecv = groups[g]
        return [
            send(zsend.at[(z + d) % nz], zrecv.at[d - 1], zs.at[g, d - 1], zr.at[g, d - 1], zpeer[d - 1])
            for d in range(1, nz)
        ]

    def group_end(g, copies):
        zsend, zrecv = groups[g]
        s = zsend[z]
        for i, copy in enumerate(copies):
            copy.wait_recv()
            s = s + zrecv[i]
        start = 0
        for c in range(nchunk):
            if (c < 4) != (g == 0):
                continue
            if c == 0:
                gproj[...] = s[:, 0:C]
            else:
                p = c - 1
                for part in range(3):
                    at = start + 128 * part
                    gqkv[:, C * part + 128 * p : C * part + 128 * p + 128] = s[:, at : at + 128]
            start += cols[c]

    def window_back(o, lane0):
        def place_window(w):
            wr, wc = w // wcols, w % wcols
            slot = jnp.minimum(place[w], SLOTS - 1)
            for i in range(WIN_LAT):
                c0 = HALF_LON + WIN_LON * wc
                at = slice(WIN_LON * i, WIN_LON * i + WIN_LON)
                of[o, HALF_LAT + WIN_LAT * wr + i, c0 : c0 + WIN_LON, :] = jnp.where(
                    place[w] < SLOTS, res[slot, at, :], win[w, at, lane0 : lane0 + C]
                )

        for w in range(wcols - 1, nwin, wcols):
            place_window(w)
        colf[0 : 6 * HALF_LAT, 0:C] = jnp.zeros((6 * HALF_LAT, C), F32)
        for r in range(HALF_LAT, lat_dev):
            colf[6 * r : 6 * r + 6, 0:C] = of[o, r, lon_dev : lon_dev + HALF_LON, :]
        ocs[o, 0:112] = colf[0:112, 0:C].astype(BF16)
        for r in range(HALF_LAT):
            colf[6 * r : 6 * r + 6, 0:C] = of[o, lat_dev + r, lon_dev : lon_dev + HALF_LON, :]
        ocs[o, 112:144] = colf[0:32, 0:C].astype(BF16)
        copies = [
            send(ocs.at[o, 0:112], ocr.at[o], os_.at[o, 0], or_.at[o, 0], forth[0]),
            send(ocs.at[o, 112:144], occ.at[o], os_.at[o, 2], or_.at[o, 2], forth[2]),
        ]
        for w in range(nwin - wcols, nwin - 1):
            place_window(w)
        for r in range(HALF_LAT):
            ors[o, r] = of[o, lat_dev + r, 0:lon_dev, :].astype(BF16)
        copies.insert(1, send(ors.at[o], orr.at[o], os_.at[o, 1], or_.at[o, 1], forth[1]))
        for w in range(nwin - wcols):
            if w % wcols < wcols - 1:
                place_window(w)
        return copies

    def finish(o, copies, out):
        copies[1].wait_recv()
        for r in range(HALF_LAT):
            of[o, r, 0:lon_dev, :] = orr[o, r].astype(F32)
        copies[0].wait_recv()
        colf[0:112, 0:C] = ocr[o].astype(F32)
        for r in range(HALF_LAT, lat_dev):
            of[o, r, 0:HALF_LON, :] = colf[6 * r : 6 * r + 6, 0:C]
        copies[2].wait_recv()
        colf[0:32, 0:C] = occ[o].astype(F32)
        for r in range(HALF_LAT):
            of[o, r, 0:HALF_LON, :] = colf[6 * r : 6 * r + 6, 0:C]
        for r in range(lat_dev):
            out[r] = of[o, r, 0:lon_dev, :].astype(BF16)

    mtp[...] = nt(perm[...], mixed[...]).astype(BF16)
    st = {}
    st[0] = chunk_start(0, mtp, gz)

    gnacc[...] = nn(mixed[0:ROWS, :], wproj[...])

    def updated_step(k, carry):
        w = idx[k]
        m = win[w, :, M0 : M0 + 128]
        res[k] = win[w, :, X0 : X0 + C] + jnp.concatenate([m] * 4, axis=1) * gnacc[rows_of(k), :]
        return carry

    lax.fori_loop(0, SLOTS // 3, by_three(updated_step), 0)
    out_copies = [window_back(0, X0), None]

    def backward(p):
        ks = list(range(SLOTS))
        d2s, dps = [], []
        for k in ks:
            rows = slice(TP * k, TP * k + TP)
            d2s.append(both_heads(gm[rows, 128 * p : 128 * p + 128], one_lo, one_hi))
            dps.append(nt(packed[rows, 2 * C + 128 * p : 2 * C + 128 * p + 128], d2s[-1]))
        dss, dvs = [], []
        for k in ks:
            pr = probs[k * PAIRS + p]
            t = pr * dps[k]
            dss.append(t - pr * jnp.sum(t, axis=0, keepdims=True))
            dvs.append(nn(pr.astype(BF16), d2s[k]))
        bacc[p] = functools.reduce(lambda a, b: a + b, dss)
        dqs = []
        for k in ks:
            rows = slice(TP * k, TP * k + TP)
            ds = dss[k].astype(BF16)
            q2 = both_heads(packed[rows, 128 * p : 128 * p + 128], q_lo, q_hi)
            dqs.append(tn(packed[rows, C + 128 * p : C + 128 * p + 128], ds))
            dp3[p, rows, 128:256] = nn(ds, q2).astype(BF16)
            dp3[p, rows, 256:384] = dvs[k].astype(BF16)
        for k in ks:
            dp3[p, TP * k : TP * k + TP, 0:128] = (own_head(dqs[k]) * 0.125).astype(BF16)

    def weight_pair(p):
        return jnp.concatenate([wqkv[:, C * part + 128 * p : C * part + 128 * p + 128] for part in range(3)], axis=1)

    def grad_normed(p):
        g = nt(dp3[p, 0:ROWS, :], weight_pair(p))
        gnacc[...] = g if p == 0 else gnacc[...] + g

    for p in range(PAIRS):
        backward(p)
        st[p + 1] = chunk_start(p + 1, ntp, dp3.at[p])
        st[p] = chunk_y(p, st[p])
        if p >= 1:
            st[p - 1] = chunk_x(p - 1, st[p - 1])
        if p >= 2:
            chunk_z(p - 2, st[p - 2])
        grad_normed(p)
    st[4] = chunk_y(4, st[4])

    def norm_back(k, total):
        w = idx[k]
        rows = rows_of(k)
        gn = gnacc[rows, :]
        hat = xhat[rows, :]
        g = gn * gain
        prod = g * hat
        mid = g - jnp.mean(g, axis=1, keepdims=True) - hat * jnp.mean(prod, axis=1, keepdims=True)
        inv = jnp.concatenate([invd[rows, :]] * 4, axis=1)
        res[k] = win[w, :, D0 : D0 + C] + inv * mid
        return total + jnp.sum(gn * hat, axis=0, keepdims=True)

    gsum = lax.fori_loop(0, SLOTS // 3, by_three(norm_back), jnp.zeros((1, C), F32))
    out_copies[1] = window_back(1, D0)
    st[3] = chunk_x(3, st[3])

    stacked = jnp.concatenate([bacc[h // 2, :, 128 * (h % 2) : 128 * (h % 2) + 128] for h in range(HEADS)], axis=0)
    by_place = sum(nn(v, self_[...]) for v in pieces(stacked, 2))
    by_place = jnp.concatenate([by_place[TP * h : TP * h + TP] for h in range(HEADS)], axis=1)
    spread = sum(nn(selrt[:, 0:TP], v) for v in pieces(by_place, 2))
    for h in range(HEADS):
        wide = jnp.concatenate([spread[:, 128 * h : 128 * h + 128], jnp.zeros((128, 128), F32)], axis=1)
        sums[0][h : h + 1, 0:256] = jnp.sum(pltpu.roll(wide, 0, 1, stride=1, stride_axis=0), axis=0, keepdims=True)
    sm, smc, smy, sma, smx, smz = sums
    sm[4:8, 256:384] = jnp.zeros((4, 128), F32)
    for j in range(4):
        sm[j : j + 1, 256:384] = gsum[:, 128 * j : 128 * j + 128]
    copy = send(sm, smc, ss.at[0], sr.at[0], partner)
    chunk_z(2, st[2])
    chunk_z(3, st[3])
    group0 = group_send(0)
    st[4] = chunk_x(4, st[4])
    copy.wait_recv()
    smy[y] = sm[...] + smc[...]
    copies = [send(smy.at[y], smy.at[y], ss.at[d], sr.at[d], ypeer[d - 1]) for d in range(1, ny)]
    finish(0, out_copies[0], upd)
    stores[0].start()
    chunk_z(4, st[4])
    group1 = group_send(1)
    for copy in copies:
        copy.wait_recv()
    acc = smy[0]
    for j in range(1, ny):
        acc = acc + smy[j]
    sma[...] = acc
    copy = send(sma, smx, ss.at[ny], sr.at[ny], xpeer)
    group_end(0, group0)
    copy.wait_recv()
    smz[z] = sma[...] + smx[...]
    copies = [send(smz.at[z], smz.at[z], ss.at[ny + d], sr.at[ny + d], zpeer[d - 1]) for d in range(1, nz)]
    finish(1, out_copies[1], gin)
    stores[1].start()
    group_end(1, group1)
    for copy in copies:
        copy.wait_recv()
    acc = smz[0]
    for j in range(1, nz):
        acc = acc + smz[j]
    bias_out[...] = acc[:, 0:REL]
    for j in range(4):
        gain_out[:, 128 * j : 128 * j + 128] = acc[j : j + 1, 256:384]
    for store in stores[2:]:
        store.start()
    for copy in sends:
        copy.wait_send()
    for store in stores:
        store.wait()


def hand_over(*refs):
    arrived, left = refs[18:20]
    steps = []
    for i in range(6):
        rows = refs[i].shape[0]
        size = 3 if i < 2 else rows
        steps += [(i, pl.ds(start, size)) for start in range(0, rows, size)]
    fetches = [
        pltpu.make_async_copy(refs[i].at[at], refs[12 + i].at[at], arrived.at[n]) for n, (i, at) in enumerate(steps)
    ]
    stores = [
        pltpu.make_async_copy(refs[12 + i].at[at], refs[6 + i].at[at], left.at[n]) for n, (i, at) in enumerate(steps)
    ]
    for fetch in fetches:
        fetch.start()
    for fetch, store in zip(fetches, stores):
        fetch.wait()
        store.start()
    for store in stores:
        store.wait()


def constants(ny, nx, nz):
    share = C // (ny * nx * nz * 2)
    perm = np.zeros((C, C), np.float32)
    for core in range(2):
        for y in range(ny):
            for xh in range(nx):
                for z in range(nz):
                    to = (((core * ny + y) * nx + xh) * nz + z) * share
                    start = (((y * nx + xh) * nz + z) * 2 + core) * share
                    perm[to + np.arange(share), start + np.arange(share)] = 1
    a = np.arange(T)
    pa = (a // WIN_LON) * (2 * WIN_LON - 1) + a % WIN_LON
    selrt = np.zeros((128, 128), np.float32)
    selrt[126 - pa, a] = 1
    self_ = np.zeros((128, 128), np.float32)
    self_[a, pa] = 1
    return perm, self_, self_.T, selrt


def solution(mesh):
    nlon, nlat = mesh.shape["lon"], mesh.shape["lat"]
    nx, nz = 2, nlat // 2
    ny = nlon // nx
    nxz = nx * nz
    half = C // 2
    ysz = half // ny
    share = ysz // nxz
    cols = [C] + [384] * PAIRS
    lat_dev, lon_dev = 18, 48
    nwin = 12
    vm = pltpu.VMEM
    dma = lambda *s: pltpu.SemaphoreType.DMA(s)
    perm, self_, selft, selrt = (jnp.asarray(v, BF16) for v in constants(ny, nx, nz))

    def on_device(fields, grad_out, layernorm_gain, qkv_weight, proj_weight, bias_table, sea_mask):
        shapes = (
            jax.ShapeDtypeStruct((lat_dev, lon_dev, C), BF16),
            jax.ShapeDtypeStruct((lat_dev, lon_dev, C), BF16),
            jax.ShapeDtypeStruct((1, C), F32),
            jax.ShapeDtypeStruct((HEADS, REL), F32),
            jax.ShapeDtypeStruct((share, 3 * C), F32),
            jax.ShapeDtypeStruct((share, C), F32),
        )
        scratch = [
            vm((lat_dev, lon_dev, C), BF16),
            vm((lat_dev, lon_dev), jnp.int32),
            vm((lat_dev, lon_dev, C), BF16),
            vm((HEADS, REL), F32),
            vm((128, 128), BF16),
            vm((128, 128), BF16),
            vm((128, 128), BF16),
            vm((1, C), F32),
            vm((C, 3 * C), BF16),
            vm((C, C), BF16),
            vm((C, C), BF16),
        ]
        scratch += [vm(v.shape, v.dtype) for v in shapes]
        scratch += [
            vm((lat_dev + 3, 56, FW), F32),
            vm((nwin, TP, FW), F32),
            vm((112, FW), F32),
        ]
        for wide in (C, C):
            scratch += [
                vm((112, wide), BF16),
                vm((112, wide), BF16),
                vm((3, lon_dev, wide), BF16),
                vm((3, lon_dev, wide), BF16),
                vm((32, wide), BF16),
            ]
        scratch += [vm((lat_dev, lon_dev), jnp.int32)] * 3
        scratch += [
            pltpu.SMEM((16,), jnp.int32),
            vm((HEADS, 256), F32),
            vm((PAIRS, TP, 256), F32),
            vm((SLOTS, TP, 128), F32),
            vm((ROWS, C), F32),
            vm((ROWS, 128), F32),
            vm((RP, C), BF16),
            vm((RP, C), BF16),
            vm((ROWS, C), BF16),
            vm((ROWS, 3 * C), BF16),
            vm((RP, C), BF16),
            vm((C, RP), BF16),
            vm((C, RP), BF16),
            vm((SLOTS * PAIRS, TP, 256), F32),
            vm((PAIRS, RP, 384), BF16),
            vm((ROWS, C), F32),
            vm((PAIRS, TP, 256), F32),
            vm((SLOTS, TP, C), F32),
            vm((2, lat_dev + 3, 56, C), F32),
            vm((2, 144, C), BF16),
            vm((2, 3, lon_dev, C), BF16),
            vm((2, 112, C), BF16),
            vm((2, 3, lon_dev, C), BF16),
            vm((2, 32, C), BF16),
        ]
        for n in cols:
            scratch += [
                vm((half, n), BF16),
                vm((half, n), BF16),
                vm((half, n), F32),
                vm((half, n), BF16),
                vm((ny - 1, ysz, n), BF16),
                vm((ysz // 2, n), BF16),
                vm((ysz // 2, n), BF16),
                vm((ysz // 2, n), F32),
            ]
        for n in (sum(cols[:4]), cols[4]):
            scratch += [vm((nz, share, n), F32), vm((nz - 1, share, n), F32)]
        sm = (8, 384)
        scratch += [vm(sm, F32), vm(sm, F32), vm((ny,) + sm, F32), vm(sm, F32), vm(sm, F32), vm((nz,) + sm, F32)]
        nc = len(cols)
        small = ny + nz
        scratch += [
            dma(2, 3), dma(2, 3), dma(3), dma(3), dma(2, 3), dma(2, 3), dma(nc), dma(nc), dma(nc, ny - 1),
            dma(nc, ny - 1), dma(nc), dma(nc), dma(2, nz - 1), dma(2, nz - 1), dma(small), dma(small), dma(11), dma(6),
        ]
        anywhere = pl.BlockSpec(memory_space=pl.ANY)
        outs = pl.pallas_call(
            functools.partial(kernel, (ny, nx, nz), cols),
            out_shape=shapes,
            in_specs=[anywhere] * 11,
            out_specs=(anywhere,) * 6,
            scratch_shapes=scratch,
            compiler_params=pltpu.CompilerParams(
                collective_id=0, has_side_effects=True, vmem_limit_bytes=60 * 1024 * 1024
            ),
        )(
            fields, sea_mask, grad_out, bias_table, self_, selft, selrt,
            layernorm_gain.reshape(1, C), qkv_weight, proj_weight, perm,
        )
        outs = pl.pallas_call(
            hand_over,
            out_shape=shapes,
            in_specs=[anywhere] * 6,
            out_specs=(anywhere,) * 6,
            scratch_shapes=[vm(v.shape, v.dtype) for v in shapes] + [dma(16), dma(16)],
            compiler_params=pltpu.CompilerParams(vmem_limit_bytes=60 * 1024 * 1024),
        )(*outs)
        updated, grad_in, grad_gain, grad_bias, grad_qkv, grad_proj = outs
        return (updated, grad_in, grad_gain.reshape(C), grad_bias, grad_qkv, grad_proj)

    grid = P(("batch", "lat"), "lon", None)
    return jax.shard_map(
        on_device,
        mesh=mesh,
        in_specs=(grid, grid, P(), P(), P(), P(), P(("batch", "lat"), "lon")),
        out_specs=(
            grid,
            grid,
            P("batch"),
            P("batch", None),
            P(("batch", "lon", "lat"), None),
            P(("batch", "lon", "lat"), None),
        ),
        check_vma=False,
    )
```

```python
import functools

import jax
import jax.numpy as jnp
import numpy as np
from jax import lax
from jax.experimental import pallas as pl
from jax.experimental.pallas import tpu as pltpu
from jax.sharding import PartitionSpec as P

MESH = pl.DeviceIdType.MESH
F32 = jnp.float32
BF16 = jnp.bfloat16
C = 512
HEADS = 8
PAIRS = 4
WIN_LAT = 6
WIN_LON = 12
HALF_LAT = 3
HALF_LON = 6
T = 72
TP = 80
SLOTS = 9
ROWS = SLOTS * TP
RP = 768
REL = 253
X0, M0, D0, FW = 0, 512, 640, 1152
EARLY = 3
EPS = 1e-5


def nn(a, b, **kw):
    return lax.dot_general(a, b, (((1,), (0,)), ((), ())), preferred_element_type=F32, **kw)


def nt(a, b, **kw):
    return lax.dot_general(a, b, (((1,), (1,)), ((), ())), preferred_element_type=F32, **kw)


def tn(a, b, **kw):
    return lax.dot_general(a, b, (((0,), (0,)), ((), ())), preferred_element_type=F32, **kw)


def pad_rows(v, rows):
    return jnp.concatenate([v, jnp.zeros((rows - v.shape[0], v.shape[1]), v.dtype)], axis=0)


def kernel(dims, cols, *refs):
    ny, nx, nz = dims
    nlon, nlat = ny * nx, 2 * nz
    nxz = nx * nz
    lat_dev, lon_dev = 18, 48
    wrows, wcols = lat_dev // WIN_LAT, lon_dev // WIN_LON
    nwin = wrows * wcols
    half = C // 2
    ysz = half // ny
    share = ysz // nxz
    nchunk = len(cols)

    it = iter(refs)
    take = lambda n=None: next(it) if n is None else [next(it) for _ in range(n)]
    given = take(11)
    results = take(6)
    held = take(11)
    x_ref, mask_ref, dy_ref, table, self_, selft, selrt, gain_ref, wqkv, wproj, perm = held
    staged = take(6)
    upd, gin, gain_out, bias_out, gqkv, gproj = staged
    frame, win, colf = take(3)
    halos = [take(5) for _ in range(2)]
    masks = take(3)
    idx = take()
    tb, bias2, madd, xhat, invd, normed, gz, gm, packed, mixed, ntp, mtp, probs, dp3, gnacc, bacc = take(16)
    res, of = take(2)
    ocs, ors, occs, ocr, orr, occ = take(6)
    chunks = [take(11) for _ in range(nchunk)]
    sums = take(6)
    hs, hr, ms, mr, os_, or_, as_, ar, ys, yr, xs, xr, zs, zr, ss, sr = take(16)
    ins, outs = take(2)

    lon = lax.axis_index("lon")
    lat = lax.axis_index("lat")
    y, xh = lon // nx, lon % nx
    z, core = lat // 2, lat % 2

    def dev(a, b):
        return {"lon": a, "lat": b}

    partner = dev(lon, z * 2 + (1 - core))
    ypeer = [dev(((y + d) % ny) * nx + xh, lat) for d in range(1, ny)]
    xpeer = dev(y * nx + (1 - xh), lat)
    zpeer = [dev(lon, ((z + d) % nz) * 2 + core) for d in range(1, nz)]
    west, east = (lon + nlon - 1) % nlon, (lon + 1) % nlon
    north, south = (lat + nlat - 1) % nlat, (lat + 1) % nlat
    back = [dev(west, lat), dev(lon, north), dev(west, north)]
    forth = [dev(east, lat), dev(lon, south), dev(east, south)]

    barrier = pltpu.get_barrier_semaphore()
    everyone = [partner, xpeer] + ypeer + zpeer + back + forth
    for d in everyone:
        pl.semaphore_signal(barrier, inc=1, device_id=d, device_id_type=MESH)

    loads = [pltpu.make_async_copy(a, b, ins.at[i]) for i, (a, b) in enumerate(zip(given, held))]
    for load in loads:
        load.start()

    stores = [pltpu.make_async_copy(a, b, outs.at[i]) for i, (a, b) in enumerate(zip(staged, results))]
    sends = []

    def send(src, dst, ssem, rsem, d):
        copy = pltpu.make_async_remote_copy(
            src_ref=src, dst_ref=dst, send_sem=ssem, recv_sem=rsem, device_id=d, device_id_type=MESH
        )
        copy.start()
        sends.append(copy)
        return copy

    lane_row = lax.broadcasted_iota(jnp.int32, (lat_dev, lat_dev * 128), 1) // 128
    pick = (lane_row == lax.broadcasted_iota(jnp.int32, (lat_dev, lat_dev * 128), 0)).astype(F32)

    def spread_mask(ref):
        return tn(ref[...].astype(F32), pick)

    loads[1].wait()
    sea = spread_mask(mask_ref)
    colf[96:112, :] = jnp.zeros((16, FW), F32)

    def halo_pack(h, lanes):
        colsend, colrecv, rowsend, rowrecv, cornrecv = halos[h]
        for r in range(lat_dev):
            colf[6 * r : 6 * r + 6, lanes] = frame[r, 0:HALF_LON, lanes]
        colsend[...] = colf[:, lanes].astype(BF16)
        for r in range(HALF_LAT):
            rowsend[r] = frame[r, 0:lon_dev, lanes].astype(BF16)

    def halo_send(h):
        colsend, colrecv, rowsend, rowrecv, cornrecv = halos[h]
        return [
            send(colsend, colrecv, hs.at[h, 0], hr.at[h, 0], back[0]),
            send(rowsend, rowrecv, hs.at[h, 1], hr.at[h, 1], back[1]),
            send(colsend.at[0:32], cornrecv, hs.at[h, 2], hr.at[h, 2], back[2]),
        ]

    def halo_land(h, lanes, copies):
        colsend, colrecv, rowsend, rowrecv, cornrecv = halos[h]
        copies[1].wait_recv()
        for r in range(HALF_LAT):
            frame[lat_dev + r, 0:lon_dev, lanes] = rowrecv[r].astype(F32)
        copies[2].wait_recv()
        colf[0:32, lanes] = cornrecv[...].astype(F32)
        for r in range(HALF_LAT):
            frame[lat_dev + r, lon_dev : lon_dev + HALF_LON, lanes] = colf[6 * r : 6 * r + 6, lanes]
        copies[0].wait_recv()
        colf[:, lanes] = colrecv[...].astype(F32)
        for r in range(lat_dev):
            frame[r, lon_dev : lon_dev + HALF_LON, lanes] = colf[6 * r : 6 * r + 6, lanes]

    xlanes, dlanes = slice(X0, X0 + C), slice(D0, D0 + C)
    loads[0].wait()
    for r in range(lat_dev):
        frame[r, 0:lon_dev, X0 : X0 + C] = x_ref[r].astype(F32)
        frame[r, 0:lon_dev, M0 : M0 + 128] = sea[:, 128 * r : 128 * r + 128]
    halo_pack(0, xlanes)
    pl.semaphore_wait(barrier, len(everyone))
    mcopies = [send(mask_ref, masks[i], ms.at[i], mr.at[i], back[i]) for i in range(3)]
    xcopies = halo_send(0)
    loads[2].wait()
    for r in range(lat_dev):
        frame[r, 0:lon_dev, D0 : D0 + C] = dy_ref[r].astype(F32)
    halo_pack(1, dlanes)
    dcopies = halo_send(1)

    def pieces(v, n):
        out = []
        for i in range(n):
            part = v.astype(BF16)
            out.append(part)
            if i < n - 1:
                v = v - part.astype(F32)
        return out

    for i in range(3, 11):
        loads[i].wait()
    tb[...] = jnp.zeros_like(tb)
    tb[:, 0:REL] = table[...]
    shifted = []
    for h in range(HEADS):
        line = jnp.broadcast_to(tb[h : h + 1, :], (128, 256))
        shifted.append(pltpu.roll(pltpu.roll(line, 2, 1), 128, 1, stride=1, stride_axis=0)[:, 0:128])
    by_query = sum(nn(v, selft[...]) for v in pieces(jnp.concatenate(shifted, axis=0), 3))
    by_query = jnp.concatenate([by_query[128 * h : 128 * h + 128] for h in range(HEADS)], axis=1)
    whole_bias = sum(nn(self_[0:TP, :], v) for v in pieces(by_query, 3))
    for p in range(PAIRS):
        bias2[p] = whole_bias[:, 256 * p : 256 * p + 256]

    zero_tail = jnp.zeros((RP - ROWS, C), BF16)
    normed[ROWS:RP, :] = zero_tail
    gz[ROWS:RP, :] = zero_tail
    mixed[ROWS:RP, :] = zero_tail
    for p in range(PAIRS):
        dp3[p, ROWS:RP, :] = jnp.zeros((RP - ROWS, 384), BF16)
    for w in range(nwin):
        win[w, T:TP, :] = jnp.zeros((TP - T, FW), F32)

    def cut(w, lanes):
        wr, wc = w // wcols, w % wcols
        c0 = HALF_LON + WIN_LON * wc
        for i in range(WIN_LAT):
            win[w, WIN_LON * i : WIN_LON * i + WIN_LON, lanes] = frame[
                HALF_LAT + WIN_LAT * wr + i, c0 : c0 + WIN_LON, lanes
            ]

    def holds_sea(w):
        return (jnp.max(win[w, :, M0 : M0 + 128]) > 0.5).astype(jnp.int32)

    def ranks(flags, counted):
        total = jnp.int32(0)
        for f, c in zip(flags, counted):
            total = total + f * c
        out, on, off = [], jnp.int32(0), total
        for f, c in zip(flags, counted):
            out.append(jnp.where(f > 0, on, off))
            on = on + f * c
            off = off + (1 - f) * c
        return out

    def slot_window(k, places):
        slot = jnp.int32(0)
        for w, at in places:
            slot = slot + jnp.where(at == k, w, 0)
        idx[k] = slot

    inner = [w for w in range(nwin) if w // wcols < wrows - 1 and w % wcols < wcols - 1]
    outer = [w for w in range(nwin) if w not in inner]
    active = [None] * nwin
    place = [None] * nwin

    at_end = (lat == nlat - 1).astype(F32)
    gain = gain_ref[...]

    def rows_of(k):
        return pl.ds(pl.multiple_of(k * TP, TP), TP)

    def by_three(step):
        def body(i, carry):
            for j in range(3):
                carry = step(3 * i + j, carry)
            return carry

        return body

    def ln_step(k, carry):
        w = idx[k]
        x = win[w, :, X0 : X0 + C]
        mean = jnp.mean(x, axis=1, keepdims=True)
        xc = x - mean
        inv = lax.rsqrt(jnp.mean(xc * xc, axis=1, keepdims=True) + EPS)
        hat = xc * inv
        rows = rows_of(k)
        xhat[rows, :] = hat
        invd[rows, :] = jnp.broadcast_to(inv, (TP, 128))
        normed[rows, :] = (hat * gain).astype(BF16)
        keys = win[w, :, M0 : M0 + 128]
        side_b = lax.broadcasted_iota(jnp.int32, (TP, 128), 0) >= T // 2
        side_a = lax.broadcasted_iota(jnp.int32, (TP, 128), 1) >= T // 2
        apart = jnp.where(side_a != side_b, 1.0, 0.0)
        wrap = at_end * jnp.where(w >= nwin - wcols, 1.0, 0.0)
        madd[k] = (keys * (1.0 - apart * wrap) - 1.0) * 1e9
        return carry

    def dy_step(k, carry):
        w = idx[k]
        m = win[w, :, M0 : M0 + 128]
        gz[rows_of(k), :] = (win[w, :, D0 : D0 + C] * jnp.concatenate([m] * 4, axis=1)).astype(BF16)
        return carry

    lane = lax.broadcasted_iota(jnp.int32, (TP, 128), 1)
    low = lane < 64
    one_lo = jnp.where(low, 1.0, 0.0).astype(BF16)
    one_hi = jnp.where(low, 0.0, 1.0).astype(BF16)
    q_lo = jnp.where(low, 0.125, 0.0).astype(BF16)
    q_hi = jnp.where(low, 0.0, 0.125).astype(BF16)

    def both_heads(v, lo, hi):
        return jnp.concatenate([pad_rows(v * lo, 128), pad_rows(v * hi, 128)], axis=0)

    def own_head(v):
        return jnp.transpose(jnp.concatenate([v[0:64, 0:128], v[64:128, 128:256]], axis=0))[0:TP]

    def attend(i, carry):
        chains = [(3 * i + j, p) for j in range(3) for p in range(PAIRS)]
        scores = []
        for k, p in chains:
            rows = rows_of(k)
            q2 = both_heads(packed[rows, 128 * p : 128 * p + 128], q_lo, q_hi)
            add = madd[k]
            add2 = jnp.concatenate([add, add], axis=1)
            scores.append(nt(packed[rows, C + 128 * p : C + 128 * p + 128], q2) + bias2[p] + add2)
        mixes = []
        for (k, p), s in zip(chains, scores):
            e = jnp.exp(s - jnp.max(s, axis=0, keepdims=True))
            pr = e * (1.0 / jnp.sum(e, axis=0, keepdims=True))
            probs[k * PAIRS + p] = pr
            mixes.append(tn(packed[rows_of(k), 2 * C + 128 * p : 2 * C + 128 * p + 128], pr.astype(BF16)))
        for (k, p), mix in zip(chains, mixes):
            mixed[rows_of(k), 128 * p : 128 * p + 128] = own_head(mix).astype(BF16)
        return carry

    def forward(first, last):
        lax.fori_loop(first // 3, last // 3, by_three(ln_step), 0)
        rows = slice(first * TP, last * TP)
        packed[rows, :] = nn(normed[rows, :], wqkv[...]).astype(BF16)
        lax.fori_loop(first // 3, last // 3, attend, 0)

    for w in inner:
        cut(w, slice(0, FW))
        active[w] = holds_sea(w)
    inner_rank = ranks([active[w] for w in inner], [1] * len(inner))
    for k in range(EARLY):
        slot_window(k, list(zip(inner, inner_rank)))
    forward(0, EARLY)

    mlanes = slice(M0, M0 + 128)
    for copy in mcopies:
        copy.wait_recv()
    sea = spread_mask(masks[0])
    for r in range(lat_dev):
        frame[r, lon_dev : lon_dev + HALF_LON, mlanes] = sea[0:HALF_LON, 128 * r : 128 * r + 128]
    sea = spread_mask(masks[1])
    for r in range(HALF_LAT):
        frame[lat_dev + r, 0:lon_dev, mlanes] = sea[:, 128 * r : 128 * r + 128]
    sea = spread_mask(masks[2])
    for r in range(HALF_LAT):
        frame[lat_dev + r, lon_dev : lon_dev + HALF_LON, mlanes] = sea[0:HALF_LON, 128 * r : 128 * r + 128]
    halo_land(0, xlanes, xcopies)
    for w in outer:
        cut(w, slice(X0, M0 + 128))
        active[w] = holds_sea(w)
    rest = [jnp.int32(1)] * nwin
    for w, at in zip(inner, inner_rank):
        rest[w] = (at >= EARLY).astype(jnp.int32)
    late_rank = ranks(active, rest)
    for w in range(nwin):
        place[w] = late_rank[w] + EARLY
    for w, at in zip(inner, inner_rank):
        place[w] = jnp.where(at < EARLY, at, place[w])
    for k in range(EARLY, SLOTS):
        slot_window(k, list(enumerate(place)))
    forward(EARLY, SLOTS)

    halo_land(1, dlanes, dcopies)
    for w in outer:
        cut(w, dlanes)
    lax.fori_loop(0, SLOTS // 3, by_three(dy_step), 0)
    gm[...] = nt(gz[0:ROWS, :], wproj[...]).astype(BF16)
    ntp[...] = nt(perm[...], normed[...]).astype(BF16)

    def chunk_start(c, lhs, rhs):
        asend, arecv, own = chunks[c][0:3]
        right = rhs[...]
        other = pl.multiple_of((1 - core) * half, half)
        mine = pl.multiple_of(core * half, half)
        asend[...] = nn(lhs[pl.ds(other, half), :], right).astype(BF16)
        copy = send(asend, arecv, as_.at[c], ar.at[c], partner)
        own[...] = nn(lhs[pl.ds(mine, half), :], right)
        return [copy]

    def chunk_y(c, copies):
        asend, arecv, own, ysend, yrecv = chunks[c][0:5]
        copies[0].wait_recv()
        s = own[...] + arecv[...].astype(F32)
        own[...] = s
        ysend[...] = s.astype(BF16)
        out = []
        for d in range(1, ny):
            start = pl.multiple_of(((y + d) % ny) * ysz, ysz)
            out.append(
                send(ysend.at[pl.ds(start, ysz)], yrecv.at[d - 1], ys.at[c, d - 1], yr.at[c, d - 1], ypeer[d - 1])
            )
        return out

    def chunk_x(c, copies):
        own, ysend, yrecv, xsend, xrecv, xown = chunks[c][2:8]
        s = own[pl.ds(pl.multiple_of(y * ysz, ysz), ysz), :]
        for d in range(1, ny):
            copies[d - 1].wait_recv()
            s = s + yrecv[d - 1].astype(F32)
        top, low_half = s[0 : ysz // 2], s[ysz // 2 : ysz]
        first = xh == 0
        xsend[...] = jnp.where(first, low_half, top).astype(BF16)
        xown[...] = jnp.where(first, top, low_half)
        return [send(xsend, xrecv, xs.at[c], xr.at[c], xpeer)]

    def chunk_z(c, copies):
        xsend, xrecv, xown, zown, zsend, zrecv = chunks[c][5:11]
        copies[0].wait_recv()
        s = xown[...] + xrecv[...].astype(F32)
        blocks = cols[c] // 128
        for j in range(nz):
            part = s[share * j : share * j + share]
            piece = jnp.concatenate([part[:, 128 * min(q, blocks - 1) :][:, 0:128] for q in range(4)], axis=0)
            zown[j] = piece
            zsend[j] = piece.astype(BF16)
        return [
            send(zsend.at[(z + d) % nz], zrecv.at[d - 1], zs.at[c, d - 1], zr.at[c, d - 1], zpeer[d - 1])
            for d in range(1, nz)
        ]

    def chunk_end(c, copies):
        zown, zsend, zrecv = chunks[c][8:11]
        s = zown[z]
        for i, copy in enumerate(copies):
            copy.wait_recv()
            s = s + zrecv[i].astype(F32)
        for q in range(cols[c] // 128):
            block = s[share * q : share * q + share]
            if c == 0:
                gproj[:, 128 * q : 128 * q + 128] = block
            else:
                gqkv[:, C * q + 128 * (c - 1) : C * q + 128 * c] = block

    def window_back(o, lane0):
        def place_window(w):
            wr, wc = w // wcols, w % wcols
            slot = jnp.minimum(place[w], SLOTS - 1)
            for i in range(WIN_LAT):
                c0 = HALF_LON + WIN_LON * wc
                at = slice(WIN_LON * i, WIN_LON * i + WIN_LON)
                of[o, HALF_LAT + WIN_LAT * wr + i, c0 : c0 + WIN_LON, :] = jnp.where(
                    place[w] < SLOTS, res[slot, at, :], win[w, at, lane0 : lane0 + C]
                )

        for w in range(wcols - 1, nwin, wcols):
            place_window(w)
        colf[88:96, 0:C] = jnp.zeros((8, C), F32)
        for r in range(HALF_LAT, lat_dev):
            at = 6 * (r - HALF_LAT)
            colf[at : at + 6, 0:C] = of[o, r, lon_dev : lon_dev + HALF_LON, :]
        ocs[o] = colf[0:96, 0:C].astype(BF16)
        for r in range(HALF_LAT):
            colf[6 * r : 6 * r + 6, 0:C] = of[o, lat_dev + r, lon_dev : lon_dev + HALF_LON, :]
        colf[8:16, C : C + 128] = jnp.zeros((8, 128), F32)
        for j in range(8):
            colf[j : j + 1, C : C + 128] = colf[16 + j // 4 : 17 + j // 4, 128 * (j % 4) : 128 * (j % 4) + 128]
        occs[o] = colf[0:16, 0 : C + 128].astype(BF16)
        copies = [
            send(ocs.at[o], ocr.at[o], os_.at[o, 0], or_.at[o, 0], forth[0]),
            send(occs.at[o], occ.at[o], os_.at[o, 2], or_.at[o, 2], forth[2]),
        ]
        for w in range(nwin - wcols, nwin - 1):
            place_window(w)
        for r in range(HALF_LAT):
            ors[o, r] = of[o, lat_dev + r, 0:lon_dev, :].astype(BF16)
        copies.insert(1, send(ors.at[o], orr.at[o], os_.at[o, 1], or_.at[o, 1], forth[1]))
        for w in range(nwin - wcols):
            if w % wcols < wcols - 1:
                place_window(w)
        return copies

    def finish(o, copies, out):
        copies[1].wait_recv()
        for r in range(HALF_LAT):
            of[o, r, 0:lon_dev, :] = orr[o, r].astype(F32)
        copies[0].wait_recv()
        colf[0:96, 0:C] = ocr[o].astype(F32)
        for r in range(HALF_LAT, lat_dev):
            at = 6 * (r - HALF_LAT)
            of[o, r, 0:HALF_LON, :] = colf[at : at + 6, 0:C]
        copies[2].wait_recv()
        colf[0:16, 0 : C + 128] = occ[o].astype(F32)
        for j in range(8):
            colf[16 + j // 4 : 17 + j // 4, 128 * (j % 4) : 128 * (j % 4) + 128] = colf[j : j + 1, C : C + 128]
        for r in range(HALF_LAT):
            of[o, r, 0:HALF_LON, :] = colf[6 * r : 6 * r + 6, 0:C]
        for r in range(lat_dev):
            out[r] = of[o, r, 0:lon_dev, :].astype(BF16)

    mtp[...] = nt(perm[...], mixed[...]).astype(BF16)
    st = {}
    st[0] = chunk_start(0, mtp, gz)

    gnacc[...] = nn(mixed[0:ROWS, :], wproj[...])

    def updated_step(k, carry):
        w = idx[k]
        m = win[w, :, M0 : M0 + 128]
        res[k] = win[w, :, X0 : X0 + C] + jnp.concatenate([m] * 4, axis=1) * gnacc[rows_of(k), :]
        return carry

    lax.fori_loop(0, SLOTS // 3, by_three(updated_step), 0)
    out_copies = [window_back(0, X0), None]

    def backward(p):
        ks = list(range(SLOTS))
        d2s, dps = [], []
        for k in ks:
            rows = slice(TP * k, TP * k + TP)
            d2s.append(both_heads(gm[rows, 128 * p : 128 * p + 128], one_lo, one_hi))
            dps.append(nt(packed[rows, 2 * C + 128 * p : 2 * C + 128 * p + 128], d2s[-1]))
        dss, dvs = [], []
        for k in ks:
            pr = probs[k * PAIRS + p]
            t = pr * dps[k]
            dss.append(t - pr * jnp.sum(t, axis=0, keepdims=True))
            dvs.append(nn(pr.astype(BF16), d2s[k]))
        bacc[p] = functools.reduce(lambda a, b: a + b, dss)
        dqs = []
        for k in ks:
            rows = slice(TP * k, TP * k + TP)
            ds = dss[k].astype(BF16)
            q2 = both_heads(packed[rows, 128 * p : 128 * p + 128], q_lo, q_hi)
            dqs.append(tn(packed[rows, C + 128 * p : C + 128 * p + 128], ds))
            dp3[p, rows, 128:256] = nn(ds, q2).astype(BF16)
            dp3[p, rows, 256:384] = dvs[k].astype(BF16)
        for k in ks:
            dp3[p, TP * k : TP * k + TP, 0:128] = (own_head(dqs[k]) * 0.125).astype(BF16)

    def weight_pair(p):
        return jnp.concatenate([wqkv[:, C * part + 128 * p : C * part + 128 * p + 128] for part in range(3)], axis=1)

    def grad_normed(p):
        g = nt(dp3[p, 0:ROWS, :], weight_pair(p))
        gnacc[...] = g if p == 0 else gnacc[...] + g

    st[0] = chunk_y(0, st[0])
    for p in range(PAIRS):
        backward(p)
        st[p] = chunk_x(p, st[p])
        st[p + 1] = chunk_start(p + 1, ntp, dp3.at[p])
        grad_normed(p)
        st[p] = chunk_z(p, st[p])
        st[p + 1] = chunk_y(p + 1, st[p + 1])

    def norm_back(k, total):
        w = idx[k]
        rows = rows_of(k)
        gn = gnacc[rows, :]
        hat = xhat[rows, :]
        g = gn * gain
        prod = g * hat
        mid = g - jnp.mean(g, axis=1, keepdims=True) - hat * jnp.mean(prod, axis=1, keepdims=True)
        inv = jnp.concatenate([invd[rows, :]] * 4, axis=1)
        res[k] = win[w, :, D0 : D0 + C] + inv * mid
        return total + jnp.sum(gn * hat, axis=0, keepdims=True)

    gsum = lax.fori_loop(0, SLOTS // 3, by_three(norm_back), jnp.zeros((1, C), F32))
    out_copies[1] = window_back(1, D0)

    stacked = jnp.concatenate([bacc[h // 2, :, 128 * (h % 2) : 128 * (h % 2) + 128] for h in range(HEADS)], axis=0)
    by_place = sum(nn(v, self_[...]) for v in pieces(stacked, 2))
    by_place = jnp.concatenate([by_place[TP * h : TP * h + TP] for h in range(HEADS)], axis=1)
    spread = sum(nn(selrt[:, 0:TP], v) for v in pieces(by_place, 2))
    for h in range(HEADS):
        wide = jnp.concatenate([spread[:, 128 * h : 128 * h + 128], jnp.zeros((128, 128), F32)], axis=1)
        sums[0][h : h + 1, 0:256] = jnp.sum(pltpu.roll(wide, 0, 1, stride=1, stride_axis=0), axis=0, keepdims=True)
    sm, smc, smy, sma, smx, smz = sums
    sm[4:8, 256:384] = jnp.zeros((4, 128), F32)
    for j in range(4):
        sm[j : j + 1, 256:384] = gsum[:, 128 * j : 128 * j + 128]
    copy = send(sm, smc, ss.at[0], sr.at[0], partner)
    st[4] = chunk_x(4, st[4])
    copy.wait_recv()
    smy[y] = sm[...] + smc[...]
    copies = [send(smy.at[y], smy.at[y], ss.at[d], sr.at[d], ypeer[d - 1]) for d in range(1, ny)]
    finish(0, out_copies[0], upd)
    stores[0].start()
    st[4] = chunk_z(4, st[4])
    for copy in copies:
        copy.wait_recv()
    acc = smy[0]
    for j in range(1, ny):
        acc = acc + smy[j]
    sma[...] = acc
    copy = send(sma, smx, ss.at[ny], sr.at[ny], xpeer)
    for c in range(nchunk - 1):
        chunk_end(c, st[c])
    copy.wait_recv()
    smz[z] = sma[...] + smx[...]
    copies = [send(smz.at[z], smz.at[z], ss.at[ny + d], sr.at[ny + d], zpeer[d - 1]) for d in range(1, nz)]
    finish(1, out_copies[1], gin)
    stores[1].start()
    chunk_end(nchunk - 1, st[nchunk - 1])
    for copy in copies:
        copy.wait_recv()
    acc = smz[0]
    for j in range(1, nz):
        acc = acc + smz[j]
    bias_out[...] = acc[:, 0:REL]
    for j in range(4):
        gain_out[:, 128 * j : 128 * j + 128] = acc[j : j + 1, 256:384]
    for store in stores[2:]:
        store.start()
    for copy in sends:
        copy.wait_send()
    for store in stores:
        store.wait()


def hand_over(*refs):
    arrived, left = refs[18:20]
    steps = []
    for i in range(6):
        rows = refs[i].shape[0]
        size = 3 if i < 2 else rows
        steps += [(i, pl.ds(start, size)) for start in range(0, rows, size)]
    fetches = [
        pltpu.make_async_copy(refs[i].at[at], refs[12 + i].at[at], arrived.at[n]) for n, (i, at) in enumerate(steps)
    ]
    stores = [
        pltpu.make_async_copy(refs[12 + i].at[at], refs[6 + i].at[at], left.at[n]) for n, (i, at) in enumerate(steps)
    ]
    for fetch in fetches:
        fetch.start()
    for fetch, store in zip(fetches, stores):
        fetch.wait()
        store.start()
    for store in stores:
        store.wait()


def constants(ny, nx, nz):
    share = C // (ny * nx * nz * 2)
    perm = np.zeros((C, C), np.float32)
    for core in range(2):
        for y in range(ny):
            for xh in range(nx):
                for z in range(nz):
                    to = (((core * ny + y) * nx + xh) * nz + z) * share
                    start = (((y * nx + xh) * nz + z) * 2 + core) * share
                    perm[to + np.arange(share), start + np.arange(share)] = 1
    a = np.arange(T)
    pa = (a // WIN_LON) * (2 * WIN_LON - 1) + a % WIN_LON
    selrt = np.zeros((128, 128), np.float32)
    selrt[126 - pa, a] = 1
    self_ = np.zeros((128, 128), np.float32)
    self_[a, pa] = 1
    return perm, self_, self_.T, selrt


def solution(mesh):
    nlon, nlat = mesh.shape["lon"], mesh.shape["lat"]
    nx, nz = 2, nlat // 2
    ny = nlon // nx
    nxz = nx * nz
    half = C // 2
    ysz = half // ny
    share = ysz // nxz
    cols = [C] + [384] * PAIRS
    lat_dev, lon_dev = 18, 48
    nwin = 12
    vm = pltpu.VMEM
    dma = lambda *s: pltpu.SemaphoreType.DMA(s)
    perm, self_, selft, selrt = (jnp.asarray(v, BF16) for v in constants(ny, nx, nz))

    def on_device(fields, grad_out, layernorm_gain, qkv_weight, proj_weight, bias_table, sea_mask):
        shapes = (
            jax.ShapeDtypeStruct((lat_dev, lon_dev, C), BF16),
            jax.ShapeDtypeStruct((lat_dev, lon_dev, C), BF16),
            jax.ShapeDtypeStruct((1, C), F32),
            jax.ShapeDtypeStruct((HEADS, REL), F32),
            jax.ShapeDtypeStruct((share, 3 * C), F32),
            jax.ShapeDtypeStruct((share, C), F32),
        )
        scratch = [
            vm((lat_dev, lon_dev, C), BF16),
            vm((lat_dev, lon_dev), jnp.int32),
            vm((lat_dev, lon_dev, C), BF16),
            vm((HEADS, REL), F32),
            vm((128, 128), BF16),
            vm((128, 128), BF16),
            vm((128, 128), BF16),
            vm((1, C), F32),
            vm((C, 3 * C), BF16),
            vm((C, C), BF16),
            vm((C, C), BF16),
        ]
        scratch += [vm(v.shape, v.dtype) for v in shapes]
        scratch += [
            vm((lat_dev + 3, 56, FW), F32),
            vm((nwin, TP, FW), F32),
            vm((112, FW), F32),
        ]
        for wide in (C, C):
            scratch += [
                vm((112, wide), BF16),
                vm((112, wide), BF16),
                vm((3, lon_dev, wide), BF16),
                vm((3, lon_dev, wide), BF16),
                vm((32, wide), BF16),
            ]
        scratch += [vm((lat_dev, lon_dev), jnp.int32)] * 3
        scratch += [
            pltpu.SMEM((16,), jnp.int32),
            vm((HEADS, 256), F32),
            vm((PAIRS, TP, 256), F32),
            vm((SLOTS, TP, 128), F32),
            vm((ROWS, C), F32),
            vm((ROWS, 128), F32),
            vm((RP, C), BF16),
            vm((RP, C), BF16),
            vm((ROWS, C), BF16),
            vm((ROWS, 3 * C), BF16),
            vm((RP, C), BF16),
            vm((C, RP), BF16),
            vm((C, RP), BF16),
            vm((SLOTS * PAIRS, TP, 256), F32),
            vm((PAIRS, RP, 384), BF16),
            vm((ROWS, C), F32),
            vm((PAIRS, TP, 256), F32),
            vm((SLOTS, TP, C), F32),
            vm((2, lat_dev + 3, 56, C), F32),
            vm((2, 96, C), BF16),
            vm((2, 3, lon_dev, C), BF16),
            vm((2, 16, C + 128), BF16),
            vm((2, 96, C), BF16),
            vm((2, 3, lon_dev, C), BF16),
            vm((2, 16, C + 128), BF16),
        ]
        for n in cols:
            scratch += [
                vm((half, n), BF16),
                vm((half, n), BF16),
                vm((half, n), F32),
                vm((half, n), BF16),
                vm((ny - 1, ysz, n), BF16),
                vm((ysz // 2, n), BF16),
                vm((ysz // 2, n), BF16),
                vm((ysz // 2, n), F32),
                vm((nz, 4 * share, 128), F32),
                vm((nz, 4 * share, 128), BF16),
                vm((nz - 1, 4 * share, 128), BF16),
            ]
        sm = (8, 384)
        scratch += [vm(sm, F32), vm(sm, F32), vm((ny,) + sm, F32), vm(sm, F32), vm(sm, F32), vm((nz,) + sm, F32)]
        nc = len(cols)
        small = ny + nz
        scratch += [
            dma(2, 3), dma(2, 3), dma(3), dma(3), dma(2, 3), dma(2, 3), dma(nc), dma(nc), dma(nc, ny - 1),
            dma(nc, ny - 1), dma(nc), dma(nc), dma(nc, nz - 1), dma(nc, nz - 1), dma(small), dma(small), dma(11), dma(6),
        ]
        anywhere = pl.BlockSpec(memory_space=pl.ANY)
        outs = pl.pallas_call(
            functools.partial(kernel, (ny, nx, nz), cols),
            out_shape=shapes,
            in_specs=[anywhere] * 11,
            out_specs=(anywhere,) * 6,
            scratch_shapes=scratch,
            compiler_params=pltpu.CompilerParams(
                collective_id=0, has_side_effects=True, vmem_limit_bytes=60 * 1024 * 1024
            ),
        )(
            fields, sea_mask, grad_out, bias_table, self_, selft, selrt,
            layernorm_gain.reshape(1, C), qkv_weight, proj_weight, perm,
        )
        outs = pl.pallas_call(
            hand_over,
            out_shape=shapes,
            in_specs=[anywhere] * 6,
            out_specs=(anywhere,) * 6,
            scratch_shapes=[vm(v.shape, v.dtype) for v in shapes] + [dma(16), dma(16)],
            compiler_params=pltpu.CompilerParams(vmem_limit_bytes=60 * 1024 * 1024),
        )(*outs)
        updated, grad_in, grad_gain, grad_bias, grad_qkv, grad_proj = outs
        return (updated, grad_in, grad_gain.reshape(C), grad_bias, grad_qkv, grad_proj)

    grid = P(("batch", "lat"), "lon", None)
    return jax.shard_map(
        on_device,
        mesh=mesh,
        in_specs=(grid, grid, P(), P(), P(), P(), P(("batch", "lat"), "lon")),
        out_specs=(
            grid,
            grid,
            P("batch"),
            P("batch", None),
            P(("batch", "lon", "lat"), None),
            P(("batch", "lon", "lat"), None),
        ),
        check_vma=False,
    )
```

```python
import functools

import jax
import jax.numpy as jnp
import numpy as np
from jax import lax
from jax.experimental import pallas as pl
from jax.experimental.pallas import tpu as pltpu
from jax.sharding import PartitionSpec as P

MESH = pl.DeviceIdType.MESH
F32 = jnp.float32
BF16 = jnp.bfloat16
C = 512
HEADS = 8
PAIRS = 4
WIN_LAT = 6
WIN_LON = 12
HALF_LAT = 3
HALF_LON = 6
T = 72
TP = 80
SLOTS = 9
ROWS = SLOTS * TP
RP = 768
REL = 253
X0, M0, D0, FW = 0, 512, 640, 1152
GROUPS = ((0, 1, 2), (3, 4))
EARLY = 3
EPS = 1e-5


def nn(a, b, **kw):
    return lax.dot_general(a, b, (((1,), (0,)), ((), ())), preferred_element_type=F32, **kw)


def nt(a, b, **kw):
    return lax.dot_general(a, b, (((1,), (1,)), ((), ())), preferred_element_type=F32, **kw)


def tn(a, b, **kw):
    return lax.dot_general(a, b, (((0,), (0,)), ((), ())), preferred_element_type=F32, **kw)


def pad_rows(v, rows):
    return jnp.concatenate([v, jnp.zeros((rows - v.shape[0], v.shape[1]), v.dtype)], axis=0)


def kernel(dims, cols, *refs):
    ny, nx, nz = dims
    nlon, nlat = ny * nx, 2 * nz
    nxz = nx * nz
    lat_dev, lon_dev = 18, 48
    wrows, wcols = lat_dev // WIN_LAT, lon_dev // WIN_LON
    nwin = wrows * wcols
    half = C // 2
    ysz = half // ny
    share = ysz // nxz
    nchunk = len(cols)

    it = iter(refs)
    take = lambda n=None: next(it) if n is None else [next(it) for _ in range(n)]
    given = take(11)
    results = take(6)
    held = take(11)
    x_ref, mask_ref, dy_ref, table, self_, selft, selrt, gain_ref, wqkv, wproj, perm = held
    staged = take(6)
    upd, gin, gain_out, bias_out, gqkv, gproj = staged
    frame, win, colf = take(3)
    halos = [take(5) for _ in range(2)]
    masks = take(3)
    idx = take()
    tb, bias2, madd, xhat, invd, normed, gz, gm, packed, mixed, ntp, mtp, probs, dp3, gnacc, bacc, wperm, gacc = take(18)
    res, of = take(2)
    ocs, ors, occs, ocr, orr, occ = take(6)
    chunks = [take(8) for _ in range(nchunk)]
    groups = [take(3) for _ in range(len(GROUPS))]
    sums = take(6)
    hs, hr, ms, mr, os_, or_, as_, ar, ys, yr, xs, xr, zs, zr, ss, sr = take(16)
    ins, outs = take(2)

    lon = lax.axis_index("lon")
    lat = lax.axis_index("lat")
    y, xh = lon // nx, lon % nx
    z, core = lat // 2, lat % 2

    def dev(a, b):
        return {"lon": a, "lat": b}

    partner = dev(lon, z * 2 + (1 - core))
    ypeer = [dev(((y + d) % ny) * nx + xh, lat) for d in range(1, ny)]
    xpeer = dev(y * nx + (1 - xh), lat)
    zpeer = [dev(lon, ((z + d) % nz) * 2 + core) for d in range(1, nz)]
    west, east = (lon + nlon - 1) % nlon, (lon + 1) % nlon
    north, south = (lat + nlat - 1) % nlat, (lat + 1) % nlat
    back = [dev(west, lat), dev(lon, north), dev(west, north)]
    forth = [dev(east, lat), dev(lon, south), dev(east, south)]

    barrier = pltpu.get_barrier_semaphore()
    everyone = [partner, xpeer] + ypeer + zpeer + back + forth
    for d in everyone:
        pl.semaphore_signal(barrier, inc=1, device_id=d, device_id_type=MESH)

    loads = [pltpu.make_async_copy(a, b, ins.at[i]) for i, (a, b) in enumerate(zip(given, held))]
    for load in loads:
        load.start()

    stores = [pltpu.make_async_copy(a, b, outs.at[i]) for i, (a, b) in enumerate(zip(staged, results))]
    sends = []

    def send(src, dst, ssem, rsem, d):
        copy = pltpu.make_async_remote_copy(
            src_ref=src, dst_ref=dst, send_sem=ssem, recv_sem=rsem, device_id=d, device_id_type=MESH
        )
        copy.start()
        sends.append(copy)
        return copy

    lane_row = lax.broadcasted_iota(jnp.int32, (lat_dev, lat_dev * 128), 1) // 128
    pick = (lane_row == lax.broadcasted_iota(jnp.int32, (lat_dev, lat_dev * 128), 0)).astype(F32)

    def spread_mask(ref):
        return tn(ref[...].astype(F32), pick)

    loads[1].wait()
    sea = spread_mask(mask_ref)
    colf[96:112, :] = jnp.zeros((16, FW), F32)

    def halo_pack(h, lanes):
        colsend, colrecv, rowsend, rowrecv, cornrecv = halos[h]
        for r in range(lat_dev):
            colf[6 * r : 6 * r + 6, lanes] = frame[r, 0:HALF_LON, lanes]
        colsend[...] = colf[:, lanes].astype(BF16)
        for r in range(HALF_LAT):
            rowsend[r] = frame[r, 0:lon_dev, lanes].astype(BF16)

    def halo_send(h):
        colsend, colrecv, rowsend, rowrecv, cornrecv = halos[h]
        return [
            send(colsend, colrecv, hs.at[h, 0], hr.at[h, 0], back[0]),
            send(rowsend, rowrecv, hs.at[h, 1], hr.at[h, 1], back[1]),
            send(colsend.at[0:32], cornrecv, hs.at[h, 2], hr.at[h, 2], back[2]),
        ]

    def halo_land(h, lanes, copies):
        colsend, colrecv, rowsend, rowrecv, cornrecv = halos[h]
        copies[1].wait_recv()
        for r in range(HALF_LAT):
            frame[lat_dev + r, 0:lon_dev, lanes] = rowrecv[r].astype(F32)
        copies[2].wait_recv()
        colf[0:32, lanes] = cornrecv[...].astype(F32)
        for r in range(HALF_LAT):
            frame[lat_dev + r, lon_dev : lon_dev + HALF_LON, lanes] = colf[6 * r : 6 * r + 6, lanes]
        copies[0].wait_recv()
        colf[:, lanes] = colrecv[...].astype(F32)
        for r in range(lat_dev):
            frame[r, lon_dev : lon_dev + HALF_LON, lanes] = colf[6 * r : 6 * r + 6, lanes]

    xlanes, dlanes = slice(X0, X0 + C), slice(D0, D0 + C)
    loads[0].wait()
    for r in range(lat_dev):
        frame[r, 0:lon_dev, X0 : X0 + C] = x_ref[r].astype(F32)
        frame[r, 0:lon_dev, M0 : M0 + 128] = sea[:, 128 * r : 128 * r + 128]
    halo_pack(0, xlanes)
    pl.semaphore_wait(barrier, len(everyone))
    mcopies = [send(mask_ref, masks[i], ms.at[i], mr.at[i], back[i]) for i in range(3)]
    xcopies = halo_send(0)
    loads[2].wait()
    for r in range(lat_dev):
        frame[r, 0:lon_dev, D0 : D0 + C] = dy_ref[r].astype(F32)
    halo_pack(1, dlanes)
    dcopies = halo_send(1)

    def pieces(v, n):
        out = []
        for i in range(n):
            part = v.astype(BF16)
            out.append(part)
            if i < n - 1:
                v = v - part.astype(F32)
        return out

    for i in range(3, 11):
        loads[i].wait()
    tb[...] = jnp.zeros_like(tb)
    tb[:, 0:REL] = table[...]
    shifted = []
    for h in range(HEADS):
        line = jnp.broadcast_to(tb[h : h + 1, :], (128, 256))
        shifted.append(pltpu.roll(pltpu.roll(line, 2, 1), 128, 1, stride=1, stride_axis=0)[:, 0:128])
    by_query = sum(nn(v, selft[...]) for v in pieces(jnp.concatenate(shifted, axis=0), 3))
    by_query = jnp.concatenate([by_query[128 * h : 128 * h + 128] for h in range(HEADS)], axis=1)
    whole_bias = sum(nn(self_[0:TP, :], v) for v in pieces(by_query, 3))
    for p in range(PAIRS):
        bias2[p] = whole_bias[:, 256 * p : 256 * p + 256]

    wperm[...] = nn(perm[...], wqkv[...]).astype(BF16)
    gacc[...] = jnp.zeros_like(gacc)
    for g in range(len(GROUPS)):
        groups[g][0][...] = jnp.zeros_like(groups[g][0])
    zero_tail = jnp.zeros((RP - ROWS, C), BF16)
    normed[ROWS:RP, :] = zero_tail
    gz[ROWS:RP, :] = zero_tail
    mixed[ROWS:RP, :] = zero_tail
    for p in range(PAIRS):
        dp3[p, ROWS:RP, :] = jnp.zeros((RP - ROWS, 384), BF16)
    for w in range(nwin):
        win[w, T:TP, :] = jnp.zeros((TP - T, FW), F32)

    def cut(w, lanes):
        wr, wc = w // wcols, w % wcols
        c0 = HALF_LON + WIN_LON * wc
        for i in range(WIN_LAT):
            win[w, WIN_LON * i : WIN_LON * i + WIN_LON, lanes] = frame[
                HALF_LAT + WIN_LAT * wr + i, c0 : c0 + WIN_LON, lanes
            ]

    def holds_sea(w):
        return (jnp.max(win[w, :, M0 : M0 + 128]) > 0.5).astype(jnp.int32)

    def ranks(flags, counted):
        total = jnp.int32(0)
        for f, c in zip(flags, counted):
            total = total + f * c
        out, on, off = [], jnp.int32(0), total
        for f, c in zip(flags, counted):
            out.append(jnp.where(f > 0, on, off))
            on = on + f * c
            off = off + (1 - f) * c
        return out

    def slot_window(k, places):
        slot = jnp.int32(0)
        for w, at in places:
            slot = slot + jnp.where(at == k, w, 0)
        idx[k] = slot

    inner = [w for w in range(nwin) if w // wcols < wrows - 1 and w % wcols < wcols - 1]
    outer = [w for w in range(nwin) if w not in inner]
    active = [None] * nwin
    place = [None] * nwin

    at_end = (lat == nlat - 1).astype(F32)
    gain = gain_ref[...]

    def rows_of(k):
        return pl.ds(pl.multiple_of(k * TP, TP), TP)

    def by_three(step):
        def body(i, carry):
            for j in range(3):
                carry = step(3 * i + j, carry)
            return carry

        return body

    def ln_step(k, carry):
        w = idx[k]
        x = win[w, :, X0 : X0 + C]
        mean = jnp.mean(x, axis=1, keepdims=True)
        xc = x - mean
        inv = lax.rsqrt(jnp.mean(xc * xc, axis=1, keepdims=True) + EPS)
        hat = xc * inv
        rows = rows_of(k)
        xhat[rows, :] = hat
        invd[rows, :] = jnp.broadcast_to(inv, (TP, 128))
        normed[rows, :] = (hat * gain).astype(BF16)
        keys = win[w, :, M0 : M0 + 128]
        side_b = lax.broadcasted_iota(jnp.int32, (TP, 128), 0) >= T // 2
        side_a = lax.broadcasted_iota(jnp.int32, (TP, 128), 1) >= T // 2
        apart = jnp.where(side_a != side_b, 1.0, 0.0)
        wrap = at_end * jnp.where(w >= nwin - wcols, 1.0, 0.0)
        madd[k] = (keys * (1.0 - apart * wrap) - 1.0) * 1e9
        return carry

    def dy_step(k, carry):
        w = idx[k]
        m = win[w, :, M0 : M0 + 128]
        gz[rows_of(k), :] = (win[w, :, D0 : D0 + C] * jnp.concatenate([m] * 4, axis=1)).astype(BF16)
        return carry

    lane = lax.broadcasted_iota(jnp.int32, (TP, 128), 1)
    low = lane < 64
    one_lo = jnp.where(low, 1.0, 0.0).astype(BF16)
    one_hi = jnp.where(low, 0.0, 1.0).astype(BF16)
    q_lo = jnp.where(low, 0.125, 0.0).astype(BF16)
    q_hi = jnp.where(low, 0.0, 0.125).astype(BF16)

    def both_heads(v, lo, hi):
        return jnp.concatenate([pad_rows(v * lo, 128), pad_rows(v * hi, 128)], axis=0)

    def own_head(v):
        return jnp.transpose(jnp.concatenate([v[0:64, 0:128], v[64:128, 128:256]], axis=0))[0:TP]

    def attend(i, carry):
        chains = [(3 * i + j, p) for j in range(3) for p in range(PAIRS)]
        scores = []
        for k, p in chains:
            rows = rows_of(k)
            q2 = both_heads(packed[rows, 128 * p : 128 * p + 128], q_lo, q_hi)
            add = madd[k]
            add2 = jnp.concatenate([add, add], axis=1)
            scores.append(nt(packed[rows, C + 128 * p : C + 128 * p + 128], q2) + bias2[p] + add2)
        mixes = []
        for (k, p), s in zip(chains, scores):
            e = jnp.exp(s - jnp.max(s, axis=0, keepdims=True))
            pr = e * (1.0 / jnp.sum(e, axis=0, keepdims=True))
            probs[k * PAIRS + p] = pr
            mixes.append(tn(packed[rows_of(k), 2 * C + 128 * p : 2 * C + 128 * p + 128], pr.astype(BF16)))
        for (k, p), mix in zip(chains, mixes):
            mixed[rows_of(k), 128 * p : 128 * p + 128] = own_head(mix).astype(BF16)
        return carry

    def forward(first, last):
        lax.fori_loop(first // 3, last // 3, by_three(ln_step), 0)
        rows = slice(first * TP, last * TP)
        packed[rows, :] = nn(normed[rows, :], wqkv[...]).astype(BF16)
        lax.fori_loop(first // 3, last // 3, attend, 0)

    for w in inner:
        cut(w, slice(0, FW))
        active[w] = holds_sea(w)
    inner_rank = ranks([active[w] for w in inner], [1] * len(inner))
    for k in range(EARLY):
        slot_window(k, list(zip(inner, inner_rank)))
    forward(0, EARLY)

    mlanes = slice(M0, M0 + 128)
    for copy in mcopies:
        copy.wait_recv()
    sea = spread_mask(masks[0])
    for r in range(lat_dev):
        frame[r, lon_dev : lon_dev + HALF_LON, mlanes] = sea[0:HALF_LON, 128 * r : 128 * r + 128]
    sea = spread_mask(masks[1])
    for r in range(HALF_LAT):
        frame[lat_dev + r, 0:lon_dev, mlanes] = sea[:, 128 * r : 128 * r + 128]
    sea = spread_mask(masks[2])
    for r in range(HALF_LAT):
        frame[lat_dev + r, lon_dev : lon_dev + HALF_LON, mlanes] = sea[0:HALF_LON, 128 * r : 128 * r + 128]
    halo_land(0, xlanes, xcopies)
    for w in outer:
        cut(w, slice(X0, M0 + 128))
        active[w] = holds_sea(w)
    rest = [jnp.int32(1)] * nwin
    for w, at in zip(inner, inner_rank):
        rest[w] = (at >= EARLY).astype(jnp.int32)
    late_rank = ranks(active, rest)
    for w in range(nwin):
        place[w] = late_rank[w] + EARLY
    for w, at in zip(inner, inner_rank):
        place[w] = jnp.where(at < EARLY, at, place[w])
    for k in range(EARLY, SLOTS):
        slot_window(k, list(enumerate(place)))
    forward(EARLY, SLOTS)

    def window_back(o, lane0):
        def place_window(w):
            wr, wc = w // wcols, w % wcols
            slot = jnp.minimum(place[w], SLOTS - 1)
            for i in range(WIN_LAT):
                c0 = HALF_LON + WIN_LON * wc
                at = slice(WIN_LON * i, WIN_LON * i + WIN_LON)
                of[o, HALF_LAT + WIN_LAT * wr + i, c0 : c0 + WIN_LON, :] = jnp.where(
                    place[w] < SLOTS, res[slot, at, :], win[w, at, lane0 : lane0 + C]
                )

        for w in range(wcols - 1, nwin, wcols):
            place_window(w)
        colf[88:96, 0:C] = jnp.zeros((8, C), F32)
        for r in range(HALF_LAT, lat_dev):
            at = 6 * (r - HALF_LAT)
            colf[at : at + 6, 0:C] = of[o, r, lon_dev : lon_dev + HALF_LON, :]
        ocs[o] = colf[0:96, 0:C].astype(BF16)
        for r in range(HALF_LAT):
            colf[6 * r : 6 * r + 6, 0:C] = of[o, lat_dev + r, lon_dev : lon_dev + HALF_LON, :]
        colf[8:16, C : C + 128] = jnp.zeros((8, 128), F32)
        for j in range(8):
            colf[j : j + 1, C : C + 128] = colf[16 + j // 4 : 17 + j // 4, 128 * (j % 4) : 128 * (j % 4) + 128]
        occs[o] = colf[0:16, 0 : C + 128].astype(BF16)
        copies = [
            send(ocs.at[o], ocr.at[o], os_.at[o, 0], or_.at[o, 0], forth[0]),
            send(occs.at[o], occ.at[o], os_.at[o, 2], or_.at[o, 2], forth[2]),
        ]
        for w in range(nwin - wcols, nwin - 1):
            place_window(w)
        for r in range(HALF_LAT):
            ors[o, r] = of[o, lat_dev + r, 0:lon_dev, :].astype(BF16)
        copies.insert(1, send(ors.at[o], orr.at[o], os_.at[o, 1], or_.at[o, 1], forth[1]))
        for w in range(nwin - wcols):
            if w % wcols < wcols - 1:
                place_window(w)
        return copies

    def finish(o, copies, out):
        copies[1].wait_recv()
        for r in range(HALF_LAT):
            of[o, r, 0:lon_dev, :] = orr[o, r].astype(F32)
        copies[0].wait_recv()
        colf[0:96, 0:C] = ocr[o].astype(F32)
        for r in range(HALF_LAT, lat_dev):
            at = 6 * (r - HALF_LAT)
            of[o, r, 0:HALF_LON, :] = colf[at : at + 6, 0:C]
        copies[2].wait_recv()
        colf[0:16, 0 : C + 128] = occ[o].astype(F32)
        for j in range(8):
            colf[16 + j // 4 : 17 + j // 4, 128 * (j % 4) : 128 * (j % 4) + 128] = colf[j : j + 1, C : C + 128]
        for r in range(HALF_LAT):
            of[o, r, 0:HALF_LON, :] = colf[6 * r : 6 * r + 6, 0:C]
        for r in range(lat_dev):
            out[r] = of[o, r, 0:lon_dev, :].astype(BF16)

    gnacc[...] = nn(mixed[0:ROWS, :], wproj[...])

    def updated_step(k, carry):
        w = idx[k]
        m = win[w, :, M0 : M0 + 128]
        res[k] = win[w, :, X0 : X0 + C] + jnp.concatenate([m] * 4, axis=1) * gnacc[rows_of(k), :]
        return carry

    lax.fori_loop(0, SLOTS // 3, by_three(updated_step), 0)
    out_copies = [window_back(0, X0)]

    halo_land(1, dlanes, dcopies)
    for w in outer:
        cut(w, dlanes)
    lax.fori_loop(0, SLOTS // 3, by_three(dy_step), 0)
    gm[...] = nt(gz[0:ROWS, :], wproj[...]).astype(BF16)
    ntp[...] = nt(perm[...], normed[...]).astype(BF16)

    def gain_part(c, rows, product):
        weight = [wperm[rows, C * i + 128 * (c - 1) : C * i + 128 * c].astype(F32) for i in range(3)]
        gacc[rows, :] += sum(product[:, 128 * i : 128 * i + 128] * weight[i] for i in range(3))

    def chunk_start(c, lhs, rhs):
        asend, arecv, own = chunks[c][0:3]
        right = rhs[...]
        other = pl.ds(pl.multiple_of((1 - core) * half, half), half)
        mine = pl.ds(pl.multiple_of(core * half, half), half)
        product = nn(lhs[other, :], right)
        asend[...] = product.astype(BF16)
        copy = send(asend, arecv, as_.at[c], ar.at[c], partner)
        if c > 0:
            gain_part(c, other, product)
        product = nn(lhs[mine, :], right)
        own[...] = product
        if c > 0:
            gain_part(c, mine, product)
        return [copy]

    def chunk_y(c, copies):
        asend, arecv, own, ysend, yrecv = chunks[c][0:5]
        copies[0].wait_recv()
        s = own[...] + arecv[...].astype(F32)
        own[...] = s
        ysend[...] = s.astype(BF16)
        out = []
        for d in range(1, ny):
            start = pl.multiple_of(((y + d) % ny) * ysz, ysz)
            out.append(
                send(ysend.at[pl.ds(start, ysz)], yrecv.at[d - 1], ys.at[c, d - 1], yr.at[c, d - 1], ypeer[d - 1])
            )
        return out

    def chunk_x(c, copies):
        own, ysend, yrecv, xsend, xrecv, xown = chunks[c][2:8]
        s = own[pl.ds(pl.multiple_of(y * ysz, ysz), ysz), :]
        for d in range(1, ny):
            copies[d - 1].wait_recv()
            s = s + yrecv[d - 1].astype(F32)
        top, low_half = s[0 : ysz // 2], s[ysz // 2 : ysz]
        first = xh == 0
        xsend[...] = jnp.where(first, low_half, top).astype(BF16)
        xown[...] = jnp.where(first, top, low_half)
        return [send(xsend, xrecv, xs.at[c], xr.at[c], xpeer)]

    def blocks_before(c):
        g = next(i for i, members in enumerate(GROUPS) if c in members)
        return g, sum(cols[m] // 128 for m in GROUPS[g] if m < c)

    def chunk_z(c, copies):
        xsend, xrecv, xown = chunks[c][5:8]
        g, first = blocks_before(c)
        zown = groups[g][0]
        copies[0].wait_recv()
        s = xown[...] + xrecv[...].astype(F32)
        for j in range(nz):
            part = s[share * j : share * j + share]
            for q in range(cols[c] // 128):
                at = share * (first + q)
                zown[j, at : at + share, :] = part[:, 128 * q : 128 * q + 128]

    def group_send(g):
        zown, zsend, zrecv = groups[g]
        zsend[...] = zown[...].astype(BF16)
        return [
            send(zsend.at[(z + d) % nz], zrecv.at[d - 1], zs.at[g, d - 1], zr.at[g, d - 1], zpeer[d - 1])
            for d in range(1, nz)
        ]

    def group_end(g, copies):
        zown, zsend, zrecv = groups[g]
        s = zown[z]
        for i, copy in enumerate(copies):
            copy.wait_recv()
            s = s + zrecv[i].astype(F32)
        for c in GROUPS[g]:
            first = blocks_before(c)[1]
            for q in range(cols[c] // 128):
                at = share * (first + q)
                block = s[at : at + share]
                if c == 0:
                    gproj[:, 128 * q : 128 * q + 128] = block
                else:
                    gqkv[:, C * q + 128 * (c - 1) : C * q + 128 * c] = block

    mtp[...] = nt(perm[...], mixed[...]).astype(BF16)
    st = {}
    st[0] = chunk_start(0, mtp, gz)

    def backward(p):
        ks = list(range(SLOTS))
        d2s, dps = [], []
        for k in ks:
            rows = slice(TP * k, TP * k + TP)
            d2s.append(both_heads(gm[rows, 128 * p : 128 * p + 128], one_lo, one_hi))
            dps.append(nt(packed[rows, 2 * C + 128 * p : 2 * C + 128 * p + 128], d2s[-1]))
        dss, dvs = [], []
        for k in ks:
            pr = probs[k * PAIRS + p]
            t = pr * dps[k]
            dss.append(t - pr * jnp.sum(t, axis=0, keepdims=True))
            dvs.append(nn(pr.astype(BF16), d2s[k]))
        bacc[p] = functools.reduce(lambda a, b: a + b, dss)
        dqs = []
        for k in ks:
            rows = slice(TP * k, TP * k + TP)
            ds = dss[k].astype(BF16)
            q2 = both_heads(packed[rows, 128 * p : 128 * p + 128], q_lo, q_hi)
            dqs.append(tn(packed[rows, C + 128 * p : C + 128 * p + 128], ds))
            dp3[p, rows, 128:256] = nn(ds, q2).astype(BF16)
            dp3[p, rows, 256:384] = dvs[k].astype(BF16)
        for k in ks:
            dp3[p, TP * k : TP * k + TP, 0:128] = (own_head(dqs[k]) * 0.125).astype(BF16)

    def weight_pair(p):
        return jnp.concatenate([wqkv[:, C * part + 128 * p : C * part + 128 * p + 128] for part in range(3)], axis=1)

    def grad_normed(p, q):
        return nt(dp3[p, 0:ROWS, :], weight_pair(p)) + nt(dp3[q, 0:ROWS, :], weight_pair(q))

    for p in range(PAIRS):
        backward(p)
        st[p + 1] = chunk_start(p + 1, ntp, dp3.at[p])
        st[p] = chunk_y(p, st[p])
        if p >= 2:
            st[p - 2] = chunk_x(p - 2, st[p - 2])
        if p >= 3:
            chunk_z(p - 3, st[p - 3])

    stacked = jnp.concatenate([bacc[h // 2, :, 128 * (h % 2) : 128 * (h % 2) + 128] for h in range(HEADS)], axis=0)
    by_place = sum(nn(v, self_[...]) for v in pieces(stacked, 2))
    by_place = jnp.concatenate([by_place[TP * h : TP * h + TP] for h in range(HEADS)], axis=1)
    spread = sum(nn(selrt[:, 0:TP], v) for v in pieces(by_place, 2))
    for h in range(HEADS):
        wide = jnp.concatenate([spread[:, 128 * h : 128 * h + 128], jnp.zeros((128, 128), F32)], axis=1)
        sums[0][h : h + 1, 0:256] = jnp.sum(pltpu.roll(wide, 0, 1, stride=1, stride_axis=0), axis=0, keepdims=True)
    gain_row = sum(tn(v, perm[...]) for v in pieces(gacc[...], 2))
    gain_row = jnp.sum(gain_row, axis=0, keepdims=True) / gain
    sm, smc, smy, sma, smx, smz = sums
    sm[4:8, 256:384] = jnp.zeros((4, 128), F32)
    for j in range(4):
        sm[j : j + 1, 256:384] = gain_row[:, 128 * j : 128 * j + 128]
    copy = send(sm, smc, ss.at[0], sr.at[0], partner)

    gnacc[...] = grad_normed(0, 1)
    st[4] = chunk_y(4, st[4])
    st[2] = chunk_x(2, st[2])
    gnacc[...] += grad_normed(2, 3)
    copy.wait_recv()
    smy[y] = sm[...] + smc[...]
    copies = [send(smy.at[y], smy.at[y], ss.at[d], sr.at[d], ypeer[d - 1]) for d in range(1, ny)]

    def norm_back(k, carry):
        w = idx[k]
        rows = rows_of(k)
        gn = gnacc[rows, :]
        hat = xhat[rows, :]
        g = gn * gain
        prod = g * hat
        mid = g - jnp.mean(g, axis=1, keepdims=True) - hat * jnp.mean(prod, axis=1, keepdims=True)
        inv = jnp.concatenate([invd[rows, :]] * 4, axis=1)
        res[k] = win[w, :, D0 : D0 + C] + inv * mid
        return carry

    lax.fori_loop(0, SLOTS // 3, by_three(norm_back), 0)
    chunk_z(1, st[1])
    st[3] = chunk_x(3, st[3])
    out_copies.append(window_back(1, D0))
    for copy in copies:
        copy.wait_recv()
    acc = smy[0]
    for j in range(1, ny):
        acc = acc + smy[j]
    sma[...] = acc
    copy = send(sma, smx, ss.at[ny], sr.at[ny], xpeer)
    st[4] = chunk_x(4, st[4])
    chunk_z(2, st[2])
    group0 = group_send(0)
    finish(0, out_copies[0], upd)
    stores[0].start()
    copy.wait_recv()
    smz[z] = sma[...] + smx[...]
    copies = [send(smz.at[z], smz.at[z], ss.at[ny + d], sr.at[ny + d], zpeer[d - 1]) for d in range(1, nz)]
    chunk_z(3, st[3])
    chunk_z(4, st[4])
    group1 = group_send(1)
    finish(1, out_copies[1], gin)
    stores[1].start()
    group_end(0, group0)
    for copy in copies:
        copy.wait_recv()
    acc = smz[0]
    for j in range(1, nz):
        acc = acc + smz[j]
    bias_out[...] = acc[:, 0:REL]
    for j in range(4):
        gain_out[:, 128 * j : 128 * j + 128] = acc[j : j + 1, 256:384]
    group_end(1, group1)
    for store in stores[2:]:
        store.start()
    for copy in sends:
        copy.wait_send()
    for store in stores:
        store.wait()


def hand_over(*refs):
    arrived, left = refs[18:20]
    steps = []
    for i in range(6):
        rows = refs[i].shape[0]
        size = 3 if i < 2 else rows
        steps += [(i, pl.ds(start, size)) for start in range(0, rows, size)]
    fetches = [
        pltpu.make_async_copy(refs[i].at[at], refs[12 + i].at[at], arrived.at[n]) for n, (i, at) in enumerate(steps)
    ]
    stores = [
        pltpu.make_async_copy(refs[12 + i].at[at], refs[6 + i].at[at], left.at[n]) for n, (i, at) in enumerate(steps)
    ]
    for fetch in fetches:
        fetch.start()
    for fetch, store in zip(fetches, stores):
        fetch.wait()
        store.start()
    for store in stores:
        store.wait()


def constants(ny, nx, nz):
    share = C // (ny * nx * nz * 2)
    perm = np.zeros((C, C), np.float32)
    for core in range(2):
        for y in range(ny):
            for xh in range(nx):
                for z in range(nz):
                    to = (((core * ny + y) * nx + xh) * nz + z) * share
                    start = (((y * nx + xh) * nz + z) * 2 + core) * share
                    perm[to + np.arange(share), start + np.arange(share)] = 1
    a = np.arange(T)
    pa = (a // WIN_LON) * (2 * WIN_LON - 1) + a % WIN_LON
    selrt = np.zeros((128, 128), np.float32)
    selrt[126 - pa, a] = 1
    self_ = np.zeros((128, 128), np.float32)
    self_[a, pa] = 1
    return perm, self_, self_.T, selrt


def solution(mesh):
    nlon, nlat = mesh.shape["lon"], mesh.shape["lat"]
    nx, nz = 2, nlat // 2
    ny = nlon // nx
    nxz = nx * nz
    half = C // 2
    ysz = half // ny
    share = ysz // nxz
    cols = [C] + [384] * PAIRS
    lat_dev, lon_dev = 18, 48
    nwin = 12
    vm = pltpu.VMEM
    dma = lambda *s: pltpu.SemaphoreType.DMA(s)
    perm, self_, selft, selrt = (jnp.asarray(v, BF16) for v in constants(ny, nx, nz))

    def on_device(fields, grad_out, layernorm_gain, qkv_weight, proj_weight, bias_table, sea_mask):
        shapes = (
            jax.ShapeDtypeStruct((lat_dev, lon_dev, C), BF16),
            jax.ShapeDtypeStruct((lat_dev, lon_dev, C), BF16),
            jax.ShapeDtypeStruct((1, C), F32),
            jax.ShapeDtypeStruct((HEADS, REL), F32),
            jax.ShapeDtypeStruct((share, 3 * C), F32),
            jax.ShapeDtypeStruct((share, C), F32),
        )
        scratch = [
            vm((lat_dev, lon_dev, C), BF16),
            vm((lat_dev, lon_dev), jnp.int32),
            vm((lat_dev, lon_dev, C), BF16),
            vm((HEADS, REL), F32),
            vm((128, 128), BF16),
            vm((128, 128), BF16),
            vm((128, 128), BF16),
            vm((1, C), F32),
            vm((C, 3 * C), BF16),
            vm((C, C), BF16),
            vm((C, C), BF16),
        ]
        scratch += [vm(v.shape, v.dtype) for v in shapes]
        scratch += [
            vm((lat_dev + 3, 56, FW), F32),
            vm((nwin, TP, FW), F32),
            vm((112, FW), F32),
        ]
        for wide in (C, C):
            scratch += [
                vm((112, wide), BF16),
                vm((112, wide), BF16),
                vm((3, lon_dev, wide), BF16),
                vm((3, lon_dev, wide), BF16),
                vm((32, wide), BF16),
            ]
        scratch += [vm((lat_dev, lon_dev), jnp.int32)] * 3
        scratch += [
            pltpu.SMEM((16,), jnp.int32),
            vm((HEADS, 256), F32),
            vm((PAIRS, TP, 256), F32),
            vm((SLOTS, TP, 128), F32),
            vm((ROWS, C), F32),
            vm((ROWS, 128), F32),
            vm((RP, C), BF16),
            vm((RP, C), BF16),
            vm((ROWS, C), BF16),
            vm((ROWS, 3 * C), BF16),
            vm((RP, C), BF16),
            vm((C, RP), BF16),
            vm((C, RP), BF16),
            vm((SLOTS * PAIRS, TP, 256), F32),
            vm((PAIRS, RP, 384), BF16),
            vm((ROWS, C), F32),
            vm((PAIRS, TP, 256), F32),
            vm((C, 3 * C), BF16),
            vm((C, 128), F32),
            vm((SLOTS, TP, C), F32),
            vm((2, lat_dev + 3, 56, C), F32),
            vm((2, 96, C), BF16),
            vm((2, 3, lon_dev, C), BF16),
            vm((2, 16, C + 128), BF16),
            vm((2, 96, C), BF16),
            vm((2, 3, lon_dev, C), BF16),
            vm((2, 16, C + 128), BF16),
        ]
        for n in cols:
            scratch += [
                vm((half, n), BF16),
                vm((half, n), BF16),
                vm((half, n), F32),
                vm((half, n), BF16),
                vm((ny - 1, ysz, n), BF16),
                vm((ysz // 2, n), BF16),
                vm((ysz // 2, n), BF16),
                vm((ysz // 2, n), F32),
            ]
        for members in GROUPS:
            rows = -(-share * sum(cols[c] // 128 for c in members) // 16) * 16
            scratch += [vm((nz, rows, 128), F32), vm((nz, rows, 128), BF16), vm((nz - 1, rows, 128), BF16)]
        sm = (8, 384)
        scratch += [vm(sm, F32), vm(sm, F32), vm((ny,) + sm, F32), vm(sm, F32), vm(sm, F32), vm((nz,) + sm, F32)]
        nc = len(cols)
        small = ny + nz
        scratch += [
            dma(2, 3), dma(2, 3), dma(3), dma(3), dma(2, 3), dma(2, 3), dma(nc), dma(nc), dma(nc, ny - 1),
            dma(nc, ny - 1), dma(nc), dma(nc), dma(nc, nz - 1), dma(nc, nz - 1), dma(small), dma(small), dma(11), dma(6),
        ]
        anywhere = pl.BlockSpec(memory_space=pl.ANY)
        outs = pl.pallas_call(
            functools.partial(kernel, (ny, nx, nz), cols),
            out_shape=shapes,
            in_specs=[anywhere] * 11,
            out_specs=(anywhere,) * 6,
            scratch_shapes=scratch,
            compiler_params=pltpu.CompilerParams(
                collective_id=0, has_side_effects=True, vmem_limit_bytes=60 * 1024 * 1024
            ),
        )(
            fields, sea_mask, grad_out, bias_table, self_, selft, selrt,
            layernorm_gain.reshape(1, C), qkv_weight, proj_weight, perm,
        )
        outs = pl.pallas_call(
            hand_over,
            out_shape=shapes,
            in_specs=[anywhere] * 6,
            out_specs=(anywhere,) * 6,
            scratch_shapes=[vm(v.shape, v.dtype) for v in shapes] + [dma(16), dma(16)],
            compiler_params=pltpu.CompilerParams(vmem_limit_bytes=60 * 1024 * 1024),
        )(*outs)
        updated, grad_in, grad_gain, grad_bias, grad_qkv, grad_proj = outs
        return (updated, grad_in, grad_gain.reshape(C), grad_bias, grad_qkv, grad_proj)

    grid = P(("batch", "lat"), "lon", None)
    return jax.shard_map(
        on_device,
        mesh=mesh,
        in_specs=(grid, grid, P(), P(), P(), P(), P(("batch", "lat"), "lon")),
        out_specs=(
            grid,
            grid,
            P("batch"),
            P("batch", None),
            P(("batch", "lon", "lat"), None),
            P(("batch", "lon", "lat"), None),
        ),
        check_vma=False,
    )
```

```python
import functools

import jax
import jax.numpy as jnp
import numpy as np
from jax import lax
from jax.experimental import pallas as pl
from jax.experimental.pallas import tpu as pltpu
from jax.sharding import PartitionSpec as P

MESH = pl.DeviceIdType.MESH
F32 = jnp.float32
BF16 = jnp.bfloat16
C = 512
HEADS = 8
PAIRS = 4
WIN_LAT = 6
WIN_LON = 12
HALF_LAT = 3
HALF_LON = 6
T = 72
TP = 80
SLOTS = 9
ROWS = SLOTS * TP
RP = 768
REL = 253
X0, M0, D0, FW = 0, 512, 640, 1152
GROUPS = ((0, 1, 2),)
LAST = (3, 4)
EARLY = 3
EPS = 1e-5


def nn(a, b, **kw):
    return lax.dot_general(a, b, (((1,), (0,)), ((), ())), preferred_element_type=F32, **kw)


def nt(a, b, **kw):
    return lax.dot_general(a, b, (((1,), (1,)), ((), ())), preferred_element_type=F32, **kw)


def tn(a, b, **kw):
    return lax.dot_general(a, b, (((0,), (0,)), ((), ())), preferred_element_type=F32, **kw)


def pad_rows(v, rows):
    return jnp.concatenate([v, jnp.zeros((rows - v.shape[0], v.shape[1]), v.dtype)], axis=0)


def kernel(dims, cols, *refs):
    ny, nx, nz = dims
    nlon, nlat = ny * nx, 2 * nz
    nxz = nx * nz
    lat_dev, lon_dev = 18, 48
    wrows, wcols = lat_dev // WIN_LAT, lon_dev // WIN_LON
    nwin = wrows * wcols
    half = C // 2
    ysz = half // ny
    share = ysz // nxz
    nchunk = len(cols)

    it = iter(refs)
    take = lambda n=None: next(it) if n is None else [next(it) for _ in range(n)]
    given = take(11)
    results = take(6)
    held = take(11)
    x_ref, mask_ref, dy_ref, table, self_, selft, selrt, gain_ref, wqkv, wproj, perm = held
    staged = take(6)
    upd, gin, gain_out, bias_out, gqkv, gproj = staged
    frame, win, colf = take(3)
    halos = [take(4) for _ in range(2)]
    masks = take(3)
    idx = take()
    tb, bias2, madd, xhat, invd, normed, gz, gm, packed, mixed, ntp, mtp, probs, dp3, gnacc, bacc, wperm, gacc = take(18)
    res, of = take(2)
    ocs, ors, occs, ocr, orr, occ = take(6)
    chunks = [take(8) for _ in range(nchunk)]
    groups = [take(3) for _ in range(len(GROUPS))]
    lastown, lastsend, lastrecv = take(3)
    sums = take(4)
    hs, hr, ms, mr, os_, or_, as_, ar, ys, yr, xs, xr, zs, zr, ss, sr, ls, lr = take(18)
    ins, outs = take(2)

    lon = lax.axis_index("lon")
    lat = lax.axis_index("lat")
    y, xh = lon // nx, lon % nx
    z, core = lat // 2, lat % 2

    def dev(a, b):
        return {"lon": a, "lat": b}

    partner = dev(lon, z * 2 + (1 - core))
    ypeer = [dev(((y + d) % ny) * nx + xh, lat) for d in range(1, ny)]
    xpeer = dev(y * nx + (1 - xh), lat)
    zpeer = [dev(lon, ((z + d) % nz) * 2 + core) for d in range(1, nz)]
    crossy = [dev(((y + d) % ny) * nx + xh, z * 2 + (1 - core)) for d in range(1, ny)]
    crossz = [dev(y * nx + (1 - xh), ((z + d) % nz) * 2 + core) for d in range(1, nz)]
    west, east = (lon + nlon - 1) % nlon, (lon + 1) % nlon
    north, south = (lat + nlat - 1) % nlat, (lat + 1) % nlat
    back = [dev(west, lat), dev(lon, north), dev(west, north)]
    forth = [dev(east, lat), dev(lon, south), dev(east, south)]

    barrier = pltpu.get_barrier_semaphore()
    everyone = [partner, xpeer] + ypeer + zpeer + crossy + crossz + back + forth
    for d in everyone:
        pl.semaphore_signal(barrier, inc=1, device_id=d, device_id_type=MESH)

    loads = [pltpu.make_async_copy(a, b, ins.at[i]) for i, (a, b) in enumerate(zip(given, held)) if i != 8]
    for p in range(PAIRS):
        for i in range(3):
            src = given[8].at[:, C * i + 128 * p : C * i + 128 * p + 128]
            dst = wqkv.at[:, 384 * p + 128 * i : 384 * p + 128 * i + 128]
            loads.append(pltpu.make_async_copy(src, dst, ins.at[11 + 3 * p + i]))
    for load in loads:
        load.start()

    stores = [pltpu.make_async_copy(a, b, outs.at[i]) for i, (a, b) in enumerate(zip(staged, results))]
    sends = []

    def send(src, dst, ssem, rsem, d):
        copy = pltpu.make_async_remote_copy(
            src_ref=src, dst_ref=dst, send_sem=ssem, recv_sem=rsem, device_id=d, device_id_type=MESH
        )
        copy.start()
        sends.append(copy)
        return copy

    lane_row = lax.broadcasted_iota(jnp.int32, (lat_dev, lat_dev * 128), 1) // 128
    pick = (lane_row == lax.broadcasted_iota(jnp.int32, (lat_dev, lat_dev * 128), 0)).astype(F32)

    def spread_mask(ref):
        return tn(ref[...].astype(F32), pick)

    colf[96:112, :] = jnp.zeros((16, FW), F32)

    def halo_send(h, block, source):
        colsend, colrecv, rowrecv, cornrecv = halos[h]
        for r in range(lat_dev):
            colf[6 * r : 6 * r + 6, 0:C] = block[r, 0:16, :].astype(F32)[0:HALF_LON]
        colsend[...] = colf[:, 0:C].astype(BF16)
        if h == 0:
            pl.semaphore_wait(barrier, len(everyone))
        return [
            send(colsend, colrecv, hs.at[h, 0], hr.at[h, 0], back[0]),
            send(source.at[0:HALF_LAT], rowrecv, hs.at[h, 1], hr.at[h, 1], back[1]),
            send(colsend.at[0:32], cornrecv, hs.at[h, 2], hr.at[h, 2], back[2]),
        ]

    def halo_land(h, lanes, copies):
        colsend, colrecv, rowrecv, cornrecv = halos[h]
        copies[1].wait_recv()
        for r in range(HALF_LAT):
            frame[lat_dev + r, 0:lon_dev, lanes] = rowrecv[r].astype(F32)
        copies[2].wait_recv()
        colf[0:32, lanes] = cornrecv[...].astype(F32)
        for r in range(HALF_LAT):
            frame[lat_dev + r, lon_dev : lon_dev + HALF_LON, lanes] = colf[6 * r : 6 * r + 6, lanes]
        copies[0].wait_recv()
        colf[:, lanes] = colrecv[...].astype(F32)
        for r in range(lat_dev):
            frame[r, lon_dev : lon_dev + HALF_LON, lanes] = colf[6 * r : 6 * r + 6, lanes]

    xlanes, dlanes = slice(X0, X0 + C), slice(D0, D0 + C)
    loads[0].wait()
    xcopies = halo_send(0, x_ref, given[0])
    loads[1].wait()
    mcopies = [send(mask_ref, masks[i], ms.at[i], mr.at[i], back[i]) for i in range(3)]
    loads[2].wait()
    dcopies = halo_send(1, dy_ref, given[2])
    sea = spread_mask(mask_ref)
    for r in range(lat_dev):
        frame[r, 0:lon_dev, X0 : X0 + C] = x_ref[r].astype(F32)
        frame[r, 0:lon_dev, M0 : M0 + 128] = sea[:, 128 * r : 128 * r + 128]
        frame[r, 0:lon_dev, D0 : D0 + C] = dy_ref[r].astype(F32)

    def pieces(v, n):
        out = []
        for i in range(n):
            part = v.astype(BF16)
            out.append(part)
            if i < n - 1:
                v = v - part.astype(F32)
        return out

    for load in loads[3:]:
        load.wait()
    tb[...] = jnp.zeros_like(tb)
    tb[:, 0:REL] = table[...]
    shifted = []
    for h in range(HEADS):
        line = jnp.broadcast_to(tb[h : h + 1, :], (128, 256))
        shifted.append(pltpu.roll(pltpu.roll(line, 2, 1), 128, 1, stride=1, stride_axis=0)[:, 0:128])
    by_query = sum(nn(v, selft[...]) for v in pieces(jnp.concatenate(shifted, axis=0), 3))
    by_query = jnp.concatenate([by_query[128 * h : 128 * h + 128] for h in range(HEADS)], axis=1)
    whole_bias = sum(nn(self_[0:TP, :], v) for v in pieces(by_query, 3))
    for p in range(PAIRS):
        bias2[p] = whole_bias[:, 256 * p : 256 * p + 256]

    wperm[...] = nn(perm[...], wqkv[...]).astype(BF16)
    gacc[...] = jnp.zeros_like(gacc)
    for g in range(len(GROUPS)):
        groups[g][0][...] = jnp.zeros_like(groups[g][0])
    zero_tail = jnp.zeros((RP - ROWS, C), BF16)
    normed[ROWS:RP, :] = zero_tail
    gz[ROWS:RP, :] = zero_tail
    mixed[ROWS:RP, :] = zero_tail
    dp3[ROWS:RP, :] = jnp.zeros((RP - ROWS, 3 * C), BF16)
    for w in range(nwin):
        win[w, T:TP, :] = jnp.zeros((TP - T, FW), F32)

    def cut(w, lanes):
        wr, wc = w // wcols, w % wcols
        c0 = HALF_LON + WIN_LON * wc
        for i in range(WIN_LAT):
            win[w, WIN_LON * i : WIN_LON * i + WIN_LON, lanes] = frame[
                HALF_LAT + WIN_LAT * wr + i, c0 : c0 + WIN_LON, lanes
            ]

    def holds_sea(w):
        return (jnp.max(win[w, :, M0 : M0 + 128]) > 0.5).astype(jnp.int32)

    def ranks(flags, counted):
        total = jnp.int32(0)
        for f, c in zip(flags, counted):
            total = total + f * c
        out, on, off = [], jnp.int32(0), total
        for f, c in zip(flags, counted):
            out.append(jnp.where(f > 0, on, off))
            on = on + f * c
            off = off + (1 - f) * c
        return out

    def slot_window(k, places):
        slot = jnp.int32(0)
        for w, at in places:
            slot = slot + jnp.where(at == k, w, 0)
        idx[k] = slot

    inner = [w for w in range(nwin) if w // wcols < wrows - 1 and w % wcols < wcols - 1]
    outer = [w for w in range(nwin) if w not in inner]
    active = [None] * nwin
    place = [None] * nwin

    at_end = (lat == nlat - 1).astype(F32)
    gain = gain_ref[...]

    def rows_of(k):
        return pl.ds(pl.multiple_of(k * TP, TP), TP)

    def by_three(step):
        def body(i, carry):
            for j in range(3):
                carry = step(3 * i + j, carry)
            return carry

        return body

    def ln_step(k, carry):
        w = idx[k]
        x = win[w, :, X0 : X0 + C]
        mean = jnp.mean(x, axis=1, keepdims=True)
        xc = x - mean
        inv = lax.rsqrt(jnp.mean(xc * xc, axis=1, keepdims=True) + EPS)
        hat = xc * inv
        rows = rows_of(k)
        xhat[rows, :] = hat
        invd[rows, :] = jnp.broadcast_to(inv, (TP, 128))
        normed[rows, :] = (hat * gain).astype(BF16)
        keys = win[w, :, M0 : M0 + 128]
        side_b = lax.broadcasted_iota(jnp.int32, (TP, 128), 0) >= T // 2
        side_a = lax.broadcasted_iota(jnp.int32, (TP, 128), 1) >= T // 2
        apart = jnp.where(side_a != side_b, 1.0, 0.0)
        wrap = at_end * jnp.where(w >= nwin - wcols, 1.0, 0.0)
        madd[k] = (keys * (1.0 - apart * wrap) - 1.0) * 1e9
        return carry

    def dy_step(k, carry):
        w = idx[k]
        m = win[w, :, M0 : M0 + 128]
        gz[rows_of(k), :] = (win[w, :, D0 : D0 + C] * jnp.concatenate([m] * 4, axis=1)).astype(BF16)
        return carry

    lane = lax.broadcasted_iota(jnp.int32, (TP, 128), 1)
    low = lane < 64
    one_lo = jnp.where(low, 1.0, 0.0).astype(BF16)
    one_hi = jnp.where(low, 0.0, 1.0).astype(BF16)
    q_lo = jnp.where(low, 0.125, 0.0).astype(BF16)
    q_hi = jnp.where(low, 0.0, 0.125).astype(BF16)

    def both_heads(v, lo, hi):
        return jnp.concatenate([pad_rows(v * lo, 128), pad_rows(v * hi, 128)], axis=0)

    def own_head(v):
        return jnp.transpose(jnp.concatenate([v[0:64, 0:128], v[64:128, 128:256]], axis=0))[0:TP]

    def attend(i, carry):
        chains = [(3 * i + j, p) for j in range(3) for p in range(PAIRS)]
        scores = []
        for k, p in chains:
            rows = rows_of(k)
            q2 = both_heads(packed[rows, 384 * p : 384 * p + 128], q_lo, q_hi)
            add = madd[k]
            add2 = jnp.concatenate([add, add], axis=1)
            scores.append(nt(packed[rows, 384 * p + 128 : 384 * p + 256], q2) + bias2[p] + add2)
        mixes = []
        for (k, p), s in zip(chains, scores):
            e = jnp.exp(s - jnp.max(s, axis=0, keepdims=True))
            pr = e * (1.0 / jnp.sum(e, axis=0, keepdims=True))
            probs[k * PAIRS + p] = pr
            mixes.append(tn(packed[rows_of(k), 384 * p + 256 : 384 * p + 384], pr.astype(BF16)))
        for (k, p), mix in zip(chains, mixes):
            mixed[rows_of(k), 128 * p : 128 * p + 128] = own_head(mix).astype(BF16)
        return carry

    def forward(first, last):
        lax.fori_loop(first // 3, last // 3, by_three(ln_step), 0)
        rows = slice(first * TP, last * TP)
        packed[rows, :] = nn(normed[rows, :], wqkv[...]).astype(BF16)
        lax.fori_loop(first // 3, last // 3, attend, 0)

    for w in inner:
        cut(w, slice(0, FW))
        active[w] = holds_sea(w)
    inner_rank = ranks([active[w] for w in inner], [1] * len(inner))
    for k in range(EARLY):
        slot_window(k, list(zip(inner, inner_rank)))
    forward(0, EARLY)

    mlanes = slice(M0, M0 + 128)
    for copy in mcopies:
        copy.wait_recv()
    sea = spread_mask(masks[0])
    for r in range(lat_dev):
        frame[r, lon_dev : lon_dev + HALF_LON, mlanes] = sea[0:HALF_LON, 128 * r : 128 * r + 128]
    sea = spread_mask(masks[1])
    for r in range(HALF_LAT):
        frame[lat_dev + r, 0:lon_dev, mlanes] = sea[:, 128 * r : 128 * r + 128]
    sea = spread_mask(masks[2])
    for r in range(HALF_LAT):
        frame[lat_dev + r, lon_dev : lon_dev + HALF_LON, mlanes] = sea[0:HALF_LON, 128 * r : 128 * r + 128]
    halo_land(0, xlanes, xcopies)
    for w in outer:
        cut(w, slice(X0, M0 + 128))
        active[w] = holds_sea(w)
    rest = [jnp.int32(1)] * nwin
    for w, at in zip(inner, inner_rank):
        rest[w] = (at >= EARLY).astype(jnp.int32)
    late_rank = ranks(active, rest)
    for w in range(nwin):
        place[w] = late_rank[w] + EARLY
    for w, at in zip(inner, inner_rank):
        place[w] = jnp.where(at < EARLY, at, place[w])
    for k in range(EARLY, SLOTS):
        slot_window(k, list(enumerate(place)))
    forward(EARLY, SLOTS)

    def window_back(o, lane0):
        def place_window(w):
            wr, wc = w // wcols, w % wcols
            slot = jnp.minimum(place[w], SLOTS - 1)
            for i in range(WIN_LAT):
                c0 = HALF_LON + WIN_LON * wc
                at = slice(WIN_LON * i, WIN_LON * i + WIN_LON)
                of[o, HALF_LAT + WIN_LAT * wr + i, c0 : c0 + WIN_LON, :] = jnp.where(
                    place[w] < SLOTS, res[slot, at, :], win[w, at, lane0 : lane0 + C]
                )

        for w in range(wcols - 1, nwin, wcols):
            place_window(w)
        colf[88:96, 0:C] = jnp.zeros((8, C), F32)
        for r in range(HALF_LAT, lat_dev):
            at = 6 * (r - HALF_LAT)
            colf[at : at + 6, 0:C] = of[o, r, lon_dev : lon_dev + HALF_LON, :]
        ocs[o] = colf[0:96, 0:C].astype(BF16)
        for r in range(HALF_LAT):
            colf[6 * r : 6 * r + 6, 0:C] = of[o, lat_dev + r, lon_dev : lon_dev + HALF_LON, :]
        colf[8:16, C : C + 128] = jnp.zeros((8, 128), F32)
        for j in range(8):
            colf[j : j + 1, C : C + 128] = colf[16 + j // 4 : 17 + j // 4, 128 * (j % 4) : 128 * (j % 4) + 128]
        occs[o] = colf[0:16, 0 : C + 128].astype(BF16)
        copies = [
            send(ocs.at[o], ocr.at[o], os_.at[o, 0], or_.at[o, 0], forth[0]),
            send(occs.at[o], occ.at[o], os_.at[o, 2], or_.at[o, 2], forth[2]),
        ]
        for w in range(nwin - wcols, nwin - 1):
            place_window(w)
        for r in range(HALF_LAT):
            ors[o, r] = of[o, lat_dev + r, 0:lon_dev, :].astype(BF16)
        copies.insert(1, send(ors.at[o], orr.at[o], os_.at[o, 1], or_.at[o, 1], forth[1]))
        for w in range(nwin - wcols):
            if w % wcols < wcols - 1:
                place_window(w)
        return copies

    def finish(o, copies, out):
        copies[1].wait_recv()
        for r in range(HALF_LAT):
            of[o, r, 0:lon_dev, :] = orr[o, r].astype(F32)
        copies[0].wait_recv()
        colf[0:96, 0:C] = ocr[o].astype(F32)
        for r in range(HALF_LAT, lat_dev):
            at = 6 * (r - HALF_LAT)
            of[o, r, 0:HALF_LON, :] = colf[at : at + 6, 0:C]
        copies[2].wait_recv()
        colf[0:16, 0 : C + 128] = occ[o].astype(F32)
        for j in range(8):
            colf[16 + j // 4 : 17 + j // 4, 128 * (j % 4) : 128 * (j % 4) + 128] = colf[j : j + 1, C : C + 128]
        for r in range(HALF_LAT):
            of[o, r, 0:HALF_LON, :] = colf[6 * r : 6 * r + 6, 0:C]
        for r in range(lat_dev):
            out[r] = of[o, r, 0:lon_dev, :].astype(BF16)

    gnacc[...] = nn(mixed[0:ROWS, :], wproj[...])

    def updated_step(k, carry):
        w = idx[k]
        m = win[w, :, M0 : M0 + 128]
        res[k] = win[w, :, X0 : X0 + C] + jnp.concatenate([m] * 4, axis=1) * gnacc[rows_of(k), :]
        return carry

    lax.fori_loop(0, SLOTS // 3, by_three(updated_step), 0)
    out_copies = [window_back(0, X0)]

    halo_land(1, dlanes, dcopies)
    for w in outer:
        cut(w, dlanes)
    lax.fori_loop(0, SLOTS // 3, by_three(dy_step), 0)
    gm[...] = nt(gz[0:ROWS, :], wproj[...]).astype(BF16)
    ntp[...] = nt(perm[...], normed[...]).astype(BF16)

    def gain_part(c, rows, product):
        weight = [wperm[rows, 384 * (c - 1) + 128 * i : 384 * (c - 1) + 128 * i + 128].astype(F32) for i in range(3)]
        gacc[rows, :] += sum(product[:, 128 * i : 128 * i + 128] * weight[i] for i in range(3))

    def chunk_start(c, lhs, rhs):
        asend, arecv, own = chunks[c][0:3]
        right = rhs[...] if c == 0 else rhs[:, 384 * (c - 1) : 384 * c]
        other = pl.ds(pl.multiple_of((1 - core) * half, half), half)
        mine = pl.ds(pl.multiple_of(core * half, half), half)
        product = nn(lhs[other, :], right)
        asend[...] = product.astype(BF16)
        copy = send(asend, arecv, as_.at[c], ar.at[c], partner)
        if c > 0:
            gain_part(c, other, product)
        product = nn(lhs[mine, :], right)
        own[...] = product
        if c > 0:
            gain_part(c, mine, product)
        return [copy]

    def chunk_y(c, copies):
        asend, arecv, own, ysend, yrecv = chunks[c][0:5]
        copies[0].wait_recv()
        s = own[...] + arecv[...].astype(F32)
        own[...] = s
        ysend[...] = s.astype(BF16)
        out = []
        for d in range(1, ny):
            start = pl.multiple_of(((y + d) % ny) * ysz, ysz)
            out.append(
                send(ysend.at[pl.ds(start, ysz)], yrecv.at[d - 1], ys.at[c, d - 1], yr.at[c, d - 1], ypeer[d - 1])
            )
        return out

    def chunk_x(c, copies):
        own, ysend, yrecv, xsend, xrecv, xown = chunks[c][2:8]
        s = own[pl.ds(pl.multiple_of(y * ysz, ysz), ysz), :]
        for d in range(1, ny):
            copies[d - 1].wait_recv()
            s = s + yrecv[d - 1].astype(F32)
        top, low_half = s[0 : ysz // 2], s[ysz // 2 : ysz]
        first = xh == 0
        xsend[...] = jnp.where(first, low_half, top).astype(BF16)
        xown[...] = jnp.where(first, top, low_half)
        return [send(xsend, xrecv, xs.at[c], xr.at[c], xpeer)]

    def blocks_before(c):
        g = next(i for i, members in enumerate(GROUPS) if c in members)
        return g, sum(cols[m] // 128 for m in GROUPS[g] if m < c)

    def chunk_z(c, copies):
        xsend, xrecv, xown = chunks[c][5:8]
        g, first = blocks_before(c)
        zown = groups[g][0]
        copies[0].wait_recv()
        s = xown[...] + xrecv[...].astype(F32)
        for j in range(nz):
            part = s[share * j : share * j + share]
            for q in range(cols[c] // 128):
                at = share * (first + q)
                zown[j, at : at + share, :] = part[:, 128 * q : 128 * q + 128]

    def group_send(g):
        zown, zsend, zrecv = groups[g]
        zsend[...] = zown[...].astype(BF16)
        return [
            send(zsend.at[(z + d) % nz], zrecv.at[d - 1], zs.at[g, d - 1], zr.at[g, d - 1], zpeer[d - 1])
            for d in range(1, nz)
        ]

    def last_send(copies):
        lastown[...] = jnp.zeros_like(lastown)
        first = 0
        for c in LAST:
            own, ysend, yrecv = chunks[c][2:5]
            s = own[pl.ds(pl.multiple_of(y * ysz, ysz), ysz), :]
            for d in range(1, ny):
                copies[c][d - 1].wait_recv()
                s = s + yrecv[d - 1].astype(F32)
            for j in range(nxz):
                part = s[share * j : share * j + share]
                for q in range(cols[c] // 128):
                    at = share * (first + q)
                    lastown[j, at : at + share, :] = part[:, 128 * q : 128 * q + 128]
            first += cols[c] // 128
        lastsend[...] = lastown[...].astype(BF16)
        out = []
        for a in range(nx):
            for d in range(nz):
                if (a, d) == (0, 0):
                    continue
                to = (xpeer if d == 0 else crossz[d - 1]) if a else zpeer[d - 1]
                j = ((xh + a) % nx) * nz + (z + d) % nz
                i = a * nz + d - 1
                out.append(send(lastsend.at[j], lastrecv.at[i], ls.at[i], lr.at[i], to))
        return out

    def last_end(copies):
        s = lastown[xh * nz + z]
        for i, copy in enumerate(copies):
            copy.wait_recv()
            s = s + lastrecv[i].astype(F32)
        first = 0
        for c in LAST:
            for q in range(cols[c] // 128):
                at = share * (first + q)
                gqkv[:, C * q + 128 * (c - 1) : C * q + 128 * c] = s[at : at + share]
            first += cols[c] // 128

    def group_end(g, copies):
        zown, zsend, zrecv = groups[g]
        s = zown[z]
        for i, copy in enumerate(copies):
            copy.wait_recv()
            s = s + zrecv[i].astype(F32)
        for c in GROUPS[g]:
            first = blocks_before(c)[1]
            for q in range(cols[c] // 128):
                at = share * (first + q)
                block = s[at : at + share]
                if c == 0:
                    gproj[:, 128 * q : 128 * q + 128] = block
                else:
                    gqkv[:, C * q + 128 * (c - 1) : C * q + 128 * c] = block

    mtp[...] = nt(perm[...], mixed[...]).astype(BF16)
    st = {}
    st[0] = chunk_start(0, mtp, gz)

    def backward(p):
        ks = list(range(SLOTS))
        d2s, dps = [], []
        for k in ks:
            rows = slice(TP * k, TP * k + TP)
            d2s.append(both_heads(gm[rows, 128 * p : 128 * p + 128], one_lo, one_hi))
            dps.append(nt(packed[rows, 384 * p + 256 : 384 * p + 384], d2s[-1]))
        dss, dvs = [], []
        for k in ks:
            pr = probs[k * PAIRS + p]
            t = pr * dps[k]
            dss.append(t - pr * jnp.sum(t, axis=0, keepdims=True))
            dvs.append(nn(pr.astype(BF16), d2s[k]))
        bacc[p] = functools.reduce(lambda a, b: a + b, dss)
        dqs = []
        for k in ks:
            rows = slice(TP * k, TP * k + TP)
            ds = dss[k].astype(BF16)
            q2 = both_heads(packed[rows, 384 * p : 384 * p + 128], q_lo, q_hi)
            dqs.append(tn(packed[rows, 384 * p + 128 : 384 * p + 256], ds))
            dp3[rows, 384 * p + 128 : 384 * p + 256] = nn(ds, q2).astype(BF16)
            dp3[rows, 384 * p + 256 : 384 * p + 384] = dvs[k].astype(BF16)
        for k in ks:
            dp3[TP * k : TP * k + TP, 384 * p : 384 * p + 128] = (own_head(dqs[k]) * 0.125).astype(BF16)

    for p in range(PAIRS):
        backward(p)
        st[p + 1] = chunk_start(p + 1, ntp, dp3)
        st[p] = chunk_y(p, st[p])
        if p >= 2:
            st[p - 2] = chunk_x(p - 2, st[p - 2])

    stacked = jnp.concatenate([bacc[h // 2, :, 128 * (h % 2) : 128 * (h % 2) + 128] for h in range(HEADS)], axis=0)
    by_place = sum(nn(v, self_[...]) for v in pieces(stacked, 2))
    by_place = jnp.concatenate([by_place[TP * h : TP * h + TP] for h in range(HEADS)], axis=1)
    spread = sum(nn(selrt[:, 0:TP], v) for v in pieces(by_place, 2))
    for h in range(HEADS):
        wide = jnp.concatenate([spread[:, 128 * h : 128 * h + 128], jnp.zeros((128, 128), F32)], axis=1)
        sums[0][core * ny + y, h : h + 1, 0:256] = jnp.sum(pltpu.roll(wide, 0, 1, stride=1, stride_axis=0), axis=0, keepdims=True)
    gain_row = sum(tn(v, perm[...]) for v in pieces(gacc[...], 2))
    gain_row = jnp.sum(gain_row, axis=0, keepdims=True) / gain
    smy, sma, smx, smz = sums
    slot = core * ny + y
    sm = smy.at[slot]
    sm[4:8, 256:384] = jnp.zeros((4, 128), F32)
    for j in range(4):
        sm[j : j + 1, 256:384] = gain_row[:, 128 * j : 128 * j + 128]
    copies = [
        send(sm, sm, ss.at[i], sr.at[i], to) for i, to in enumerate([partner] + ypeer + crossy)
    ]
    st[4] = chunk_y(4, st[4])
    st[2] = chunk_x(2, st[2])
    for part in range(2):
        rows = slice(part * ROWS // 2, (part + 1) * ROWS // 2)
        gnacc[rows, :] = nt(dp3[rows, :], wqkv[...])

    def norm_back(k, carry):
        w = idx[k]
        rows = rows_of(k)
        gn = gnacc[rows, :]
        hat = xhat[rows, :]
        g = gn * gain
        prod = g * hat
        mid = g - jnp.mean(g, axis=1, keepdims=True) - hat * jnp.mean(prod, axis=1, keepdims=True)
        inv = jnp.concatenate([invd[rows, :]] * 4, axis=1)
        res[k] = win[w, :, D0 : D0 + C] + inv * mid
        return carry

    lax.fori_loop(0, SLOTS // 3, by_three(norm_back), 0)
    out_copies.append(window_back(1, D0))
    for copy in copies:
        copy.wait_recv()
    acc = smy[0]
    for j in range(1, 2 * ny):
        acc = acc + smy[j]
    sma[...] = acc
    copy = send(sma, smx, ss.at[2 * ny - 1], sr.at[2 * ny - 1], xpeer)
    last = last_send(st)
    for c in GROUPS[0]:
        chunk_z(c, st[c])
    group0 = group_send(0)
    finish(0, out_copies[0], upd)
    stores[0].start()
    copy.wait_recv()
    smz[z] = sma[...] + smx[...]
    copies = [
        send(smz.at[z], smz.at[z], ss.at[2 * ny + d - 1], sr.at[2 * ny + d - 1], zpeer[d - 1]) for d in range(1, nz)
    ]
    group_end(0, group0)
    finish(1, out_copies[1], gin)
    stores[1].start()
    last_end(last)
    for copy in copies:
        copy.wait_recv()
    acc = smz[0]
    for j in range(1, nz):
        acc = acc + smz[j]
    bias_out[...] = acc[:, 0:REL]
    for j in range(4):
        gain_out[:, 128 * j : 128 * j + 128] = acc[j : j + 1, 256:384]
    for store in stores[2:]:
        store.start()
    for copy in sends:
        copy.wait_send()
    for store in stores:
        store.wait()


def hand_over(*refs):
    arrived, left = refs[18:20]
    steps = []
    for i in range(6):
        rows = refs[i].shape[0]
        size = 3 if i < 2 else rows
        steps += [(i, pl.ds(start, size)) for start in range(0, rows, size)]
    fetches = [
        pltpu.make_async_copy(refs[i].at[at], refs[12 + i].at[at], arrived.at[n]) for n, (i, at) in enumerate(steps)
    ]
    stores = [
        pltpu.make_async_copy(refs[12 + i].at[at], refs[6 + i].at[at], left.at[n]) for n, (i, at) in enumerate(steps)
    ]
    for fetch in fetches:
        fetch.start()
    for fetch, store in zip(fetches, stores):
        fetch.wait()
        store.start()
    for store in stores:
        store.wait()


def constants(ny, nx, nz):
    share = C // (ny * nx * nz * 2)
    perm = np.zeros((C, C), np.float32)
    for core in range(2):
        for y in range(ny):
            for xh in range(nx):
                for z in range(nz):
                    to = (((core * ny + y) * nx + xh) * nz + z) * share
                    start = (((y * nx + xh) * nz + z) * 2 + core) * share
                    perm[to + np.arange(share), start + np.arange(share)] = 1
    a = np.arange(T)
    pa = (a // WIN_LON) * (2 * WIN_LON - 1) + a % WIN_LON
    selrt = np.zeros((128, 128), np.float32)
    selrt[126 - pa, a] = 1
    self_ = np.zeros((128, 128), np.float32)
    self_[a, pa] = 1
    return perm, self_, self_.T, selrt


def solution(mesh):
    nlon, nlat = mesh.shape["lon"], mesh.shape["lat"]
    nx, nz = 2, nlat // 2
    ny = nlon // nx
    nxz = nx * nz
    half = C // 2
    ysz = half // ny
    share = ysz // nxz
    cols = [C] + [384] * PAIRS
    lat_dev, lon_dev = 18, 48
    nwin = 12
    vm = pltpu.VMEM
    dma = lambda *s: pltpu.SemaphoreType.DMA(s)
    perm, self_, selft, selrt = (jnp.asarray(v, BF16) for v in constants(ny, nx, nz))

    def on_device(fields, grad_out, layernorm_gain, qkv_weight, proj_weight, bias_table, sea_mask):
        shapes = (
            jax.ShapeDtypeStruct((lat_dev, lon_dev, C), BF16),
            jax.ShapeDtypeStruct((lat_dev, lon_dev, C), BF16),
            jax.ShapeDtypeStruct((1, C), F32),
            jax.ShapeDtypeStruct((HEADS, REL), F32),
            jax.ShapeDtypeStruct((share, 3 * C), F32),
            jax.ShapeDtypeStruct((share, C), F32),
        )
        scratch = [
            vm((lat_dev, lon_dev, C), BF16),
            vm((lat_dev, lon_dev), jnp.int32),
            vm((lat_dev, lon_dev, C), BF16),
            vm((HEADS, REL), F32),
            vm((128, 128), BF16),
            vm((128, 128), BF16),
            vm((128, 128), BF16),
            vm((1, C), F32),
            vm((C, 3 * C), BF16),
            vm((C, C), BF16),
            vm((C, C), BF16),
        ]
        scratch += [vm(v.shape, v.dtype) for v in shapes]
        scratch += [
            vm((lat_dev + 3, 56, FW), F32),
            vm((nwin, TP, FW), F32),
            vm((112, FW), F32),
        ]
        for wide in (C, C):
            scratch += [
                vm((112, wide), BF16),
                vm((112, wide), BF16),
                vm((3, lon_dev, wide), BF16),
                vm((32, wide), BF16),
            ]
        scratch += [vm((lat_dev, lon_dev), jnp.int32)] * 3
        scratch += [
            pltpu.SMEM((16,), jnp.int32),
            vm((HEADS, 256), F32),
            vm((PAIRS, TP, 256), F32),
            vm((SLOTS, TP, 128), F32),
            vm((ROWS, C), F32),
            vm((ROWS, 128), F32),
            vm((RP, C), BF16),
            vm((RP, C), BF16),
            vm((ROWS, C), BF16),
            vm((ROWS, 3 * C), BF16),
            vm((RP, C), BF16),
            vm((C, RP), BF16),
            vm((C, RP), BF16),
            vm((SLOTS * PAIRS, TP, 256), F32),
            vm((RP, 3 * C), BF16),
            vm((ROWS, C), F32),
            vm((PAIRS, TP, 256), F32),
            vm((C, 3 * C), BF16),
            vm((C, 128), F32),
            vm((SLOTS, TP, C), F32),
            vm((2, lat_dev + 3, 56, C), F32),
            vm((2, 96, C), BF16),
            vm((2, 3, lon_dev, C), BF16),
            vm((2, 16, C + 128), BF16),
            vm((2, 96, C), BF16),
            vm((2, 3, lon_dev, C), BF16),
            vm((2, 16, C + 128), BF16),
        ]
        for n in cols:
            scratch += [
                vm((half, n), BF16),
                vm((half, n), BF16),
                vm((half, n), F32),
                vm((half, n), BF16),
                vm((ny - 1, ysz, n), BF16),
                vm((ysz // 2, n), BF16),
                vm((ysz // 2, n), BF16),
                vm((ysz // 2, n), F32),
            ]
        for members in GROUPS:
            rows = -(-share * sum(cols[c] // 128 for c in members) // 16) * 16
            scratch += [vm((nz, rows, 128), F32), vm((nz, rows, 128), BF16), vm((nz - 1, rows, 128), BF16)]
        rows = -(-share * sum(cols[c] // 128 for c in LAST) // 16) * 16
        scratch += [vm((nxz, rows, 128), F32), vm((nxz, rows, 128), BF16), vm((nxz - 1, rows, 128), BF16)]
        sm = (8, 384)
        scratch += [vm((2 * ny,) + sm, F32), vm(sm, F32), vm(sm, F32), vm((nz,) + sm, F32)]
        nc = len(cols)
        small = 2 * ny + nz
        scratch += [
            dma(2, 3), dma(2, 3), dma(3), dma(3), dma(2, 3), dma(2, 3), dma(nc), dma(nc), dma(nc, ny - 1),
            dma(nc, ny - 1), dma(nc), dma(nc), dma(nc, nz - 1), dma(nc, nz - 1), dma(small), dma(small), dma(nxz - 1), dma(nxz - 1), dma(23), dma(6),
        ]
        anywhere = pl.BlockSpec(memory_space=pl.ANY)
        outs = pl.pallas_call(
            functools.partial(kernel, (ny, nx, nz), cols),
            out_shape=shapes,
            in_specs=[anywhere] * 11,
            out_specs=(anywhere,) * 6,
            scratch_shapes=scratch,
            compiler_params=pltpu.CompilerParams(
                collective_id=0, has_side_effects=True, vmem_limit_bytes=60 * 1024 * 1024
            ),
        )(
            fields, sea_mask, grad_out, bias_table, self_, selft, selrt,
            layernorm_gain.reshape(1, C), qkv_weight, proj_weight, perm,
        )
        outs = pl.pallas_call(
            hand_over,
            out_shape=shapes,
            in_specs=[anywhere] * 6,
            out_specs=(anywhere,) * 6,
            scratch_shapes=[vm(v.shape, v.dtype) for v in shapes] + [dma(16), dma(16)],
            compiler_params=pltpu.CompilerParams(vmem_limit_bytes=60 * 1024 * 1024),
        )(*outs)
        updated, grad_in, grad_gain, grad_bias, grad_qkv, grad_proj = outs
        return (updated, grad_in, grad_gain.reshape(C), grad_bias, grad_qkv, grad_proj)

    grid = P(("batch", "lat"), "lon", None)
    return jax.shard_map(
        on_device,
        mesh=mesh,
        in_specs=(grid, grid, P(), P(), P(), P(), P(("batch", "lat"), "lon")),
        out_specs=(
            grid,
            grid,
            P("batch"),
            P("batch", None),
            P(("batch", "lon", "lat"), None),
            P(("batch", "lon", "lat"), None),
        ),
        check_vma=False,
    )
```

```python
import functools

import jax
import jax.numpy as jnp
import numpy as np
from jax import lax
from jax.experimental import pallas as pl
from jax.experimental.pallas import tpu as pltpu
from jax.sharding import PartitionSpec as P

MESH = pl.DeviceIdType.MESH
F32 = jnp.float32
BF16 = jnp.bfloat16
C = 512
HEADS = 8
PAIRS = 4
WIN_LAT = 6
WIN_LON = 12
HALF_LAT = 3
HALF_LON = 6
T = 72
TP = 80
SLOTS = 9
ROWS = SLOTS * TP
RP = 768
REL = 253
X0, M0, D0, FW = 0, 512, 640, 1152
GROUPS = ((0, 1, 2), (3, 4))
EARLY = 3
EPS = 1e-5


def nn(a, b, **kw):
    return lax.dot_general(a, b, (((1,), (0,)), ((), ())), preferred_element_type=F32, **kw)


def nt(a, b, **kw):
    return lax.dot_general(a, b, (((1,), (1,)), ((), ())), preferred_element_type=F32, **kw)


def tn(a, b, **kw):
    return lax.dot_general(a, b, (((0,), (0,)), ((), ())), preferred_element_type=F32, **kw)


def pad_rows(v, rows):
    return jnp.concatenate([v, jnp.zeros((rows - v.shape[0], v.shape[1]), v.dtype)], axis=0)


def kernel(dims, cols, *refs):
    ny, nx, nz = dims
    nlon, nlat = ny * nx, 2 * nz
    nxz = nx * nz
    lat_dev, lon_dev = 18, 48
    wrows, wcols = lat_dev // WIN_LAT, lon_dev // WIN_LON
    nwin = wrows * wcols
    half = C // 2
    ysz = half // ny
    share = ysz // nxz
    nchunk = len(cols)

    it = iter(refs)
    take = lambda n=None: next(it) if n is None else [next(it) for _ in range(n)]
    given = take(11)
    results = take(6)
    held = take(11)
    x_ref, mask_ref, dy_ref, table, self_, selft, selrt, gain_ref, wqkv, wproj, perm = held
    staged = take(6)
    upd, gin, gain_out, bias_out, gqkv, gproj = staged
    frame, win, colf = take(3)
    halos = [take(4) for _ in range(2)]
    masks = take(3)
    idx = take()
    tb, bias2, madd, xhat, invd, normed, gz, gm, packed, mixed, ntp, mtp, probs, dp3, gnacc, bacc = take(16)
    res, of = take(2)
    ocs, ors, occs, ocr, orr, occ = take(6)
    chunks = [take(8) for _ in range(nchunk)]
    groups = [take(3) for _ in range(len(GROUPS))]
    sums = take(4)
    hs, hr, ms, mr, os_, or_, as_, ar, ys, yr, xs, xr, zs, zr, ss, sr = take(16)
    ins, outs = take(2)

    lon = lax.axis_index("lon")
    lat = lax.axis_index("lat")
    y, xh = lon // nx, lon % nx
    z, core = lat // 2, lat % 2

    def dev(a, b):
        return {"lon": a, "lat": b}

    partner = dev(lon, z * 2 + (1 - core))
    ypeer = [dev(((y + d) % ny) * nx + xh, lat) for d in range(1, ny)]
    xpeer = dev(y * nx + (1 - xh), lat)
    zpeer = [dev(lon, ((z + d) % nz) * 2 + core) for d in range(1, nz)]
    crossy = [dev(((y + d) % ny) * nx + xh, z * 2 + (1 - core)) for d in range(1, ny)]
    west, east = (lon + nlon - 1) % nlon, (lon + 1) % nlon
    north, south = (lat + nlat - 1) % nlat, (lat + 1) % nlat
    back = [dev(west, lat), dev(lon, north), dev(west, north)]
    forth = [dev(east, lat), dev(lon, south), dev(east, south)]

    barrier = pltpu.get_barrier_semaphore()
    everyone = [partner, xpeer] + ypeer + zpeer + crossy + back + forth
    for d in everyone:
        pl.semaphore_signal(barrier, inc=1, device_id=d, device_id_type=MESH)

    loads = [pltpu.make_async_copy(a, b, ins.at[i]) for i, (a, b) in enumerate(zip(given, held)) if i != 8]
    for p in range(PAIRS):
        for i in range(3):
            src = given[8].at[:, C * i + 128 * p : C * i + 128 * p + 128]
            dst = wqkv.at[:, 384 * p + 128 * i : 384 * p + 128 * i + 128]
            loads.append(pltpu.make_async_copy(src, dst, ins.at[11 + 3 * p + i]))
    for load in loads:
        load.start()

    stores = [pltpu.make_async_copy(a, b, outs.at[i]) for i, (a, b) in enumerate(zip(staged, results))]
    sends = []

    def send(src, dst, ssem, rsem, d):
        copy = pltpu.make_async_remote_copy(
            src_ref=src, dst_ref=dst, send_sem=ssem, recv_sem=rsem, device_id=d, device_id_type=MESH
        )
        copy.start()
        sends.append(copy)
        return copy

    lane_row = lax.broadcasted_iota(jnp.int32, (lat_dev, lat_dev * 128), 1) // 128
    pick = (lane_row == lax.broadcasted_iota(jnp.int32, (lat_dev, lat_dev * 128), 0)).astype(F32)

    def spread_mask(ref):
        return tn(ref[...].astype(F32), pick)

    colf[96:112, :] = jnp.zeros((16, FW), F32)

    def halo_send(h, block, source):
        colsend, colrecv, rowrecv, cornrecv = halos[h]
        for r in range(lat_dev):
            colf[6 * r : 6 * r + 6, 0:C] = block[r, 0:16, :].astype(F32)[0:HALF_LON]
        colsend[...] = colf[:, 0:C].astype(BF16)
        if h == 0:
            pl.semaphore_wait(barrier, len(everyone))
        return [
            send(colsend, colrecv, hs.at[h, 0], hr.at[h, 0], back[0]),
            send(source.at[0:HALF_LAT], rowrecv, hs.at[h, 1], hr.at[h, 1], back[1]),
            send(colsend.at[0:32], cornrecv, hs.at[h, 2], hr.at[h, 2], back[2]),
        ]

    def halo_land(h, lanes, copies):
        colsend, colrecv, rowrecv, cornrecv = halos[h]
        copies[1].wait_recv()
        for r in range(HALF_LAT):
            frame[lat_dev + r, 0:lon_dev, lanes] = rowrecv[r].astype(F32)
        copies[2].wait_recv()
        colf[0:32, lanes] = cornrecv[...].astype(F32)
        for r in range(HALF_LAT):
            frame[lat_dev + r, lon_dev : lon_dev + HALF_LON, lanes] = colf[6 * r : 6 * r + 6, lanes]
        copies[0].wait_recv()
        colf[:, lanes] = colrecv[...].astype(F32)
        for r in range(lat_dev):
            frame[r, lon_dev : lon_dev + HALF_LON, lanes] = colf[6 * r : 6 * r + 6, lanes]

    xlanes, dlanes = slice(X0, X0 + C), slice(D0, D0 + C)
    loads[0].wait()
    xcopies = halo_send(0, x_ref, given[0])
    loads[1].wait()
    mcopies = [send(mask_ref, masks[i], ms.at[i], mr.at[i], back[i]) for i in range(3)]
    loads[2].wait()
    dcopies = halo_send(1, dy_ref, given[2])
    sea = spread_mask(mask_ref)
    for r in range(lat_dev):
        frame[r, 0:lon_dev, X0 : X0 + C] = x_ref[r].astype(F32)
        frame[r, 0:lon_dev, M0 : M0 + 128] = sea[:, 128 * r : 128 * r + 128]
        frame[r, 0:lon_dev, D0 : D0 + C] = dy_ref[r].astype(F32)

    def pieces(v, n):
        out = []
        for i in range(n):
            part = v.astype(BF16)
            out.append(part)
            if i < n - 1:
                v = v - part.astype(F32)
        return out

    for load in loads[3:]:
        load.wait()
    tb[...] = jnp.zeros_like(tb)
    tb[:, 0:REL] = table[...]
    shifted = []
    for h in range(HEADS):
        line = jnp.broadcast_to(tb[h : h + 1, :], (128, 256))
        shifted.append(pltpu.roll(pltpu.roll(line, 2, 1), 128, 1, stride=1, stride_axis=0)[:, 0:128])
    by_query = sum(nn(v, selft[...]) for v in pieces(jnp.concatenate(shifted, axis=0), 3))
    by_query = jnp.concatenate([by_query[128 * h : 128 * h + 128] for h in range(HEADS)], axis=1)
    whole_bias = sum(nn(self_[0:TP, :], v) for v in pieces(by_query, 3))
    for p in range(PAIRS):
        bias2[p] = whole_bias[:, 256 * p : 256 * p + 256]

    for g in range(len(GROUPS)):
        groups[g][0][...] = jnp.zeros_like(groups[g][0])
    zero_tail = jnp.zeros((RP - ROWS, C), BF16)
    normed[ROWS:RP, :] = zero_tail
    gz[ROWS:RP, :] = zero_tail
    mixed[ROWS:RP, :] = zero_tail
    dp3[ROWS:RP, :] = jnp.zeros((RP - ROWS, 3 * C), BF16)
    for w in range(nwin):
        win[w, T:TP, :] = jnp.zeros((TP - T, FW), F32)

    def cut(w, lanes):
        wr, wc = w // wcols, w % wcols
        c0 = HALF_LON + WIN_LON * wc
        for i in range(WIN_LAT):
            win[w, WIN_LON * i : WIN_LON * i + WIN_LON, lanes] = frame[
                HALF_LAT + WIN_LAT * wr + i, c0 : c0 + WIN_LON, lanes
            ]

    def holds_sea(w):
        return (jnp.max(win[w, :, M0 : M0 + 128]) > 0.5).astype(jnp.int32)

    def ranks(flags, counted):
        total = jnp.int32(0)
        for f, c in zip(flags, counted):
            total = total + f * c
        out, on, off = [], jnp.int32(0), total
        for f, c in zip(flags, counted):
            out.append(jnp.where(f > 0, on, off))
            on = on + f * c
            off = off + (1 - f) * c
        return out

    def slot_window(k, places):
        slot = jnp.int32(0)
        for w, at in places:
            slot = slot + jnp.where(at == k, w, 0)
        idx[k] = slot

    inner = [w for w in range(nwin) if w // wcols < wrows - 1 and w % wcols < wcols - 1]
    outer = [w for w in range(nwin) if w not in inner]
    active = [None] * nwin
    place = [None] * nwin

    at_end = (lat == nlat - 1).astype(F32)
    gain = gain_ref[...]

    def rows_of(k):
        return pl.ds(pl.multiple_of(k * TP, TP), TP)

    def by_three(step):
        def body(i, carry):
            for j in range(3):
                carry = step(3 * i + j, carry)
            return carry

        return body

    def ln_step(k, carry):
        w = idx[k]
        x = win[w, :, X0 : X0 + C]
        mean = jnp.mean(x, axis=1, keepdims=True)
        xc = x - mean
        inv = lax.rsqrt(jnp.mean(xc * xc, axis=1, keepdims=True) + EPS)
        hat = xc * inv
        rows = rows_of(k)
        xhat[rows, :] = hat
        invd[rows, :] = jnp.broadcast_to(inv, (TP, 128))
        normed[rows, :] = (hat * gain).astype(BF16)
        keys = win[w, :, M0 : M0 + 128]
        side_b = lax.broadcasted_iota(jnp.int32, (TP, 128), 0) >= T // 2
        side_a = lax.broadcasted_iota(jnp.int32, (TP, 128), 1) >= T // 2
        apart = jnp.where(side_a != side_b, 1.0, 0.0)
        wrap = at_end * jnp.where(w >= nwin - wcols, 1.0, 0.0)
        madd[k] = (keys * (1.0 - apart * wrap) - 1.0) * 1e9
        return carry

    def dy_step(k, carry):
        w = idx[k]
        m = win[w, :, M0 : M0 + 128]
        gz[rows_of(k), :] = (win[w, :, D0 : D0 + C] * jnp.concatenate([m] * 4, axis=1)).astype(BF16)
        return carry

    lane = lax.broadcasted_iota(jnp.int32, (TP, 128), 1)
    low = lane < 64
    one_lo = jnp.where(low, 1.0, 0.0).astype(BF16)
    one_hi = jnp.where(low, 0.0, 1.0).astype(BF16)
    q_lo = jnp.where(low, 0.125, 0.0).astype(BF16)
    q_hi = jnp.where(low, 0.0, 0.125).astype(BF16)

    def both_heads(v, lo, hi):
        return jnp.concatenate([pad_rows(v * lo, 128), pad_rows(v * hi, 128)], axis=0)

    def own_head(v):
        return jnp.transpose(jnp.concatenate([v[0:64, 0:128], v[64:128, 128:256]], axis=0))[0:TP]

    def attend(i, carry):
        chains = [(3 * i + j, p) for j in range(3) for p in range(PAIRS)]
        scores = []
        for k, p in chains:
            rows = rows_of(k)
            q2 = both_heads(packed[rows, 384 * p : 384 * p + 128], q_lo, q_hi)
            add = madd[k]
            add2 = jnp.concatenate([add, add], axis=1)
            scores.append(nt(packed[rows, 384 * p + 128 : 384 * p + 256], q2) + bias2[p] + add2)
        mixes = []
        for (k, p), s in zip(chains, scores):
            e = jnp.exp(s - jnp.max(s, axis=0, keepdims=True))
            pr = e * (1.0 / jnp.sum(e, axis=0, keepdims=True))
            probs[k * PAIRS + p] = pr
            mixes.append(tn(packed[rows_of(k), 384 * p + 256 : 384 * p + 384], pr.astype(BF16)))
        for (k, p), mix in zip(chains, mixes):
            mixed[rows_of(k), 128 * p : 128 * p + 128] = own_head(mix).astype(BF16)
        return carry

    def forward(first, last):
        lax.fori_loop(first // 3, last // 3, by_three(ln_step), 0)
        rows = slice(first * TP, last * TP)
        packed[rows, :] = nn(normed[rows, :], wqkv[...]).astype(BF16)
        lax.fori_loop(first // 3, last // 3, attend, 0)

    for w in inner:
        cut(w, slice(0, FW))
        active[w] = holds_sea(w)
    inner_rank = ranks([active[w] for w in inner], [1] * len(inner))
    for k in range(EARLY):
        slot_window(k, list(zip(inner, inner_rank)))
    forward(0, EARLY)

    mlanes = slice(M0, M0 + 128)
    for copy in mcopies:
        copy.wait_recv()
    sea = spread_mask(masks[0])
    for r in range(lat_dev):
        frame[r, lon_dev : lon_dev + HALF_LON, mlanes] = sea[0:HALF_LON, 128 * r : 128 * r + 128]
    sea = spread_mask(masks[1])
    for r in range(HALF_LAT):
        frame[lat_dev + r, 0:lon_dev, mlanes] = sea[:, 128 * r : 128 * r + 128]
    sea = spread_mask(masks[2])
    for r in range(HALF_LAT):
        frame[lat_dev + r, lon_dev : lon_dev + HALF_LON, mlanes] = sea[0:HALF_LON, 128 * r : 128 * r + 128]
    halo_land(0, xlanes, xcopies)
    for w in outer:
        cut(w, slice(X0, M0 + 128))
        active[w] = holds_sea(w)
    rest = [jnp.int32(1)] * nwin
    for w, at in zip(inner, inner_rank):
        rest[w] = (at >= EARLY).astype(jnp.int32)
    late_rank = ranks(active, rest)
    for w in range(nwin):
        place[w] = late_rank[w] + EARLY
    for w, at in zip(inner, inner_rank):
        place[w] = jnp.where(at < EARLY, at, place[w])
    for k in range(EARLY, SLOTS):
        slot_window(k, list(enumerate(place)))
    forward(EARLY, SLOTS)

    def window_back(o, lane0):
        def place_window(w):
            wr, wc = w // wcols, w % wcols
            slot = jnp.minimum(place[w], SLOTS - 1)
            for i in range(WIN_LAT):
                c0 = HALF_LON + WIN_LON * wc
                at = slice(WIN_LON * i, WIN_LON * i + WIN_LON)
                of[o, HALF_LAT + WIN_LAT * wr + i, c0 : c0 + WIN_LON, :] = jnp.where(
                    place[w] < SLOTS, res[slot, at, :], win[w, at, lane0 : lane0 + C]
                )

        for w in range(nwin - wcols, nwin):
            place_window(w)
        for r in range(HALF_LAT):
            ors[o, r] = of[o, lat_dev + r, 0:lon_dev, :].astype(BF16)
        rows = send(ors.at[o], orr.at[o], os_.at[o, 1], or_.at[o, 1], forth[1])
        for r in range(HALF_LAT):
            colf[6 * r : 6 * r + 6, 0:C] = of[o, lat_dev + r, lon_dev : lon_dev + HALF_LON, :]
        colf[8:16, C : C + 128] = jnp.zeros((8, 128), F32)
        for j in range(8):
            colf[j : j + 1, C : C + 128] = colf[16 + j // 4 : 17 + j // 4, 128 * (j % 4) : 128 * (j % 4) + 128]
        occs[o] = colf[0:16, 0 : C + 128].astype(BF16)
        corner = send(occs.at[o], occ.at[o], os_.at[o, 2], or_.at[o, 2], forth[2])
        for w in range(wcols - 1, nwin - wcols, wcols):
            place_window(w)
        colf[88:96, 0:C] = jnp.zeros((8, C), F32)
        for r in range(HALF_LAT, lat_dev):
            at = 6 * (r - HALF_LAT)
            colf[at : at + 6, 0:C] = of[o, r, lon_dev : lon_dev + HALF_LON, :]
        ocs[o] = colf[0:96, 0:C].astype(BF16)
        copies = [send(ocs.at[o], ocr.at[o], os_.at[o, 0], or_.at[o, 0], forth[0]), rows, corner]
        for w in range(nwin - wcols):
            if w % wcols < wcols - 1:
                place_window(w)
        return copies

    def finish(o, copies, out):
        copies[1].wait_recv()
        for r in range(HALF_LAT):
            of[o, r, 0:lon_dev, :] = orr[o, r].astype(F32)
        copies[0].wait_recv()
        colf[0:96, 0:C] = ocr[o].astype(F32)
        for r in range(HALF_LAT, lat_dev):
            at = 6 * (r - HALF_LAT)
            of[o, r, 0:HALF_LON, :] = colf[at : at + 6, 0:C]
        copies[2].wait_recv()
        colf[0:16, 0 : C + 128] = occ[o].astype(F32)
        for j in range(8):
            colf[16 + j // 4 : 17 + j // 4, 128 * (j % 4) : 128 * (j % 4) + 128] = colf[j : j + 1, C : C + 128]
        for r in range(HALF_LAT):
            of[o, r, 0:HALF_LON, :] = colf[6 * r : 6 * r + 6, 0:C]
        for r in range(lat_dev):
            out[r] = of[o, r, 0:lon_dev, :].astype(BF16)

    gnacc[...] = nn(mixed[0:ROWS, :], wproj[...])

    def updated_step(k, carry):
        w = idx[k]
        m = win[w, :, M0 : M0 + 128]
        res[k] = win[w, :, X0 : X0 + C] + jnp.concatenate([m] * 4, axis=1) * gnacc[rows_of(k), :]
        return carry

    lax.fori_loop(0, SLOTS // 3, by_three(updated_step), 0)
    out_copies = [window_back(0, X0)]

    halo_land(1, dlanes, dcopies)
    for w in outer:
        cut(w, dlanes)
    lax.fori_loop(0, SLOTS // 3, by_three(dy_step), 0)
    gm[...] = nt(gz[0:ROWS, :], wproj[...]).astype(BF16)
    ntp[...] = nt(perm[...], normed[...]).astype(BF16)

    def chunk_start(c, lhs, rhs):
        asend, arecv, own = chunks[c][0:3]
        right = rhs[...] if c == 0 else rhs[:, 384 * (c - 1) : 384 * c]
        other = pl.ds(pl.multiple_of((1 - core) * half, half), half)
        mine = pl.ds(pl.multiple_of(core * half, half), half)
        asend[...] = nn(lhs[other, :], right).astype(BF16)
        copy = send(asend, arecv, as_.at[c], ar.at[c], partner)
        own[...] = nn(lhs[mine, :], right)
        return [copy]

    def chunk_y(c, copies):
        asend, arecv, own, ysend, yrecv = chunks[c][0:5]
        copies[0].wait_recv()
        s = own[...] + arecv[...].astype(F32)
        own[...] = s
        ysend[...] = s.astype(BF16)
        out = []
        for d in range(1, ny):
            start = pl.multiple_of(((y + d) % ny) * ysz, ysz)
            out.append(
                send(ysend.at[pl.ds(start, ysz)], yrecv.at[d - 1], ys.at[c, d - 1], yr.at[c, d - 1], ypeer[d - 1])
            )
        return out

    def chunk_x(c, copies):
        own, ysend, yrecv, xsend, xrecv, xown = chunks[c][2:8]
        s = own[pl.ds(pl.multiple_of(y * ysz, ysz), ysz), :]
        for d in range(1, ny):
            copies[d - 1].wait_recv()
            s = s + yrecv[d - 1].astype(F32)
        top, low_half = s[0 : ysz // 2], s[ysz // 2 : ysz]
        first = xh == 0
        xsend[...] = jnp.where(first, low_half, top).astype(BF16)
        xown[...] = jnp.where(first, top, low_half)
        return [send(xsend, xrecv, xs.at[c], xr.at[c], xpeer)]

    def blocks_before(c):
        g = next(i for i, members in enumerate(GROUPS) if c in members)
        return g, sum(cols[m] // 128 for m in GROUPS[g] if m < c)

    def chunk_z(c, copies):
        xsend, xrecv, xown = chunks[c][5:8]
        g, first = blocks_before(c)
        zown = groups[g][0]
        copies[0].wait_recv()
        s = xown[...] + xrecv[...].astype(F32)
        for j in range(nz):
            part = s[share * j : share * j + share]
            for q in range(cols[c] // 128):
                at = share * (first + q)
                zown[j, at : at + share, :] = part[:, 128 * q : 128 * q + 128]

    def group_send(g):
        zown, zsend, zrecv = groups[g]
        zsend[...] = zown[...].astype(BF16)
        return [
            send(zsend.at[(z + d) % nz], zrecv.at[d - 1], zs.at[g, d - 1], zr.at[g, d - 1], zpeer[d - 1])
            for d in range(1, nz)
        ]

    def group_end(g, copies):
        zown, zsend, zrecv = groups[g]
        s = zown[z]
        for i, copy in enumerate(copies):
            copy.wait_recv()
            s = s + zrecv[i].astype(F32)
        for c in GROUPS[g]:
            first = blocks_before(c)[1]
            for q in range(cols[c] // 128):
                at = share * (first + q)
                block = s[at : at + share]
                if c == 0:
                    gproj[:, 128 * q : 128 * q + 128] = block
                else:
                    gqkv[:, C * q + 128 * (c - 1) : C * q + 128 * c] = block

    mtp[...] = nt(perm[...], mixed[...]).astype(BF16)
    st = {}
    st[0] = chunk_start(0, mtp, gz)

    def backward(p):
        ks = list(range(SLOTS))
        d2s, dps = [], []
        for k in ks:
            rows = slice(TP * k, TP * k + TP)
            d2s.append(both_heads(gm[rows, 128 * p : 128 * p + 128], one_lo, one_hi))
            dps.append(nt(packed[rows, 384 * p + 256 : 384 * p + 384], d2s[-1]))
        dss, dvs = [], []
        for k in ks:
            pr = probs[k * PAIRS + p]
            t = pr * dps[k]
            dss.append(t - pr * jnp.sum(t, axis=0, keepdims=True))
            dvs.append(nn(pr.astype(BF16), d2s[k]))
        bacc[p] = functools.reduce(lambda a, b: a + b, dss)
        dqs = []
        for k in ks:
            rows = slice(TP * k, TP * k + TP)
            ds = dss[k].astype(BF16)
            q2 = both_heads(packed[rows, 384 * p : 384 * p + 128], q_lo, q_hi)
            dqs.append(tn(packed[rows, 384 * p + 128 : 384 * p + 256], ds))
            dp3[rows, 384 * p + 128 : 384 * p + 256] = nn(ds, q2).astype(BF16)
            dp3[rows, 384 * p + 256 : 384 * p + 384] = dvs[k].astype(BF16)
        for k in ks:
            dp3[TP * k : TP * k + TP, 384 * p : 384 * p + 128] = (own_head(dqs[k]) * 0.125).astype(BF16)

    for p in range(PAIRS):
        backward(p)
        st[p + 1] = chunk_start(p + 1, ntp, dp3)
        st[p] = chunk_y(p, st[p])
        if p >= 2:
            st[p - 2] = chunk_x(p - 2, st[p - 2])

    smy, sma, smx, smz = sums
    stacked = jnp.concatenate([bacc[h // 2, :, 128 * (h % 2) : 128 * (h % 2) + 128] for h in range(HEADS)], axis=0)
    by_place = sum(nn(v, self_[...]) for v in pieces(stacked, 2))
    by_place = jnp.concatenate([by_place[TP * h : TP * h + TP] for h in range(HEADS)], axis=1)
    spread = sum(nn(selrt[:, 0:TP], v) for v in pieces(by_place, 2))
    for h in range(HEADS):
        wide = jnp.concatenate([spread[:, 128 * h : 128 * h + 128], jnp.zeros((128, 128), F32)], axis=1)
        sums[0][core * ny + y, h : h + 1, 0:256] = jnp.sum(pltpu.roll(wide, 0, 1, stride=1, stride_axis=0), axis=0, keepdims=True)
    for part in range(2):
        rows = slice(part * ROWS // 2, (part + 1) * ROWS // 2)
        gnacc[rows, :] = nt(dp3[rows, :], wqkv[...])
        if part == 0:
            st[4] = chunk_y(4, st[4])
            st[2] = chunk_x(2, st[2])

    def norm_back(k, total):
        w = idx[k]
        rows = rows_of(k)
        gn = gnacc[rows, :]
        hat = xhat[rows, :]
        g = gn * gain
        prod = g * hat
        mid = g - jnp.mean(g, axis=1, keepdims=True) - hat * jnp.mean(prod, axis=1, keepdims=True)
        inv = jnp.concatenate([invd[rows, :]] * 4, axis=1)
        res[k] = win[w, :, D0 : D0 + C] + inv * mid
        return total + jnp.sum(gn * hat, axis=0, keepdims=True)

    gsum = lax.fori_loop(0, SLOTS // 3, by_three(norm_back), jnp.zeros((1, C), F32))
    slot = core * ny + y
    smy[slot, 4:8, 256:384] = jnp.zeros((4, 128), F32)
    for j in range(4):
        smy[slot, j : j + 1, 256:384] = gsum[:, 128 * j : 128 * j + 128]
    sm = smy.at[slot]
    copies = [
        send(sm, sm, ss.at[i], sr.at[i], to) for i, to in enumerate([partner] + ypeer + crossy)
    ]
    out_copies.append(window_back(1, D0))
    st[3] = chunk_x(3, st[3])
    chunk_z(0, st[0])
    chunk_z(1, st[1])
    st[4] = chunk_x(4, st[4])
    for copy in copies:
        copy.wait_recv()
    acc = smy[0]
    for j in range(1, 2 * ny):
        acc = acc + smy[j]
    sma[...] = acc
    copy = send(sma, smx, ss.at[2 * ny - 1], sr.at[2 * ny - 1], xpeer)
    chunk_z(2, st[2])
    group0 = group_send(0)
    finish(0, out_copies[0], upd)
    stores[0].start()
    chunk_z(3, st[3])
    chunk_z(4, st[4])
    group1 = group_send(1)
    copy.wait_recv()
    smz[z] = sma[...] + smx[...]
    copies = [
        send(smz.at[z], smz.at[z], ss.at[2 * ny + d - 1], sr.at[2 * ny + d - 1], zpeer[d - 1]) for d in range(1, nz)
    ]
    group_end(0, group0)
    finish(1, out_copies[1], gin)
    stores[1].start()
    group_end(1, group1)
    for copy in copies:
        copy.wait_recv()
    acc = smz[0]
    for j in range(1, nz):
        acc = acc + smz[j]
    bias_out[...] = acc[:, 0:REL]
    for j in range(4):
        gain_out[:, 128 * j : 128 * j + 128] = acc[j : j + 1, 256:384]
    for store in stores[2:]:
        store.start()
    for copy in sends:
        copy.wait_send()
    for store in stores:
        store.wait()


def hand_over(*refs):
    arrived, left = refs[18:20]
    steps = []
    for i in range(6):
        rows = refs[i].shape[0]
        size = 3 if i < 2 else rows
        steps += [(i, pl.ds(start, size)) for start in range(0, rows, size)]
    fetches = [
        pltpu.make_async_copy(refs[i].at[at], refs[12 + i].at[at], arrived.at[n]) for n, (i, at) in enumerate(steps)
    ]
    stores = [
        pltpu.make_async_copy(refs[12 + i].at[at], refs[6 + i].at[at], left.at[n]) for n, (i, at) in enumerate(steps)
    ]
    for fetch in fetches:
        fetch.start()
    for fetch, store in zip(fetches, stores):
        fetch.wait()
        store.start()
    for store in stores:
        store.wait()


def constants(ny, nx, nz):
    share = C // (ny * nx * nz * 2)
    perm = np.zeros((C, C), np.float32)
    for core in range(2):
        for y in range(ny):
            for xh in range(nx):
                for z in range(nz):
                    to = (((core * ny + y) * nx + xh) * nz + z) * share
                    start = (((y * nx + xh) * nz + z) * 2 + core) * share
                    perm[to + np.arange(share), start + np.arange(share)] = 1
    a = np.arange(T)
    pa = (a // WIN_LON) * (2 * WIN_LON - 1) + a % WIN_LON
    selrt = np.zeros((128, 128), np.float32)
    selrt[126 - pa, a] = 1
    self_ = np.zeros((128, 128), np.float32)
    self_[a, pa] = 1
    return perm, self_, self_.T, selrt


def solution(mesh):
    nlon, nlat = mesh.shape["lon"], mesh.shape["lat"]
    nx, nz = 2, nlat // 2
    ny = nlon // nx
    nxz = nx * nz
    half = C // 2
    ysz = half // ny
    share = ysz // nxz
    cols = [C] + [384] * PAIRS
    lat_dev, lon_dev = 18, 48
    nwin = 12
    vm = pltpu.VMEM
    dma = lambda *s: pltpu.SemaphoreType.DMA(s)
    perm, self_, selft, selrt = (jnp.asarray(v, BF16) for v in constants(ny, nx, nz))

    def on_device(fields, grad_out, layernorm_gain, qkv_weight, proj_weight, bias_table, sea_mask):
        shapes = (
            jax.ShapeDtypeStruct((lat_dev, lon_dev, C), BF16),
            jax.ShapeDtypeStruct((lat_dev, lon_dev, C), BF16),
            jax.ShapeDtypeStruct((1, C), F32),
            jax.ShapeDtypeStruct((HEADS, REL), F32),
            jax.ShapeDtypeStruct((share, 3 * C), F32),
            jax.ShapeDtypeStruct((share, C), F32),
        )
        scratch = [
            vm((lat_dev, lon_dev, C), BF16),
            vm((lat_dev, lon_dev), jnp.int32),
            vm((lat_dev, lon_dev, C), BF16),
            vm((HEADS, REL), F32),
            vm((128, 128), BF16),
            vm((128, 128), BF16),
            vm((128, 128), BF16),
            vm((1, C), F32),
            vm((C, 3 * C), BF16),
            vm((C, C), BF16),
            vm((C, C), BF16),
        ]
        scratch += [vm(v.shape, v.dtype) for v in shapes]
        scratch += [
            vm((lat_dev + 3, 56, FW), F32),
            vm((nwin, TP, FW), F32),
            vm((112, FW), F32),
        ]
        for wide in (C, C):
            scratch += [
                vm((112, wide), BF16),
                vm((112, wide), BF16),
                vm((3, lon_dev, wide), BF16),
                vm((32, wide), BF16),
            ]
        scratch += [vm((lat_dev, lon_dev), jnp.int32)] * 3
        scratch += [
            pltpu.SMEM((16,), jnp.int32),
            vm((HEADS, 256), F32),
            vm((PAIRS, TP, 256), F32),
            vm((SLOTS, TP, 128), F32),
            vm((ROWS, C), F32),
            vm((ROWS, 128), F32),
            vm((RP, C), BF16),
            vm((RP, C), BF16),
            vm((ROWS, C), BF16),
            vm((ROWS, 3 * C), BF16),
            vm((RP, C), BF16),
            vm((C, RP), BF16),
            vm((C, RP), BF16),
            vm((SLOTS * PAIRS, TP, 256), F32),
            vm((RP, 3 * C), BF16),
            vm((ROWS, C), F32),
            vm((PAIRS, TP, 256), F32),
            vm((SLOTS, TP, C), F32),
            vm((2, lat_dev + 3, 56, C), F32),
            vm((2, 96, C), BF16),
            vm((2, 3, lon_dev, C), BF16),
            vm((2, 16, C + 128), BF16),
            vm((2, 96, C), BF16),
            vm((2, 3, lon_dev, C), BF16),
            vm((2, 16, C + 128), BF16),
        ]
        for n in cols:
            scratch += [
                vm((half, n), BF16),
                vm((half, n), BF16),
                vm((half, n), F32),
                vm((half, n), BF16),
                vm((ny - 1, ysz, n), BF16),
                vm((ysz // 2, n), BF16),
                vm((ysz // 2, n), BF16),
                vm((ysz // 2, n), F32),
            ]
        for members in GROUPS:
            rows = -(-share * sum(cols[c] // 128 for c in members) // 16) * 16
            scratch += [vm((nz, rows, 128), F32), vm((nz, rows, 128), BF16), vm((nz - 1, rows, 128), BF16)]
        sm = (8, 384)
        scratch += [vm((2 * ny,) + sm, F32), vm(sm, F32), vm(sm, F32), vm((nz,) + sm, F32)]
        nc = len(cols)
        small = 2 * ny + nz
        scratch += [
            dma(2, 3), dma(2, 3), dma(3), dma(3), dma(2, 3), dma(2, 3), dma(nc), dma(nc), dma(nc, ny - 1),
            dma(nc, ny - 1), dma(nc), dma(nc), dma(nc, nz - 1), dma(nc, nz - 1), dma(small), dma(small), dma(23), dma(6),
        ]
        anywhere = pl.BlockSpec(memory_space=pl.ANY)
        outs = pl.pallas_call(
            functools.partial(kernel, (ny, nx, nz), cols),
            out_shape=shapes,
            in_specs=[anywhere] * 11,
            out_specs=(anywhere,) * 6,
            scratch_shapes=scratch,
            compiler_params=pltpu.CompilerParams(
                collective_id=0, has_side_effects=True, vmem_limit_bytes=60 * 1024 * 1024
            ),
        )(
            fields, sea_mask, grad_out, bias_table, self_, selft, selrt,
            layernorm_gain.reshape(1, C), qkv_weight, proj_weight, perm,
        )
        outs = pl.pallas_call(
            hand_over,
            out_shape=shapes,
            in_specs=[anywhere] * 6,
            out_specs=(anywhere,) * 6,
            scratch_shapes=[vm(v.shape, v.dtype) for v in shapes] + [dma(16), dma(16)],
            compiler_params=pltpu.CompilerParams(vmem_limit_bytes=60 * 1024 * 1024),
        )(*outs)
        updated, grad_in, grad_gain, grad_bias, grad_qkv, grad_proj = outs
        return (updated, grad_in, grad_gain.reshape(C), grad_bias, grad_qkv, grad_proj)

    grid = P(("batch", "lat"), "lon", None)
    return jax.shard_map(
        on_device,
        mesh=mesh,
        in_specs=(grid, grid, P(), P(), P(), P(), P(("batch", "lat"), "lon")),
        out_specs=(
            grid,
            grid,
            P("batch"),
            P("batch", None),
            P(("batch", "lon", "lat"), None),
            P(("batch", "lon", "lat"), None),
        ),
        check_vma=False,
    )
```

```python
import functools

import jax
import jax.numpy as jnp
import numpy as np
from jax import lax
from jax.experimental import pallas as pl
from jax.experimental.pallas import tpu as pltpu
from jax.sharding import PartitionSpec as P

MESH = pl.DeviceIdType.MESH
F32 = jnp.float32
BF16 = jnp.bfloat16
C = 512
HEADS = 8
PAIRS = 4
WIN_LAT = 6
WIN_LON = 12
HALF_LAT = 3
HALF_LON = 6
T = 72
TP = 80
SLOTS = 9
ROWS = SLOTS * TP
RP = 768
REL = 253
X0, M0, D0, FW = 0, 512, 640, 1152
GROUPS = ((0, 1, 2), (3, 4))
EARLY = 3
EPS = 1e-5


def nn(a, b, **kw):
    return lax.dot_general(a, b, (((1,), (0,)), ((), ())), preferred_element_type=F32, **kw)


def nt(a, b, **kw):
    return lax.dot_general(a, b, (((1,), (1,)), ((), ())), preferred_element_type=F32, **kw)


def tn(a, b, **kw):
    return lax.dot_general(a, b, (((0,), (0,)), ((), ())), preferred_element_type=F32, **kw)


def pad_rows(v, rows):
    return jnp.concatenate([v, jnp.zeros((rows - v.shape[0], v.shape[1]), v.dtype)], axis=0)


def kernel(dims, cols, *refs):
    ny, nx, nz = dims
    nlon, nlat = ny * nx, 2 * nz
    nxz = nx * nz
    lat_dev, lon_dev = 18, 48
    wrows, wcols = lat_dev // WIN_LAT, lon_dev // WIN_LON
    nwin = wrows * wcols
    half = C // 2
    ysz = half // ny
    share = ysz // nxz
    nchunk = len(cols)

    it = iter(refs)
    take = lambda n=None: next(it) if n is None else [next(it) for _ in range(n)]
    given = take(11)
    results = take(6)
    held = take(11)
    x_ref, mask_ref, dy_ref, table, self_, selft, selrt, gain_ref, wqkv, wproj, perm = held
    staged = take(6)
    upd, gin, gain_out, bias_out, gqkv, gproj = staged
    frame, win, colf = take(3)
    halos = [take(4) for _ in range(2)]
    masks = take(3)
    idx = take()
    tb, bias2, madd, xhat, invd, normed, gz, gm, packed, mixed, ntp, mtp, probs, dp3, gnacc, bacc = take(16)
    res, of = take(2)
    ocs, ors, occs, ocr, orr, occ = take(6)
    chunks = [take(8) for _ in range(nchunk)]
    groups = [take(3) for _ in range(len(GROUPS))]
    sums = take(4)
    hs, hr, ms, mr, os_, or_, as_, ar, ys, yr, xs, xr, zs, zr, ss, sr = take(16)
    ins, outs = take(2)

    lon = lax.axis_index("lon")
    lat = lax.axis_index("lat")
    y, xh = lon // nx, lon % nx
    z, core = lat // 2, lat % 2

    def dev(a, b):
        return {"lon": a, "lat": b}

    partner = dev(lon, z * 2 + (1 - core))
    ypeer = [dev(((y + d) % ny) * nx + xh, lat) for d in range(1, ny)]
    xpeer = dev(y * nx + (1 - xh), lat)
    zpeer = [dev(lon, ((z + d) % nz) * 2 + core) for d in range(1, nz)]
    crossy = [dev(((y + d) % ny) * nx + xh, z * 2 + (1 - core)) for d in range(1, ny)]
    west, east = (lon + nlon - 1) % nlon, (lon + 1) % nlon
    north, south = (lat + nlat - 1) % nlat, (lat + 1) % nlat
    back = [dev(west, lat), dev(lon, north), dev(west, north)]
    forth = [dev(east, lat), dev(lon, south), dev(east, south)]

    loads = [pltpu.make_async_copy(a, b, ins.at[i]) for i, (a, b) in enumerate(zip(given, held)) if i != 8]
    for p in range(PAIRS):
        for i in range(3):
            src = given[8].at[:, C * i + 128 * p : C * i + 128 * p + 128]
            dst = wqkv.at[:, 384 * p + 128 * i : 384 * p + 128 * i + 128]
            loads.append(pltpu.make_async_copy(src, dst, ins.at[11 + 3 * p + i]))
    loads[0].start()
    barrier = pltpu.get_barrier_semaphore()
    everyone = back + forth + [partner, xpeer] + ypeer + zpeer + crossy
    for d in everyone:
        pl.semaphore_signal(barrier, inc=1, device_id=d, device_id_type=MESH)
    loads[1].start()
    loads[2].start()

    stores = [pltpu.make_async_copy(a, b, outs.at[i]) for i, (a, b) in enumerate(zip(staged, results))]
    sends = []

    def send(src, dst, ssem, rsem, d):
        copy = pltpu.make_async_remote_copy(
            src_ref=src, dst_ref=dst, send_sem=ssem, recv_sem=rsem, device_id=d, device_id_type=MESH
        )
        copy.start()
        sends.append(copy)
        return copy

    lane_row = lax.broadcasted_iota(jnp.int32, (lat_dev, lat_dev * 128), 1) // 128
    pick = (lane_row == lax.broadcasted_iota(jnp.int32, (lat_dev, lat_dev * 128), 0)).astype(F32)

    def spread_mask(ref):
        return tn(ref[...].astype(F32), pick)

    colf[96:112, :] = jnp.zeros((16, FW), F32)

    def halo_send(h, block, source):
        colsend, colrecv, rowrecv, cornrecv = halos[h]
        for r in range(lat_dev):
            colf[6 * r : 6 * r + 6, 0:C] = block[r, 0:16, :].astype(F32)[0:HALF_LON]
        colsend[...] = colf[:, 0:C].astype(BF16)
        if h == 0:
            pl.semaphore_wait(barrier, len(everyone))
        return [
            send(colsend, colrecv, hs.at[h, 0], hr.at[h, 0], back[0]),
            send(source.at[0:HALF_LAT], rowrecv, hs.at[h, 1], hr.at[h, 1], back[1]),
            send(colsend.at[0:32], cornrecv, hs.at[h, 2], hr.at[h, 2], back[2]),
        ]

    def halo_land(h, lanes, copies):
        colsend, colrecv, rowrecv, cornrecv = halos[h]
        copies[1].wait_recv()
        for r in range(HALF_LAT):
            frame[lat_dev + r, 0:lon_dev, lanes] = rowrecv[r].astype(F32)
        copies[2].wait_recv()
        colf[0:32, lanes] = cornrecv[...].astype(F32)
        for r in range(HALF_LAT):
            frame[lat_dev + r, lon_dev : lon_dev + HALF_LON, lanes] = colf[6 * r : 6 * r + 6, lanes]
        copies[0].wait_recv()
        colf[:, lanes] = colrecv[...].astype(F32)
        for r in range(lat_dev):
            frame[r, lon_dev : lon_dev + HALF_LON, lanes] = colf[6 * r : 6 * r + 6, lanes]

    xlanes, dlanes = slice(X0, X0 + C), slice(D0, D0 + C)
    loads[0].wait()
    xcopies = halo_send(0, x_ref, x_ref)
    loads[1].wait()
    mcopies = [send(mask_ref, masks[i], ms.at[i], mr.at[i], back[i]) for i in range(3)]
    for load in loads[3:]:
        load.start()
    loads[2].wait()
    dcopies = halo_send(1, dy_ref, dy_ref)
    sea = spread_mask(mask_ref)
    for r in range(lat_dev):
        frame[r, 0:lon_dev, X0 : X0 + C] = x_ref[r].astype(F32)
        frame[r, 0:lon_dev, M0 : M0 + 128] = sea[:, 128 * r : 128 * r + 128]
        frame[r, 0:lon_dev, D0 : D0 + C] = dy_ref[r].astype(F32)

    def pieces(v, n):
        out = []
        for i in range(n):
            part = v.astype(BF16)
            out.append(part)
            if i < n - 1:
                v = v - part.astype(F32)
        return out

    for load in loads[3:]:
        load.wait()
    tb[...] = jnp.zeros_like(tb)
    tb[:, 0:REL] = table[...]
    shifted = []
    for h in range(HEADS):
        line = jnp.broadcast_to(tb[h : h + 1, :], (128, 256))
        shifted.append(pltpu.roll(pltpu.roll(line, 2, 1), 128, 1, stride=1, stride_axis=0)[:, 0:128])
    by_query = sum(nn(v, selft[...]) for v in pieces(jnp.concatenate(shifted, axis=0), 3))
    by_query = jnp.concatenate([by_query[128 * h : 128 * h + 128] for h in range(HEADS)], axis=1)
    whole_bias = sum(nn(self_[0:TP, :], v) for v in pieces(by_query, 3))
    for p in range(PAIRS):
        bias2[p] = whole_bias[:, 256 * p : 256 * p + 256]

    for g in range(len(GROUPS)):
        groups[g][0][...] = jnp.zeros_like(groups[g][0])
    zero_tail = jnp.zeros((RP - ROWS, C), BF16)
    normed[ROWS:RP, :] = zero_tail
    gz[ROWS:RP, :] = zero_tail
    mixed[ROWS:RP, :] = zero_tail
    dp3[ROWS:RP, :] = jnp.zeros((RP - ROWS, 3 * C), BF16)
    for w in range(nwin):
        win[w, T:TP, :] = jnp.zeros((TP - T, FW), F32)

    def cut(w, lanes):
        wr, wc = w // wcols, w % wcols
        c0 = HALF_LON + WIN_LON * wc
        for i in range(WIN_LAT):
            win[w, WIN_LON * i : WIN_LON * i + WIN_LON, lanes] = frame[
                HALF_LAT + WIN_LAT * wr + i, c0 : c0 + WIN_LON, lanes
            ]

    def holds_sea(w):
        return (jnp.max(win[w, :, M0 : M0 + 128]) > 0.5).astype(jnp.int32)

    def ranks(flags, counted):
        total = jnp.int32(0)
        for f, c in zip(flags, counted):
            total = total + f * c
        out, on, off = [], jnp.int32(0), total
        for f, c in zip(flags, counted):
            out.append(jnp.where(f > 0, on, off))
            on = on + f * c
            off = off + (1 - f) * c
        return out

    def slot_window(k, places):
        slot = jnp.int32(0)
        for w, at in places:
            slot = slot + jnp.where(at == k, w, 0)
        idx[k] = slot

    inner = [w for w in range(nwin) if w // wcols < wrows - 1 and w % wcols < wcols - 1]
    outer = [w for w in range(nwin) if w not in inner]
    active = [None] * nwin
    place = [None] * nwin

    at_end = (lat == nlat - 1).astype(F32)
    gain = gain_ref[...]

    def rows_of(k):
        return pl.ds(pl.multiple_of(k * TP, TP), TP)

    def by_three(step):
        def body(i, carry):
            for j in range(3):
                carry = step(3 * i + j, carry)
            return carry

        return body

    def ln_step(k, carry):
        w = idx[k]
        x = win[w, :, X0 : X0 + C]
        mean = jnp.mean(x, axis=1, keepdims=True)
        xc = x - mean
        inv = lax.rsqrt(jnp.mean(xc * xc, axis=1, keepdims=True) + EPS)
        hat = xc * inv
        rows = rows_of(k)
        xhat[rows, :] = hat
        invd[rows, :] = jnp.broadcast_to(inv, (TP, 128))
        normed[rows, :] = (hat * gain).astype(BF16)
        keys = win[w, :, M0 : M0 + 128]
        side_b = lax.broadcasted_iota(jnp.int32, (TP, 128), 0) >= T // 2
        side_a = lax.broadcasted_iota(jnp.int32, (TP, 128), 1) >= T // 2
        apart = jnp.where(side_a != side_b, 1.0, 0.0)
        wrap = at_end * jnp.where(w >= nwin - wcols, 1.0, 0.0)
        madd[k] = (keys * (1.0 - apart * wrap) - 1.0) * 1e9
        return carry

    def dy_step(k, carry):
        w = idx[k]
        m = win[w, :, M0 : M0 + 128]
        gz[rows_of(k), :] = (win[w, :, D0 : D0 + C] * jnp.concatenate([m] * 4, axis=1)).astype(BF16)
        return carry

    lane = lax.broadcasted_iota(jnp.int32, (TP, 128), 1)
    low = lane < 64
    one_lo = jnp.where(low, 1.0, 0.0).astype(BF16)
    one_hi = jnp.where(low, 0.0, 1.0).astype(BF16)
    q_lo = jnp.where(low, 0.125, 0.0).astype(BF16)
    q_hi = jnp.where(low, 0.0, 0.125).astype(BF16)

    def both_heads(v, lo, hi):
        return jnp.concatenate([pad_rows(v * lo, 128), pad_rows(v * hi, 128)], axis=0)

    def own_head(v):
        return jnp.transpose(jnp.concatenate([v[0:64, 0:128], v[64:128, 128:256]], axis=0))[0:TP]

    def attend(i, carry):
        chains = [(3 * i + j, p) for j in range(3) for p in range(PAIRS)]
        scores = []
        for k, p in chains:
            rows = rows_of(k)
            q2 = both_heads(packed[rows, 384 * p : 384 * p + 128], q_lo, q_hi)
            add = madd[k]
            add2 = jnp.concatenate([add, add], axis=1)
            scores.append(nt(packed[rows, 384 * p + 128 : 384 * p + 256], q2) + bias2[p] + add2)
        mixes = []
        for (k, p), s in zip(chains, scores):
            e = jnp.exp(s - jnp.max(s, axis=0, keepdims=True))
            pr = e * (1.0 / jnp.sum(e, axis=0, keepdims=True))
            probs[k * PAIRS + p] = pr
            mixes.append(tn(packed[rows_of(k), 384 * p + 256 : 384 * p + 384], pr.astype(BF16)))
        for (k, p), mix in zip(chains, mixes):
            mixed[rows_of(k), 128 * p : 128 * p + 128] = own_head(mix).astype(BF16)
        return carry

    def forward(first, last):
        lax.fori_loop(first // 3, last // 3, by_three(ln_step), 0)
        rows = slice(first * TP, last * TP)
        packed[rows, :] = nn(normed[rows, :], wqkv[...]).astype(BF16)
        lax.fori_loop(first // 3, last // 3, attend, 0)

    for w in inner:
        cut(w, slice(0, FW))
        active[w] = holds_sea(w)
    inner_rank = ranks([active[w] for w in inner], [1] * len(inner))
    for k in range(EARLY):
        slot_window(k, list(zip(inner, inner_rank)))
    forward(0, EARLY)

    mlanes = slice(M0, M0 + 128)
    for copy in mcopies:
        copy.wait_recv()
    sea = spread_mask(masks[0])
    for r in range(lat_dev):
        frame[r, lon_dev : lon_dev + HALF_LON, mlanes] = sea[0:HALF_LON, 128 * r : 128 * r + 128]
    sea = spread_mask(masks[1])
    for r in range(HALF_LAT):
        frame[lat_dev + r, 0:lon_dev, mlanes] = sea[:, 128 * r : 128 * r + 128]
    sea = spread_mask(masks[2])
    for r in range(HALF_LAT):
        frame[lat_dev + r, lon_dev : lon_dev + HALF_LON, mlanes] = sea[0:HALF_LON, 128 * r : 128 * r + 128]
    halo_land(0, xlanes, xcopies)
    for w in outer:
        cut(w, slice(X0, M0 + 128))
        active[w] = holds_sea(w)
    rest = [jnp.int32(1)] * nwin
    for w, at in zip(inner, inner_rank):
        rest[w] = (at >= EARLY).astype(jnp.int32)
    late_rank = ranks(active, rest)
    for w in range(nwin):
        place[w] = late_rank[w] + EARLY
    for w, at in zip(inner, inner_rank):
        place[w] = jnp.where(at < EARLY, at, place[w])
    for k in range(EARLY, SLOTS):
        slot_window(k, list(enumerate(place)))
    forward(EARLY, SLOTS)

    def window_back(o, lane0):
        def place_window(w):
            wr, wc = w // wcols, w % wcols
            slot = jnp.minimum(place[w], SLOTS - 1)
            for i in range(WIN_LAT):
                c0 = HALF_LON + WIN_LON * wc
                at = slice(WIN_LON * i, WIN_LON * i + WIN_LON)
                of[o, HALF_LAT + WIN_LAT * wr + i, c0 : c0 + WIN_LON, :] = jnp.where(
                    place[w] < SLOTS, res[slot, at, :], win[w, at, lane0 : lane0 + C]
                )

        for w in range(nwin - wcols, nwin):
            place_window(w)
        for r in range(HALF_LAT):
            ors[o, r] = of[o, lat_dev + r, 0:lon_dev, :].astype(BF16)
        rows = send(ors.at[o], orr.at[o], os_.at[o, 1], or_.at[o, 1], forth[1])
        for r in range(HALF_LAT):
            colf[6 * r : 6 * r + 6, 0:C] = of[o, lat_dev + r, lon_dev : lon_dev + HALF_LON, :]
        colf[8:16, C : C + 128] = jnp.zeros((8, 128), F32)
        for j in range(8):
            colf[j : j + 1, C : C + 128] = colf[16 + j // 4 : 17 + j // 4, 128 * (j % 4) : 128 * (j % 4) + 128]
        occs[o] = colf[0:16, 0 : C + 128].astype(BF16)
        corner = send(occs.at[o], occ.at[o], os_.at[o, 2], or_.at[o, 2], forth[2])
        for w in range(wcols - 1, nwin - wcols, wcols):
            place_window(w)
        colf[88:96, 0:C] = jnp.zeros((8, C), F32)
        for r in range(HALF_LAT, lat_dev):
            at = 6 * (r - HALF_LAT)
            colf[at : at + 6, 0:C] = of[o, r, lon_dev : lon_dev + HALF_LON, :]
        ocs[o] = colf[0:96, 0:C].astype(BF16)
        copies = [send(ocs.at[o], ocr.at[o], os_.at[o, 0], or_.at[o, 0], forth[0]), rows, corner]
        for w in range(nwin - wcols):
            if w % wcols < wcols - 1:
                place_window(w)
        return copies

    def finish(o, copies, out):
        copies[1].wait_recv()
        for r in range(HALF_LAT):
            of[o, r, 0:lon_dev, :] = orr[o, r].astype(F32)
        copies[0].wait_recv()
        colf[0:96, 0:C] = ocr[o].astype(F32)
        for r in range(HALF_LAT, lat_dev):
            at = 6 * (r - HALF_LAT)
            of[o, r, 0:HALF_LON, :] = colf[at : at + 6, 0:C]
        copies[2].wait_recv()
        colf[0:16, 0 : C + 128] = occ[o].astype(F32)
        for j in range(8):
            colf[16 + j // 4 : 17 + j // 4, 128 * (j % 4) : 128 * (j % 4) + 128] = colf[j : j + 1, C : C + 128]
        for r in range(HALF_LAT):
            of[o, r, 0:HALF_LON, :] = colf[6 * r : 6 * r + 6, 0:C]
        for r in range(lat_dev):
            out[r] = of[o, r, 0:lon_dev, :].astype(BF16)

    gnacc[...] = nn(mixed[0:ROWS, :], wproj[...])

    def updated_step(k, carry):
        w = idx[k]
        m = win[w, :, M0 : M0 + 128]
        res[k] = win[w, :, X0 : X0 + C] + jnp.concatenate([m] * 4, axis=1) * gnacc[rows_of(k), :]
        return carry

    lax.fori_loop(0, SLOTS // 3, by_three(updated_step), 0)
    out_copies = [window_back(0, X0)]

    ntp[...] = nt(perm[...], normed[...]).astype(BF16)
    mtp[...] = nt(perm[...], mixed[...]).astype(BF16)
    halo_land(1, dlanes, dcopies)
    for w in outer:
        cut(w, dlanes)
    lax.fori_loop(0, SLOTS // 3, by_three(dy_step), 0)

    def chunk_start(c, lhs, rhs):
        asend, arecv, own = chunks[c][0:3]
        right = rhs[...] if c == 0 else rhs[:, 384 * (c - 1) : 384 * c]
        other = pl.ds(pl.multiple_of((1 - core) * half, half), half)
        mine = pl.ds(pl.multiple_of(core * half, half), half)
        asend[...] = nn(lhs[other, :], right).astype(BF16)
        copy = send(asend, arecv, as_.at[c], ar.at[c], partner)
        own[...] = nn(lhs[mine, :], right)
        return [copy]

    def chunk_y(c, copies):
        asend, arecv, own, ysend, yrecv = chunks[c][0:5]
        copies[0].wait_recv()
        s = own[...] + arecv[...].astype(F32)
        own[...] = s
        ysend[...] = s.astype(BF16)
        out = []
        for d in range(1, ny):
            start = pl.multiple_of(((y + d) % ny) * ysz, ysz)
            out.append(
                send(ysend.at[pl.ds(start, ysz)], yrecv.at[d - 1], ys.at[c, d - 1], yr.at[c, d - 1], ypeer[d - 1])
            )
        return out

    def chunk_x(c, copies):
        own, ysend, yrecv, xsend, xrecv, xown = chunks[c][2:8]
        s = own[pl.ds(pl.multiple_of(y * ysz, ysz), ysz), :]
        for d in range(1, ny):
            copies[d - 1].wait_recv()
            s = s + yrecv[d - 1].astype(F32)
        top, low_half = s[0 : ysz // 2], s[ysz // 2 : ysz]
        first = xh == 0
        xsend[...] = jnp.where(first, low_half, top).astype(BF16)
        xown[...] = jnp.where(first, top, low_half)
        return [send(xsend, xrecv, xs.at[c], xr.at[c], xpeer)]

    def blocks_before(c):
        g = next(i for i, members in enumerate(GROUPS) if c in members)
        return g, sum(cols[m] // 128 for m in GROUPS[g] if m < c)

    def chunk_z(c, copies):
        xsend, xrecv, xown = chunks[c][5:8]
        g, first = blocks_before(c)
        zown = groups[g][0]
        copies[0].wait_recv()
        s = xown[...] + xrecv[...].astype(F32)
        for j in range(nz):
            part = s[share * j : share * j + share]
            for q in range(cols[c] // 128):
                at = share * (first + q)
                zown[j, at : at + share, :] = part[:, 128 * q : 128 * q + 128]

    def group_send(g):
        zown, zsend, zrecv = groups[g]
        zsend[...] = zown[...].astype(BF16)
        return [
            send(zsend.at[(z + d) % nz], zrecv.at[d - 1], zs.at[g, d - 1], zr.at[g, d - 1], zpeer[d - 1])
            for d in range(1, nz)
        ]

    def group_end(g, copies):
        zown, zsend, zrecv = groups[g]
        s = zown[z]
        for i, copy in enumerate(copies):
            copy.wait_recv()
            s = s + zrecv[i].astype(F32)
        for c in GROUPS[g]:
            first = blocks_before(c)[1]
            for q in range(cols[c] // 128):
                at = share * (first + q)
                block = s[at : at + share]
                if c == 0:
                    gproj[:, 128 * q : 128 * q + 128] = block
                else:
                    gqkv[:, C * q + 128 * (c - 1) : C * q + 128 * c] = block

    st = {}
    st[0] = chunk_start(0, mtp, gz)
    gm[...] = nt(gz[0:ROWS, :], wproj[...]).astype(BF16)

    def backward(p):
        ks = list(range(SLOTS))
        d2s, dps = [], []
        for k in ks:
            rows = slice(TP * k, TP * k + TP)
            d2s.append(both_heads(gm[rows, 128 * p : 128 * p + 128], one_lo, one_hi))
            dps.append(nt(packed[rows, 384 * p + 256 : 384 * p + 384], d2s[-1]))
        dss, dvs = [], []
        for k in ks:
            pr = probs[k * PAIRS + p]
            t = pr * dps[k]
            dss.append(t - pr * jnp.sum(t, axis=0, keepdims=True))
            dvs.append(nn(pr.astype(BF16), d2s[k]))
        bacc[p] = functools.reduce(lambda a, b: a + b, dss)
        dqs = []
        for k in ks:
            rows = slice(TP * k, TP * k + TP)
            ds = dss[k].astype(BF16)
            q2 = both_heads(packed[rows, 384 * p : 384 * p + 128], q_lo, q_hi)
            dqs.append(tn(packed[rows, 384 * p + 128 : 384 * p + 256], ds))
            dp3[rows, 384 * p + 128 : 384 * p + 256] = nn(ds, q2).astype(BF16)
            dp3[rows, 384 * p + 256 : 384 * p + 384] = dvs[k].astype(BF16)
        for k in ks:
            dp3[TP * k : TP * k + TP, 384 * p : 384 * p + 128] = (own_head(dqs[k]) * 0.125).astype(BF16)

    for p in range(PAIRS):
        backward(p)
        st[p] = chunk_y(p, st[p])
        st[p + 1] = chunk_start(p + 1, ntp, dp3)
        if p >= 2:
            st[p - 2] = chunk_x(p - 2, st[p - 2])

    smy, sma, smx, smz = sums
    stacked = jnp.concatenate([bacc[h // 2, :, 128 * (h % 2) : 128 * (h % 2) + 128] for h in range(HEADS)], axis=0)
    by_place = sum(nn(v, self_[...]) for v in pieces(stacked, 2))
    by_place = jnp.concatenate([by_place[TP * h : TP * h + TP] for h in range(HEADS)], axis=1)
    spread = sum(nn(selrt[:, 0:TP], v) for v in pieces(by_place, 2))
    for h in range(HEADS):
        wide = jnp.concatenate([spread[:, 128 * h : 128 * h + 128], jnp.zeros((128, 128), F32)], axis=1)
        sums[0][core * ny + y, h : h + 1, 0:256] = jnp.sum(pltpu.roll(wide, 0, 1, stride=1, stride_axis=0), axis=0, keepdims=True)
    for part in range(2):
        rows = slice(part * ROWS // 2, (part + 1) * ROWS // 2)
        gnacc[rows, :] = nt(dp3[rows, :], wqkv[...])
        if part == 0:
            st[4] = chunk_y(4, st[4])
            st[2] = chunk_x(2, st[2])

    def norm_back(k, total):
        w = idx[k]
        rows = rows_of(k)
        gn = gnacc[rows, :]
        hat = xhat[rows, :]
        g = gn * gain
        prod = g * hat
        mid = g - jnp.mean(g, axis=1, keepdims=True) - hat * jnp.mean(prod, axis=1, keepdims=True)
        inv = jnp.concatenate([invd[rows, :]] * 4, axis=1)
        res[k] = win[w, :, D0 : D0 + C] + inv * mid
        return total + jnp.sum(gn * hat, axis=0, keepdims=True)

    gsum = lax.fori_loop(0, SLOTS // 3, by_three(norm_back), jnp.zeros((1, C), F32))
    slot = core * ny + y
    smy[slot, 4:8, 256:384] = jnp.zeros((4, 128), F32)
    for j in range(4):
        smy[slot, j : j + 1, 256:384] = gsum[:, 128 * j : 128 * j + 128]
    sm = smy.at[slot]
    copies = [
        send(sm, sm, ss.at[i], sr.at[i], to) for i, to in enumerate([partner] + ypeer + crossy)
    ]
    out_copies.append(window_back(1, D0))
    st[3] = chunk_x(3, st[3])
    chunk_z(0, st[0])
    chunk_z(1, st[1])
    st[4] = chunk_x(4, st[4])
    for copy in copies:
        copy.wait_recv()
    acc = smy[0]
    for j in range(1, 2 * ny):
        acc = acc + smy[j]
    sma[...] = acc
    copy = send(sma, smx, ss.at[2 * ny - 1], sr.at[2 * ny - 1], xpeer)
    chunk_z(2, st[2])
    group0 = group_send(0)
    finish(0, out_copies[0], upd)
    stores[0].start()
    chunk_z(3, st[3])
    chunk_z(4, st[4])
    group1 = group_send(1)
    copy.wait_recv()
    smz[z] = sma[...] + smx[...]
    copies = [
        send(smz.at[z], smz.at[z], ss.at[2 * ny + d - 1], sr.at[2 * ny + d - 1], zpeer[d - 1]) for d in range(1, nz)
    ]
    group_end(0, group0)
    finish(1, out_copies[1], gin)
    stores[1].start()
    group_end(1, group1)
    for copy in copies:
        copy.wait_recv()
    acc = smz[0]
    for j in range(1, nz):
        acc = acc + smz[j]
    bias_out[...] = acc[:, 0:REL]
    for j in range(4):
        gain_out[:, 128 * j : 128 * j + 128] = acc[j : j + 1, 256:384]
    for store in stores[2:]:
        store.start()
    for copy in sends:
        copy.wait_send()
    for store in stores:
        store.wait()


def hand_over(*refs):
    arrived, left = refs[18:20]
    steps = []
    for i in range(6):
        rows = refs[i].shape[0]
        size = 3 if i < 2 else rows
        steps += [(i, pl.ds(start, size)) for start in range(0, rows, size)]
    fetches = [
        pltpu.make_async_copy(refs[i].at[at], refs[12 + i].at[at], arrived.at[n]) for n, (i, at) in enumerate(steps)
    ]
    stores = [
        pltpu.make_async_copy(refs[12 + i].at[at], refs[6 + i].at[at], left.at[n]) for n, (i, at) in enumerate(steps)
    ]
    for fetch in fetches:
        fetch.start()
    for fetch, store in zip(fetches, stores):
        fetch.wait()
        store.start()
    for store in stores:
        store.wait()


def constants(ny, nx, nz):
    share = C // (ny * nx * nz * 2)
    perm = np.zeros((C, C), np.float32)
    for core in range(2):
        for y in range(ny):
            for xh in range(nx):
                for z in range(nz):
                    to = (((core * ny + y) * nx + xh) * nz + z) * share
                    start = (((y * nx + xh) * nz + z) * 2 + core) * share
                    perm[to + np.arange(share), start + np.arange(share)] = 1
    a = np.arange(T)
    pa = (a // WIN_LON) * (2 * WIN_LON - 1) + a % WIN_LON
    selrt = np.zeros((128, 128), np.float32)
    selrt[126 - pa, a] = 1
    self_ = np.zeros((128, 128), np.float32)
    self_[a, pa] = 1
    return perm, self_, self_.T, selrt


def solution(mesh):
    nlon, nlat = mesh.shape["lon"], mesh.shape["lat"]
    nx, nz = 2, nlat // 2
    ny = nlon // nx
    nxz = nx * nz
    half = C // 2
    ysz = half // ny
    share = ysz // nxz
    cols = [C] + [384] * PAIRS
    lat_dev, lon_dev = 18, 48
    nwin = 12
    vm = pltpu.VMEM
    dma = lambda *s: pltpu.SemaphoreType.DMA(s)
    perm, self_, selft, selrt = (jnp.asarray(v, BF16) for v in constants(ny, nx, nz))

    def on_device(fields, grad_out, layernorm_gain, qkv_weight, proj_weight, bias_table, sea_mask):
        shapes = (
            jax.ShapeDtypeStruct((lat_dev, lon_dev, C), BF16),
            jax.ShapeDtypeStruct((lat_dev, lon_dev, C), BF16),
            jax.ShapeDtypeStruct((1, C), F32),
            jax.ShapeDtypeStruct((HEADS, REL), F32),
            jax.ShapeDtypeStruct((share, 3 * C), F32),
            jax.ShapeDtypeStruct((share, C), F32),
        )
        scratch = [
            vm((lat_dev, lon_dev, C), BF16),
            vm((lat_dev, lon_dev), jnp.int32),
            vm((lat_dev, lon_dev, C), BF16),
            vm((HEADS, REL), F32),
            vm((128, 128), BF16),
            vm((128, 128), BF16),
            vm((128, 128), BF16),
            vm((1, C), F32),
            vm((C, 3 * C), BF16),
            vm((C, C), BF16),
            vm((C, C), BF16),
        ]
        scratch += [vm(v.shape, v.dtype) for v in shapes]
        scratch += [
            vm((lat_dev + 3, 56, FW), F32),
            vm((nwin, TP, FW), F32),
            vm((112, FW), F32),
        ]
        for wide in (C, C):
            scratch += [
                vm((112, wide), BF16),
                vm((112, wide), BF16),
                vm((3, lon_dev, wide), BF16),
                vm((32, wide), BF16),
            ]
        scratch += [vm((lat_dev, lon_dev), jnp.int32)] * 3
        scratch += [
            pltpu.SMEM((16,), jnp.int32),
            vm((HEADS, 256), F32),
            vm((PAIRS, TP, 256), F32),
            vm((SLOTS, TP, 128), F32),
            vm((ROWS, C), F32),
            vm((ROWS, 128), F32),
            vm((RP, C), BF16),
            vm((RP, C), BF16),
            vm((ROWS, C), BF16),
            vm((ROWS, 3 * C), BF16),
            vm((RP, C), BF16),
            vm((C, RP), BF16),
            vm((C, RP), BF16),
            vm((SLOTS * PAIRS, TP, 256), F32),
            vm((RP, 3 * C), BF16),
            vm((ROWS, C), F32),
            vm((PAIRS, TP, 256), F32),
            vm((SLOTS, TP, C), F32),
            vm((2, lat_dev + 3, 56, C), F32),
            vm((2, 96, C), BF16),
            vm((2, 3, lon_dev, C), BF16),
            vm((2, 16, C + 128), BF16),
            vm((2, 96, C), BF16),
            vm((2, 3, lon_dev, C), BF16),
            vm((2, 16, C + 128), BF16),
        ]
        for n in cols:
            scratch += [
                vm((half, n), BF16),
                vm((half, n), BF16),
                vm((half, n), F32),
                vm((half, n), BF16),
                vm((ny - 1, ysz, n), BF16),
                vm((ysz // 2, n), BF16),
                vm((ysz // 2, n), BF16),
                vm((ysz // 2, n), F32),
            ]
        for members in GROUPS:
            rows = -(-share * sum(cols[c] // 128 for c in members) // 16) * 16
            scratch += [vm((nz, rows, 128), F32), vm((nz, rows, 128), BF16), vm((nz - 1, rows, 128), BF16)]
        sm = (8, 384)
        scratch += [vm((2 * ny,) + sm, F32), vm(sm, F32), vm(sm, F32), vm((nz,) + sm, F32)]
        nc = len(cols)
        small = 2 * ny + nz
        scratch += [
            dma(2, 3), dma(2, 3), dma(3), dma(3), dma(2, 3), dma(2, 3), dma(nc), dma(nc), dma(nc, ny - 1),
            dma(nc, ny - 1), dma(nc), dma(nc), dma(nc, nz - 1), dma(nc, nz - 1), dma(small), dma(small), dma(23), dma(6),
        ]
        anywhere = pl.BlockSpec(memory_space=pl.ANY)
        outs = pl.pallas_call(
            functools.partial(kernel, (ny, nx, nz), cols),
            out_shape=shapes,
            in_specs=[anywhere] * 11,
            out_specs=(anywhere,) * 6,
            scratch_shapes=scratch,
            compiler_params=pltpu.CompilerParams(
                collective_id=0, has_side_effects=True, vmem_limit_bytes=60 * 1024 * 1024
            ),
        )(
            fields, sea_mask, grad_out, bias_table, self_, selft, selrt,
            layernorm_gain.reshape(1, C), qkv_weight, proj_weight, perm,
        )
        outs = pl.pallas_call(
            hand_over,
            out_shape=shapes,
            in_specs=[anywhere] * 6,
            out_specs=(anywhere,) * 6,
            scratch_shapes=[vm(v.shape, v.dtype) for v in shapes] + [dma(16), dma(16)],
            compiler_params=pltpu.CompilerParams(vmem_limit_bytes=60 * 1024 * 1024),
        )(*outs)
        updated, grad_in, grad_gain, grad_bias, grad_qkv, grad_proj = outs
        return (updated, grad_in, grad_gain.reshape(C), grad_bias, grad_qkv, grad_proj)

    grid = P(("batch", "lat"), "lon", None)
    return jax.shard_map(
        on_device,
        mesh=mesh,
        in_specs=(grid, grid, P(), P(), P(), P(), P(("batch", "lat"), "lon")),
        out_specs=(
            grid,
            grid,
            P("batch"),
            P("batch", None),
            P(("batch", "lon", "lat"), None),
            P(("batch", "lon", "lat"), None),
        ),
        check_vma=False,
    )
```

```python
import functools

import jax
import jax.numpy as jnp
import numpy as np
from jax import lax
from jax.experimental import pallas as pl
from jax.experimental.pallas import tpu as pltpu
from jax.sharding import PartitionSpec as P

MESH = pl.DeviceIdType.MESH
F32 = jnp.float32
BF16 = jnp.bfloat16
C = 512
HEADS = 8
PAIRS = 4
WIN_LAT = 6
WIN_LON = 12
HALF_LAT = 3
HALF_LON = 6
T = 72
TP = 80
SLOTS = 9
ROWS = SLOTS * TP
RP = 768
REL = 253
X0, M0, D0, FW = 0, 512, 640, 1152
GROUPS = ((0, 1, 2), (3, 4))
EARLY = 3
EPS = 1e-5


def nn(a, b, **kw):
    return lax.dot_general(a, b, (((1,), (0,)), ((), ())), preferred_element_type=F32, **kw)


def nt(a, b, **kw):
    return lax.dot_general(a, b, (((1,), (1,)), ((), ())), preferred_element_type=F32, **kw)


def tn(a, b, **kw):
    return lax.dot_general(a, b, (((0,), (0,)), ((), ())), preferred_element_type=F32, **kw)


def pad_rows(v, rows):
    return jnp.concatenate([v, jnp.zeros((rows - v.shape[0], v.shape[1]), v.dtype)], axis=0)


def kernel(dims, cols, *refs):
    ny, nx, nz = dims
    nlon, nlat = ny * nx, 2 * nz
    nxz = nx * nz
    lat_dev, lon_dev = 18, 48
    wrows, wcols = lat_dev // WIN_LAT, lon_dev // WIN_LON
    nwin = wrows * wcols
    half = C // 2
    ysz = half // ny
    share = ysz // nxz
    nchunk = len(cols)

    it = iter(refs)
    take = lambda n=None: next(it) if n is None else [next(it) for _ in range(n)]
    given = take(11)
    results = take(6)
    held = take(11)
    x_ref, mask_ref, dy_ref, table, self_, selft, selrt, gain_ref, wqkv, wproj, perm = held
    staged = take(6)
    upd, gin, gain_out, bias_out, gqkv, gproj = staged
    frame, win, colf = take(3)
    halos = [take(4) for _ in range(2)]
    masks = take(3)
    idx = take()
    tb, bias2, madd, xhat, invd, normed, gz, gm, packed, mixed, ntp, mtp, probs, dp3, gnacc, bacc = take(16)
    res, of = take(2)
    ocs, ors, occs, ocr, orr, occ = take(6)
    chunks = [take(10) for _ in range(nchunk)]
    groups = [take(3) for _ in range(len(GROUPS))]
    sums = take(4)
    hs, hr, ms, mr, os_, or_, as_, ar, ys, yr, xs, xr, zs, zr, ss, sr = take(16)
    ins, outs = take(2)

    lon = lax.axis_index("lon")
    lat = lax.axis_index("lat")
    y, xh = lon // nx, lon % nx
    z, core = lat // 2, lat % 2

    def dev(a, b):
        return {"lon": a, "lat": b}

    partner = dev(lon, z * 2 + (1 - core))
    ypeer = [dev(((y + d) % ny) * nx + xh, lat) for d in range(1, ny)]
    xpeer = dev(y * nx + (1 - xh), lat)
    zpeer = [dev(lon, ((z + d) % nz) * 2 + core) for d in range(1, nz)]
    crossy = [dev(((y + d) % ny) * nx + xh, z * 2 + (1 - core)) for d in range(1, ny)]
    west, east = (lon + nlon - 1) % nlon, (lon + 1) % nlon
    north, south = (lat + nlat - 1) % nlat, (lat + 1) % nlat
    back = [dev(west, lat), dev(lon, north), dev(west, north)]
    forth = [dev(east, lat), dev(lon, south), dev(east, south)]

    loads = [pltpu.make_async_copy(a, b, ins.at[i]) for i, (a, b) in enumerate(zip(given, held)) if i != 8]
    for p in range(PAIRS):
        for i in range(3):
            src = given[8].at[:, C * i + 128 * p : C * i + 128 * p + 128]
            dst = wqkv.at[:, 384 * p + 128 * i : 384 * p + 128 * i + 128]
            loads.append(pltpu.make_async_copy(src, dst, ins.at[11 + 3 * p + i]))
    loads[0].start()
    barrier = pltpu.get_barrier_semaphore()
    everyone = back + forth + [partner, xpeer] + ypeer + zpeer + crossy
    for d in everyone:
        pl.semaphore_signal(barrier, inc=1, device_id=d, device_id_type=MESH)
    loads[1].start()
    loads[2].start()

    stores = [pltpu.make_async_copy(a, b, outs.at[i]) for i, (a, b) in enumerate(zip(staged, results))]
    sends = []

    def send(src, dst, ssem, rsem, d):
        copy = pltpu.make_async_remote_copy(
            src_ref=src, dst_ref=dst, send_sem=ssem, recv_sem=rsem, device_id=d, device_id_type=MESH
        )
        copy.start()
        sends.append(copy)
        return copy

    lane_row = lax.broadcasted_iota(jnp.int32, (lat_dev, lat_dev * 128), 1) // 128
    pick = (lane_row == lax.broadcasted_iota(jnp.int32, (lat_dev, lat_dev * 128), 0)).astype(F32)

    def spread_mask(ref):
        return tn(ref[...].astype(F32), pick)

    colf[96:112, :] = jnp.zeros((16, FW), F32)

    def halo_send(h, block, source):
        colsend, colrecv, rowrecv, cornrecv = halos[h]
        for r in range(lat_dev):
            colf[6 * r : 6 * r + 6, 0:C] = block[r, 0:16, :].astype(F32)[0:HALF_LON]
        colsend[...] = colf[:, 0:C].astype(BF16)
        if h == 0:
            pl.semaphore_wait(barrier, len(everyone))
        return [
            send(colsend, colrecv, hs.at[h, 0], hr.at[h, 0], back[0]),
            send(source.at[0:HALF_LAT], rowrecv, hs.at[h, 1], hr.at[h, 1], back[1]),
            send(colsend.at[0:32], cornrecv, hs.at[h, 2], hr.at[h, 2], back[2]),
        ]

    def halo_land(h, lanes, copies):
        colsend, colrecv, rowrecv, cornrecv = halos[h]
        copies[1].wait_recv()
        for r in range(HALF_LAT):
            frame[lat_dev + r, 0:lon_dev, lanes] = rowrecv[r].astype(F32)
        copies[2].wait_recv()
        colf[0:32, lanes] = cornrecv[...].astype(F32)
        for r in range(HALF_LAT):
            frame[lat_dev + r, lon_dev : lon_dev + HALF_LON, lanes] = colf[6 * r : 6 * r + 6, lanes]
        copies[0].wait_recv()
        colf[:, lanes] = colrecv[...].astype(F32)
        for r in range(lat_dev):
            frame[r, lon_dev : lon_dev + HALF_LON, lanes] = colf[6 * r : 6 * r + 6, lanes]

    xlanes, dlanes = slice(X0, X0 + C), slice(D0, D0 + C)
    loads[0].wait()
    xcopies = halo_send(0, x_ref, x_ref)
    loads[1].wait()
    mcopies = [send(mask_ref, masks[i], ms.at[i], mr.at[i], back[i]) for i in range(3)]
    for load in loads[3:]:
        load.start()
    loads[2].wait()
    dcopies = halo_send(1, dy_ref, dy_ref)
    sea = spread_mask(mask_ref)
    for r in range(lat_dev):
        frame[r, 0:lon_dev, X0 : X0 + C] = x_ref[r].astype(F32)
        frame[r, 0:lon_dev, M0 : M0 + 128] = sea[:, 128 * r : 128 * r + 128]
        frame[r, 0:lon_dev, D0 : D0 + C] = dy_ref[r].astype(F32)

    def pieces(v, n):
        out = []
        for i in range(n):
            part = v.astype(BF16)
            out.append(part)
            if i < n - 1:
                v = v - part.astype(F32)
        return out

    for load in loads[3:]:
        load.wait()
    tb[...] = jnp.zeros_like(tb)
    tb[:, 0:REL] = table[...]
    shifted = []
    for h in range(HEADS):
        line = jnp.broadcast_to(tb[h : h + 1, :], (128, 256))
        shifted.append(pltpu.roll(pltpu.roll(line, 2, 1), 128, 1, stride=1, stride_axis=0)[:, 0:128])
    by_query = sum(nn(v, selft[...]) for v in pieces(jnp.concatenate(shifted, axis=0), 3))
    by_query = jnp.concatenate([by_query[128 * h : 128 * h + 128] for h in range(HEADS)], axis=1)
    whole_bias = sum(nn(self_[0:TP, :], v) for v in pieces(by_query, 3))
    for p in range(PAIRS):
        bias2[p] = whole_bias[:, 256 * p : 256 * p + 256]

    for g in range(len(GROUPS)):
        groups[g][0][...] = jnp.zeros_like(groups[g][0])
    zero_tail = jnp.zeros((RP - ROWS, C), BF16)
    normed[ROWS:RP, :] = zero_tail
    gz[ROWS:RP, :] = zero_tail
    mixed[ROWS:RP, :] = zero_tail
    dp3[ROWS:RP, :] = jnp.zeros((RP - ROWS, 3 * C), BF16)
    for w in range(nwin):
        win[w, T:TP, :] = jnp.zeros((TP - T, FW), F32)

    def cut(w, lanes):
        wr, wc = w // wcols, w % wcols
        c0 = HALF_LON + WIN_LON * wc
        for i in range(WIN_LAT):
            win[w, WIN_LON * i : WIN_LON * i + WIN_LON, lanes] = frame[
                HALF_LAT + WIN_LAT * wr + i, c0 : c0 + WIN_LON, lanes
            ]

    def holds_sea(w):
        return (jnp.max(win[w, :, M0 : M0 + 128]) > 0.5).astype(jnp.int32)

    def ranks(flags, counted):
        total = jnp.int32(0)
        for f, c in zip(flags, counted):
            total = total + f * c
        out, on, off = [], jnp.int32(0), total
        for f, c in zip(flags, counted):
            out.append(jnp.where(f > 0, on, off))
            on = on + f * c
            off = off + (1 - f) * c
        return out

    def slot_window(k, places):
        slot = jnp.int32(0)
        for w, at in places:
            slot = slot + jnp.where(at == k, w, 0)
        idx[k] = slot

    inner = [w for w in range(nwin) if w // wcols < wrows - 1 and w % wcols < wcols - 1]
    outer = [w for w in range(nwin) if w not in inner]
    active = [None] * nwin
    place = [None] * nwin

    at_end = (lat == nlat - 1).astype(F32)
    gain = gain_ref[...]

    def rows_of(k):
        return pl.ds(pl.multiple_of(k * TP, TP), TP)

    def by_three(step):
        def body(i, carry):
            for j in range(3):
                carry = step(3 * i + j, carry)
            return carry

        return body

    def ln_step(k, carry):
        w = idx[k]
        x = win[w, :, X0 : X0 + C]
        mean = jnp.mean(x, axis=1, keepdims=True)
        xc = x - mean
        inv = lax.rsqrt(jnp.mean(xc * xc, axis=1, keepdims=True) + EPS)
        hat = xc * inv
        rows = rows_of(k)
        xhat[rows, :] = hat
        invd[rows, :] = jnp.broadcast_to(inv, (TP, 128))
        normed[rows, :] = (hat * gain).astype(BF16)
        keys = win[w, :, M0 : M0 + 128]
        side_b = lax.broadcasted_iota(jnp.int32, (TP, 128), 0) >= T // 2
        side_a = lax.broadcasted_iota(jnp.int32, (TP, 128), 1) >= T // 2
        apart = jnp.where(side_a != side_b, 1.0, 0.0)
        wrap = at_end * jnp.where(w >= nwin - wcols, 1.0, 0.0)
        madd[k] = (keys * (1.0 - apart * wrap) - 1.0) * 1e9
        return carry

    def dy_step(k, carry):
        w = idx[k]
        m = win[w, :, M0 : M0 + 128]
        gz[rows_of(k), :] = (win[w, :, D0 : D0 + C] * jnp.concatenate([m] * 4, axis=1)).astype(BF16)
        return carry

    lane = lax.broadcasted_iota(jnp.int32, (TP, 128), 1)
    low = lane < 64
    one_lo = jnp.where(low, 1.0, 0.0).astype(BF16)
    one_hi = jnp.where(low, 0.0, 1.0).astype(BF16)
    q_lo = jnp.where(low, 0.125, 0.0).astype(BF16)
    q_hi = jnp.where(low, 0.0, 0.125).astype(BF16)

    def both_heads(v, lo, hi):
        return jnp.concatenate([pad_rows(v * lo, 128), pad_rows(v * hi, 128)], axis=0)

    def own_head(v):
        return jnp.transpose(jnp.concatenate([v[0:64, 0:128], v[64:128, 128:256]], axis=0))[0:TP]

    def attend(i, carry):
        chains = [(3 * i + j, p) for j in range(3) for p in range(PAIRS)]
        scores = []
        for k, p in chains:
            rows = rows_of(k)
            q2 = both_heads(packed[rows, 384 * p : 384 * p + 128], q_lo, q_hi)
            add = madd[k]
            add2 = jnp.concatenate([add, add], axis=1)
            scores.append(nt(packed[rows, 384 * p + 128 : 384 * p + 256], q2) + bias2[p] + add2)
        mixes = []
        for (k, p), s in zip(chains, scores):
            e = jnp.exp(s - jnp.max(s, axis=0, keepdims=True))
            pr = e * (1.0 / jnp.sum(e, axis=0, keepdims=True))
            probs[k * PAIRS + p] = pr
            mixes.append(tn(packed[rows_of(k), 384 * p + 256 : 384 * p + 384], pr.astype(BF16)))
        for (k, p), mix in zip(chains, mixes):
            mixed[rows_of(k), 128 * p : 128 * p + 128] = own_head(mix).astype(BF16)
        return carry

    def forward(first, last):
        lax.fori_loop(first // 3, last // 3, by_three(ln_step), 0)
        rows = slice(first * TP, last * TP)
        packed[rows, :] = nn(normed[rows, :], wqkv[...]).astype(BF16)
        lax.fori_loop(first // 3, last // 3, attend, 0)

    for w in inner:
        cut(w, slice(0, FW))
        active[w] = holds_sea(w)
    inner_rank = ranks([active[w] for w in inner], [1] * len(inner))
    for k in range(EARLY):
        slot_window(k, list(zip(inner, inner_rank)))
    forward(0, EARLY)

    mlanes = slice(M0, M0 + 128)
    for copy in mcopies:
        copy.wait_recv()
    sea = spread_mask(masks[0])
    for r in range(lat_dev):
        frame[r, lon_dev : lon_dev + HALF_LON, mlanes] = sea[0:HALF_LON, 128 * r : 128 * r + 128]
    sea = spread_mask(masks[1])
    for r in range(HALF_LAT):
        frame[lat_dev + r, 0:lon_dev, mlanes] = sea[:, 128 * r : 128 * r + 128]
    sea = spread_mask(masks[2])
    for r in range(HALF_LAT):
        frame[lat_dev + r, lon_dev : lon_dev + HALF_LON, mlanes] = sea[0:HALF_LON, 128 * r : 128 * r + 128]
    halo_land(0, xlanes, xcopies)
    for w in outer:
        cut(w, slice(X0, M0 + 128))
        active[w] = holds_sea(w)
    rest = [jnp.int32(1)] * nwin
    for w, at in zip(inner, inner_rank):
        rest[w] = (at >= EARLY).astype(jnp.int32)
    late_rank = ranks(active, rest)
    for w in range(nwin):
        place[w] = late_rank[w] + EARLY
    for w, at in zip(inner, inner_rank):
        place[w] = jnp.where(at < EARLY, at, place[w])
    for k in range(EARLY, SLOTS):
        slot_window(k, list(enumerate(place)))
    forward(EARLY, SLOTS)

    def window_back(o, lane0):
        def place_window(w):
            wr, wc = w // wcols, w % wcols
            slot = jnp.minimum(place[w], SLOTS - 1)
            for i in range(WIN_LAT):
                c0 = HALF_LON + WIN_LON * wc
                at = slice(WIN_LON * i, WIN_LON * i + WIN_LON)
                of[o, HALF_LAT + WIN_LAT * wr + i, c0 : c0 + WIN_LON, :] = jnp.where(
                    place[w] < SLOTS, res[slot, at, :], win[w, at, lane0 : lane0 + C]
                )

        for w in range(nwin - wcols, nwin):
            place_window(w)
        for r in range(HALF_LAT):
            ors[o, r] = of[o, lat_dev + r, 0:lon_dev, :].astype(BF16)
        rows = send(ors.at[o], orr.at[o], os_.at[o, 1], or_.at[o, 1], forth[1])
        for r in range(HALF_LAT):
            colf[6 * r : 6 * r + 6, 0:C] = of[o, lat_dev + r, lon_dev : lon_dev + HALF_LON, :]
        colf[8:16, C : C + 128] = jnp.zeros((8, 128), F32)
        for j in range(8):
            colf[j : j + 1, C : C + 128] = colf[16 + j // 4 : 17 + j // 4, 128 * (j % 4) : 128 * (j % 4) + 128]
        occs[o] = colf[0:16, 0 : C + 128].astype(BF16)
        corner = send(occs.at[o], occ.at[o], os_.at[o, 2], or_.at[o, 2], forth[2])
        for w in range(wcols - 1, nwin - wcols, wcols):
            place_window(w)
        colf[88:96, 0:C] = jnp.zeros((8, C), F32)
        for r in range(HALF_LAT, lat_dev):
            at = 6 * (r - HALF_LAT)
            colf[at : at + 6, 0:C] = of[o, r, lon_dev : lon_dev + HALF_LON, :]
        ocs[o] = colf[0:96, 0:C].astype(BF16)
        copies = [send(ocs.at[o], ocr.at[o], os_.at[o, 0], or_.at[o, 0], forth[0]), rows, corner]
        for w in range(nwin - wcols):
            if w % wcols < wcols - 1:
                place_window(w)
        return copies

    def finish(o, copies, out):
        copies[1].wait_recv()
        for r in range(HALF_LAT):
            of[o, r, 0:lon_dev, :] = orr[o, r].astype(F32)
        copies[0].wait_recv()
        colf[0:96, 0:C] = ocr[o].astype(F32)
        for r in range(HALF_LAT, lat_dev):
            at = 6 * (r - HALF_LAT)
            of[o, r, 0:HALF_LON, :] = colf[at : at + 6, 0:C]
        copies[2].wait_recv()
        colf[0:16, 0 : C + 128] = occ[o].astype(F32)
        for j in range(8):
            colf[16 + j // 4 : 17 + j // 4, 128 * (j % 4) : 128 * (j % 4) + 128] = colf[j : j + 1, C : C + 128]
        for r in range(HALF_LAT):
            of[o, r, 0:HALF_LON, :] = colf[6 * r : 6 * r + 6, 0:C]
        for r in range(lat_dev):
            out[r] = of[o, r, 0:lon_dev, :].astype(BF16)

    gnacc[...] = nn(mixed[0:ROWS, :], wproj[...])

    def updated_step(k, carry):
        w = idx[k]
        m = win[w, :, M0 : M0 + 128]
        res[k] = win[w, :, X0 : X0 + C] + jnp.concatenate([m] * 4, axis=1) * gnacc[rows_of(k), :]
        return carry

    lax.fori_loop(0, SLOTS // 3, by_three(updated_step), 0)
    out_copies = [window_back(0, X0)]

    ntp[...] = nt(perm[...], normed[...]).astype(BF16)
    mtp[...] = nt(perm[...], mixed[...]).astype(BF16)
    halo_land(1, dlanes, dcopies)
    for w in outer:
        cut(w, dlanes)
    lax.fori_loop(0, SLOTS // 3, by_three(dy_step), 0)

    def chunk_start(c, lhs, rhs):
        asend, arecv, own = chunks[c][0:3]
        right = rhs[...] if c == 0 else rhs[:, 384 * (c - 1) : 384 * c]
        other = pl.ds(pl.multiple_of((1 - core) * half, half), half)
        mine = pl.ds(pl.multiple_of(core * half, half), half)
        asend[...] = nn(lhs[other, :], right).astype(BF16)
        copy = send(asend, arecv, as_.at[c], ar.at[c], partner)
        own[...] = nn(lhs[mine, :], right)
        return [copy]

    def y_piece(c, d):
        return chunks[c][2][pl.ds(pl.multiple_of(((y + d) % ny) * ysz, ysz), ysz), :]

    def chunk_y(c, copies):
        asend, arecv, own, ysend, yvia = chunks[c][0:5]
        copies[0].wait_recv()
        own[...] += arecv[...].astype(F32)
        ysend[...] = y_piece(c, 2).astype(BF16)
        hy = ysz // 2
        return [
            send(ysend.at[0:hy], yvia.at[0], ys.at[c, 0], yr.at[c, 0], ypeer[ny - 2]),
            send(ysend.at[hy:ysz], yvia.at[1], ys.at[c, 1], yr.at[c, 1], ypeer[0]),
        ]

    def chunk_near(c, copies):
        yvia, nsend, nrecv = chunks[c][4:7]
        hy = ysz // 2
        copies[0].wait_recv()
        before = y_piece(c, ny - 1)
        nsend[0] = jnp.concatenate([before[0:hy] + yvia[0].astype(F32), before[hy:ysz]], axis=0).astype(BF16)
        copies[1].wait_recv()
        after = y_piece(c, 1)
        nsend[1] = jnp.concatenate([after[0:hy], after[hy:ysz] + yvia[1].astype(F32)], axis=0).astype(BF16)
        return [
            send(nsend.at[0], nrecv.at[0], ys.at[c, 2], yr.at[c, 2], ypeer[ny - 2]),
            send(nsend.at[1], nrecv.at[1], ys.at[c, 3], yr.at[c, 3], ypeer[0]),
        ]

    def chunk_x(c, copies):
        nrecv, xsend, xrecv, xown = chunks[c][6:10]
        s = y_piece(c, 0)
        for d in range(2):
            copies[d].wait_recv()
            s = s + nrecv[d].astype(F32)
        top, low_half = s[0 : ysz // 2], s[ysz // 2 : ysz]
        first = xh == 0
        xsend[...] = jnp.where(first, low_half, top).astype(BF16)
        xown[...] = jnp.where(first, top, low_half)
        return [send(xsend, xrecv, xs.at[c], xr.at[c], xpeer)]

    def blocks_before(c):
        g = next(i for i, members in enumerate(GROUPS) if c in members)
        return g, sum(cols[m] // 128 for m in GROUPS[g] if m < c)

    def chunk_z(c, copies):
        xsend, xrecv, xown = chunks[c][7:10]
        g, first = blocks_before(c)
        zown = groups[g][0]
        copies[0].wait_recv()
        s = xown[...] + xrecv[...].astype(F32)
        for j in range(nz):
            part = s[share * j : share * j + share]
            for q in range(cols[c] // 128):
                at = share * (first + q)
                zown[j, at : at + share, :] = part[:, 128 * q : 128 * q + 128]

    def group_send(g):
        zown, zsend, zrecv = groups[g]
        zsend[...] = zown[...].astype(BF16)
        return [
            send(zsend.at[(z + d) % nz], zrecv.at[d - 1], zs.at[g, d - 1], zr.at[g, d - 1], zpeer[d - 1])
            for d in range(1, nz)
        ]

    def group_end(g, copies):
        zown, zsend, zrecv = groups[g]
        s = zown[z]
        for i, copy in enumerate(copies):
            copy.wait_recv()
            s = s + zrecv[i].astype(F32)
        for c in GROUPS[g]:
            first = blocks_before(c)[1]
            for q in range(cols[c] // 128):
                at = share * (first + q)
                block = s[at : at + share]
                if c == 0:
                    gproj[:, 128 * q : 128 * q + 128] = block
                else:
                    gqkv[:, C * q + 128 * (c - 1) : C * q + 128 * c] = block

    st = {}
    st[0] = chunk_start(0, mtp, gz)
    gm[...] = nt(gz[0:ROWS, :], wproj[...]).astype(BF16)

    def backward(p):
        ks = list(range(SLOTS))
        d2s, dps = [], []
        for k in ks:
            rows = slice(TP * k, TP * k + TP)
            d2s.append(both_heads(gm[rows, 128 * p : 128 * p + 128], one_lo, one_hi))
            dps.append(nt(packed[rows, 384 * p + 256 : 384 * p + 384], d2s[-1]))
        dss, dvs = [], []
        for k in ks:
            pr = probs[k * PAIRS + p]
            t = pr * dps[k]
            dss.append(t - pr * jnp.sum(t, axis=0, keepdims=True))
            dvs.append(nn(pr.astype(BF16), d2s[k]))
        bacc[p] = functools.reduce(lambda a, b: a + b, dss)
        dqs = []
        for k in ks:
            rows = slice(TP * k, TP * k + TP)
            ds = dss[k].astype(BF16)
            q2 = both_heads(packed[rows, 384 * p : 384 * p + 128], q_lo, q_hi)
            dqs.append(tn(packed[rows, 384 * p + 128 : 384 * p + 256], ds))
            dp3[rows, 384 * p + 128 : 384 * p + 256] = nn(ds, q2).astype(BF16)
            dp3[rows, 384 * p + 256 : 384 * p + 384] = dvs[k].astype(BF16)
        for k in ks:
            dp3[TP * k : TP * k + TP, 384 * p : 384 * p + 128] = (own_head(dqs[k]) * 0.125).astype(BF16)

    for p in range(PAIRS):
        backward(p)
        st[p] = chunk_y(p, st[p])
        if p >= 1:
            st[p - 1] = chunk_near(p - 1, st[p - 1])
        st[p + 1] = chunk_start(p + 1, ntp, dp3)
        if p >= 3:
            st[p - 3] = chunk_x(p - 3, st[p - 3])

    smy, sma, smx, smz = sums
    stacked = jnp.concatenate([bacc[h // 2, :, 128 * (h % 2) : 128 * (h % 2) + 128] for h in range(HEADS)], axis=0)
    by_place = sum(nn(v, self_[...]) for v in pieces(stacked, 2))
    by_place = jnp.concatenate([by_place[TP * h : TP * h + TP] for h in range(HEADS)], axis=1)
    spread = sum(nn(selrt[:, 0:TP], v) for v in pieces(by_place, 2))
    for h in range(HEADS):
        wide = jnp.concatenate([spread[:, 128 * h : 128 * h + 128], jnp.zeros((128, 128), F32)], axis=1)
        sums[0][core * ny + y, h : h + 1, 0:256] = jnp.sum(pltpu.roll(wide, 0, 1, stride=1, stride_axis=0), axis=0, keepdims=True)
    for part in range(2):
        rows = slice(part * ROWS // 2, (part + 1) * ROWS // 2)
        gnacc[rows, :] = nt(dp3[rows, :], wqkv[...])
        if part == 0:
            st[4] = chunk_y(4, st[4])
            st[3] = chunk_near(3, st[3])
            st[1] = chunk_x(1, st[1])

    def norm_back(k, total):
        w = idx[k]
        rows = rows_of(k)
        gn = gnacc[rows, :]
        hat = xhat[rows, :]
        g = gn * gain
        prod = g * hat
        mid = g - jnp.mean(g, axis=1, keepdims=True) - hat * jnp.mean(prod, axis=1, keepdims=True)
        inv = jnp.concatenate([invd[rows, :]] * 4, axis=1)
        res[k] = win[w, :, D0 : D0 + C] + inv * mid
        return total + jnp.sum(gn * hat, axis=0, keepdims=True)

    gsum = lax.fori_loop(0, SLOTS // 3, by_three(norm_back), jnp.zeros((1, C), F32))
    slot = core * ny + y
    smy[slot, 4:8, 256:384] = jnp.zeros((4, 128), F32)
    for j in range(4):
        smy[slot, j : j + 1, 256:384] = gsum[:, 128 * j : 128 * j + 128]
    sm = smy.at[slot]
    copies = [
        send(sm, sm, ss.at[i], sr.at[i], to) for i, to in enumerate([partner] + ypeer + crossy)
    ]
    st[4] = chunk_near(4, st[4])
    st[2] = chunk_x(2, st[2])
    out_copies.append(window_back(1, D0))
    st[3] = chunk_x(3, st[3])
    chunk_z(0, st[0])
    chunk_z(1, st[1])
    for copy in copies:
        copy.wait_recv()
    acc = smy[0]
    for j in range(1, 2 * ny):
        acc = acc + smy[j]
    sma[...] = acc
    copy = send(sma, smx, ss.at[2 * ny - 1], sr.at[2 * ny - 1], xpeer)
    chunk_z(2, st[2])
    group0 = group_send(0)
    st[4] = chunk_x(4, st[4])
    finish(0, out_copies[0], upd)
    stores[0].start()
    chunk_z(3, st[3])
    chunk_z(4, st[4])
    group1 = group_send(1)
    copy.wait_recv()
    smz[z] = sma[...] + smx[...]
    copies = [
        send(smz.at[z], smz.at[z], ss.at[2 * ny + d - 1], sr.at[2 * ny + d - 1], zpeer[d - 1]) for d in range(1, nz)
    ]
    group_end(0, group0)
    finish(1, out_copies[1], gin)
    stores[1].start()
    group_end(1, group1)
    for copy in copies:
        copy.wait_recv()
    acc = smz[0]
    for j in range(1, nz):
        acc = acc + smz[j]
    bias_out[...] = acc[:, 0:REL]
    for j in range(4):
        gain_out[:, 128 * j : 128 * j + 128] = acc[j : j + 1, 256:384]
    for store in stores[2:]:
        store.start()
    for copy in sends:
        copy.wait_send()
    for store in stores:
        store.wait()


def hand_over(*refs):
    arrived, left = refs[18:20]
    steps = []
    for i in range(6):
        rows = refs[i].shape[0]
        size = 3 if i < 2 else rows
        steps += [(i, pl.ds(start, size)) for start in range(0, rows, size)]
    fetches = [
        pltpu.make_async_copy(refs[i].at[at], refs[12 + i].at[at], arrived.at[n]) for n, (i, at) in enumerate(steps)
    ]
    stores = [
        pltpu.make_async_copy(refs[12 + i].at[at], refs[6 + i].at[at], left.at[n]) for n, (i, at) in enumerate(steps)
    ]
    for fetch in fetches:
        fetch.start()
    for fetch, store in zip(fetches, stores):
        fetch.wait()
        store.start()
    for store in stores:
        store.wait()


def constants(ny, nx, nz):
    share = C // (ny * nx * nz * 2)
    perm = np.zeros((C, C), np.float32)
    for core in range(2):
        for y in range(ny):
            for xh in range(nx):
                for z in range(nz):
                    to = (((core * ny + y) * nx + xh) * nz + z) * share
                    start = (((y * nx + xh) * nz + z) * 2 + core) * share
                    perm[to + np.arange(share), start + np.arange(share)] = 1
    a = np.arange(T)
    pa = (a // WIN_LON) * (2 * WIN_LON - 1) + a % WIN_LON
    selrt = np.zeros((128, 128), np.float32)
    selrt[126 - pa, a] = 1
    self_ = np.zeros((128, 128), np.float32)
    self_[a, pa] = 1
    return perm, self_, self_.T, selrt


def solution(mesh):
    nlon, nlat = mesh.shape["lon"], mesh.shape["lat"]
    nx, nz = 2, nlat // 2
    ny = nlon // nx
    nxz = nx * nz
    half = C // 2
    ysz = half // ny
    share = ysz // nxz
    cols = [C] + [384] * PAIRS
    lat_dev, lon_dev = 18, 48
    nwin = 12
    vm = pltpu.VMEM
    dma = lambda *s: pltpu.SemaphoreType.DMA(s)
    perm, self_, selft, selrt = (jnp.asarray(v, BF16) for v in constants(ny, nx, nz))

    def on_device(fields, grad_out, layernorm_gain, qkv_weight, proj_weight, bias_table, sea_mask):
        shapes = (
            jax.ShapeDtypeStruct((lat_dev, lon_dev, C), BF16),
            jax.ShapeDtypeStruct((lat_dev, lon_dev, C), BF16),
            jax.ShapeDtypeStruct((1, C), F32),
            jax.ShapeDtypeStruct((HEADS, REL), F32),
            jax.ShapeDtypeStruct((share, 3 * C), F32),
            jax.ShapeDtypeStruct((share, C), F32),
        )
        scratch = [
            vm((lat_dev, lon_dev, C), BF16),
            vm((lat_dev, lon_dev), jnp.int32),
            vm((lat_dev, lon_dev, C), BF16),
            vm((HEADS, REL), F32),
            vm((128, 128), BF16),
            vm((128, 128), BF16),
            vm((128, 128), BF16),
            vm((1, C), F32),
            vm((C, 3 * C), BF16),
            vm((C, C), BF16),
            vm((C, C), BF16),
        ]
        scratch += [vm(v.shape, v.dtype) for v in shapes]
        scratch += [
            vm((lat_dev + 3, 56, FW), F32),
            vm((nwin, TP, FW), F32),
            vm((112, FW), F32),
        ]
        for wide in (C, C):
            scratch += [
                vm((112, wide), BF16),
                vm((112, wide), BF16),
                vm((3, lon_dev, wide), BF16),
                vm((32, wide), BF16),
            ]
        scratch += [vm((lat_dev, lon_dev), jnp.int32)] * 3
        scratch += [
            pltpu.SMEM((16,), jnp.int32),
            vm((HEADS, 256), F32),
            vm((PAIRS, TP, 256), F32),
            vm((SLOTS, TP, 128), F32),
            vm((ROWS, C), F32),
            vm((ROWS, 128), F32),
            vm((RP, C), BF16),
            vm((RP, C), BF16),
            vm((ROWS, C), BF16),
            vm((ROWS, 3 * C), BF16),
            vm((RP, C), BF16),
            vm((C, RP), BF16),
            vm((C, RP), BF16),
            vm((SLOTS * PAIRS, TP, 256), F32),
            vm((RP, 3 * C), BF16),
            vm((ROWS, C), F32),
            vm((PAIRS, TP, 256), F32),
            vm((SLOTS, TP, C), F32),
            vm((2, lat_dev + 3, 56, C), F32),
            vm((2, 96, C), BF16),
            vm((2, 3, lon_dev, C), BF16),
            vm((2, 16, C + 128), BF16),
            vm((2, 96, C), BF16),
            vm((2, 3, lon_dev, C), BF16),
            vm((2, 16, C + 128), BF16),
        ]
        for n in cols:
            scratch += [
                vm((half, n), BF16),
                vm((half, n), BF16),
                vm((half, n), F32),
                vm((ysz, n), BF16),
                vm((2, ysz // 2, n), BF16),
                vm((2, ysz, n), BF16),
                vm((2, ysz, n), BF16),
                vm((ysz // 2, n), BF16),
                vm((ysz // 2, n), BF16),
                vm((ysz // 2, n), F32),
            ]
        for members in GROUPS:
            rows = -(-share * sum(cols[c] // 128 for c in members) // 16) * 16
            scratch += [vm((nz, rows, 128), F32), vm((nz, rows, 128), BF16), vm((max(nz - 1, 1), rows, 128), BF16)]
        sm = (8, 384)
        scratch += [vm((2 * ny,) + sm, F32), vm(sm, F32), vm(sm, F32), vm((nz,) + sm, F32)]
        nc = len(cols)
        small = 2 * ny + nz
        scratch += [
            dma(2, 3), dma(2, 3), dma(3), dma(3), dma(2, 3), dma(2, 3), dma(nc), dma(nc), dma(nc, 4),
            dma(nc, 4), dma(nc), dma(nc), dma(nc, max(nz - 1, 1)), dma(nc, max(nz - 1, 1)), dma(small), dma(small), dma(23), dma(6),
        ]
        anywhere = pl.BlockSpec(memory_space=pl.ANY)
        outs = pl.pallas_call(
            functools.partial(kernel, (ny, nx, nz), cols),
            out_shape=shapes,
            in_specs=[anywhere] * 11,
            out_specs=(anywhere,) * 6,
            scratch_shapes=scratch,
            compiler_params=pltpu.CompilerParams(
                collective_id=0, has_side_effects=True, vmem_limit_bytes=60 * 1024 * 1024
            ),
        )(
            fields, sea_mask, grad_out, bias_table, self_, selft, selrt,
            layernorm_gain.reshape(1, C), qkv_weight, proj_weight, perm,
        )
        outs = pl.pallas_call(
            hand_over,
            out_shape=shapes,
            in_specs=[anywhere] * 6,
            out_specs=(anywhere,) * 6,
            scratch_shapes=[vm(v.shape, v.dtype) for v in shapes] + [dma(16), dma(16)],
            compiler_params=pltpu.CompilerParams(vmem_limit_bytes=60 * 1024 * 1024),
        )(*outs)
        updated, grad_in, grad_gain, grad_bias, grad_qkv, grad_proj = outs
        return (updated, grad_in, grad_gain.reshape(C), grad_bias, grad_qkv, grad_proj)

    grid = P(("batch", "lat"), "lon", None)
    return jax.shard_map(
        on_device,
        mesh=mesh,
        in_specs=(grid, grid, P(), P(), P(), P(), P(("batch", "lat"), "lon")),
        out_specs=(
            grid,
            grid,
            P("batch"),
            P("batch", None),
            P(("batch", "lon", "lat"), None),
            P(("batch", "lon", "lat"), None),
        ),
        check_vma=False,
    )
```

```python
import functools

import jax
import jax.numpy as jnp
import numpy as np
from jax import lax
from jax.experimental import pallas as pl
from jax.experimental.pallas import tpu as pltpu
from jax.sharding import PartitionSpec as P

MESH = pl.DeviceIdType.MESH
F32 = jnp.float32
BF16 = jnp.bfloat16
C = 512
HEADS = 8
PAIRS = 4
WIN_LAT = 6
WIN_LON = 12
HALF_LAT = 3
HALF_LON = 6
T = 72
TP = 80
SLOTS = 9
ROWS = SLOTS * TP
RP = 768
REL = 253
X0, M0, D0, FW = 0, 512, 640, 1152
GROUPS = ((0, 1, 2), (3, 4))
EARLY = 3
EPS = 1e-5


def nn(a, b, **kw):
    return lax.dot_general(a, b, (((1,), (0,)), ((), ())), preferred_element_type=F32, **kw)


def nt(a, b, **kw):
    return lax.dot_general(a, b, (((1,), (1,)), ((), ())), preferred_element_type=F32, **kw)


def tn(a, b, **kw):
    return lax.dot_general(a, b, (((0,), (0,)), ((), ())), preferred_element_type=F32, **kw)


def pad_rows(v, rows):
    return jnp.concatenate([v, jnp.zeros((rows - v.shape[0], v.shape[1]), v.dtype)], axis=0)


def kernel(dims, cols, *refs):
    ny, nx, nz = dims
    nlon, nlat = ny * nx, 2 * nz
    nxz = nx * nz
    lat_dev, lon_dev = 18, 48
    wrows, wcols = lat_dev // WIN_LAT, lon_dev // WIN_LON
    nwin = wrows * wcols
    half = C // 2
    ysz = half // ny
    share = ysz // nxz
    nchunk = len(cols)

    it = iter(refs)
    take = lambda n=None: next(it) if n is None else [next(it) for _ in range(n)]
    given = take(11)
    results = take(6)
    held = take(11)
    x_ref, mask_ref, dy_ref, table, self_, selft, selrt, gain_ref, wqkv, wproj, perm = held
    staged = take(6)
    upd, gin, gain_out, bias_out, gqkv, gproj = staged
    frame, win, colf = take(3)
    halos = [take(4) for _ in range(2)]
    masks = take(3)
    idx = take()
    tb, bias2, madd, xhat, invd, normed, gz, gm, packed, mixed, ntp, mtp, probs, dp3, gnacc, bacc = take(16)
    res, of = take(2)
    ocs, ors, occs, ocr, orr, occ = take(6)
    chunks = [take(8) for _ in range(nchunk)]
    groups = [take(3) for _ in range(len(GROUPS))]
    sums = take(4)
    hs, hr, ms, mr, os_, or_, as_, ar, ys, yr, xs, xr, zs, zr, ss, sr = take(16)
    ins, outs = take(2)

    lon = lax.axis_index("lon")
    lat = lax.axis_index("lat")
    y, xh = lon // nx, lon % nx
    z, core = lat // 2, lat % 2

    def dev(a, b):
        return {"lon": a, "lat": b}

    partner = dev(lon, z * 2 + (1 - core))
    ypeer = [dev(((y + d) % ny) * nx + xh, lat) for d in range(1, ny)]
    xpeer = dev(y * nx + (1 - xh), lat)
    zpeer = [dev(lon, ((z + d) % nz) * 2 + core) for d in range(1, nz)]
    crossy = [dev(((y + d) % ny) * nx + xh, z * 2 + (1 - core)) for d in range(1, ny)]
    west, east = (lon + nlon - 1) % nlon, (lon + 1) % nlon
    north, south = (lat + nlat - 1) % nlat, (lat + 1) % nlat
    back = [dev(west, lat), dev(lon, north), dev(west, north)]
    forth = [dev(east, lat), dev(lon, south), dev(east, south)]

    loads = [pltpu.make_async_copy(a, b, ins.at[i]) for i, (a, b) in enumerate(zip(given, held)) if i != 8]
    for p in range(PAIRS):
        for i in range(3):
            src = given[8].at[:, C * i + 128 * p : C * i + 128 * p + 128]
            dst = wqkv.at[:, 384 * p + 128 * i : 384 * p + 128 * i + 128]
            loads.append(pltpu.make_async_copy(src, dst, ins.at[11 + 3 * p + i]))
    loads[0].start()
    barrier = pltpu.get_barrier_semaphore()
    everyone = back + forth + [partner, xpeer] + ypeer + zpeer + crossy
    for d in everyone:
        pl.semaphore_signal(barrier, inc=1, device_id=d, device_id_type=MESH)
    loads[1].start()
    loads[2].start()

    stores = [pltpu.make_async_copy(a, b, outs.at[i]) for i, (a, b) in enumerate(zip(staged, results))]
    sends = []

    def send(src, dst, ssem, rsem, d):
        copy = pltpu.make_async_remote_copy(
            src_ref=src, dst_ref=dst, send_sem=ssem, recv_sem=rsem, device_id=d, device_id_type=MESH
        )
        copy.start()
        sends.append(copy)
        return copy

    lane_row = lax.broadcasted_iota(jnp.int32, (lat_dev, lat_dev * 128), 1) // 128
    pick = (lane_row == lax.broadcasted_iota(jnp.int32, (lat_dev, lat_dev * 128), 0)).astype(F32)

    def spread_mask(ref):
        return tn(ref[...].astype(F32), pick)

    colf[96:112, :] = jnp.zeros((16, FW), F32)

    def halo_send(h, block, source):
        colsend, colrecv, rowrecv, cornrecv = halos[h]
        for r in range(lat_dev):
            colf[6 * r : 6 * r + 6, 0:C] = block[r, 0:16, :].astype(F32)[0:HALF_LON]
        colsend[...] = colf[:, 0:C].astype(BF16)
        if h == 0:
            pl.semaphore_wait(barrier, len(everyone))
        return [
            send(colsend, colrecv, hs.at[h, 0], hr.at[h, 0], back[0]),
            send(source.at[0:HALF_LAT], rowrecv, hs.at[h, 1], hr.at[h, 1], back[1]),
            send(colsend.at[0:32], cornrecv, hs.at[h, 2], hr.at[h, 2], back[2]),
        ]

    def halo_land(h, lanes, copies):
        colsend, colrecv, rowrecv, cornrecv = halos[h]
        copies[1].wait_recv()
        for r in range(HALF_LAT):
            frame[lat_dev + r, 0:lon_dev, lanes] = rowrecv[r].astype(F32)
        copies[2].wait_recv()
        colf[0:32, lanes] = cornrecv[...].astype(F32)
        for r in range(HALF_LAT):
            frame[lat_dev + r, lon_dev : lon_dev + HALF_LON, lanes] = colf[6 * r : 6 * r + 6, lanes]
        copies[0].wait_recv()
        colf[:, lanes] = colrecv[...].astype(F32)
        for r in range(lat_dev):
            frame[r, lon_dev : lon_dev + HALF_LON, lanes] = colf[6 * r : 6 * r + 6, lanes]

    xlanes, dlanes = slice(X0, X0 + C), slice(D0, D0 + C)
    loads[0].wait()
    xcopies = halo_send(0, x_ref, x_ref)
    loads[1].wait()
    mcopies = [send(mask_ref, masks[i], ms.at[i], mr.at[i], back[i]) for i in range(3)]
    for load in loads[3:]:
        load.start()
    loads[2].wait()
    dcopies = halo_send(1, dy_ref, dy_ref)
    sea = spread_mask(mask_ref)
    for r in range(lat_dev):
        frame[r, 0:lon_dev, X0 : X0 + C] = x_ref[r].astype(F32)
        frame[r, 0:lon_dev, M0 : M0 + 128] = sea[:, 128 * r : 128 * r + 128]
        frame[r, 0:lon_dev, D0 : D0 + C] = dy_ref[r].astype(F32)

    def pieces(v, n):
        out = []
        for i in range(n):
            part = v.astype(BF16)
            out.append(part)
            if i < n - 1:
                v = v - part.astype(F32)
        return out

    for load in loads[3:]:
        load.wait()
    tb[...] = jnp.zeros_like(tb)
    tb[:, 0:REL] = table[...]
    shifted = []
    for h in range(HEADS):
        line = jnp.broadcast_to(tb[h : h + 1, :], (128, 256))
        shifted.append(pltpu.roll(pltpu.roll(line, 2, 1), 128, 1, stride=1, stride_axis=0)[:, 0:128])
    by_query = sum(nn(v, selft[...]) for v in pieces(jnp.concatenate(shifted, axis=0), 3))
    by_query = jnp.concatenate([by_query[128 * h : 128 * h + 128] for h in range(HEADS)], axis=1)
    whole_bias = sum(nn(self_[0:TP, :], v) for v in pieces(by_query, 3))
    for p in range(PAIRS):
        bias2[p] = whole_bias[:, 256 * p : 256 * p + 256]

    for g in range(len(GROUPS)):
        groups[g][0][...] = jnp.zeros_like(groups[g][0])
    zero_tail = jnp.zeros((RP - ROWS, C), BF16)
    normed[ROWS:RP, :] = zero_tail
    gz[ROWS:RP, :] = zero_tail
    mixed[ROWS:RP, :] = zero_tail
    dp3[ROWS:RP, :] = jnp.zeros((RP - ROWS, 3 * C), BF16)
    for w in range(nwin):
        win[w, T:TP, :] = jnp.zeros((TP - T, FW), F32)

    def cut(w, lanes):
        wr, wc = w // wcols, w % wcols
        c0 = HALF_LON + WIN_LON * wc
        for i in range(WIN_LAT):
            win[w, WIN_LON * i : WIN_LON * i + WIN_LON, lanes] = frame[
                HALF_LAT + WIN_LAT * wr + i, c0 : c0 + WIN_LON, lanes
            ]

    def holds_sea(w):
        return (jnp.max(win[w, :, M0 : M0 + 128]) > 0.5).astype(jnp.int32)

    def ranks(flags, counted):
        total = jnp.int32(0)
        for f, c in zip(flags, counted):
            total = total + f * c
        out, on, off = [], jnp.int32(0), total
        for f, c in zip(flags, counted):
            out.append(jnp.where(f > 0, on, off))
            on = on + f * c
            off = off + (1 - f) * c
        return out

    def slot_window(k, places):
        slot = jnp.int32(0)
        for w, at in places:
            slot = slot + jnp.where(at == k, w, 0)
        idx[k] = slot

    inner = [w for w in range(nwin) if w // wcols < wrows - 1 and w % wcols < wcols - 1]
    outer = [w for w in range(nwin) if w not in inner]
    active = [None] * nwin
    place = [None] * nwin

    at_end = (lat == nlat - 1).astype(F32)
    gain = gain_ref[...]

    def rows_of(k):
        return pl.ds(pl.multiple_of(k * TP, TP), TP)

    def by_three(step):
        def body(i, carry):
            for j in range(3):
                carry = step(3 * i + j, carry)
            return carry

        return body

    def ln_step(k, carry):
        w = idx[k]
        x = win[w, :, X0 : X0 + C]
        mean = jnp.mean(x, axis=1, keepdims=True)
        xc = x - mean
        inv = lax.rsqrt(jnp.mean(xc * xc, axis=1, keepdims=True) + EPS)
        hat = xc * inv
        rows = rows_of(k)
        xhat[rows, :] = hat
        invd[rows, :] = jnp.broadcast_to(inv, (TP, 128))
        normed[rows, :] = (hat * gain).astype(BF16)
        keys = win[w, :, M0 : M0 + 128]
        side_b = lax.broadcasted_iota(jnp.int32, (TP, 128), 0) >= T // 2
        side_a = lax.broadcasted_iota(jnp.int32, (TP, 128), 1) >= T // 2
        apart = jnp.where(side_a != side_b, 1.0, 0.0)
        wrap = at_end * jnp.where(w >= nwin - wcols, 1.0, 0.0)
        madd[k] = (keys * (1.0 - apart * wrap) - 1.0) * 1e9
        return carry

    def dy_step(k, carry):
        w = idx[k]
        m = win[w, :, M0 : M0 + 128]
        gz[rows_of(k), :] = (win[w, :, D0 : D0 + C] * jnp.concatenate([m] * 4, axis=1)).astype(BF16)
        return carry

    lane = lax.broadcasted_iota(jnp.int32, (TP, 128), 1)
    low = lane < 64
    one_lo = jnp.where(low, 1.0, 0.0).astype(BF16)
    one_hi = jnp.where(low, 0.0, 1.0).astype(BF16)
    q_lo = jnp.where(low, 0.125, 0.0).astype(BF16)
    q_hi = jnp.where(low, 0.0, 0.125).astype(BF16)

    def both_heads(v, lo, hi):
        return jnp.concatenate([pad_rows(v * lo, 128), pad_rows(v * hi, 128)], axis=0)

    def own_head(v):
        return jnp.transpose(jnp.concatenate([v[0:64, 0:128], v[64:128, 128:256]], axis=0))[0:TP]

    def attend(i, carry):
        chains = [(3 * i + j, p) for j in range(3) for p in range(PAIRS)]
        scores = []
        for k, p in chains:
            rows = rows_of(k)
            q2 = both_heads(packed[rows, 384 * p : 384 * p + 128], q_lo, q_hi)
            add = madd[k]
            add2 = jnp.concatenate([add, add], axis=1)
            scores.append(nt(packed[rows, 384 * p + 128 : 384 * p + 256], q2) + bias2[p] + add2)
        mixes = []
        for (k, p), s in zip(chains, scores):
            e = jnp.exp(s - jnp.max(s, axis=0, keepdims=True))
            pr = e * (1.0 / jnp.sum(e, axis=0, keepdims=True))
            probs[k * PAIRS + p] = pr
            mixes.append(tn(packed[rows_of(k), 384 * p + 256 : 384 * p + 384], pr.astype(BF16)))
        for (k, p), mix in zip(chains, mixes):
            mixed[rows_of(k), 128 * p : 128 * p + 128] = own_head(mix).astype(BF16)
        return carry

    def forward(first, last):
        lax.fori_loop(first // 3, last // 3, by_three(ln_step), 0)
        rows = slice(first * TP, last * TP)
        packed[rows, :] = nn(normed[rows, :], wqkv[...]).astype(BF16)
        lax.fori_loop(first // 3, last // 3, attend, 0)

    def backward(chains):
        d2s, dps = [], []
        for k, p in chains:
            rows = slice(TP * k, TP * k + TP)
            d2s.append(both_heads(gm[rows, 128 * p : 128 * p + 128], one_lo, one_hi))
            dps.append(nt(packed[rows, 384 * p + 256 : 384 * p + 384], d2s[-1]))
        dss, dvs = [], []
        for (k, p), d2, dp in zip(chains, d2s, dps):
            pr = probs[k * PAIRS + p]
            t = pr * dp
            dss.append(t - pr * jnp.sum(t, axis=0, keepdims=True))
            dvs.append(nn(pr.astype(BF16), d2))
        for p in sorted({p for _, p in chains}):
            bacc[p] += functools.reduce(lambda a, b: a + b, [ds for (_, q), ds in zip(chains, dss) if q == p])
        dqs = []
        for (k, p), ds, dv in zip(chains, dss, dvs):
            rows = slice(TP * k, TP * k + TP)
            ds = ds.astype(BF16)
            q2 = both_heads(packed[rows, 384 * p : 384 * p + 128], q_lo, q_hi)
            dqs.append(tn(packed[rows, 384 * p + 128 : 384 * p + 256], ds))
            dp3[rows, 384 * p + 128 : 384 * p + 256] = nn(ds, q2).astype(BF16)
            dp3[rows, 384 * p + 256 : 384 * p + 384] = dv.astype(BF16)
        for (k, p), dq in zip(chains, dqs):
            dp3[TP * k : TP * k + TP, 384 * p : 384 * p + 128] = (own_head(dq) * 0.125).astype(BF16)

    def grad_mixed(first, last):
        lax.fori_loop(first // 3, last // 3, by_three(dy_step), 0)
        rows = slice(first * TP, last * TP)
        gm[rows, :] = nt(gz[rows, :], wproj[...]).astype(BF16)

    for w in inner:
        cut(w, slice(0, FW))
        active[w] = holds_sea(w)
    inner_rank = ranks([active[w] for w in inner], [1] * len(inner))
    for k in range(EARLY):
        slot_window(k, list(zip(inner, inner_rank)))
    forward(0, EARLY)
    bacc[...] = jnp.zeros_like(bacc)
    grad_mixed(0, EARLY)
    backward([(k, p) for k in range(EARLY) for p in range(PAIRS)])

    mlanes = slice(M0, M0 + 128)
    for copy in mcopies:
        copy.wait_recv()
    sea = spread_mask(masks[0])
    for r in range(lat_dev):
        frame[r, lon_dev : lon_dev + HALF_LON, mlanes] = sea[0:HALF_LON, 128 * r : 128 * r + 128]
    sea = spread_mask(masks[1])
    for r in range(HALF_LAT):
        frame[lat_dev + r, 0:lon_dev, mlanes] = sea[:, 128 * r : 128 * r + 128]
    sea = spread_mask(masks[2])
    for r in range(HALF_LAT):
        frame[lat_dev + r, lon_dev : lon_dev + HALF_LON, mlanes] = sea[0:HALF_LON, 128 * r : 128 * r + 128]
    halo_land(0, xlanes, xcopies)
    for w in outer:
        cut(w, slice(X0, M0 + 128))
        active[w] = holds_sea(w)
    rest = [jnp.int32(1)] * nwin
    for w, at in zip(inner, inner_rank):
        rest[w] = (at >= EARLY).astype(jnp.int32)
    late_rank = ranks(active, rest)
    for w in range(nwin):
        place[w] = late_rank[w] + EARLY
    for w, at in zip(inner, inner_rank):
        place[w] = jnp.where(at < EARLY, at, place[w])
    for k in range(EARLY, SLOTS):
        slot_window(k, list(enumerate(place)))
    forward(EARLY, SLOTS)

    def window_back(o, lane0):
        def place_window(w):
            wr, wc = w // wcols, w % wcols
            slot = jnp.minimum(place[w], SLOTS - 1)
            for i in range(WIN_LAT):
                c0 = HALF_LON + WIN_LON * wc
                at = slice(WIN_LON * i, WIN_LON * i + WIN_LON)
                of[o, HALF_LAT + WIN_LAT * wr + i, c0 : c0 + WIN_LON, :] = jnp.where(
                    place[w] < SLOTS, res[slot, at, :], win[w, at, lane0 : lane0 + C]
                )

        for w in range(nwin - wcols, nwin):
            place_window(w)
        for r in range(HALF_LAT):
            ors[o, r] = of[o, lat_dev + r, 0:lon_dev, :].astype(BF16)
        rows = send(ors.at[o], orr.at[o], os_.at[o, 1], or_.at[o, 1], forth[1])
        for r in range(HALF_LAT):
            colf[6 * r : 6 * r + 6, 0:C] = of[o, lat_dev + r, lon_dev : lon_dev + HALF_LON, :]
        colf[8:16, C : C + 128] = jnp.zeros((8, 128), F32)
        for j in range(8):
            colf[j : j + 1, C : C + 128] = colf[16 + j // 4 : 17 + j // 4, 128 * (j % 4) : 128 * (j % 4) + 128]
        occs[o] = colf[0:16, 0 : C + 128].astype(BF16)
        corner = send(occs.at[o], occ.at[o], os_.at[o, 2], or_.at[o, 2], forth[2])
        for w in range(wcols - 1, nwin - wcols, wcols):
            place_window(w)
        colf[88:96, 0:C] = jnp.zeros((8, C), F32)
        for r in range(HALF_LAT, lat_dev):
            at = 6 * (r - HALF_LAT)
            colf[at : at + 6, 0:C] = of[o, r, lon_dev : lon_dev + HALF_LON, :]
        ocs[o] = colf[0:96, 0:C].astype(BF16)
        copies = [send(ocs.at[o], ocr.at[o], os_.at[o, 0], or_.at[o, 0], forth[0]), rows, corner]
        for w in range(nwin - wcols):
            if w % wcols < wcols - 1:
                place_window(w)
        return copies

    def finish(o, copies, out):
        copies[1].wait_recv()
        for r in range(HALF_LAT):
            of[o, r, 0:lon_dev, :] = orr[o, r].astype(F32)
        copies[0].wait_recv()
        colf[0:96, 0:C] = ocr[o].astype(F32)
        for r in range(HALF_LAT, lat_dev):
            at = 6 * (r - HALF_LAT)
            of[o, r, 0:HALF_LON, :] = colf[at : at + 6, 0:C]
        copies[2].wait_recv()
        colf[0:16, 0 : C + 128] = occ[o].astype(F32)
        for j in range(8):
            colf[16 + j // 4 : 17 + j // 4, 128 * (j % 4) : 128 * (j % 4) + 128] = colf[j : j + 1, C : C + 128]
        for r in range(HALF_LAT):
            of[o, r, 0:HALF_LON, :] = colf[6 * r : 6 * r + 6, 0:C]
        for r in range(lat_dev):
            out[r] = of[o, r, 0:lon_dev, :].astype(BF16)

    gnacc[...] = nn(mixed[0:ROWS, :], wproj[...])

    def updated_step(k, carry):
        w = idx[k]
        m = win[w, :, M0 : M0 + 128]
        res[k] = win[w, :, X0 : X0 + C] + jnp.concatenate([m] * 4, axis=1) * gnacc[rows_of(k), :]
        return carry

    lax.fori_loop(0, SLOTS // 3, by_three(updated_step), 0)
    out_copies = [window_back(0, X0)]

    ntp[...] = nt(perm[...], normed[...]).astype(BF16)
    mtp[...] = nt(perm[...], mixed[...]).astype(BF16)
    halo_land(1, dlanes, dcopies)
    for w in outer:
        cut(w, dlanes)
    grad_mixed(EARLY, SLOTS)

    def chunk_start(c, lhs, rhs):
        asend, arecv, own = chunks[c][0:3]
        right = rhs[...] if c == 0 else rhs[:, 384 * (c - 1) : 384 * c]
        other = pl.ds(pl.multiple_of((1 - core) * half, half), half)
        mine = pl.ds(pl.multiple_of(core * half, half), half)
        asend[...] = nn(lhs[other, :], right).astype(BF16)
        copy = send(asend, arecv, as_.at[c], ar.at[c], partner)
        own[...] = nn(lhs[mine, :], right)
        return [copy]

    def chunk_y(c, copies):
        asend, arecv, own, ysend, yrecv = chunks[c][0:5]
        copies[0].wait_recv()
        s = own[...] + arecv[...].astype(F32)
        own[...] = s
        ysend[...] = s.astype(BF16)
        out = []
        for d in range(1, ny):
            start = pl.multiple_of(((y + d) % ny) * ysz, ysz)
            out.append(
                send(ysend.at[pl.ds(start, ysz)], yrecv.at[d - 1], ys.at[c, d - 1], yr.at[c, d - 1], ypeer[d - 1])
            )
        return out

    def chunk_x(c, copies):
        own, ysend, yrecv, xsend, xrecv, xown = chunks[c][2:8]
        s = own[pl.ds(pl.multiple_of(y * ysz, ysz), ysz), :]
        for d in range(1, ny):
            copies[d - 1].wait_recv()
            s = s + yrecv[d - 1].astype(F32)
        top, low_half = s[0 : ysz // 2], s[ysz // 2 : ysz]
        first = xh == 0
        xsend[...] = jnp.where(first, low_half, top).astype(BF16)
        xown[...] = jnp.where(first, top, low_half)
        return [send(xsend, xrecv, xs.at[c], xr.at[c], xpeer)]

    def blocks_before(c):
        g = next(i for i, members in enumerate(GROUPS) if c in members)
        return g, sum(cols[m] // 128 for m in GROUPS[g] if m < c)

    def chunk_z(c, copies):
        xsend, xrecv, xown = chunks[c][5:8]
        g, first = blocks_before(c)
        zown = groups[g][0]
        copies[0].wait_recv()
        s = xown[...] + xrecv[...].astype(F32)
        for j in range(nz):
            part = s[share * j : share * j + share]
            for q in range(cols[c] // 128):
                at = share * (first + q)
                zown[j, at : at + share, :] = part[:, 128 * q : 128 * q + 128]

    def group_send(g):
        zown, zsend, zrecv = groups[g]
        zsend[...] = zown[...].astype(BF16)
        return [
            send(zsend.at[(z + d) % nz], zrecv.at[d - 1], zs.at[g, d - 1], zr.at[g, d - 1], zpeer[d - 1])
            for d in range(1, nz)
        ]

    def group_end(g, copies):
        zown, zsend, zrecv = groups[g]
        s = zown[z]
        for i, copy in enumerate(copies):
            copy.wait_recv()
            s = s + zrecv[i].astype(F32)
        for c in GROUPS[g]:
            first = blocks_before(c)[1]
            for q in range(cols[c] // 128):
                at = share * (first + q)
                block = s[at : at + share]
                if c == 0:
                    gproj[:, 128 * q : 128 * q + 128] = block
                else:
                    gqkv[:, C * q + 128 * (c - 1) : C * q + 128 * c] = block

    st = {}
    st[0] = chunk_start(0, mtp, gz)

    for p in range(PAIRS):
        backward([(k, p) for k in range(EARLY, SLOTS)])
        st[p] = chunk_y(p, st[p])
        st[p + 1] = chunk_start(p + 1, ntp, dp3)
        if p >= 2:
            st[p - 2] = chunk_x(p - 2, st[p - 2])

    smy, sma, smx, smz = sums
    stacked = jnp.concatenate([bacc[h // 2, :, 128 * (h % 2) : 128 * (h % 2) + 128] for h in range(HEADS)], axis=0)
    by_place = sum(nn(v, self_[...]) for v in pieces(stacked, 2))
    by_place = jnp.concatenate([by_place[TP * h : TP * h + TP] for h in range(HEADS)], axis=1)
    spread = sum(nn(selrt[:, 0:TP], v) for v in pieces(by_place, 2))
    for h in range(HEADS):
        wide = jnp.concatenate([spread[:, 128 * h : 128 * h + 128], jnp.zeros((128, 128), F32)], axis=1)
        sums[0][core * ny + y, h : h + 1, 0:256] = jnp.sum(pltpu.roll(wide, 0, 1, stride=1, stride_axis=0), axis=0, keepdims=True)
    for part in range(2):
        rows = slice(part * ROWS // 2, (part + 1) * ROWS // 2)
        gnacc[rows, :] = nt(dp3[rows, :], wqkv[...])
        if part == 0:
            st[4] = chunk_y(4, st[4])
            st[2] = chunk_x(2, st[2])

    def norm_back(k, total):
        w = idx[k]
        rows = rows_of(k)
        gn = gnacc[rows, :]
        hat = xhat[rows, :]
        g = gn * gain
        prod = g * hat
        mid = g - jnp.mean(g, axis=1, keepdims=True) - hat * jnp.mean(prod, axis=1, keepdims=True)
        inv = jnp.concatenate([invd[rows, :]] * 4, axis=1)
        res[k] = win[w, :, D0 : D0 + C] + inv * mid
        return total + jnp.sum(gn * hat, axis=0, keepdims=True)

    gsum = lax.fori_loop(0, SLOTS // 3, by_three(norm_back), jnp.zeros((1, C), F32))
    slot = core * ny + y
    smy[slot, 4:8, 256:384] = jnp.zeros((4, 128), F32)
    for j in range(4):
        smy[slot, j : j + 1, 256:384] = gsum[:, 128 * j : 128 * j + 128]
    sm = smy.at[slot]
    copies = [
        send(sm, sm, ss.at[i], sr.at[i], to) for i, to in enumerate([partner] + ypeer + crossy)
    ]
    out_copies.append(window_back(1, D0))
    st[3] = chunk_x(3, st[3])
    chunk_z(0, st[0])
    chunk_z(1, st[1])
    st[4] = chunk_x(4, st[4])
    for copy in copies:
        copy.wait_recv()
    acc = smy[0]
    for j in range(1, 2 * ny):
        acc = acc + smy[j]
    sma[...] = acc
    copy = send(sma, smx, ss.at[2 * ny - 1], sr.at[2 * ny - 1], xpeer)
    chunk_z(2, st[2])
    group0 = group_send(0)
    finish(0, out_copies[0], upd)
    stores[0].start()
    chunk_z(3, st[3])
    chunk_z(4, st[4])
    group1 = group_send(1)
    copy.wait_recv()
    smz[z] = sma[...] + smx[...]
    copies = [
        send(smz.at[z], smz.at[z], ss.at[2 * ny + d - 1], sr.at[2 * ny + d - 1], zpeer[d - 1]) for d in range(1, nz)
    ]
    group_end(0, group0)
    finish(1, out_copies[1], gin)
    stores[1].start()
    group_end(1, group1)
    for copy in copies:
        copy.wait_recv()
    acc = smz[0]
    for j in range(1, nz):
        acc = acc + smz[j]
    bias_out[...] = acc[:, 0:REL]
    for j in range(4):
        gain_out[:, 128 * j : 128 * j + 128] = acc[j : j + 1, 256:384]
    for store in stores[2:]:
        store.start()
    for copy in sends:
        copy.wait_send()
    for store in stores:
        store.wait()


def hand_over(*refs):
    arrived, left = refs[18:20]
    steps = []
    for i in range(6):
        rows = refs[i].shape[0]
        size = 3 if i < 2 else rows
        steps += [(i, pl.ds(start, size)) for start in range(0, rows, size)]
    fetches = [
        pltpu.make_async_copy(refs[i].at[at], refs[12 + i].at[at], arrived.at[n]) for n, (i, at) in enumerate(steps)
    ]
    stores = [
        pltpu.make_async_copy(refs[12 + i].at[at], refs[6 + i].at[at], left.at[n]) for n, (i, at) in enumerate(steps)
    ]
    for fetch in fetches:
        fetch.start()
    for fetch, store in zip(fetches, stores):
        fetch.wait()
        store.start()
    for store in stores:
        store.wait()


def constants(ny, nx, nz):
    share = C // (ny * nx * nz * 2)
    perm = np.zeros((C, C), np.float32)
    for core in range(2):
        for y in range(ny):
            for xh in range(nx):
                for z in range(nz):
                    to = (((core * ny + y) * nx + xh) * nz + z) * share
                    start = (((y * nx + xh) * nz + z) * 2 + core) * share
                    perm[to + np.arange(share), start + np.arange(share)] = 1
    a = np.arange(T)
    pa = (a // WIN_LON) * (2 * WIN_LON - 1) + a % WIN_LON
    selrt = np.zeros((128, 128), np.float32)
    selrt[126 - pa, a] = 1
    self_ = np.zeros((128, 128), np.float32)
    self_[a, pa] = 1
    return perm, self_, self_.T, selrt


def solution(mesh):
    nlon, nlat = mesh.shape["lon"], mesh.shape["lat"]
    nx, nz = 2, nlat // 2
    ny = nlon // nx
    nxz = nx * nz
    half = C // 2
    ysz = half // ny
    share = ysz // nxz
    cols = [C] + [384] * PAIRS
    lat_dev, lon_dev = 18, 48
    nwin = 12
    vm = pltpu.VMEM
    dma = lambda *s: pltpu.SemaphoreType.DMA(s)
    perm, self_, selft, selrt = (jnp.asarray(v, BF16) for v in constants(ny, nx, nz))

    def on_device(fields, grad_out, layernorm_gain, qkv_weight, proj_weight, bias_table, sea_mask):
        shapes = (
            jax.ShapeDtypeStruct((lat_dev, lon_dev, C), BF16),
            jax.ShapeDtypeStruct((lat_dev, lon_dev, C), BF16),
            jax.ShapeDtypeStruct((1, C), F32),
            jax.ShapeDtypeStruct((HEADS, REL), F32),
            jax.ShapeDtypeStruct((share, 3 * C), F32),
            jax.ShapeDtypeStruct((share, C), F32),
        )
        scratch = [
            vm((lat_dev, lon_dev, C), BF16),
            vm((lat_dev, lon_dev), jnp.int32),
            vm((lat_dev, lon_dev, C), BF16),
            vm((HEADS, REL), F32),
            vm((128, 128), BF16),
            vm((128, 128), BF16),
            vm((128, 128), BF16),
            vm((1, C), F32),
            vm((C, 3 * C), BF16),
            vm((C, C), BF16),
            vm((C, C), BF16),
        ]
        scratch += [vm(v.shape, v.dtype) for v in shapes]
        scratch += [
            vm((lat_dev + 3, 56, FW), F32),
            vm((nwin, TP, FW), F32),
            vm((112, FW), F32),
        ]
        for wide in (C, C):
            scratch += [
                vm((112, wide), BF16),
                vm((112, wide), BF16),
                vm((3, lon_dev, wide), BF16),
                vm((32, wide), BF16),
            ]
        scratch += [vm((lat_dev, lon_dev), jnp.int32)] * 3
        scratch += [
            pltpu.SMEM((16,), jnp.int32),
            vm((HEADS, 256), F32),
            vm((PAIRS, TP, 256), F32),
            vm((SLOTS, TP, 128), F32),
            vm((ROWS, C), F32),
            vm((ROWS, 128), F32),
            vm((RP, C), BF16),
            vm((RP, C), BF16),
            vm((ROWS, C), BF16),
            vm((ROWS, 3 * C), BF16),
            vm((RP, C), BF16),
            vm((C, RP), BF16),
            vm((C, RP), BF16),
            vm((SLOTS * PAIRS, TP, 256), F32),
            vm((RP, 3 * C), BF16),
            vm((ROWS, C), F32),
            vm((PAIRS, TP, 256), F32),
            vm((SLOTS, TP, C), F32),
            vm((2, lat_dev + 3, 56, C), F32),
            vm((2, 96, C), BF16),
            vm((2, 3, lon_dev, C), BF16),
            vm((2, 16, C + 128), BF16),
            vm((2, 96, C), BF16),
            vm((2, 3, lon_dev, C), BF16),
            vm((2, 16, C + 128), BF16),
        ]
        for n in cols:
            scratch += [
                vm((half, n), BF16),
                vm((half, n), BF16),
                vm((half, n), F32),
                vm((half, n), BF16),
                vm((ny - 1, ysz, n), BF16),
                vm((ysz // 2, n), BF16),
                vm((ysz // 2, n), BF16),
                vm((ysz // 2, n), F32),
            ]
        for members in GROUPS:
            rows = -(-share * sum(cols[c] // 128 for c in members) // 16) * 16
            scratch += [vm((nz, rows, 128), F32), vm((nz, rows, 128), BF16), vm((nz - 1, rows, 128), BF16)]
        sm = (8, 384)
        scratch += [vm((2 * ny,) + sm, F32), vm(sm, F32), vm(sm, F32), vm((nz,) + sm, F32)]
        nc = len(cols)
        small = 2 * ny + nz
        scratch += [
            dma(2, 3), dma(2, 3), dma(3), dma(3), dma(2, 3), dma(2, 3), dma(nc), dma(nc), dma(nc, ny - 1),
            dma(nc, ny - 1), dma(nc), dma(nc), dma(nc, nz - 1), dma(nc, nz - 1), dma(small), dma(small), dma(23), dma(6),
        ]
        anywhere = pl.BlockSpec(memory_space=pl.ANY)
        outs = pl.pallas_call(
            functools.partial(kernel, (ny, nx, nz), cols),
            out_shape=shapes,
            in_specs=[anywhere] * 11,
            out_specs=(anywhere,) * 6,
            scratch_shapes=scratch,
            compiler_params=pltpu.CompilerParams(
                collective_id=0, has_side_effects=True, vmem_limit_bytes=60 * 1024 * 1024
            ),
        )(
            fields, sea_mask, grad_out, bias_table, self_, selft, selrt,
            layernorm_gain.reshape(1, C), qkv_weight, proj_weight, perm,
        )
        outs = pl.pallas_call(
            hand_over,
            out_shape=shapes,
            in_specs=[anywhere] * 6,
            out_specs=(anywhere,) * 6,
            scratch_shapes=[vm(v.shape, v.dtype) for v in shapes] + [dma(16), dma(16)],
            compiler_params=pltpu.CompilerParams(vmem_limit_bytes=60 * 1024 * 1024),
        )(*outs)
        updated, grad_in, grad_gain, grad_bias, grad_qkv, grad_proj = outs
        return (updated, grad_in, grad_gain.reshape(C), grad_bias, grad_qkv, grad_proj)

    grid = P(("batch", "lat"), "lon", None)
    return jax.shard_map(
        on_device,
        mesh=mesh,
        in_specs=(grid, grid, P(), P(), P(), P(), P(("batch", "lat"), "lon")),
        out_specs=(
            grid,
            grid,
            P("batch"),
            P("batch", None),
            P(("batch", "lon", "lat"), None),
            P(("batch", "lon", "lat"), None),
        ),
        check_vma=False,
    )
```
